32 devices in a mesh: rows: 4 (over y, x), cols: 8 (over z, core).
Axes of the slice: x: 2, y: 2, z: 4, core: 2. Of those that a mesh axis runs over, the one named last changes fastest.
Arguments:
- model: bfloat16 [64, 512, 512], P(('rows', 'cols')), may hold values from -6 to 6
- dirty: bfloat16 [64, 512, 512], P(('rows', 'cols')), may hold values from -6 to 6
- psf: bfloat16 [64, 256, 256], P(('rows', 'cols')), may hold values from -0.0234375 to 0.0234375
- step_size: float32 [64], P(('rows', 'cols')), may hold values from 0.2 to 1
- gain: float32 [64], replicated, may hold values from 0.1 to 1.9
- w_in: bfloat16 [64, 256], replicated, may hold values from -0.75 to 0.75
- b_in: float32 [256], replicated, may hold values from -3 to 3
- w_out: bfloat16 [256, 64], replicated, may hold values from -0.375 to 0.375
- kernel: float32 [3, 3, 64], replicated, may hold values from -2 to 2
Outputs:
- updated_model: bfloat16 [64, 512, 512], P(('rows', 'cols'))
The draws below stay inside these ranges and needn't reach their ends.
All inputs are finite; a program needn't handle non-finite values.
Results may differ from the reference program's by a relative error of at most 0.0095.
Values may be sent and summed in bfloat16 or wider, within the bound.
No kernel may reach another device: no remote copies, remote signals or barrier semaphores. Data moves between devices by JAX's collectives and lax.ppermute only.
A program may use at most 64 MiB of HBM per device.

```python
import math
import jax
import jax.numpy as jnp
from jax import lax

IMG = 512
FFT = 1024
PSF = 256
HIDDEN_SIZE = 256
CHANNELS = 64


def block_scale(stream_key, extent, pieces, low, top_value):
    def one(position, shards_of):
        steps = jax.random.uniform(jax.random.fold_in(jax.random.fold_in(stream_key, 6), position), (shards_of,), jnp.float32, low / len(pieces), top_value / len(pieces))
        return jnp.repeat(jnp.exp(steps), extent[position] // shards_of).reshape((-1,) + (1,) * (len(extent) - position - 1))

    level = one(*pieces[0])
    for cut in pieces[1:]:
        level = level * one(*cut)
    return level


def bell_draw(own_key, dims, scale, bound, cuts=(), held_as=jnp.bfloat16):
    level = block_scale(own_key, dims, cuts, -0.22, 0.18) if cuts else 1.0
    entries = jax.random.normal(own_key, dims, jnp.float32) * scale * level
    return jnp.minimum(jnp.maximum(entries, -bound), bound).astype(held_as)


def setup_inputs(seed: int = 0) -> dict:
    arg_keys = jax.random.split(jax.random.key(seed), 10)
    return {
        "model": bell_draw(arg_keys[0], (CHANNELS, IMG, IMG), 1.0, 6.0, ((0, 32),)),
        "dirty": bell_draw(arg_keys[1], (CHANNELS, IMG, IMG), 1.0, 6.0, ((0, 32),)),
        "psf": bell_draw(arg_keys[2], (CHANNELS, PSF, PSF), (PSF * PSF) ** -0.5, 0.0234375, ((0, 32),)),
        "step_size": jnp.clip(jnp.exp(math.log(1.0) - 1.609438 * jax.random.uniform(arg_keys[3], (CHANNELS,), jnp.float32) ** block_scale(arg_keys[3], (CHANNELS,), ((0, 32),), -0.2, 0.2)), 0.2, 1.0),
        "gain": jnp.clip(1.0 + 0.18 * jax.random.normal(arg_keys[4], (CHANNELS,), jnp.float32), 0.1, 1.9),
        "w_in": bell_draw(arg_keys[5], (CHANNELS, HIDDEN_SIZE), CHANNELS ** -0.5, 0.75),
        "b_in": bell_draw(arg_keys[6], (HIDDEN_SIZE,), 0.5, 3.0, (), jnp.float32),
        "w_out": bell_draw(arg_keys[7], (HIDDEN_SIZE, CHANNELS), HIDDEN_SIZE ** -0.5, 0.375),
        "kernel": bell_draw(arg_keys[8], (3, 3, CHANNELS), 9 ** -0.5, 2.0, (), jnp.float32),
    }


def tables(length, count, offset):
    freq = jnp.arange(length, dtype=jnp.int32)[:, None]
    place = jnp.arange(count, dtype=jnp.int32)[None, :] + offset
    phase = (freq * place % length).astype(jnp.float32) * (2.0 * math.pi / length)
    return (jnp.cos(phase).astype(jnp.bfloat16), jnp.sin(phase).astype(jnp.bfloat16))

def spectrum(plane, cos_t, sin_t):
    real_a = jnp.dot(cos_t, plane, preferred_element_type=jnp.float32).astype(jnp.bfloat16)
    imag_a = (-jnp.dot(sin_t, plane, preferred_element_type=jnp.float32)).astype(jnp.bfloat16)
    real_s = jnp.dot(real_a, cos_t.T, preferred_element_type=jnp.float32) + jnp.dot(imag_a, sin_t.T, preferred_element_type=jnp.float32)
    imag_s = jnp.dot(imag_a, cos_t.T, preferred_element_type=jnp.float32) - jnp.dot(real_a, sin_t.T, preferred_element_type=jnp.float32)
    return (real_s, imag_s)

def convolve(plane, spread_fn, image_tabs, psf_tabs, window_tabs, length):
    real_x, imag_x = spectrum(plane, image_tabs[0], image_tabs[1])
    real_q, imag_q = spectrum(spread_fn, psf_tabs[0], psf_tabs[1])
    factor = 1.0 / (length * length)
    real_p = ((real_x * real_q - imag_x * imag_q) * factor).astype(jnp.bfloat16)
    imag_p = ((real_x * imag_q + imag_x * real_q) * factor).astype(jnp.bfloat16)
    cos_w, sin_w = window_tabs
    real_b = (jnp.dot(real_p, cos_w, preferred_element_type=jnp.float32) - jnp.dot(imag_p, sin_w, preferred_element_type=jnp.float32)).astype(jnp.bfloat16)
    imag_b = (jnp.dot(real_p, sin_w, preferred_element_type=jnp.float32) + jnp.dot(imag_p, cos_w, preferred_element_type=jnp.float32)).astype(jnp.bfloat16)
    return jnp.dot(cos_w.T, real_b, preferred_element_type=jnp.float32) - jnp.dot(sin_w.T, imag_b, preferred_element_type=jnp.float32)

def prior_mix(pixels, gain, w_in, b_in, w_out):
    values = pixels.astype(jnp.float32)
    power = lax.optimization_barrier(jnp.mean(values * values, axis=0, keepdims=True))
    normed = (values / jnp.sqrt(power + 1e-06) * gain[:, None]).astype(jnp.bfloat16)
    inner = jnp.dot(w_in.T, normed, preferred_element_type=jnp.float32) + b_in[:, None]
    hidden = jax.nn.gelu(inner, approximate=True).astype(jnp.bfloat16)
    return jnp.dot(w_out.T, hidden, preferred_element_type=jnp.float32).astype(jnp.bfloat16)

def spread(padded, kernel, height, width):
    total = jnp.zeros((padded.shape[0], height, width), jnp.float32)
    for row_tap in range(3):
        for col_tap in range(3):
            total = total + kernel[row_tap, col_tap][:, None, None] * padded[:, row_tap:row_tap + height, col_tap:col_tap + width].astype(jnp.float32)
    return total

def reference(model, dirty, psf, step_size, gain, w_in, b_in, w_out, kernel):
    image_tabs = tables(FFT, IMG, 0)
    psf_tabs = tables(FFT, PSF, 0)
    window_tabs = tables(FFT, IMG, PSF // 2)

    def one_channel(items):
        plane, dirty_plane, psf_plane, rate = items
        blurred = convolve(plane, psf_plane, image_tabs, psf_tabs, window_tabs, FFT)
        return (plane.astype(jnp.float32) + rate * (dirty_plane.astype(jnp.float32) - blurred)).astype(jnp.bfloat16)
    stepped = lax.map(one_channel, (model, dirty, psf, step_size))
    mixed = prior_mix(stepped.reshape(CHANNELS, IMG * IMG), gain, w_in, b_in, w_out).reshape(CHANNELS, IMG, IMG)
    padded = jnp.pad(mixed, ((0, 0), (1, 1), (1, 1)))
    return (stepped.astype(jnp.float32) + spread(padded, kernel, IMG, IMG)).astype(jnp.bfloat16)
```

```python
import math

import jax
import jax.numpy as jnp
import ml_dtypes
import numpy as np
from jax import lax
from jax.experimental import pallas as pl
from jax.experimental.pallas import tpu as pltpu
from jax.sharding import PartitionSpec as P

BAND = 16
VMEM_BYTES = 56 * 1024 * 1024


def trig(places, half, length):
    phase = (2 * np.arange(half)[:, None] + 1) * places[None, :] % (2 * length)
    angle = phase * (math.pi / length)
    return np.cos(angle), np.sin(angle)


def tables(img, psf):
    length = img + psf // 2
    half = length // 2
    pad = -half % 128
    cos_t, sin_t = trig(np.arange(img), half, length)
    cos_w, sin_w = trig(np.arange(img) + psf // 2, half, length)

    def columns(table, low, high):
        return np.pad(table.T, ((0, 0), (low, high)))

    right = [
        np.concatenate([columns(cos_t, *side), columns(sin_t, *side)], axis=1)
        for side in ((0, pad), (pad, 0))
    ]
    left = np.concatenate([cos_t, sin_t], axis=0)
    back_left = np.concatenate([cos_w, sin_w], axis=0).T
    back_right = [
        np.concatenate([columns(cos_w, *side), columns(sin_w, *side)], axis=1).T
        for side in ((0, pad), (pad, 0))
    ]
    return [
        jnp.asarray(table.astype(ml_dtypes.bfloat16))
        for table in (*right, left, back_left, *back_right)
    ]


def dot(a, b):
    return jnp.dot(a, b, preferred_element_type=jnp.float32)


def conv_kernel(
    rate, model, dirty, psf, right_a, right_b, left, back_left, back_a, back_b, out,
    cols_x, cols_q, spec_x, spec_q, prod, rows_y,
):
    img = model.shape[1]
    half = left.shape[0] // 2
    wide = right_a.shape[1] // 2
    both = 2 * half
    shared = 2 * wide - both
    own = wide - shared
    bands, parts, _, band, part = out.shape

    def columns(source, count, target):
        step = 128

        @pl.loop(0, count // step)
        def _(i):
            rows = pl.ds(pl.multiple_of(i * step, step), step)
            depth = source.shape[2]
            first = dot(source[0, rows, :], right_a[:depth, :])
            second = dot(source[1, rows, :], right_b[:depth, :])
            for k in range(2):
                a = first[:, k * wide : (k + 1) * wide]
                b = second[:, k * wide : (k + 1) * wide]
                at = k * both
                target[rows, at : at + own] = a[:, :own].astype(jnp.bfloat16)
                target[rows, at + own : at + wide] = (a[:, own:] + b[:, :shared]).astype(jnp.bfloat16)
                target[rows, at + wide : at + both] = b[:, shared:].astype(jnp.bfloat16)

    columns(psf, psf.shape[1], cols_q)
    columns(model, img, cols_x)

    for k in range(2):
        rows = pl.ds(k * half, half)
        spec_q[rows, :] = dot(left[rows, : psf.shape[1]], cols_q[...])
        spec_x[rows, :] = dot(left[rows, :], cols_x[...])

    @pl.loop(0, half // 16)
    def _(i):
        c = pl.ds(pl.multiple_of(i * 16, 16), 16)
        s = pl.ds(pl.multiple_of(half + i * 16, 16), 16)
        for j in range(0, both, 128):
            lc, ls = slice(j, j + 128), slice(both + j, both + j + 128)
            xcc, xcs, xsc, xss = spec_x[c, lc], spec_x[c, ls], spec_x[s, lc], spec_x[s, ls]
            qcc, qcs, qsc, qss = spec_q[c, lc], spec_q[c, ls], spec_q[s, lc], spec_q[s, ls]
            prod[c, lc] = ((xcc * qcc + xss * qss) - (xsc * qsc + xcs * qcs)).astype(jnp.bfloat16)
            prod[s, ls] = ((xcc * qss + xss * qcc) + (xsc * qcs + xcs * qsc)).astype(jnp.bfloat16)
            prod[s, lc] = ((xcc * qsc - xss * qcs) + (xsc * qcc - xcs * qss)).astype(jnp.bfloat16)
            prod[c, ls] = ((xcc * qcs - xss * qsc) + (xcs * qcc - xsc * qss)).astype(jnp.bfloat16)

    for k in range(2):
        rows = pl.ds(k * img // 2, img // 2)
        rows_y[rows, :] = dot(back_left[rows, :], prod[...]).astype(jnp.bfloat16)

    factor = 4.0 / (both * both)
    step = 128

    @pl.loop(0, img // step)
    def _(i):
        rows = pl.ds(pl.multiple_of(i * step, step), step)
        for ch, table in ((0, back_a), (1, back_b)):
            at = ch * (both - wide)
            inner = jnp.concatenate(
                [rows_y[rows, at : at + wide], rows_y[rows, both + at : both + at + wide]], axis=1
            )
            blurred = dot(inner, table[...]) * factor
            plane = model[ch, rows, :].astype(jnp.float32)
            stepped = plane + rate[ch] * (dirty[ch, rows, :].astype(jnp.float32) - blurred)
            stepped = stepped.astype(jnp.bfloat16)
            for p in range(parts):
                piece = stepped[:, p * part : (p + 1) * part].reshape(step // band, band, part)
                out[pl.ds(i * (step // band), step // band), p, ch] = piece


def shuffle_table():
    index = np.arange(BAND * BAND)
    source = (index % BAND) * BAND + index // BAND
    table = np.zeros((BAND * BAND, BAND * BAND), np.float32)
    table[index, source] = 1.0
    return jnp.asarray(table.astype(ml_dtypes.bfloat16))


def mix_kernel(gain, b_in, w_in_t, w_out_t, swap, tiles, out, normed, mixed):
    channels, band, part = tiles.shape
    groups = channels // band
    power = jnp.zeros((band, part), jnp.float32)
    for c in range(channels):
        v = tiles[c].astype(jnp.float32)
        power = power + v * v
    inverse = lax.rsqrt(power * (1.0 / channels) + 1e-06)
    for g in range(groups):
        rows = []
        for c in range(g * band, (g + 1) * band):
            rows.append((tiles[c].astype(jnp.float32) * inverse * gain[c]).astype(jnp.bfloat16))
        swapped = dot(swap[...], jnp.concatenate(rows, axis=0)).astype(jnp.bfloat16)
        normed[:, g * band : (g + 1) * band, :] = swapped.reshape(band, band, part)

    a = math.sqrt(2.0 / math.pi)

    @pl.loop(0, band)
    def _(r):
        inner = dot(w_in_t[...], normed[r]) + b_in[...]
        scaled = inner * (a + (a * 0.044715) * (inner * inner))
        hidden = (0.5 * inner * (1.0 + jnp.tanh(scaled))).astype(jnp.bfloat16)
        mixed[r] = dot(w_out_t[...], hidden).astype(jnp.bfloat16)

    for g in range(groups):
        block = mixed[:, g * band : (g + 1) * band, :].reshape(band * band, part)
        swapped = dot(swap[...], block).astype(jnp.bfloat16)
        out[g * band : (g + 1) * band] = swapped.reshape(band, band, part)


def spread_kernel(first, taps, stepped, mixed, out, above, below):
    channels = taps.shape[0] // 9
    bands, parts, ch_dev, band, part = stepped.shape
    img = bands * band
    lane = lax.broadcasted_iota(jnp.int32, (band, img), 1)
    zero = jnp.zeros((8, img), jnp.float32)

    def plane(source, b, ch):
        if parts == 1:
            return source[b, 0, ch].astype(jnp.float32)
        pieces = [source[b, p, ch] for p in range(parts)]
        return jnp.concatenate(pieces, axis=1).astype(jnp.float32)

    for ch in range(ch_dev):
        k = [[taps[(3 * i + j) * channels + first[0] + ch] for j in range(3)] for i in range(3)]
        above[0:8, :] = zero
        below[img : img + 8, :] = zero

        @pl.loop(0, bands)
        def _(b):
            x = plane(mixed, b, ch)
            low = jnp.where(lane == 0, 0.0, pltpu.roll(x, 1, 1))
            high = jnp.where(lane == img - 1, 0.0, pltpu.roll(x, img - 1, 1))
            at = pl.multiple_of(b * band, band)
            above[pl.ds(at + 8, band), :] = k[0][0] * low + k[0][1] * x + k[0][2] * high
            below[pl.ds(at, band), :] = k[2][0] * low + k[2][1] * x + k[2][2] * high

        @pl.loop(0, bands)
        def _(b):
            x = plane(mixed, b, ch)
            low = jnp.where(lane == 0, 0.0, pltpu.roll(x, 1, 1))
            high = jnp.where(lane == img - 1, 0.0, pltpu.roll(x, img - 1, 1))
            at = pl.multiple_of(b * band, band)
            top = above[pl.ds(at, band + 8), :][7 : 7 + band]
            bottom = below[pl.ds(at, band + 8), :][1 : 1 + band]
            middle = k[1][0] * low + k[1][1] * x + k[1][2] * high
            total = plane(stepped, b, ch) + (top + middle + bottom)
            out[ch, pl.ds(at, band), :] = total.astype(jnp.bfloat16)


VMEM = pl.BlockSpec(memory_space=pltpu.VMEM)
SMEM = pl.BlockSpec(memory_space=pltpu.SMEM)
PARAMS = pltpu.CompilerParams(vmem_limit_bytes=VMEM_BYTES)


def exchange(blocks):
    return lax.all_to_all(blocks, ("rows", "cols"), split_axis=0, concat_axis=0, tiled=True)


def local(model, dirty, psf, step_size, gain, w_in, b_in, w_out, kernel):
    ch_dev, img, _ = model.shape
    psf_len = psf.shape[1]
    assert ch_dev == 2
    n_dev = lax.axis_size("rows") * lax.axis_size("cols")
    channels = gain.shape[0]
    hidden = b_in.shape[0]
    bands = img // BAND
    part = img * img // (n_dev * BAND)
    parts = img // part
    half = (img + psf_len // 2) // 2
    bf16, f32 = jnp.bfloat16, jnp.float32

    stepped = pl.pallas_call(
        conv_kernel,
        out_shape=jax.ShapeDtypeStruct((bands, parts, ch_dev, BAND, part), bf16),
        in_specs=[SMEM] + [VMEM] * 9,
        out_specs=VMEM,
        scratch_shapes=[
            pltpu.VMEM((img, 4 * half), bf16),
            pltpu.VMEM((psf_len, 4 * half), bf16),
            pltpu.VMEM((2 * half, 4 * half), f32),
            pltpu.VMEM((2 * half, 4 * half), f32),
            pltpu.VMEM((2 * half, 4 * half), bf16),
            pltpu.VMEM((img, 4 * half), bf16),
        ],
        compiler_params=PARAMS,
        name="conv",
    )(step_size, model, dirty, psf, *tables(img, psf_len))

    tiles = exchange(stepped.reshape(n_dev, ch_dev, BAND, part)).reshape(channels, BAND, part)

    mixed = pl.pallas_call(
        mix_kernel,
        out_shape=jax.ShapeDtypeStruct((channels, BAND, part), bf16),
        in_specs=[SMEM] + [VMEM] * 5,
        out_specs=VMEM,
        scratch_shapes=[
            pltpu.VMEM((BAND, channels, part), bf16),
            pltpu.VMEM((BAND, channels, part), bf16),
        ],
        compiler_params=PARAMS,
        name="mix",
    )(gain, b_in[:, None], w_in.T, w_out.T, shuffle_table(), tiles)

    returned = exchange(mixed.reshape(n_dev, ch_dev, BAND, part))
    position = lax.axis_index(("rows", "cols")).astype(jnp.int32) * ch_dev

    return pl.pallas_call(
        spread_kernel,
        out_shape=jax.ShapeDtypeStruct((ch_dev, img, img), bf16),
        in_specs=[SMEM, SMEM, VMEM, VMEM],
        out_specs=VMEM,
        scratch_shapes=[
            pltpu.VMEM((img + 8, img), f32),
            pltpu.VMEM((img + 8, img), f32),
        ],
        compiler_params=PARAMS,
        name="spread",
    )(position[None], kernel.reshape(-1), stepped, returned.reshape(stepped.shape))


def solution(mesh):
    return jax.shard_map(
        local,
        mesh=mesh,
        in_specs=(
            P(("rows", "cols"), None, None),
            P(("rows", "cols"), None, None),
            P(("rows", "cols"), None, None),
            P(("rows", "cols")),
            P(),
            P(),
            P(),
            P(),
            P(),
        ),
        out_specs=P(("rows", "cols"), None, None),
        check_vma=False,
    )
```

```python
import math

import jax
import jax.numpy as jnp
import ml_dtypes
import numpy as np
from jax import lax
from jax.experimental import pallas as pl
from jax.experimental.pallas import tpu as pltpu
from jax.sharding import PartitionSpec as P

BAND = 16
CHUNKS = 2
MIB = 1024 * 1024
BF16, F32 = jnp.bfloat16, jnp.float32


def tables(img, psf):
    length = img + psf // 2
    half = length // 2
    pad = -half % 128
    phase = (2 * np.arange(half)[:, None] + 1) * np.arange(length)[None, :] % (2 * length)
    angle = phase * (math.pi / length)
    table = np.concatenate([np.pad(f(angle), ((0, pad), (0, 0))) for f in (np.cos, np.sin)])
    table = table.astype(ml_dtypes.bfloat16)
    return jnp.asarray(table), jnp.asarray(np.ascontiguousarray(table.T))


def shuffle_table():
    index = np.arange(BAND * BAND)
    source = (index % BAND) * BAND + index // BAND
    table = np.zeros((BAND * BAND, BAND * BAND), np.float32)
    table[index, source] = 1.0
    return jnp.asarray(table.astype(ml_dtypes.bfloat16))


def dot(a, b):
    return jnp.dot(a, b, preferred_element_type=F32)


def conv_kernel(
    ch, rate, model_h, dirty_h, psf_h, table_h, turned_h, *refs
):
    outs = refs[:-12]
    (model, dirty, psf, table, turned, cols_x, cols_q, spec_x, spec_q, prod, rows_y, sems) = refs[-12:]
    img = model.shape[0]
    taps = psf.shape[0]
    shift = taps // 2
    length = table.shape[1]
    half = length // 2
    wide = table.shape[0] // 2

    copies = [
        pltpu.make_async_copy(source, target, sems.at[i])
        for i, (source, target) in enumerate(
            (
                (psf_h.at[ch], psf),
                (turned_h.at[pl.ds(0, taps)], turned.at[pl.ds(0, taps)]),
                (model_h.at[ch, pl.ds(0, img // 2)], model.at[pl.ds(0, img // 2)]),
                (turned_h.at[pl.ds(taps, length - taps)], turned.at[pl.ds(taps, length - taps)]),
                (model_h.at[ch, pl.ds(img // 2, img // 2)], model.at[pl.ds(img // 2, img // 2)]),
                (table_h.at[pl.ds(0, wide)], table.at[pl.ds(0, wide)]),
                (table_h.at[pl.ds(wide, wide)], table.at[pl.ds(wide, wide)]),
                (dirty_h.at[ch], dirty),
            )
        )
    ]
    for copy in copies:
        copy.start()

    zeros = jnp.zeros((wide - half, 2 * wide), BF16)
    prod[half:wide, :] = zeros
    prod[wide + half :, :] = zeros

    copies[0].wait()
    copies[1].wait()
    cols_q[...] = dot(psf[...], turned[:taps, :]).astype(BF16)
    copies[2].wait()
    copies[3].wait()
    right = turned[:img, :]
    cols_x[: img // 2, :] = dot(model[: img // 2, :], right).astype(BF16)
    copies[4].wait()
    cols_x[img // 2 :, :] = dot(model[img // 2 :, :], right).astype(BF16)

    for k in range(2):
        copies[5 + k].wait()
        source = slice(k * wide, k * wide + half)
        target = slice(k * half, (k + 1) * half)
        spec_q[target, :] = dot(table[source, :taps], cols_q[...])
        spec_x[target, :] = dot(table[source, :img], cols_x[...])

    @pl.loop(0, half // 16)
    def _(i):
        at = pl.multiple_of(i * 16, 16)
        c, s = pl.ds(at, 16), pl.ds(half + at, 16)
        for j in range(0, wide, 128):
            lc, ls = slice(j, j + 128), slice(wide + j, wide + j + 128)
            xcc, xcs, xsc, xss = spec_x[c, lc], spec_x[c, ls], spec_x[s, lc], spec_x[s, ls]
            qcc, qcs, qsc, qss = spec_q[c, lc], spec_q[c, ls], spec_q[s, lc], spec_q[s, ls]
            t = pl.ds(wide + at, 16)
            prod[c, lc] = ((xcc * qcc + xss * qss) - (xsc * qsc + xcs * qcs)).astype(BF16)
            prod[t, ls] = ((xcc * qss + xss * qcc) + (xsc * qcs + xcs * qsc)).astype(BF16)
            prod[t, lc] = ((xcc * qsc - xss * qcs) + (xsc * qcc - xcs * qss)).astype(BF16)
            prod[c, ls] = ((xcc * qcs - xss * qsc) + (xcs * qcc - xsc * qss)).astype(BF16)

    scale = rate[ch] * (4.0 / (length * length))
    step = 128
    for i in range(img // step):
        rows = slice(i * step, (i + 1) * step)
        back = turned[shift + i * step : shift + (i + 1) * step, :]
        rows_y[rows, :] = dot(back, prod[...]).astype(BF16)

    copies[7].wait()
    chunked = len(outs[0].shape) == 5
    bands_of, parts = outs[0].shape[:2]
    band, part = outs[0].shape[-2:]
    chunks = outs[0].shape[2] if chunked else len(outs)
    for q in range(chunks):
        for i in range(bands_of * band // step):
            at = q * bands_of * band + i * step
            rows = slice(at, at + step)
            blurred = dot(rows_y[rows, :], table[:, shift:])
            stepped = rate[ch] * dirty[rows, :].astype(F32) - scale * blurred
            stepped = (model[rows, :].astype(F32) + stepped).astype(BF16)
            where = slice(i * step // band, (i + 1) * step // band)
            for p in range(parts):
                piece = stepped[:, p * part : (p + 1) * part].reshape(step // band, band, part)
                if chunked:
                    outs[0][where, p, q] = piece
                else:
                    outs[q][where, p] = piece


def mix_kernel(chunk, gain, b_in, w_in_t, w_out_t, swap, tiles_0, tiles_1, out, bias, normed, mixed):
    sources, _, band, part = out.shape
    channels = 2 * sources
    groups = sources // band

    def tile(ch, source):
        block = tiles_0[source, chunk] if ch == 0 else tiles_1[source]
        return block.astype(F32)

    bias[...] = jnp.broadcast_to(b_in[...], bias.shape)
    power = jnp.zeros((band, part), F32)
    for source in range(sources):
        for ch in range(2):
            v = tile(ch, source)
            power = power + v * v
    inverse = lax.rsqrt(power * (1.0 / channels) + 1e-06)
    for ch in range(2):
        for g in range(groups):
            rows = [
                (tile(ch, s) * inverse * gain[2 * s + ch]).astype(BF16)
                for s in range(g * band, (g + 1) * band)
            ]
            swapped = dot(swap[...], jnp.concatenate(rows, axis=0)).astype(BF16)
            at = ch * sources + g * band
            normed[:, at : at + band, :] = swapped.reshape(band, band, part)

    a = math.sqrt(2.0 / math.pi)
    for r in range(band):
        inner = dot(w_in_t[...], normed[r]) + bias[...]
        bent = inner * (a + (a * 0.044715) * (inner * inner))
        twice = (inner + inner * jnp.tanh(bent)).astype(BF16)
        mixed[r] = (0.5 * dot(w_out_t[...], twice)).astype(BF16)

    for ch in range(2):
        for g in range(groups):
            at = ch * sources + g * band
            block = mixed[:, at : at + band, :].reshape(band * band, part)
            swapped = dot(swap[...], block).astype(BF16)
            out[g * band : (g + 1) * band, ch] = swapped.reshape(band, band, part)


def spread_kernel(chunk, chunks, first, taps, st_0, *refs):
    has_prev = chunk > 0
    last = chunk == chunks - 1
    st_1, refs = refs[:chunks], refs[chunks:]
    if has_prev:
        cur, prev, _, out, above, middle, below, result, tail, sems = refs
    else:
        cur, out, above, middle, below, result, sems = refs
    channels = taps.shape[0] // 9
    bands, parts, ch_dev, band, part = cur.shape
    img = parts * part
    lead = 2 if has_prev else 0
    count = bands + lead
    lo = 1 if has_prev else 0
    hi = count if last else count - 1
    group = 4

    if has_prev:
        fetch = pltpu.make_async_copy(prev.at[pl.ds(bands - 2, 2)], tail, sems.at[0])
        fetch.start()
        fetch.wait()

    def mixed_band(j, ch):
        source, at = (tail, j) if j < lead else (cur, j - lead)
        return jnp.concatenate([source[at, p, ch] for p in range(parts)], axis=1)

    def stepped_band(j, ch):
        at = chunk * bands + j - lead
        q, b = at // bands, at % bands
        pieces = [st_1[q][b, p] if ch else st_0[b, p, q] for p in range(parts)]
        return jnp.concatenate(pieces, axis=1)

    zero = jnp.zeros((img // 128, 8, 128), F32)
    for ch in range(ch_dev):
        k = [[taps[(3 * i + j) * channels + first[0] + ch] for j in range(3)] for i in range(3)]
        above[:, 0:8, :] = zero
        below[:, count * band : count * band + 8, :] = zero
        for start in range(0, count, group):
            js = range(start, min(start + group, count))
            size = len(js) * band
            x = jnp.concatenate([mixed_band(j, ch) for j in js], axis=0).astype(F32)
            lane = lax.broadcasted_iota(jnp.int32, (size, img), 1)
            low = jnp.where(lane == 0, 0.0, pltpu.roll(x, 1, 1))
            high = jnp.where(lane == img - 1, 0.0, pltpu.roll(x, img - 1, 1))
            at = start * band
            for target, row, off in ((above, 0, 8), (middle, 1, 0), (below, 2, 0)):
                value = k[row][0] * low + k[row][1] * x + k[row][2] * high
                for n in range(img // 128):
                    target[n, at + off : at + off + size, :] = value[:, n * 128 : (n + 1) * 128]
        for j in range(lo, hi):
            at = j * band
            base = stepped_band(j, ch).astype(F32)
            for n in range(img // 128):
                total = above[n, at + 7 : at + 7 + band, :] + below[n, at + 1 : at + 1 + band, :]
                total = total + middle[n, at : at + band, :]
                total = base[:, n * 128 : (n + 1) * 128] + total
                to = at - lo * band
                result[ch, to : to + band, n * 128 : (n + 1) * 128] = total.astype(BF16)

    rows = (hi - lo) * band
    origin = (chunk * bands - lead + lo) * band
    send = pltpu.make_async_copy(result, out.at[:, pl.ds(origin, rows), :], sems.at[1])
    send.start()
    send.wait()


VMEM = pl.BlockSpec(memory_space=pltpu.VMEM)
SMEM = pl.BlockSpec(memory_space=pltpu.SMEM)
ANY = pl.BlockSpec(memory_space=pl.ANY)
HBM = pl.BlockSpec(memory_space=pltpu.HBM)


def params(mib):
    return pltpu.CompilerParams(vmem_limit_bytes=mib * MIB)


def exchange(blocks):
    return lax.all_to_all(blocks, ("rows", "cols"), split_axis=0, concat_axis=0, tiled=True)


def local(model, dirty, psf, step_size, gain, w_in, b_in, w_out, kernel):
    ch_dev, img, _ = model.shape
    psf_len = psf.shape[1]
    assert ch_dev == 2
    n_dev = lax.axis_size("rows") * lax.axis_size("cols")
    channels = gain.shape[0]
    hidden = b_in.shape[0]
    chunks = max(1, min(CHUNKS, img * img // (n_dev * BAND * 128)))
    part = img * img // (n_dev * BAND * chunks)
    parts = img // part
    bands = img // (BAND * chunks)
    table, turned = tables(img, psf_len)
    wide, length = table.shape[0] // 2, table.shape[1]

    def conv(ch):
        one = jax.ShapeDtypeStruct((bands, parts, BAND, part), BF16)
        whole = jax.ShapeDtypeStruct((bands, parts, chunks, BAND, part), BF16)
        return pl.pallas_call(
            lambda *refs: conv_kernel(ch, *refs),
            out_shape=[one] * chunks if ch else [whole],
            in_specs=[SMEM] + [HBM] * 5,
            out_specs=[VMEM] * (chunks if ch else 1),
            scratch_shapes=[
                pltpu.VMEM((img, img), BF16),
                pltpu.VMEM((img, img), BF16),
                pltpu.VMEM((psf_len, psf_len), BF16),
                pltpu.VMEM((2 * wide, length), BF16),
                pltpu.VMEM((length, 2 * wide), BF16),
                pltpu.VMEM((img, 2 * wide), BF16),
                pltpu.VMEM((psf_len, 2 * wide), BF16),
                pltpu.VMEM((length, 2 * wide), F32),
                pltpu.VMEM((length, 2 * wide), F32),
                pltpu.VMEM((2 * wide, 2 * wide), BF16),
                pltpu.VMEM((img, 2 * wide), BF16),
                pltpu.SemaphoreType.DMA((8,)),
            ],
            compiler_params=params(24),
            cost_estimate=pl.CostEstimate(flops=4_000_000_000, bytes_accessed=4_000_000, transcendentals=0),
            name="conv",
        )(step_size, model, dirty, psf, table, turned)

    def mix(chunk, tiles_0, tiles_1):
        return pl.pallas_call(
            lambda *refs: mix_kernel(chunk, *refs),
            out_shape=jax.ShapeDtypeStruct((n_dev, ch_dev, BAND, part), BF16),
            in_specs=[SMEM] + [VMEM] * 6,
            out_specs=VMEM,
            scratch_shapes=[
                pltpu.VMEM((hidden, part), F32),
                pltpu.VMEM((BAND, channels, part), BF16),
                pltpu.VMEM((BAND, channels, part), BF16),
            ],
            compiler_params=params(16),
            cost_estimate=pl.CostEstimate(flops=4_000_000_000, bytes_accessed=2_000_000, transcendentals=0),
            name="mix",
        )(gain, b_col, w_in_t, w_out_t, swap, tiles_0, tiles_1)

    def spread(chunk, current, previous, result):
        lead = 2 if chunk else 0
        rows = (bands + lead + 1) * BAND
        out_bands = bands + (1 if chunk else 0) - (0 if chunk == chunks - 1 else 1)
        plane = pltpu.VMEM((img // 128, rows, 128), F32)
        scratch = [plane, plane, plane, pltpu.VMEM((ch_dev, out_bands * BAND, img), BF16)]
        more = []
        if chunk:
            more = [previous, result]
            scratch.append(pltpu.VMEM((2, parts, ch_dev, BAND, part), BF16))
        scratch.append(pltpu.SemaphoreType.DMA((2,)))
        return pl.pallas_call(
            lambda *refs: spread_kernel(chunk, chunks, *refs),
            out_shape=jax.ShapeDtypeStruct((ch_dev, img, img), BF16),
            in_specs=[SMEM, SMEM] + [VMEM] * (chunks + 2) + [ANY] * len(more),
            out_specs=ANY,
            input_output_aliases={chunks + 5: 0} if chunk else {},
            scratch_shapes=scratch,
            compiler_params=params(16),
            cost_estimate=pl.CostEstimate(flops=4_000_000_000, bytes_accessed=2_000_000, transcendentals=0),
            name="spread",
        )(position[None], flat_taps, st_0, *st_1, current, *more)

    (st_0,) = conv(0)
    st_0, w_in, b_in, w_out, kernel = lax.optimization_barrier((st_0, w_in, b_in, w_out, kernel))
    tiles_0 = exchange(st_0.reshape(n_dev, chunks, BAND, part))
    st_1 = conv(1)
    tiles_1 = [exchange(piece.reshape(n_dev, BAND, part)) for piece in st_1]

    b_col = b_in[:, None]
    w_in_t = w_in.reshape(n_dev, ch_dev, hidden).transpose(2, 1, 0).reshape(hidden, channels)
    w_out_t = w_out.reshape(hidden, n_dev, ch_dev).transpose(2, 1, 0).reshape(channels, hidden)
    swap = shuffle_table()
    flat_taps = kernel.reshape(-1)
    position = lax.axis_index(("rows", "cols")).astype(jnp.int32) * ch_dev

    returned = []
    for q in range(chunks):
        back = exchange(mix(q, tiles_0, tiles_1[q]))
        returned.append(back.reshape(bands, parts, ch_dev, BAND, part))
    result = None
    for q in range(chunks):
        result = spread(q, returned[q], returned[q - 1] if q else None, result)
    return result


def solution(mesh):
    return jax.shard_map(
        local,
        mesh=mesh,
        in_specs=(
            P(("rows", "cols"), None, None),
            P(("rows", "cols"), None, None),
            P(("rows", "cols"), None, None),
            P(("rows", "cols")),
            P(),
            P(),
            P(),
            P(),
            P(),
        ),
        out_specs=P(("rows", "cols"), None, None),
        check_vma=False,
    )
```

```python
import math

import jax
import jax.numpy as jnp
import ml_dtypes
import numpy as np
from jax import lax
from jax.experimental import pallas as pl
from jax.experimental.pallas import tpu as pltpu
from jax.sharding import PartitionSpec as P

BAND = 16
CHUNKS = 2
MIB = 1024 * 1024
BF16, F32 = jnp.bfloat16, jnp.float32


def tables(img, psf):
    length = img + psf // 2
    half = length // 2
    pad = -half % 128
    phase = (2 * np.arange(half)[:, None] + 1) * np.arange(length)[None, :] % (2 * length)
    angle = phase * (math.pi / length)
    table = np.concatenate([np.pad(f(angle), ((0, pad), (0, 0))) for f in (np.cos, np.sin)])
    table = table.astype(ml_dtypes.bfloat16)
    return jnp.asarray(table), jnp.asarray(np.ascontiguousarray(table.T))


def shuffle_table():
    index = np.arange(BAND * BAND)
    source = (index % BAND) * BAND + index // BAND
    table = np.zeros((BAND * BAND, BAND * BAND), np.float32)
    table[index, source] = 1.0
    return jnp.asarray(table.astype(ml_dtypes.bfloat16))


def dot(a, b):
    return jnp.dot(a, b, preferred_element_type=F32)


def conv_kernel(
    ch, rate, model_h, dirty_h, psf_h, table_h, turned_h, out,
    model, dirty, psf, table, turned, cols_x, cols_q, spec_x, spec_q, prod, rows_y, sems,
):
    img = model.shape[0]
    taps = psf.shape[0]
    shift = taps // 2
    length = table.shape[1]
    half = length // 2
    wide = table.shape[0] // 2

    copies = [
        pltpu.make_async_copy(source, target, sems.at[i])
        for i, (source, target) in enumerate(
            (
                (psf_h.at[ch], psf),
                (turned_h.at[pl.ds(0, taps)], turned.at[pl.ds(0, taps)]),
                (model_h.at[ch, pl.ds(0, img // 2)], model.at[pl.ds(0, img // 2)]),
                (turned_h.at[pl.ds(taps, length - taps)], turned.at[pl.ds(taps, length - taps)]),
                (model_h.at[ch, pl.ds(img // 2, img // 2)], model.at[pl.ds(img // 2, img // 2)]),
                (table_h.at[pl.ds(0, wide)], table.at[pl.ds(0, wide)]),
                (table_h.at[pl.ds(wide, wide)], table.at[pl.ds(wide, wide)]),
                (dirty_h.at[ch], dirty),
            )
        )
    ]
    for copy in copies:
        copy.start()

    zeros = jnp.zeros((wide - half, 2 * wide), BF16)
    prod[half:wide, :] = zeros
    prod[wide + half :, :] = zeros

    copies[0].wait()
    copies[1].wait()
    cols_q[...] = dot(psf[...], turned[:taps, :]).astype(BF16)
    copies[2].wait()
    copies[3].wait()
    right = turned[:img, :]
    cols_x[: img // 2, :] = dot(model[: img // 2, :], right).astype(BF16)
    copies[4].wait()
    cols_x[img // 2 :, :] = dot(model[img // 2 :, :], right).astype(BF16)

    for k in range(2):
        copies[5 + k].wait()
        source = slice(k * wide, k * wide + half)
        target = slice(k * half, (k + 1) * half)
        spec_q[target, :] = dot(table[source, :taps], cols_q[...])
        spec_x[target, :] = dot(table[source, :img], cols_x[...])

    @pl.loop(0, half // 16)
    def _(i):
        at = pl.multiple_of(i * 16, 16)
        c, s = pl.ds(at, 16), pl.ds(half + at, 16)
        for j in range(0, wide, 128):
            lc, ls = slice(j, j + 128), slice(wide + j, wide + j + 128)
            xcc, xcs, xsc, xss = spec_x[c, lc], spec_x[c, ls], spec_x[s, lc], spec_x[s, ls]
            qcc, qcs, qsc, qss = spec_q[c, lc], spec_q[c, ls], spec_q[s, lc], spec_q[s, ls]
            t = pl.ds(wide + at, 16)
            prod[c, lc] = ((xcc * qcc + xss * qss) - (xsc * qsc + xcs * qcs)).astype(BF16)
            prod[t, ls] = ((xcc * qss + xss * qcc) + (xsc * qcs + xcs * qsc)).astype(BF16)
            prod[t, lc] = ((xcc * qsc - xss * qcs) + (xsc * qcc - xcs * qss)).astype(BF16)
            prod[c, ls] = ((xcc * qcs - xss * qsc) + (xcs * qcc - xsc * qss)).astype(BF16)

    scale = rate[ch] * (4.0 / (length * length))
    step = 128
    for i in range(img // step):
        rows = slice(i * step, (i + 1) * step)
        back = turned[shift + i * step : shift + (i + 1) * step, :]
        rows_y[rows, :] = dot(back, prod[...]).astype(BF16)

    copies[7].wait()
    bands_of, parts, chunks, band, part = out.shape
    for q in range(chunks):
        for i in range(bands_of * band // step):
            at = q * bands_of * band + i * step
            rows = slice(at, at + step)
            blurred = dot(rows_y[rows, :], table[:, shift:])
            stepped = rate[ch] * dirty[rows, :].astype(F32) - scale * blurred
            stepped = (model[rows, :].astype(F32) + stepped).astype(BF16)
            where = slice(i * step // band, (i + 1) * step // band)
            for p in range(parts):
                piece = stepped[:, p * part : (p + 1) * part]
                out[where, p, q] = piece.reshape(step // band, band, part)


def mix_kernel(chunk, device, gain, b_in, w_in_t, w_out_t, swap, tiles_0, tiles_1, out, bias, normed, mixed):
    sources, _, band, part = out.shape
    channels = 2 * sources
    groups = sources // band

    def tile(ch, source):
        return (tiles_1 if ch else tiles_0)[source, chunk].astype(F32)

    bias[...] = jnp.broadcast_to(b_in[...], bias.shape)
    power = jnp.zeros((band, part), F32)
    for source in range(sources):
        for ch in range(2):
            v = tile(ch, source)
            power = power + v * v
    inverse = lax.rsqrt(power * (1.0 / channels) + 1e-06)
    for ch in range(2):
        for g in range(groups):
            rows = [
                (tile(ch, s) * inverse * gain[2 * device(s) + ch]).astype(BF16)
                for s in range(g * band, (g + 1) * band)
            ]
            swapped = dot(swap[...], jnp.concatenate(rows, axis=0)).astype(BF16)
            at = ch * sources + g * band
            normed[:, at : at + band, :] = swapped.reshape(band, band, part)

    a = math.sqrt(2.0 / math.pi)
    for r in range(band):
        inner = (dot(w_in_t[...], normed[r]) + bias[...]).astype(BF16)
        bent = inner * (BF16(a) + BF16(a * 0.044715) * (inner * inner))
        twice = inner + inner * jnp.tanh(bent)
        mixed[r] = (0.5 * dot(w_out_t[...], twice)).astype(BF16)

    for ch in range(2):
        for g in range(groups):
            at = ch * sources + g * band
            block = mixed[:, at : at + band, :].reshape(band * band, part)
            swapped = dot(swap[...], block).astype(BF16)
            out[g * band : (g + 1) * band, ch] = swapped.reshape(band, band, part)


def spread_kernel(chunk, chunks, first, taps, st_0, *refs):
    has_prev = chunk > 0
    last = chunk == chunks - 1
    st_1, refs = refs[0], refs[1:]
    if has_prev:
        cur, prev, _, out, above, middle, below, result, tail, sems = refs
    else:
        cur, out, above, middle, below, result, sems = refs
    channels = taps.shape[0] // 9
    bands, parts, ch_dev, band, part = cur.shape
    img = parts * part
    lead = 2 if has_prev else 0
    count = bands + lead
    lo = 1 if has_prev else 0
    hi = count if last else count - 1
    group = 4

    if has_prev:
        fetch = pltpu.make_async_copy(prev.at[pl.ds(bands - 2, 2)], tail, sems.at[0])
        fetch.start()
        fetch.wait()

    def mixed_band(j, ch):
        source, at = (tail, j) if j < lead else (cur, j - lead)
        return jnp.concatenate([source[at, p, ch] for p in range(parts)], axis=1)

    def stepped_band(j, ch):
        at = chunk * bands + j - lead
        q, b = at // bands, at % bands
        pieces = [(st_1 if ch else st_0)[b, p, q] for p in range(parts)]
        return jnp.concatenate(pieces, axis=1)

    zero = jnp.zeros((img // 128, 8, 128), F32)
    for ch in range(ch_dev):
        k = [[taps[(3 * i + j) * channels + first[0] + ch] for j in range(3)] for i in range(3)]
        above[:, 0:8, :] = zero
        below[:, count * band : count * band + 8, :] = zero
        for start in range(0, count, group):
            js = range(start, min(start + group, count))
            size = len(js) * band
            x = jnp.concatenate([mixed_band(j, ch) for j in js], axis=0).astype(F32)
            lane = lax.broadcasted_iota(jnp.int32, (size, img), 1)
            low = jnp.where(lane == 0, 0.0, pltpu.roll(x, 1, 1))
            high = jnp.where(lane == img - 1, 0.0, pltpu.roll(x, img - 1, 1))
            at = start * band
            for target, row, off in ((above, 0, 8), (middle, 1, 0), (below, 2, 0)):
                value = k[row][0] * low + k[row][1] * x + k[row][2] * high
                for n in range(img // 128):
                    target[n, at + off : at + off + size, :] = value[:, n * 128 : (n + 1) * 128]
        for j in range(lo, hi):
            at = j * band
            base = stepped_band(j, ch).astype(F32)
            for n in range(img // 128):
                total = above[n, at + 7 : at + 7 + band, :] + below[n, at + 1 : at + 1 + band, :]
                total = total + middle[n, at : at + band, :]
                total = base[:, n * 128 : (n + 1) * 128] + total
                to = at - lo * band
                result[ch, to : to + band, n * 128 : (n + 1) * 128] = total.astype(BF16)

    rows = (hi - lo) * band
    origin = (chunk * bands - lead + lo) * band
    send = pltpu.make_async_copy(result, out.at[:, pl.ds(origin, rows), :], sems.at[1])
    send.start()
    send.wait()


VMEM = pl.BlockSpec(memory_space=pltpu.VMEM)
SMEM = pl.BlockSpec(memory_space=pltpu.SMEM)
ANY = pl.BlockSpec(memory_space=pl.ANY)
HBM = pl.BlockSpec(memory_space=pltpu.HBM)


def params(mib):
    return pltpu.CompilerParams(vmem_limit_bytes=mib * MIB)


def exchange(blocks):
    return lax.all_to_all(blocks, ("cols", "rows"), split_axis=0, concat_axis=0, tiled=True)


def local(model, dirty, psf, step_size, gain, w_in, b_in, w_out, kernel):
    ch_dev, img, _ = model.shape
    psf_len = psf.shape[1]
    assert ch_dev == 2
    n_rows, n_cols = lax.axis_size("rows"), lax.axis_size("cols")
    n_dev = n_rows * n_cols
    channels = gain.shape[0]
    hidden = b_in.shape[0]
    chunks = max(1, min(CHUNKS, img * img // (n_dev * BAND * 128)))
    part = img * img // (n_dev * BAND * chunks)
    parts = img // part
    bands = img // (BAND * chunks)
    table, turned = tables(img, psf_len)
    wide, length = table.shape[0] // 2, table.shape[1]

    def conv(ch, model):
        return pl.pallas_call(
            lambda *refs: conv_kernel(ch, *refs),
            out_shape=jax.ShapeDtypeStruct((bands, parts, chunks, BAND, part), BF16),
            in_specs=[SMEM] + [HBM] * 5,
            out_specs=VMEM,
            scratch_shapes=[
                pltpu.VMEM((img, img), BF16),
                pltpu.VMEM((img, img), BF16),
                pltpu.VMEM((psf_len, psf_len), BF16),
                pltpu.VMEM((2 * wide, length), BF16),
                pltpu.VMEM((length, 2 * wide), BF16),
                pltpu.VMEM((img, 2 * wide), BF16),
                pltpu.VMEM((psf_len, 2 * wide), BF16),
                pltpu.VMEM((length, 2 * wide), F32),
                pltpu.VMEM((length, 2 * wide), F32),
                pltpu.VMEM((2 * wide, 2 * wide), BF16),
                pltpu.VMEM((img, 2 * wide), BF16),
                pltpu.SemaphoreType.DMA((8,)),
            ],
            compiler_params=params(58),
            cost_estimate=pl.CostEstimate(flops=4_000_000_000, bytes_accessed=4_000_000, transcendentals=0),
            name="conv",
        )(step_size, model, dirty, psf, table, turned)

    def mix(chunk, tiles_0, tiles_1):
        return pl.pallas_call(
            lambda *refs: mix_kernel(chunk, device, *refs),
            out_shape=jax.ShapeDtypeStruct((n_dev, ch_dev, BAND, part), BF16),
            in_specs=[SMEM] + [VMEM] * 6,
            out_specs=VMEM,
            scratch_shapes=[
                pltpu.VMEM((hidden, part), F32),
                pltpu.VMEM((BAND, channels, part), BF16),
                pltpu.VMEM((BAND, channels, part), BF16),
            ],
            compiler_params=params(16),
            cost_estimate=pl.CostEstimate(flops=4_000_000_000, bytes_accessed=2_000_000, transcendentals=0),
            name="mix",
        )(gain, b_col, w_in_t, w_out_t, swap, tiles_0, tiles_1)

    def spread(chunk, current, previous, result):
        lead = 2 if chunk else 0
        rows = (bands + lead + 1) * BAND
        out_bands = bands + (1 if chunk else 0) - (0 if chunk == chunks - 1 else 1)
        plane = pltpu.VMEM((img // 128, rows, 128), F32)
        scratch = [plane, plane, plane, pltpu.VMEM((ch_dev, out_bands * BAND, img), BF16)]
        more = []
        if chunk:
            more = [previous, result]
            scratch.append(pltpu.VMEM((2, parts, ch_dev, BAND, part), BF16))
        scratch.append(pltpu.SemaphoreType.DMA((2,)))
        return pl.pallas_call(
            lambda *refs: spread_kernel(chunk, chunks, *refs),
            out_shape=jax.ShapeDtypeStruct((ch_dev, img, img), BF16),
            in_specs=[SMEM, SMEM] + [VMEM] * 3 + [ANY] * len(more),
            out_specs=ANY,
            input_output_aliases={6: 0} if chunk else {},
            scratch_shapes=scratch,
            compiler_params=params(16),
            cost_estimate=pl.CostEstimate(flops=4_000_000_000, bytes_accessed=2_000_000, transcendentals=0),
            name="spread",
        )(position[None], flat_taps, st_0, st_1, current, *more)

    def weights(w):
        return w.reshape(hidden, n_rows, n_cols, ch_dev).transpose(0, 3, 2, 1).reshape(hidden, channels)

    def device(rank):
        return rank % n_rows * n_cols + rank // n_rows

    st_0 = conv(0, model)
    st_0, model = lax.optimization_barrier((st_0, model))
    tiles_0 = exchange(st_0.reshape(n_dev, chunks, BAND, part))
    st_1 = conv(1, model)
    st_1, w_in, b_in, w_out, kernel = lax.optimization_barrier((st_1, w_in, b_in, w_out, kernel))
    tiles_1 = exchange(st_1.reshape(n_dev, chunks, BAND, part))

    b_col = b_in[:, None]
    w_in_t = weights(w_in.T)
    w_out_t = weights(w_out).T
    swap = shuffle_table()
    flat_taps = kernel.reshape(-1)
    position = lax.axis_index(("rows", "cols")).astype(jnp.int32) * ch_dev

    returned = []
    for q in range(chunks):
        back = exchange(mix(q, tiles_0, tiles_1))
        returned.append(back.reshape(bands, parts, ch_dev, BAND, part))
    result = None
    for q in range(chunks):
        result = spread(q, returned[q], returned[q - 1] if q else None, result)
    return result


def solution(mesh):
    return jax.shard_map(
        local,
        mesh=mesh,
        in_specs=(
            P(("rows", "cols"), None, None),
            P(("rows", "cols"), None, None),
            P(("rows", "cols"), None, None),
            P(("rows", "cols")),
            P(),
            P(),
            P(),
            P(),
            P(),
        ),
        out_specs=P(("rows", "cols"), None, None),
        check_vma=False,
    )
```

```python
import math

import jax
import jax.numpy as jnp
import ml_dtypes
import numpy as np
from jax import lax
from jax.experimental import pallas as pl
from jax.experimental.pallas import tpu as pltpu
from jax.sharding import PartitionSpec as P

BAND = 16
MIB = 1024 * 1024
BF16, F32 = jnp.bfloat16, jnp.float32


def tables(img, psf):
    length = img + psf // 2
    half = length // 2
    pad = -half % 128
    phase = (2 * np.arange(half)[:, None] + 1) * np.arange(length)[None, :] % (2 * length)
    angle = phase * (math.pi / length)
    table = np.concatenate([np.pad(f(angle), ((pad, 0), (0, 0))) for f in (np.cos, np.sin)])
    table = np.pad(table, ((0, pad), (0, 0))).astype(ml_dtypes.bfloat16)
    return jnp.asarray(table), jnp.asarray(np.ascontiguousarray(table[pad:].T))


def shuffle_table():
    index = np.arange(BAND * BAND)
    source = (index % BAND) * BAND + index // BAND
    table = np.zeros((BAND * BAND, BAND * BAND), np.float32)
    table[index, source] = 1.0
    return jnp.asarray(table.astype(ml_dtypes.bfloat16))


def dot(a, b):
    return jnp.dot(a, b, preferred_element_type=F32)


def conv_kernel(
    rate, model_h, dirty_h, psf_h, table_h, turned_h, out_h,
    model, dirty, psf, table, turned, cols_x, cols_q, spec_x, spec_q, prod, rows_y, out, sems, out_sems,
):
    img = model.shape[1]
    taps = psf.shape[1]
    shift = taps // 2
    length = table.shape[1]
    half = length // 2
    wide = turned.shape[1] // 2
    pad = wide - half
    own = length - wide
    shared = wide - own

    def rows_of(source, target, start, count):
        return source.at[pl.ds(start, count)], target.at[pl.ds(start, count)]

    pairs = (
        (psf_h, psf),
        rows_of(turned_h, turned, 0, taps),
        (model_h.at[0], model.at[0]),
        rows_of(turned_h, turned, taps, img - taps),
        (model_h.at[1], model.at[1]),
        rows_of(table_h, table, 0, pad + wide),
        rows_of(table_h, table, pad + wide, wide),
        rows_of(turned_h, turned, img, length - img),
        (dirty_h, dirty),
    )
    copies = [pltpu.make_async_copy(*pair, sems.at[i]) for i, pair in enumerate(pairs)]
    for copy in copies:
        copy.start()

    zeros = jnp.zeros((pad, 2 * length), BF16)
    prod[half:wide, :] = zeros
    prod[wide + half :, :] = zeros

    def columns(source, depth, target, waits):
        copies[waits[0]].wait()
        copies[waits[1]].wait()
        first = dot(source[0], turned[:depth, :])
        if waits[2] is not None:
            copies[waits[2]].wait()
        second = dot(source[1], turned[:depth, :])
        for k in range(2):
            a = first[:, k * wide : (k + 1) * wide]
            b = pltpu.roll(second[:, k * wide : (k + 1) * wide], pad, 1)
            at = k * length
            target[:, at : at + own] = a[:, :own].astype(BF16)
            target[:, at + own : at + wide] = (a[:, own:] + b[:, :shared]).astype(BF16)
            target[:, at + wide : at + length] = b[:, shared:].astype(BF16)

    columns(psf, taps, cols_q, (0, 1, None))
    columns(model, img, cols_x, (2, 3, 4))

    for k in range(2):
        copies[5 + k].wait()
        source = slice(pad + k * wide, pad + k * wide + half)
        target = slice(k * half, (k + 1) * half)
        spec_q[target, :] = dot(table[source, :taps], cols_q[...])
        spec_x[target, :] = dot(table[source, :img], cols_x[...])

    @pl.loop(0, half // 32)
    def _(i):
        for u in range(2):
            at = pl.multiple_of(i * 32 + u * 16, 16)
            c, s, t = pl.ds(at, 16), pl.ds(half + at, 16), pl.ds(wide + at, 16)
            for j in range(0, length, 128):
                lc, ls = slice(j, j + 128), slice(length + j, length + j + 128)
                xcc, xcs, xsc, xss = spec_x[c, lc], spec_x[c, ls], spec_x[s, lc], spec_x[s, ls]
                qcc, qcs, qsc, qss = spec_q[c, lc], spec_q[c, ls], spec_q[s, lc], spec_q[s, ls]
                prod[c, lc] = ((xcc * qcc + xss * qss) - (xsc * qsc + xcs * qcs)).astype(BF16)
                prod[t, ls] = ((xcc * qss + xss * qcc) + (xsc * qcs + xcs * qsc)).astype(BF16)
                prod[t, lc] = ((xcc * qsc - xss * qcs) + (xsc * qcc - xcs * qss)).astype(BF16)
                prod[c, ls] = ((xcc * qcs - xss * qsc) + (xcs * qcc - xsc * qss)).astype(BF16)

    copies[7].wait()
    rows_y[...] = dot(turned[shift:, :], prod[...]).astype(BF16)

    copies[8].wait()
    bands, parts, _, band, part = out.shape
    step = 128
    sends = []
    for i in range(img // step):
        rows = slice(i * step, (i + 1) * step)
        where = slice(i * step // band, (i + 1) * step // band)
        for ch in range(2):
            at = ch * own
            inner = jnp.concatenate(
                [rows_y[rows, at : at + wide], rows_y[rows, length + at : length + at + wide]], axis=1
            )
            back = table[pad * (1 - ch) : pad * (1 - ch) + 2 * wide, shift:]
            scale = rate[ch] * (4.0 / (length * length))
            stepped = rate[ch] * dirty[ch, rows, :].astype(F32) - scale * dot(inner, back)
            stepped = (model[ch, rows, :].astype(F32) + stepped).astype(BF16)
            for p in range(parts):
                piece = stepped[:, p * part : (p + 1) * part]
                out[where, p, ch] = piece.reshape(step // band, band, part)
        sends.append(pltpu.make_async_copy(out.at[where], out_h.at[where], out_sems.at[i]))
        sends[-1].start()
    for send in sends:
        send.wait()


def mix_kernel(gain, b_in, w_in_t, w_out_t, swap, tiles, out, bias, normed, hidden, mixed):
    channels, band, part = tiles.shape
    groups = channels // band

    bias[...] = jnp.broadcast_to(b_in[...], bias.shape)
    power = jnp.zeros((band, part), F32)
    for c in range(channels):
        v = tiles[c].astype(F32)
        power = power + v * v
    inverse = lax.rsqrt(power * (1.0 / channels) + 1e-06)
    for g in range(groups):
        rows = [
            (tiles[c].astype(F32) * inverse * gain[c]).astype(BF16)
            for c in range(g * band, (g + 1) * band)
        ]
        swapped = dot(swap[...], jnp.concatenate(rows, axis=0)).astype(BF16)
        normed[:, g * band : (g + 1) * band, :] = swapped.reshape(band, band, part)

    a = math.sqrt(2.0 / math.pi)
    for r in range(band):
        inner = (dot(w_in_t[...], normed[r]) + bias[...]).astype(BF16)
        bent = inner * (BF16(a) + BF16(a * 0.044715) * (inner * inner))
        hidden[r] = inner + inner * jnp.tanh(bent)
    for r in range(band):
        mixed[r] = (0.5 * dot(w_out_t[...], hidden[r])).astype(BF16)

    for g in range(groups):
        block = mixed[:, g * band : (g + 1) * band, :].reshape(band * band, part)
        swapped = dot(swap[...], block).astype(BF16)
        out[g * band : (g + 1) * band] = swapped.reshape(band, band, part)


def spread_kernel(first, taps, stepped, mixed, out, above, middle, below, result, sems):
    channels = taps.shape[0] // 9
    bands, parts, ch_dev, band, part = stepped.shape
    img = parts * part
    group = 4
    size = group * band

    def rows_of(source, start, ch):
        pieces = [source[start : start + group, p, ch].reshape(size, part) for p in range(parts)]
        return jnp.concatenate(pieces, axis=1).astype(F32)

    zero = jnp.zeros((img // 128, 8, 128), F32)
    above[:, 0:8, :] = zero
    below[:, img : img + 8, :] = zero
    lane = lax.broadcasted_iota(jnp.int32, (size, img), 1)
    sends = []
    for ch in range(ch_dev):
        k = [[taps[(3 * i + j) * channels + first[0] + ch] for j in range(3)] for i in range(3)]

        def across(start):
            x = rows_of(mixed, start, ch)
            low = jnp.where(lane == 0, 0.0, pltpu.roll(x, 1, 1))
            high = jnp.where(lane == img - 1, 0.0, pltpu.roll(x, img - 1, 1))
            at = start * band
            for target, row, off in ((above, 0, 8), (middle, 1, 0), (below, 2, 0)):
                value = k[row][0] * low + k[row][1] * x + k[row][2] * high
                for n in range(img // 128):
                    target[n, at + off : at + off + size, :] = value[:, n * 128 : (n + 1) * 128]

        def down(start):
            at = start * band
            base = rows_of(stepped, start, ch)
            for n in range(img // 128):
                total = above[n, at + 7 : at + 7 + size, :] + below[n, at + 1 : at + 1 + size, :]
                total = total + middle[n, at : at + size, :]
                total = base[:, n * 128 : (n + 1) * 128] + total
                result[ch, at : at + size, n * 128 : (n + 1) * 128] = total.astype(BF16)

        for start in range(0, bands, group):
            across(start)
            if start:
                down(start - group)
        down(bands - group)
        sends.append(pltpu.make_async_copy(result.at[ch], out.at[ch], sems.at[ch]))
        sends[-1].start()
    for send in sends:
        send.wait()


VMEM = pl.BlockSpec(memory_space=pltpu.VMEM)
SMEM = pl.BlockSpec(memory_space=pltpu.SMEM)
HBM = pl.BlockSpec(memory_space=pltpu.HBM)


def params(mib):
    return pltpu.CompilerParams(vmem_limit_bytes=mib * MIB)


def exchange(blocks):
    return lax.all_to_all(blocks, ("rows", "cols"), split_axis=0, concat_axis=0, tiled=True)


def local(model, dirty, psf, step_size, gain, w_in, b_in, w_out, kernel):
    ch_dev, img, _ = model.shape
    psf_len = psf.shape[1]
    assert ch_dev == 2
    n_dev = lax.axis_size("rows") * lax.axis_size("cols")
    channels = gain.shape[0]
    hidden = b_in.shape[0]
    part = img * img // (n_dev * BAND)
    parts = img // part
    bands = img // BAND
    table, turned = tables(img, psf_len)
    length, wide = turned.shape[0], turned.shape[1] // 2
    blocks = (bands, parts, ch_dev, BAND, part)

    stepped = pl.pallas_call(
        conv_kernel,
        out_shape=jax.ShapeDtypeStruct(blocks, BF16),
        in_specs=[SMEM] + [HBM] * 5,
        out_specs=HBM,
        scratch_shapes=[
            pltpu.VMEM(model.shape, BF16),
            pltpu.VMEM(model.shape, BF16),
            pltpu.VMEM(psf.shape, BF16),
            pltpu.VMEM(table.shape, BF16),
            pltpu.VMEM(turned.shape, BF16),
            pltpu.VMEM((img, 2 * length), BF16),
            pltpu.VMEM((psf_len, 2 * length), BF16),
            pltpu.VMEM((length, 2 * length), F32),
            pltpu.VMEM((length, 2 * length), F32),
            pltpu.VMEM((2 * wide, 2 * length), BF16),
            pltpu.VMEM((img, 2 * length), BF16),
            pltpu.VMEM(blocks, BF16),
            pltpu.SemaphoreType.DMA((9,)),
            pltpu.SemaphoreType.DMA((img // 128,)),
        ],
        compiler_params=params(58),
        name="conv",
    )(step_size, model, dirty, psf, table, turned)
    stepped, w_in, b_in, w_out, kernel = lax.optimization_barrier((stepped, w_in, b_in, w_out, kernel))

    tiles = exchange(stepped.reshape(n_dev, ch_dev, BAND, part)).reshape(channels, BAND, part)

    mixed = pl.pallas_call(
        mix_kernel,
        out_shape=jax.ShapeDtypeStruct((channels, BAND, part), BF16),
        in_specs=[SMEM] + [VMEM] * 5,
        out_specs=VMEM,
        scratch_shapes=[
            pltpu.VMEM((hidden, part), F32),
            pltpu.VMEM((BAND, channels, part), BF16),
            pltpu.VMEM((BAND, hidden, part), BF16),
            pltpu.VMEM((BAND, channels, part), BF16),
        ],
        compiler_params=params(24),
        name="mix",
    )(gain, b_in[:, None], w_in.T, w_out.T, shuffle_table(), tiles)

    returned = exchange(mixed.reshape(n_dev, ch_dev, BAND, part)).reshape(blocks)
    position = lax.axis_index(("rows", "cols")).astype(jnp.int32) * ch_dev
    plane = pltpu.VMEM((img // 128, img + 8, 128), F32)

    return pl.pallas_call(
        spread_kernel,
        out_shape=jax.ShapeDtypeStruct((ch_dev, img, img), BF16),
        in_specs=[SMEM, SMEM, VMEM, VMEM],
        out_specs=HBM,
        scratch_shapes=[
            plane, plane, plane, pltpu.VMEM((ch_dev, img, img), BF16), pltpu.SemaphoreType.DMA((ch_dev,)),
        ],
        compiler_params=params(24),
        name="spread",
    )(position[None], kernel.reshape(-1), stepped, returned)


def solution(mesh):
    return jax.shard_map(
        local,
        mesh=mesh,
        in_specs=(
            P(("rows", "cols"), None, None),
            P(("rows", "cols"), None, None),
            P(("rows", "cols"), None, None),
            P(("rows", "cols")),
            P(),
            P(),
            P(),
            P(),
            P(),
        ),
        out_specs=P(("rows", "cols"), None, None),
        check_vma=False,
    )
```

```python
import math

import jax
import jax.numpy as jnp
import ml_dtypes
import numpy as np
from jax import lax
from jax.experimental import pallas as pl
from jax.experimental.pallas import tpu as pltpu
from jax.sharding import PartitionSpec as P

BAND = 16
MIB = 1024 * 1024
BF16, F32 = jnp.bfloat16, jnp.float32


def tables(img, psf):
    length = img + psf // 2
    half = length // 2
    pad = -half % 128
    phase = (2 * np.arange(half)[:, None] + 1) * np.arange(length)[None, :] % (2 * length)
    angle = phase * (math.pi / length)
    table = np.concatenate([np.pad(f(angle), ((pad, 0), (0, 0))) for f in (np.cos, np.sin)])
    table = np.pad(table, ((0, pad), (0, 0))).astype(ml_dtypes.bfloat16)
    return jnp.asarray(table), jnp.asarray(np.ascontiguousarray(table[pad:].T))


def shuffle_table():
    index = np.arange(BAND * BAND)
    source = (index % BAND) * BAND + index // BAND
    table = np.zeros((BAND * BAND, BAND * BAND), np.float32)
    table[index, source] = 1.0
    return jnp.asarray(table.astype(ml_dtypes.bfloat16))


def dot(a, b):
    return jnp.dot(a, b, preferred_element_type=F32)


def conv_kernel(
    rate, model_h, dirty_h, psf_h, table_h, turned_h, out_h,
    model, dirty, psf, table, turned, cols_x, cols_q, spec_x, spec_q, prod, rows_y, out, sems, out_sems,
):
    img = model.shape[1]
    taps = psf.shape[1]
    shift = taps // 2
    length = table.shape[1]
    half = length // 2
    wide = turned.shape[1] // 2
    pad = wide - half
    own = length - wide
    shared = wide - own

    def rows_of(source, target, start, count):
        return source.at[pl.ds(start, count)], target.at[pl.ds(start, count)]

    pairs = (
        (psf_h, psf),
        rows_of(turned_h, turned, 0, taps),
        (model_h.at[0], model.at[0]),
        rows_of(turned_h, turned, taps, img - taps),
        (model_h.at[1], model.at[1]),
        rows_of(table_h, table, 0, pad + wide),
        rows_of(table_h, table, pad + wide, wide),
        rows_of(turned_h, turned, img, length - img),
        (dirty_h, dirty),
    )
    copies = [pltpu.make_async_copy(*pair, sems.at[i]) for i, pair in enumerate(pairs)]
    for copy in copies:
        copy.start()

    zeros = jnp.zeros((pad, 2 * length), BF16)
    prod[half:wide, :] = zeros
    prod[wide + half :, :] = zeros

    def columns(source, depth, target, waits):
        step = 128
        for wait in waits[:2]:
            copies[wait].wait()
        for ch in range(2):
            if ch and waits[2] is not None:
                copies[waits[2]].wait()
            for m in range(0, depth, step):
                rows = slice(m, m + step)
                part = jnp.concatenate(
                    [dot(source[ch, rows, :], turned[:depth, n : n + 256]) for n in range(0, 2 * wide, 256)],
                    axis=1,
                )
                for k in range(2):
                    at = k * length
                    one = part[:, k * wide : (k + 1) * wide]
                    if ch == 0:
                        target[rows, at : at + wide] = one.astype(BF16)
                    else:
                        one = pltpu.roll(one, pad, 1)
                        both = one[:, :shared] + target[rows, at + own : at + wide].astype(F32)
                        target[rows, at + own : at + wide] = both.astype(BF16)
                        target[rows, at + wide : at + length] = one[:, shared:].astype(BF16)

    columns(psf, taps, cols_q, (0, 1, None))
    columns(model, img, cols_x, (2, 3, 4))

    def products(start, count):
        for row in range(start, start + count, 16):
            c, s, t = (slice(at + row, at + row + 16) for at in (0, half, wide))
            for j in range(0, length, 128):
                lc, ls = slice(j, j + 128), slice(length + j, length + j + 128)
                xcc, xcs, xsc, xss = spec_x[c, lc], spec_x[c, ls], spec_x[s, lc], spec_x[s, ls]
                qcc, qcs, qsc, qss = spec_q[c, lc], spec_q[c, ls], spec_q[s, lc], spec_q[s, ls]
                prod[c, lc] = ((xcc * qcc + xss * qss) - (xsc * qsc + xcs * qcs)).astype(BF16)
                prod[t, ls] = ((xcc * qss + xss * qcc) + (xsc * qcs + xcs * qsc)).astype(BF16)
                prod[t, lc] = ((xcc * qsc - xss * qcs) + (xsc * qcc - xcs * qss)).astype(BF16)
                prod[c, ls] = ((xcc * qcs - xss * qsc) + (xcs * qcc - xsc * qss)).astype(BF16)

    copies[5].wait()
    copies[6].wait()
    step = half // 2
    for start in range(0, half, step):
        for k in range(2):
            source = slice(pad + k * wide + start, pad + k * wide + start + step)
            target = slice(k * half + start, k * half + start + step)
            for n in range(0, 2 * length, 256):
                lanes = slice(n, n + 256)
                spec_q[target, lanes] = dot(table[source, :taps], cols_q[:, lanes])
                spec_x[target, lanes] = dot(table[source, :img], cols_x[:, lanes])
        products(start, step)

    copies[7].wait()
    for n in range(0, 2 * length, 256):
        for m in range(0, img, 128):
            back = turned[shift + m : shift + m + 128, :]
            rows_y[m : m + 128, n : n + 256] = dot(back, prod[:, n : n + 256]).astype(BF16)

    copies[8].wait()
    bands, parts, _, band, part = out.shape
    step = 128
    sends = []
    for i in range(img // step):
        rows = slice(i * step, (i + 1) * step)
        where = slice(i * step // band, (i + 1) * step // band)
        for ch in range(2):
            at = ch * own
            inner = jnp.concatenate(
                [rows_y[rows, at : at + wide], rows_y[rows, length + at : length + at + wide]], axis=1
            )
            back = table[pad * (1 - ch) : pad * (1 - ch) + 2 * wide, shift:]
            scale = rate[ch] * (4.0 / (length * length))
            blurred = jnp.concatenate([dot(inner, back[:, n : n + 256]) for n in range(0, img, 256)], axis=1)
            stepped = rate[ch] * dirty[ch, rows, :].astype(F32) - scale * blurred
            stepped = (model[ch, rows, :].astype(F32) + stepped).astype(BF16)
            for p in range(parts):
                piece = stepped[:, p * part : (p + 1) * part]
                out[where, p, ch] = piece.reshape(step // band, band, part)
        sends.append(pltpu.make_async_copy(out.at[where], out_h.at[where], out_sems.at[i]))
        sends[-1].start()
    for send in sends:
        send.wait()


def mix_kernel(gain, b_in, w_in_t, w_out_t, swap, tiles, out, bias, normed, hidden, mixed):
    channels, band, part = tiles.shape
    groups = channels // band

    bias[...] = jnp.broadcast_to(b_in[...], bias.shape)
    power = jnp.zeros((band, part), F32)
    for c in range(channels):
        v = tiles[c].astype(F32)
        power = power + v * v
    inverse = lax.rsqrt(power * (1.0 / channels) + 1e-06)
    for g in range(groups):
        rows = [
            (tiles[c].astype(F32) * inverse * gain[c]).astype(BF16)
            for c in range(g * band, (g + 1) * band)
        ]
        swapped = dot(swap[...], jnp.concatenate(rows, axis=0)).astype(BF16)
        normed[:, g * band : (g + 1) * band, :] = swapped.reshape(band, band, part)

    a = math.sqrt(2.0 / math.pi)
    blocks = [slice(n, min(n + 256, part)) for n in range(0, part, 256)]
    for r in range(band):
        for lanes in blocks:
            for h in range(0, hidden.shape[1], 128):
                rows = slice(h, h + 128)
                inner = (dot(w_in_t[rows, :], normed[r, :, lanes]) + bias[rows, lanes]).astype(BF16)
                bent = inner * (BF16(a) + BF16(a * 0.044715) * (inner * inner))
                hidden[r, rows, lanes] = inner + inner * jnp.tanh(bent)
    for r in range(band):
        for lanes in blocks:
            mixed[r, :, lanes] = (0.5 * dot(w_out_t[...], hidden[r, :, lanes])).astype(BF16)

    for g in range(groups):
        block = mixed[:, g * band : (g + 1) * band, :].reshape(band * band, part)
        swapped = dot(swap[...], block).astype(BF16)
        out[g * band : (g + 1) * band] = swapped.reshape(band, band, part)


def spread_kernel(first, taps, stepped, mixed, out, above, middle, below, result, sems):
    channels = taps.shape[0] // 9
    bands, parts, ch_dev, band, part = stepped.shape
    img = parts * part
    group = 4
    size = group * band

    def rows_of(source, start, ch):
        pieces = [source[start : start + group, p, ch].reshape(size, part) for p in range(parts)]
        return jnp.concatenate(pieces, axis=1).astype(F32)

    zero = jnp.zeros((img // 128, 8, 128), F32)
    above[:, 0:8, :] = zero
    below[:, img : img + 8, :] = zero
    lane = lax.broadcasted_iota(jnp.int32, (size, img), 1)
    sends = []
    for ch in range(ch_dev):
        k = [[taps[(3 * i + j) * channels + first[0] + ch] for j in range(3)] for i in range(3)]

        def across(start):
            x = rows_of(mixed, start, ch)
            low = jnp.where(lane == 0, 0.0, pltpu.roll(x, 1, 1))
            high = jnp.where(lane == img - 1, 0.0, pltpu.roll(x, img - 1, 1))
            at = start * band
            for target, row, off in ((above, 0, 8), (middle, 1, 0), (below, 2, 0)):
                value = k[row][0] * low + k[row][1] * x + k[row][2] * high
                for n in range(img // 128):
                    target[n, at + off : at + off + size, :] = value[:, n * 128 : (n + 1) * 128]

        def down(start):
            at = start * band
            base = rows_of(stepped, start, ch)
            for n in range(img // 128):
                total = above[n, at + 7 : at + 7 + size, :] + below[n, at + 1 : at + 1 + size, :]
                total = total + middle[n, at : at + size, :]
                total = base[:, n * 128 : (n + 1) * 128] + total
                result[ch, at : at + size, n * 128 : (n + 1) * 128] = total.astype(BF16)

        def leave(start):
            down(start)
            rows = pl.ds(start * band, size)
            at = sems.at[ch * (bands // group) + start // group]
            sends.append(pltpu.make_async_copy(result.at[ch, rows], out.at[ch, rows], at))
            sends[-1].start()

        for start in range(0, bands, group):
            across(start)
            if start:
                leave(start - group)
        leave(bands - group)
    for send in sends:
        send.wait()


VMEM = pl.BlockSpec(memory_space=pltpu.VMEM)
SMEM = pl.BlockSpec(memory_space=pltpu.SMEM)
HBM = pl.BlockSpec(memory_space=pltpu.HBM)


def params(mib):
    return pltpu.CompilerParams(vmem_limit_bytes=mib * MIB)


def exchange(blocks):
    return lax.all_to_all(blocks, ("rows", "cols"), split_axis=0, concat_axis=0, tiled=True)


def local(model, dirty, psf, step_size, gain, w_in, b_in, w_out, kernel):
    ch_dev, img, _ = model.shape
    psf_len = psf.shape[1]
    assert ch_dev == 2
    n_dev = lax.axis_size("rows") * lax.axis_size("cols")
    channels = gain.shape[0]
    hidden = b_in.shape[0]
    part = img * img // (n_dev * BAND)
    parts = img // part
    bands = img // BAND
    table, turned = tables(img, psf_len)
    length, wide = turned.shape[0], turned.shape[1] // 2
    blocks = (bands, parts, ch_dev, BAND, part)

    stepped = pl.pallas_call(
        conv_kernel,
        out_shape=jax.ShapeDtypeStruct(blocks, BF16),
        in_specs=[SMEM] + [HBM] * 5,
        out_specs=HBM,
        scratch_shapes=[
            pltpu.VMEM(model.shape, BF16),
            pltpu.VMEM(model.shape, BF16),
            pltpu.VMEM(psf.shape, BF16),
            pltpu.VMEM(table.shape, BF16),
            pltpu.VMEM(turned.shape, BF16),
            pltpu.VMEM((img, 2 * length), BF16),
            pltpu.VMEM((psf_len, 2 * length), BF16),
            pltpu.VMEM((length, 2 * length), F32),
            pltpu.VMEM((length, 2 * length), F32),
            pltpu.VMEM((2 * wide, 2 * length), BF16),
            pltpu.VMEM((img, 2 * length), BF16),
            pltpu.VMEM(blocks, BF16),
            pltpu.SemaphoreType.DMA((9,)),
            pltpu.SemaphoreType.DMA((img // 128,)),
        ],
        compiler_params=params(58),
        name="conv",
    )(step_size, model, dirty, psf, table, turned)
    stepped, w_in, b_in, w_out, kernel = lax.optimization_barrier((stepped, w_in, b_in, w_out, kernel))

    tiles = exchange(stepped.reshape(n_dev, ch_dev, BAND, part)).reshape(channels, BAND, part)

    mixed = pl.pallas_call(
        mix_kernel,
        out_shape=jax.ShapeDtypeStruct((channels, BAND, part), BF16),
        in_specs=[SMEM] + [VMEM] * 5,
        out_specs=VMEM,
        scratch_shapes=[
            pltpu.VMEM((hidden, part), F32),
            pltpu.VMEM((BAND, channels, part), BF16),
            pltpu.VMEM((BAND, hidden, part), BF16),
            pltpu.VMEM((BAND, channels, part), BF16),
        ],
        compiler_params=params(24),
        name="mix",
    )(gain, b_in[:, None], w_in.T, w_out.T, shuffle_table(), tiles)

    returned = exchange(mixed.reshape(n_dev, ch_dev, BAND, part)).reshape(blocks)
    position = lax.axis_index(("rows", "cols")).astype(jnp.int32) * ch_dev
    plane = pltpu.VMEM((img // 128, img + 8, 128), F32)

    return pl.pallas_call(
        spread_kernel,
        out_shape=jax.ShapeDtypeStruct((ch_dev, img, img), BF16),
        in_specs=[SMEM, SMEM, VMEM, VMEM],
        out_specs=HBM,
        scratch_shapes=[
            plane, plane, plane, pltpu.VMEM((ch_dev, img, img), BF16),
            pltpu.SemaphoreType.DMA((ch_dev * bands // 4,)),
        ],
        compiler_params=params(24),
        name="spread",
    )(position[None], kernel.reshape(-1), stepped, returned)


def solution(mesh):
    return jax.shard_map(
        local,
        mesh=mesh,
        in_specs=(
            P(("rows", "cols"), None, None),
            P(("rows", "cols"), None, None),
            P(("rows", "cols"), None, None),
            P(("rows", "cols")),
            P(),
            P(),
            P(),
            P(),
            P(),
        ),
        out_specs=P(("rows", "cols"), None, None),
        check_vma=False,
    )
```

```python
import math

import jax
import jax.numpy as jnp
import ml_dtypes
import numpy as np
from jax import lax
from jax.experimental import pallas as pl
from jax.experimental.pallas import tpu as pltpu
from jax.sharding import Mesh
from jax.sharding import PartitionSpec as P

BAND = 16
MIB = 1024 * 1024
BF16, F32 = jnp.bfloat16, jnp.float32


def tables(img, psf):
    length = img + psf // 2
    half = length // 2
    pad = -half % 128
    phase = (2 * np.arange(half)[:, None] + 1) * np.arange(length)[None, :] % (2 * length)
    angle = phase * (math.pi / length)
    table = np.concatenate([np.pad(f(angle), ((0, pad), (0, 0))) for f in (np.cos, np.sin)])
    table = table.astype(ml_dtypes.bfloat16)
    return jnp.asarray(table), jnp.asarray(np.ascontiguousarray(table.T))


def shuffle_table():
    index = np.arange(BAND * BAND)
    source = (index % BAND) * BAND + index // BAND
    table = np.zeros((BAND * BAND, BAND * BAND), np.float32)
    table[index, source] = 1.0
    return jnp.asarray(table.astype(ml_dtypes.bfloat16))


def dot(a, b):
    return jnp.dot(a, b, preferred_element_type=F32)


def conv_kernel(ch, rate, half_no, model_h, dirty_h, psf_h, table_h, turned_h, *refs):
    own_first = refs[0] if ch else None
    own_h, cross_h, plane_h = refs[ch : ch + 3]
    (model, dirty, psf, table, turned, cols_x, cols_q, spec_x, spec_q, prod, rows_y, plane, blocks, sems, out_sems) = (
        refs[ch + 3 :]
    )
    img = model.shape[0]
    taps = psf.shape[0]
    shift = taps // 2
    length = table.shape[1]
    half = length // 2
    wide = table.shape[0] // 2

    def rows_of(source, target, start, count):
        return source.at[pl.ds(start, count)], target.at[pl.ds(start, count)]

    pairs = (
        (psf_h.at[ch], psf),
        rows_of(turned_h, turned, 0, taps),
        (model_h.at[ch], model),
        rows_of(turned_h, turned, taps, img - taps),
        rows_of(table_h, table, 0, wide),
        rows_of(table_h, table, wide, wide),
        rows_of(turned_h, turned, img, length - img),
        (dirty_h.at[ch], dirty),
    )
    copies = [pltpu.make_async_copy(*pair, sems.at[i]) for i, pair in enumerate(pairs)]
    for copy in copies:
        copy.start()
    sends = []

    def send(source, target):
        sends.append(pltpu.make_async_copy(source, target, out_sems.at[len(sends)]))
        sends[-1].start()

    if ch:
        send(own_first, own_h.at[:, :, 0])

    zeros = jnp.zeros((wide - half, 2 * wide), BF16)
    prod[half:wide, :] = zeros
    prod[wide + half :, :] = zeros

    def columns(source, depth, target):
        for n in range(0, 2 * wide, 256):
            for m in range(0, depth, 128):
                one = dot(source[m : m + 128, :], turned[:depth, n : n + 256])
                target[m : m + 128, n : n + 256] = one.astype(BF16)

    copies[0].wait()
    copies[1].wait()
    columns(psf, taps, cols_q)
    copies[2].wait()
    copies[3].wait()
    columns(model, img, cols_x)

    def products(start, count):
        for row in range(start, start + count, 16):
            c, s, t = (slice(at + row, at + row + 16) for at in (0, half, wide))
            for j in range(0, wide, 128):
                lc, ls = slice(j, j + 128), slice(wide + j, wide + j + 128)
                xcc, xcs, xsc, xss = spec_x[c, lc], spec_x[c, ls], spec_x[s, lc], spec_x[s, ls]
                qcc, qcs, qsc, qss = spec_q[c, lc], spec_q[c, ls], spec_q[s, lc], spec_q[s, ls]
                prod[c, lc] = ((xcc * qcc + xss * qss) - (xsc * qsc + xcs * qcs)).astype(BF16)
                prod[t, ls] = ((xcc * qss + xss * qcc) + (xsc * qcs + xcs * qsc)).astype(BF16)
                prod[t, lc] = ((xcc * qsc - xss * qcs) + (xsc * qcc - xcs * qss)).astype(BF16)
                prod[c, ls] = ((xcc * qcs - xss * qsc) + (xcs * qcc - xsc * qss)).astype(BF16)

    copies[4].wait()
    copies[5].wait()
    step = half // 2
    for start in range(0, half, step):
        for k in range(2):
            source = slice(k * wide + start, k * wide + start + step)
            target = slice(k * half + start, k * half + start + step)
            for n in range(0, 2 * wide, 256):
                lanes = slice(n, n + 256)
                spec_q[target, lanes] = dot(table[source, :taps], cols_q[:, lanes])
                spec_x[target, lanes] = dot(table[source, :img], cols_x[:, lanes])
        products(start, step)

    copies[6].wait()
    for n in range(0, 2 * wide, 256):
        for m in range(0, img, 128):
            back = turned[shift + m : shift + m + 128, :]
            rows_y[m : m + 128, n : n + 256] = dot(back, prod[:, n : n + 256]).astype(BF16)

    copies[7].wait()
    bands, parts, band, part = blocks.shape[1:]
    scale = rate[ch] * (4.0 / (length * length))
    step = 128
    for i in range(img // step):
        rows = slice(i * step, (i + 1) * step)
        inner = rows_y[rows, :]
        blurred = jnp.concatenate(
            [dot(inner, table[:, shift + n : shift + n + 256]) for n in range(0, img, 256)], axis=1
        )
        stepped = rate[ch] * dirty[rows, :].astype(F32) - scale * blurred
        stepped = (model[rows, :].astype(F32) + stepped).astype(BF16)
        plane[rows, :] = stepped
        side, at = i * step // (bands * band), i * step % (bands * band) // band
        other = 1 - half_no[0] if side else half_no[0]
        for p in range(parts):
            piece = stepped[:, p * part : (p + 1) * part]
            blocks[other, at : at + step // band, p] = piece.reshape(step // band, band, part)
    send(blocks.at[1], cross_h)
    send(blocks.at[0], own_h.at[:, :, 1] if ch else own_h)
    send(plane, plane_h)
    for copy in sends:
        copy.wait()


def mix_kernel(q, gain, b_in, w_in_t, w_out_t, swap, own, cross_0, cross_1, *refs):
    earlier, refs = (refs[0], refs[1:]) if q else (None, refs)
    own_out, cross_out, bias, normed, hidden, mixed = refs
    sources, _, band, part = cross_out.shape
    channels = 4 * sources
    groups = channels // band
    lane = slice(q * part, (q + 1) * part)

    def tile(j):
        other, e, c = j // (2 * sources), j // 2 % sources, j % 2
        block = (cross_1 if c else cross_0)[e, :, lane] if other else own[e, c, :, lane]
        return block.astype(F32)

    bias[...] = jnp.broadcast_to(b_in[...], bias.shape)
    power = jnp.zeros((band, part), F32)
    for j in range(channels):
        v = tile(j)
        power = power + v * v
    inverse = lax.rsqrt(power * (1.0 / channels) + 1e-06)
    for g in range(groups):
        rows = [(tile(j) * inverse * gain[j]).astype(BF16) for j in range(g * band, (g + 1) * band)]
        swapped = dot(swap[...], jnp.concatenate(rows, axis=0)).astype(BF16)
        normed[:, g * band : (g + 1) * band, :] = swapped.reshape(band, band, part)

    a = math.sqrt(2.0 / math.pi)
    blocks = [slice(n, min(n + 256, part)) for n in range(0, part, 256)]
    for r in range(band):
        for lanes in blocks:
            for h in range(0, hidden.shape[1], 128):
                rows = slice(h, h + 128)
                inner = (dot(w_in_t[rows, :], normed[r, :, lanes]) + bias[rows, lanes]).astype(BF16)
                bent = inner * (BF16(a) + BF16(a * 0.044715) * (inner * inner))
                hidden[r, rows, lanes] = inner + inner * jnp.tanh(bent)
    for r in range(band):
        for lanes in blocks:
            mixed[r, :, lanes] = (0.5 * dot(w_out_t[...], hidden[r, :, lanes])).astype(BF16)

    if q:
        own_out[:, :q] = earlier[...]
    for g in range(groups):
        block = mixed[:, g * band : (g + 1) * band, :].reshape(band * band, part)
        swapped = dot(swap[...], block).astype(BF16).reshape(band // 2, 2, band, part)
        other, e = g // (groups // 2), g % (groups // 2) * (band // 2)
        if other:
            cross_out[e : e + band // 2] = swapped
        else:
            own_out[e : e + band // 2, q] = swapped


def spread_kernel(first, half_no, taps, plane_0, plane_1, own, *refs):
    bands, parts, chunks, ch_dev, band, part = own.shape
    cross, refs = refs[:chunks], refs[chunks:]
    out, above, middle, below, result, sems = refs
    channels = taps.shape[0] // 9
    img = parts * part * chunks
    group = 4
    size = group * band

    def rows_of(other, start, ch):
        pieces = []
        for p in range(parts):
            for q in range(chunks):
                where = slice(start, start + group)
                block = cross[q][where, p, ch] if other else own[where, p, q, ch]
                pieces.append(block.reshape(size, part))
        return jnp.concatenate(pieces, axis=1).astype(F32)

    zero = jnp.zeros((img // 128, 8, 128), F32)
    above[:, 0:8, :] = zero
    below[:, img : img + 8, :] = zero
    lane = lax.broadcasted_iota(jnp.int32, (size, img), 1)
    sends = []
    for ch in range(ch_dev):
        k = [[taps[(3 * i + j) * channels + first[0] + ch] for j in range(3)] for i in range(3)]

        def across(other, start):
            x = rows_of(other, start, ch)
            low = jnp.where(lane == 0, 0.0, pltpu.roll(x, 1, 1))
            high = jnp.where(lane == img - 1, 0.0, pltpu.roll(x, img - 1, 1))
            side = 1 - half_no[0] if other else half_no[0]
            at = side * (img // 2) + start * band
            for target, row, off in ((above, 0, 8), (middle, 1, 0), (below, 2, 0)):
                value = k[row][0] * low + k[row][1] * x + k[row][2] * high
                where = pl.ds(pl.multiple_of(at + off, 8), size)
                for n in range(img // 128):
                    target[n, where, :] = value[:, n * 128 : (n + 1) * 128]

        def leave(at):
            rows = slice(at, at + size)
            base = (plane_1 if ch else plane_0)[rows, :].astype(F32)
            for n in range(img // 128):
                total = above[n, at + 7 : at + 7 + size, :] + below[n, at + 1 : at + 1 + size, :]
                total = total + middle[n, rows, :]
                total = base[:, n * 128 : (n + 1) * 128] + total
                result[ch, rows, n * 128 : (n + 1) * 128] = total.astype(BF16)
            sem = sems.at[(ch * img + at) // size]
            sends.append(pltpu.make_async_copy(result.at[ch, pl.ds(at, size)], out.at[ch, pl.ds(at, size)], sem))
            sends[-1].start()

        for other in range(2):
            for start in range(0, bands, group):
                across(other, start)
        for at in range(0, img, size):
            leave(at)
    for send in sends:
        send.wait()


VMEM = pl.BlockSpec(memory_space=pltpu.VMEM)
SMEM = pl.BlockSpec(memory_space=pltpu.SMEM)
HBM = pl.BlockSpec(memory_space=pltpu.HBM)


def params(mib):
    return pltpu.CompilerParams(vmem_limit_bytes=mib * MIB)


def exchange(blocks):
    return lax.all_to_all(blocks, ("rows", "side"), split_axis=0, concat_axis=0, tiled=True)


def swap_halves(blocks):
    return lax.ppermute(blocks, "half", [(0, 1), (1, 0)])


def local(model, dirty, psf, step_size, gain, w_in, b_in, w_out, kernel):
    ch_dev, img, _ = model.shape
    psf_len = psf.shape[1]
    assert ch_dev == 2
    n_rows, n_side = lax.axis_size("rows"), lax.axis_size("side")
    n_half = n_rows * n_side
    channels = gain.shape[0]
    hidden = b_in.shape[0]
    part = img * img // (2 * n_half * BAND)
    parts = img // part
    bands = img // BAND // 2
    chunks = 2 if part % 256 == 0 else 1
    lanes = part // chunks
    table, turned = tables(img, psf_len)
    length, wide = turned.shape[0], table.shape[0] // 2
    half_no = lax.axis_index("half").astype(jnp.int32)

    def conv(ch, model, *own_first):
        one = jax.ShapeDtypeStruct((bands, parts, BAND, part), BF16)
        two = jax.ShapeDtypeStruct((bands, parts, 2, BAND, part), BF16)
        return pl.pallas_call(
            lambda *refs: conv_kernel(ch, *refs),
            out_shape=[two if ch else one, one, jax.ShapeDtypeStruct((img, img), BF16)],
            in_specs=[SMEM, SMEM] + [HBM] * (5 + ch),
            out_specs=[HBM] * 3,
            scratch_shapes=[
                pltpu.VMEM((img, img), BF16),
                pltpu.VMEM((img, img), BF16),
                pltpu.VMEM((psf_len, psf_len), BF16),
                pltpu.VMEM(table.shape, BF16),
                pltpu.VMEM(turned.shape, BF16),
                pltpu.VMEM((img, 2 * wide), BF16),
                pltpu.VMEM((psf_len, 2 * wide), BF16),
                pltpu.VMEM((length, 2 * wide), F32),
                pltpu.VMEM((length, 2 * wide), F32),
                pltpu.VMEM((2 * wide, 2 * wide), BF16),
                pltpu.VMEM((img, 2 * wide), BF16),
                pltpu.VMEM((img, img), BF16),
                pltpu.VMEM((2, bands, parts, BAND, part), BF16),
                pltpu.SemaphoreType.DMA((8,)),
                pltpu.SemaphoreType.DMA((4,)),
            ],
            compiler_params=params(58),
            cost_estimate=pl.CostEstimate(flops=6_000_000_000, bytes_accessed=4_000_000, transcendentals=0),
            name="conv",
        )(step_size, half_no[None], model, dirty, psf, table, turned, *own_first)

    def mix(q, *blocks):
        one = jax.ShapeDtypeStruct((n_half, ch_dev, BAND, lanes), BF16)
        own = jax.ShapeDtypeStruct((n_half, q + 1, ch_dev, BAND, lanes), BF16)
        return pl.pallas_call(
            lambda *refs: mix_kernel(q, *refs),
            out_shape=[own, one],
            in_specs=[SMEM] + [VMEM] * (4 + len(blocks)),
            out_specs=[VMEM] * 2,
            scratch_shapes=[
                pltpu.VMEM((hidden, lanes), F32),
                pltpu.VMEM((BAND, channels, lanes), BF16),
                pltpu.VMEM((BAND, hidden, lanes), BF16),
                pltpu.VMEM((BAND, channels, lanes), BF16),
            ],
            compiler_params=params(24),
            cost_estimate=pl.CostEstimate(flops=3_000_000_000, bytes_accessed=2_000_000, transcendentals=0),
            name="mix",
        )(gain, b_in[:, None], w_in.T, w_out, shuffle_table(), *blocks)

    def by_half(values):
        grid = values.reshape(n_rows, 2, n_side, ch_dev, -1).transpose(1, 0, 2, 3, 4)
        return jnp.where(half_no == 0, grid, grid[::-1]).reshape(channels, -1)

    own_first, cross_0, plane_0 = conv(0, model)
    own_first, cross_0, model = lax.optimization_barrier((own_first, cross_0, model))
    got_0 = swap_halves(cross_0.reshape(n_half, BAND, part))
    own, cross_1, plane_1 = conv(1, model, own_first)
    own, cross_1, gain, w_in, b_in, w_out, kernel = lax.optimization_barrier(
        (own, cross_1, gain, w_in, b_in, w_out, kernel)
    )
    got_1 = swap_halves(cross_1.reshape(n_half, BAND, part))
    tiles = exchange(own.reshape(n_half, ch_dev, BAND, part))
    tiles_0 = exchange(got_0)
    tiles_1 = exchange(got_1)

    gain = by_half(gain)[:, 0]
    w_in = by_half(w_in)
    w_out = by_half(w_out.T)

    earlier, returned = [], []
    for q in range(chunks):
        mixed, cross = mix(q, tiles, tiles_0, tiles_1, *earlier)
        earlier = [mixed]
        returned.append(swap_halves(cross))
    mixed = exchange(mixed).reshape(bands, parts, chunks, ch_dev, BAND, lanes)
    returned = [exchange(block).reshape(bands, parts, ch_dev, BAND, lanes) for block in returned]
    position = lax.axis_index(("rows", "half", "side")).astype(jnp.int32) * ch_dev
    scratch = pltpu.VMEM((img // 128, img + 8, 128), F32)

    return pl.pallas_call(
        spread_kernel,
        out_shape=jax.ShapeDtypeStruct((ch_dev, img, img), BF16),
        in_specs=[SMEM, SMEM, SMEM] + [VMEM] * (3 + chunks),
        out_specs=HBM,
        scratch_shapes=[
            scratch, scratch, scratch, pltpu.VMEM((ch_dev, img, img), BF16),
            pltpu.SemaphoreType.DMA((ch_dev * img // 64,)),
        ],
        compiler_params=params(24),
        name="spread",
    )(position[None], half_no[None], kernel.reshape(-1), plane_0, plane_1, mixed, *returned)


def solution(mesh):
    grid = mesh.devices
    halves = Mesh(grid.reshape(grid.shape[0], 2, grid.shape[1] // 2), ("rows", "half", "side"))
    every = ("rows", "half", "side")
    planes = P(every, None, None)
    return jax.shard_map(
        local,
        mesh=halves,
        in_specs=(planes, planes, planes, P(every), P(), P(), P(), P(), P()),
        out_specs=planes,
        check_vma=False,
    )
```

```python
import math

import jax
import jax.numpy as jnp
import ml_dtypes
import numpy as np
from jax import lax
from jax.experimental import pallas as pl
from jax.experimental.pallas import tpu as pltpu
from jax.sharding import PartitionSpec as P

BAND = 16
MIB = 1024 * 1024
BF16, F32 = jnp.bfloat16, jnp.float32


def tables(img, psf):
    length = img + psf // 2
    half = length // 2
    pad = -half % 128
    phase = (2 * np.arange(half)[:, None] + 1) * np.arange(length)[None, :] % (2 * length)
    angle = phase * (math.pi / length)
    table = np.concatenate([np.pad(f(angle), ((pad, 0), (0, 0))) for f in (np.cos, np.sin)])
    table = np.pad(table, ((0, pad), (0, 0))).astype(ml_dtypes.bfloat16)
    return jnp.asarray(table), jnp.asarray(np.ascontiguousarray(table[pad:].T))


def shuffle_table():
    index = np.arange(BAND * BAND)
    source = (index % BAND) * BAND + index // BAND
    table = np.zeros((BAND * BAND, BAND * BAND), np.float32)
    table[index, source] = 1.0
    return jnp.asarray(table.astype(ml_dtypes.bfloat16))


def dot(a, b):
    return jnp.dot(a, b, preferred_element_type=F32)


def conv_kernel(
    rate, model_h, dirty_h, psf_h, table_h, turned_h, out_h,
    model, dirty, psf, table, turned, cols_x, cols_q, spec_x, spec_q, prod, rows_y, out, sems, out_sems,
):
    img = model.shape[1]
    taps = psf.shape[1]
    shift = taps // 2
    length = table.shape[1]
    half = length // 2
    wide = turned.shape[1] // 2
    pad = wide - half
    own = length - wide
    shared = wide - own

    def rows_of(source, target, start, count):
        return source.at[pl.ds(start, count)], target.at[pl.ds(start, count)]

    pairs = (
        (psf_h, psf),
        rows_of(turned_h, turned, 0, taps),
        (model_h.at[0], model.at[0]),
        rows_of(turned_h, turned, taps, img - taps),
        (model_h.at[1], model.at[1]),
        rows_of(table_h, table, 0, pad + wide),
        rows_of(table_h, table, pad + wide, wide),
        rows_of(turned_h, turned, img, length - img),
        (dirty_h, dirty),
    )
    copies = [pltpu.make_async_copy(*pair, sems.at[i]) for i, pair in enumerate(pairs)]
    for copy in copies[:5]:
        copy.start()

    zeros = jnp.zeros((pad, 2 * length), BF16)
    prod[half:wide, :] = zeros
    prod[wide + half :, :] = zeros

    def columns(source, depth, target, waits):
        step = 128
        for wait in waits[:2]:
            copies[wait].wait()
        for copy in copies[waits[3]]:
            copy.start()
        for ch in range(2):
            if ch and waits[2] is not None:
                copies[waits[2]].wait()
            for m in range(0, depth, step):
                rows = slice(m, m + step)
                part = jnp.concatenate(
                    [dot(source[ch, rows, :], turned[:depth, n : n + 256]) for n in range(0, 2 * wide, 256)],
                    axis=1,
                )
                for k in range(2):
                    at = k * length
                    one = part[:, k * wide : (k + 1) * wide]
                    if ch == 0:
                        target[rows, at : at + wide] = one.astype(BF16)
                    else:
                        one = pltpu.roll(one, pad, 1)
                        both = one[:, :shared] + target[rows, at + own : at + wide].astype(F32)
                        target[rows, at + own : at + wide] = both.astype(BF16)
                        target[rows, at + wide : at + length] = one[:, shared:].astype(BF16)

    columns(psf, taps, cols_q, (0, 1, None, slice(5, 7)))
    columns(model, img, cols_x, (2, 3, 4, slice(7, 9)))

    def products(start, count):
        for row in range(start, start + count, 16):
            c, s, t = (slice(at + row, at + row + 16) for at in (0, half, wide))
            for j in range(0, length, 128):
                lc, ls = slice(j, j + 128), slice(length + j, length + j + 128)
                xcc, xcs, xsc, xss = spec_x[c, lc], spec_x[c, ls], spec_x[s, lc], spec_x[s, ls]
                qcc, qcs, qsc, qss = spec_q[c, lc], spec_q[c, ls], spec_q[s, lc], spec_q[s, ls]
                prod[c, lc] = ((xcc * qcc + xss * qss) - (xsc * qsc + xcs * qcs)).astype(BF16)
                prod[t, ls] = ((xcc * qss + xss * qcc) + (xsc * qcs + xcs * qsc)).astype(BF16)
                prod[t, lc] = ((xcc * qsc - xss * qcs) + (xsc * qcc - xcs * qss)).astype(BF16)
                prod[c, ls] = ((xcc * qcs - xss * qsc) + (xcs * qcc - xsc * qss)).astype(BF16)

    copies[5].wait()
    copies[6].wait()
    step = half // 2
    for start in range(0, half, step):
        for k in range(2):
            source = slice(pad + k * wide + start, pad + k * wide + start + step)
            target = slice(k * half + start, k * half + start + step)
            for n in range(0, 2 * length, 256):
                lanes = slice(n, n + 256)
                spec_q[target, lanes] = dot(table[source, :taps], cols_q[:, lanes])
                spec_x[target, lanes] = dot(table[source, :img], cols_x[:, lanes])
        products(start, step)

    copies[7].wait()
    for n in range(0, 2 * length, 256):
        for m in range(0, img, 128):
            back = turned[shift + m : shift + m + 128, :]
            rows_y[m : m + 128, n : n + 256] = dot(back, prod[:, n : n + 256]).astype(BF16)

    copies[8].wait()
    bands, parts, _, band, part = out.shape
    sends = []
    cuts = [*range(0, img - 63, 128), img - 64, img]
    for i, (start, stop) in enumerate(zip(cuts, cuts[1:])):
        step = stop - start
        rows = slice(start, stop)
        where = slice(start // band, stop // band)
        for ch in range(2):
            at = ch * own
            inner = jnp.concatenate(
                [rows_y[rows, at : at + wide], rows_y[rows, length + at : length + at + wide]], axis=1
            )
            back = table[pad * (1 - ch) : pad * (1 - ch) + 2 * wide, shift:]
            scale = rate[ch] * (4.0 / (length * length))
            blurred = jnp.concatenate([dot(inner, back[:, n : n + 256]) for n in range(0, img, 256)], axis=1)
            stepped = rate[ch] * dirty[ch, rows, :].astype(F32) - scale * blurred
            stepped = (model[ch, rows, :].astype(F32) + stepped).astype(BF16)
            for p in range(parts):
                piece = stepped[:, p * part : (p + 1) * part]
                out[where, p, ch] = piece.reshape(step // band, band, part)
        sends.append(pltpu.make_async_copy(out.at[where], out_h.at[where], out_sems.at[i]))
        sends[-1].start()
    for send in sends:
        send.wait()


def mix_kernel(gain, w_in_t, w_out_t, swap, tiles, out, normed, hidden, mixed):
    channels, band, part = tiles.shape
    groups = channels // band

    normed[:, channels:, :] = jnp.ones((band, band, part), BF16)
    power = jnp.zeros((band, part), F32)
    for c in range(channels):
        v = tiles[c].astype(F32)
        power = power + v * v
    inverse = lax.rsqrt(power * (1.0 / channels) + 1e-06)
    for g in range(groups):
        rows = [
            (tiles[c].astype(F32) * inverse * gain[c]).astype(BF16)
            for c in range(g * band, (g + 1) * band)
        ]
        swapped = dot(swap[...], jnp.concatenate(rows, axis=0)).astype(BF16)
        normed[:, g * band : (g + 1) * band, :] = swapped.reshape(band, band, part)

    a = math.sqrt(2.0 / math.pi)
    blocks = [slice(n, min(n + 256, part)) for n in range(0, part, 256)]
    for r in range(band):
        for lanes in blocks:
            for h in range(0, hidden.shape[1], 128):
                rows = slice(h, h + 128)
                inner = dot(w_in_t[rows, :], normed[r, :, lanes]).astype(BF16)
                bent = inner * (BF16(a) + BF16(a * 0.044715) * (inner * inner))
                hidden[r, rows, lanes] = inner + inner * jnp.tanh(bent)
    for r in range(band):
        for lanes in blocks:
            mixed[r, :, lanes] = (0.5 * dot(w_out_t[...], hidden[r, :, lanes])).astype(BF16)

    for g in range(groups):
        block = mixed[:, g * band : (g + 1) * band, :].reshape(band * band, part)
        swapped = dot(swap[...], block).astype(BF16)
        out[g * band : (g + 1) * band] = swapped.reshape(band, band, part)


def spread_kernel(first, taps, stepped, mixed, out, above, middle, below, result, sems):
    channels = taps.shape[0] // 9
    bands, parts, ch_dev, band, part = stepped.shape
    img = parts * part
    group = 4
    size = group * band

    def rows_of(source, start, ch):
        pieces = [source[start : start + group, p, ch].reshape(size, part) for p in range(parts)]
        return jnp.concatenate(pieces, axis=1).astype(F32)

    zero = jnp.zeros((img // 128, 8, 128), F32)
    above[:, 0:8, :] = zero
    below[:, img : img + 8, :] = zero
    lane = lax.broadcasted_iota(jnp.int32, (size, 128), 1)
    sends = []
    for ch in range(ch_dev):
        k = [[taps[(3 * i + j) * channels + first[0] + ch] for j in range(3)] for i in range(3)]

        def across(start):
            x = rows_of(mixed, start, ch)
            low = pltpu.roll(x, 1, 1)
            low = jnp.concatenate([jnp.where(lane == 0, 0.0, low[:, :128]), low[:, 128:]], axis=1)
            high = pltpu.roll(x, img - 1, 1)
            high = jnp.concatenate([high[:, :-128], jnp.where(lane == 127, 0.0, high[:, -128:])], axis=1)
            at = start * band
            for target, row, off in ((above, 0, 8), (middle, 1, 0), (below, 2, 0)):
                value = k[row][0] * low + k[row][1] * x + k[row][2] * high
                for n in range(img // 128):
                    target[n, at + off : at + off + size, :] = value[:, n * 128 : (n + 1) * 128]

        def down(start):
            at = start * band
            base = rows_of(stepped, start, ch)
            for n in range(img // 128):
                total = above[n, at + 7 : at + 7 + size, :] + below[n, at + 1 : at + 1 + size, :]
                total = total + middle[n, at : at + size, :]
                total = base[:, n * 128 : (n + 1) * 128] + total
                result[ch, at : at + size, n * 128 : (n + 1) * 128] = total.astype(BF16)

        def leave(start):
            down(start)
            rows = pl.ds(start * band, size)
            at = sems.at[ch * (bands // group) + start // group]
            sends.append(pltpu.make_async_copy(result.at[ch, rows], out.at[ch, rows], at))
            sends[-1].start()

        for start in range(0, bands, group):
            across(start)
            if start:
                leave(start - group)
        leave(bands - group)
    for send in sends:
        send.wait()


VMEM = pl.BlockSpec(memory_space=pltpu.VMEM)
SMEM = pl.BlockSpec(memory_space=pltpu.SMEM)
HBM = pl.BlockSpec(memory_space=pltpu.HBM)


def params(mib):
    return pltpu.CompilerParams(vmem_limit_bytes=mib * MIB)


def exchange(blocks):
    return lax.all_to_all(blocks, ("rows", "cols"), split_axis=0, concat_axis=0, tiled=True)


def with_bias(w_in, b_in):
    columns = []
    for _ in range(3):
        columns.append(lax.reduce_precision(b_in, 8, 7))
        b_in = b_in - columns[-1]
    bias = jnp.stack(columns, axis=1).astype(BF16)
    return jnp.concatenate([w_in.T, jnp.pad(bias, ((0, 0), (0, BAND - 3)))], axis=1)


def local(model, dirty, psf, step_size, gain, w_in, b_in, w_out, kernel):
    ch_dev, img, _ = model.shape
    psf_len = psf.shape[1]
    assert ch_dev == 2
    n_dev = lax.axis_size("rows") * lax.axis_size("cols")
    channels = gain.shape[0]
    hidden = b_in.shape[0]
    part = img * img // (n_dev * BAND)
    parts = img // part
    bands = img // BAND
    table, turned = tables(img, psf_len)
    length, wide = turned.shape[0], turned.shape[1] // 2
    blocks = (bands, parts, ch_dev, BAND, part)

    stepped = pl.pallas_call(
        conv_kernel,
        out_shape=jax.ShapeDtypeStruct(blocks, BF16),
        in_specs=[SMEM] + [HBM] * 5,
        out_specs=HBM,
        scratch_shapes=[
            pltpu.VMEM(model.shape, BF16),
            pltpu.VMEM(model.shape, BF16),
            pltpu.VMEM(psf.shape, BF16),
            pltpu.VMEM(table.shape, BF16),
            pltpu.VMEM(turned.shape, BF16),
            pltpu.VMEM((img, 2 * length), BF16),
            pltpu.VMEM((psf_len, 2 * length), BF16),
            pltpu.VMEM((length, 2 * length), F32),
            pltpu.VMEM((length, 2 * length), F32),
            pltpu.VMEM((2 * wide, 2 * length), BF16),
            pltpu.VMEM((img, 2 * length), BF16),
            pltpu.VMEM(blocks, BF16),
            pltpu.SemaphoreType.DMA((9,)),
            pltpu.SemaphoreType.DMA((img // 128 + 1,)),
        ],
        compiler_params=params(58),
        name="conv",
    )(step_size, model, dirty, psf, table, turned)
    stepped, w_in, b_in, w_out, kernel = lax.optimization_barrier((stepped, w_in, b_in, w_out, kernel))

    tiles = exchange(stepped.reshape(n_dev, ch_dev, BAND, part)).reshape(channels, BAND, part)

    mixed = pl.pallas_call(
        mix_kernel,
        out_shape=jax.ShapeDtypeStruct((channels, BAND, part), BF16),
        in_specs=[SMEM] + [VMEM] * 4,
        out_specs=VMEM,
        scratch_shapes=[
            pltpu.VMEM((BAND, channels + BAND, part), BF16),
            pltpu.VMEM((BAND, hidden, part), BF16),
            pltpu.VMEM((BAND, channels, part), BF16),
        ],
        compiler_params=params(24),
        name="mix",
    )(gain, with_bias(w_in, b_in), w_out.T, shuffle_table(), tiles)

    returned = exchange(mixed.reshape(n_dev, ch_dev, BAND, part)).reshape(blocks)
    position = lax.axis_index(("rows", "cols")).astype(jnp.int32) * ch_dev
    plane = pltpu.VMEM((img // 128, img + 8, 128), F32)

    return pl.pallas_call(
        spread_kernel,
        out_shape=jax.ShapeDtypeStruct((ch_dev, img, img), BF16),
        in_specs=[SMEM, SMEM, VMEM, VMEM],
        out_specs=HBM,
        scratch_shapes=[
            plane, plane, plane, pltpu.VMEM((ch_dev, img, img), BF16),
            pltpu.SemaphoreType.DMA((ch_dev * bands // 4,)),
        ],
        compiler_params=params(24),
        name="spread",
    )(position[None], kernel.reshape(-1), stepped, returned)


def solution(mesh):
    return jax.shard_map(
        local,
        mesh=mesh,
        in_specs=(
            P(("rows", "cols"), None, None),
            P(("rows", "cols"), None, None),
            P(("rows", "cols"), None, None),
            P(("rows", "cols")),
            P(),
            P(),
            P(),
            P(),
            P(),
        ),
        out_specs=P(("rows", "cols"), None, None),
        check_vma=False,
    )
```

```python
import math

import jax
import jax.numpy as jnp
import ml_dtypes
import numpy as np
from jax import lax
from jax.experimental import pallas as pl
from jax.experimental.pallas import tpu as pltpu
from jax.sharding import PartitionSpec as P

BAND = 16
MIB = 1024 * 1024
BF16, F32 = jnp.bfloat16, jnp.float32


def tables(img, psf):
    length = img + psf // 2
    half = length // 2
    pad = -half % 128
    phase = (2 * np.arange(half)[:, None] + 1) * np.arange(length)[None, :] % (2 * length)
    angle = phase * (math.pi / length)
    table = np.concatenate([np.pad(f(angle), ((pad, 0), (0, 0))) for f in (np.cos, np.sin)])
    table = np.pad(table, ((0, pad), (0, 0))).astype(ml_dtypes.bfloat16)
    return jnp.asarray(table), jnp.asarray(np.ascontiguousarray(table[pad:].T))


def shuffle_table():
    index = np.arange(BAND * BAND)
    source = (index % BAND) * BAND + index // BAND
    table = np.zeros((BAND * BAND, BAND * BAND), np.float32)
    table[index, source] = 1.0
    return jnp.asarray(table.astype(ml_dtypes.bfloat16))


def dot(a, b):
    return jnp.dot(a, b, preferred_element_type=F32)


def conv_kernel(
    rate_h, model_h, dirty_h, psf_h, table_h, turned_h, out_h,
    rate, model, dirty, psf, table, turned, cols_x, cols_q, spec_x, spec_q, prod, rows_y, out, sems, out_sems,
):
    img = model.shape[1]
    taps = psf.shape[1]
    shift = taps // 2
    length = table.shape[1]
    half = length // 2
    wide = turned.shape[1] // 2
    pad = wide - half
    own = length - wide
    shared = wide - own

    loads = {}

    def load(name, source, target, start, count, pieces):
        for i in range(pieces):
            rows = pl.ds(start + i * count // pieces, count // pieces)
            copy = pltpu.make_async_copy(source.at[rows], target.at[rows], sems.at[sum(map(len, loads.values()))])
            copy.start()
            loads.setdefault(name, []).append(copy)

    def arrived(name):
        for copy in loads[name]:
            copy.wait()

    load("psf", psf_h.at[0], psf.at[0], 0, taps, 1)
    load("turned_0", turned_h, turned, 0, taps, 4)
    load("psf", psf_h.at[1], psf.at[1], 0, taps, 1)
    load("model_0", model_h.at[0], model.at[0], 0, img, 2)
    load("turned_1", turned_h, turned, taps, img - taps, 2)
    load("model_1", model_h.at[1], model.at[1], 0, img, 2)
    load("table", table_h, table, 0, table.shape[0], 4)
    load("rest", turned_h, turned, img, length - img, 1)
    load("dirty", dirty_h, dirty, 0, 2, 2)
    loads["rate"] = [pltpu.make_async_copy(rate_h, rate, sems.at[sum(map(len, loads.values()))])]
    loads["rate"][0].start()

    zeros = jnp.zeros((pad, 2 * length), BF16)
    prod[half:wide, :] = zeros
    prod[wide + half :, :] = zeros

    def columns(source, depth, target, waits):
        step = 128
        for ch in range(2):
            for wait in waits[ch]:
                arrived(wait)
            for m in range(0, depth, step):
                rows = slice(m, m + step)
                part = jnp.concatenate(
                    [dot(source[ch, rows, :], turned[:depth, n : n + 256]) for n in range(0, 2 * wide, 256)],
                    axis=1,
                )
                for k in range(2):
                    at = k * length
                    one = part[:, k * wide : (k + 1) * wide]
                    if ch == 0:
                        target[rows, at : at + wide] = one.astype(BF16)
                    else:
                        one = pltpu.roll(one, pad, 1)
                        both = one[:, :shared] + target[rows, at + own : at + wide].astype(F32)
                        target[rows, at + own : at + wide] = both.astype(BF16)
                        target[rows, at + wide : at + length] = one[:, shared:].astype(BF16)

    columns(psf, taps, cols_q, (("psf", "turned_0"), ()))
    columns(model, img, cols_x, (("model_0", "turned_1"), ("model_1",)))

    def products(start, count):
        for row in range(start, start + count, 16):
            c, s, t = (slice(at + row, at + row + 16) for at in (0, half, wide))
            for j in range(0, length, 128):
                lc, ls = slice(j, j + 128), slice(length + j, length + j + 128)
                xcc, xcs, xsc, xss = spec_x[c, lc], spec_x[c, ls], spec_x[s, lc], spec_x[s, ls]
                qcc, qcs, qsc, qss = spec_q[c, lc], spec_q[c, ls], spec_q[s, lc], spec_q[s, ls]
                prod[c, lc] = ((xcc * qcc + xss * qss) - (xsc * qsc + xcs * qcs)).astype(BF16)
                prod[t, ls] = ((xcc * qss + xss * qcc) + (xsc * qcs + xcs * qsc)).astype(BF16)
                prod[t, lc] = ((xcc * qsc - xss * qcs) + (xsc * qcc - xcs * qss)).astype(BF16)
                prod[c, ls] = ((xcc * qcs - xss * qsc) + (xcs * qcc - xsc * qss)).astype(BF16)

    arrived("table")
    step = half // 2
    for start in range(0, half, step):
        for k in range(2):
            source = slice(pad + k * wide + start, pad + k * wide + start + step)
            target = slice(k * half + start, k * half + start + step)
            for n in range(0, 2 * length, 256):
                lanes = slice(n, n + 256)
                spec_q[target, lanes] = dot(table[source, :taps], cols_q[:, lanes])
                spec_x[target, lanes] = dot(table[source, :img], cols_x[:, lanes])
        products(start, step)

    arrived("rest")
    for n in range(0, 2 * length, 256):
        for m in range(0, img, 128):
            back = turned[shift + m : shift + m + 128, :]
            rows_y[m : m + 128, n : n + 256] = dot(back, prod[:, n : n + 256]).astype(BF16)

    arrived("dirty")
    arrived("rate")
    bands, parts, _, band, part = out.shape
    step = 128
    sends = []
    for i in range(img // step):
        rows = slice(i * step, (i + 1) * step)
        where = slice(i * step // band, (i + 1) * step // band)
        for ch in range(2):
            at = ch * own
            inner = jnp.concatenate(
                [rows_y[rows, at : at + wide], rows_y[rows, length + at : length + at + wide]], axis=1
            )
            back = table[pad * (1 - ch) : pad * (1 - ch) + 2 * wide, shift:]
            scale = rate[ch] * (4.0 / (length * length))
            blurred = jnp.concatenate([dot(inner, back[:, n : n + 256]) for n in range(0, img, 256)], axis=1)
            stepped = rate[ch] * dirty[ch, rows, :].astype(F32) - scale * blurred
            stepped = (model[ch, rows, :].astype(F32) + stepped).astype(BF16)
            for p in range(parts):
                piece = stepped[:, p * part : (p + 1) * part]
                out[where, p, ch] = piece.reshape(step // band, band, part)
        sends.append(pltpu.make_async_copy(out.at[where], out_h.at[where], out_sems.at[i]))
        sends[-1].start()
    for send in sends:
        send.wait()


def mix_kernel(gain, w_in_t, w_out_t, swap, tiles, out_h, normed, hidden, mixed, out, sems):
    channels, band, part = tiles.shape
    groups = channels // band

    normed[:, channels:, :] = jnp.ones((band, band, part), BF16)
    power = jnp.zeros((band, part), F32)
    for c in range(channels):
        v = tiles[c].astype(F32)
        power = power + v * v
    inverse = lax.rsqrt(power * (1.0 / channels) + 1e-06)
    for g in range(groups):
        rows = [
            (tiles[c].astype(F32) * inverse * gain[c : c + 1, :]).astype(BF16)
            for c in range(g * band, (g + 1) * band)
        ]
        swapped = dot(swap[...], jnp.concatenate(rows, axis=0)).astype(BF16)
        normed[:, g * band : (g + 1) * band, :] = swapped.reshape(band, band, part)

    a = math.sqrt(2.0 / math.pi)
    blocks = [slice(n, min(n + 256, part)) for n in range(0, part, 256)]
    for r in range(band):
        for lanes in blocks:
            for h in range(0, hidden.shape[1], 128):
                rows = slice(h, h + 128)
                inner = dot(w_in_t[rows, :], normed[r, :, lanes]).astype(BF16)
                bent = inner * (BF16(a) + BF16(a * 0.044715) * (inner * inner))
                hidden[r, rows, lanes] = inner + inner * jnp.tanh(bent)
    for r in range(band):
        for lanes in blocks:
            mixed[r, :, lanes] = (0.5 * dot(w_out_t[...], hidden[r, :, lanes])).astype(BF16)

    sends = []
    for g in range(groups):
        block = mixed[:, g * band : (g + 1) * band, :].reshape(band * band, part)
        swapped = dot(swap[...], block).astype(BF16)
        where = pl.ds(g * band, band)
        out[where] = swapped.reshape(band, band, part)
        sends.append(pltpu.make_async_copy(out.at[where], out_h.at[where], sems.at[g]))
        sends[-1].start()
    for send in sends:
        send.wait()


def spread_kernel(taps, stepped, mixed, out, above, middle, below, result, sems):
    bands, parts, ch_dev, band, part = stepped.shape
    img = parts * part
    group = 4
    size = group * band

    def rows_of(source, start, ch):
        pieces = [source[start : start + group, p, ch].reshape(size, part) for p in range(parts)]
        return jnp.concatenate(pieces, axis=1).astype(F32)

    zero = jnp.zeros((img // 128, 8, 128), F32)
    above[:, 0:8, :] = zero
    below[:, img : img + 8, :] = zero
    lane = lax.broadcasted_iota(jnp.int32, (size, 128), 1)
    sends = []
    for ch in range(ch_dev):
        k = [[taps[i, j, ch : ch + 1, :] for j in range(3)] for i in range(3)]

        def across(start):
            x = rows_of(mixed, start, ch)
            low, high = pltpu.roll(x, 1, 1), pltpu.roll(x, img - 1, 1)
            at = start * band
            for n in range(img // 128):
                lanes = slice(n * 128, (n + 1) * 128)
                left, here, right = low[:, lanes], x[:, lanes], high[:, lanes]
                if n == 0:
                    left = jnp.where(lane == 0, 0.0, left)
                if n == img // 128 - 1:
                    right = jnp.where(lane == 127, 0.0, right)
                for target, row, off in ((above, 0, 8), (middle, 1, 0), (below, 2, 0)):
                    value = k[row][0] * left + k[row][1] * here + k[row][2] * right
                    target[n, at + off : at + off + size, :] = value

        def down(start):
            at = start * band
            base = rows_of(stepped, start, ch)
            for n in range(img // 128):
                total = above[n, at + 7 : at + 7 + size, :] + below[n, at + 1 : at + 1 + size, :]
                total = total + middle[n, at : at + size, :]
                total = base[:, n * 128 : (n + 1) * 128] + total
                result[ch, at : at + size, n * 128 : (n + 1) * 128] = total.astype(BF16)

        def leave(start):
            down(start)
            rows = pl.ds(start * band, size)
            at = sems.at[ch * (bands // group) + start // group]
            sends.append(pltpu.make_async_copy(result.at[ch, rows], out.at[ch, rows], at))
            sends[-1].start()

        for start in range(0, bands, group):
            across(start)
            if start:
                leave(start - group)
        leave(bands - group)
    for send in sends:
        send.wait()


VMEM = pl.BlockSpec(memory_space=pltpu.VMEM)
SMEM = pl.BlockSpec(memory_space=pltpu.SMEM)
HBM = pl.BlockSpec(memory_space=pltpu.HBM)


def params(mib):
    return pltpu.CompilerParams(vmem_limit_bytes=mib * MIB)


def exchange(blocks):
    return lax.all_to_all(blocks, ("rows", "cols"), split_axis=0, concat_axis=0, tiled=True)


def with_bias(w_in, b_in):
    columns = []
    for _ in range(3):
        columns.append(lax.reduce_precision(b_in, 8, 7))
        b_in = b_in - columns[-1]
    bias = jnp.stack(columns, axis=1).astype(BF16)
    return jnp.concatenate([w_in.T, jnp.pad(bias, ((0, 0), (0, BAND - 3)))], axis=1)


def local(model, dirty, psf, step_size, gain, w_in, b_in, w_out, kernel):
    ch_dev, img, _ = model.shape
    psf_len = psf.shape[1]
    assert ch_dev == 2
    n_dev = lax.axis_size("rows") * lax.axis_size("cols")
    channels = gain.shape[0]
    hidden = b_in.shape[0]
    part = img * img // (n_dev * BAND)
    parts = img // part
    bands = img // BAND
    table, turned = tables(img, psf_len)
    length, wide = turned.shape[0], turned.shape[1] // 2
    blocks = (bands, parts, ch_dev, BAND, part)

    stepped = pl.pallas_call(
        conv_kernel,
        out_shape=jax.ShapeDtypeStruct(blocks, BF16),
        in_specs=[HBM] * 6,
        out_specs=HBM,
        scratch_shapes=[
            pltpu.SMEM(step_size.shape, F32),
            pltpu.VMEM(model.shape, BF16),
            pltpu.VMEM(model.shape, BF16),
            pltpu.VMEM(psf.shape, BF16),
            pltpu.VMEM(table.shape, BF16),
            pltpu.VMEM(turned.shape, BF16),
            pltpu.VMEM((img, 2 * length), BF16),
            pltpu.VMEM((psf_len, 2 * length), BF16),
            pltpu.VMEM((length, 2 * length), F32),
            pltpu.VMEM((length, 2 * length), F32),
            pltpu.VMEM((2 * wide, 2 * length), BF16),
            pltpu.VMEM((img, 2 * length), BF16),
            pltpu.VMEM(blocks, BF16),
            pltpu.SemaphoreType.DMA((20,)),
            pltpu.SemaphoreType.DMA((img // 128,)),
        ],
        compiler_params=params(58),
        name="conv",
    )(step_size, model, dirty, psf, table, turned)
    stepped, gain, w_in, b_in, w_out, kernel = lax.optimization_barrier(
        (stepped, gain, w_in, b_in, w_out, kernel)
    )

    tiles = exchange(stepped.reshape(n_dev, ch_dev, BAND, part)).reshape(channels, BAND, part)

    mixed = pl.pallas_call(
        mix_kernel,
        out_shape=jax.ShapeDtypeStruct((channels, BAND, part), BF16),
        in_specs=[VMEM] * 5,
        out_specs=HBM,
        scratch_shapes=[
            pltpu.VMEM((BAND, channels + BAND, part), BF16),
            pltpu.VMEM((BAND, hidden, part), BF16),
            pltpu.VMEM((BAND, channels, part), BF16),
            pltpu.VMEM((channels, BAND, part), BF16),
            pltpu.SemaphoreType.DMA((channels // BAND,)),
        ],
        compiler_params=params(24),
        name="mix",
    )(jnp.broadcast_to(gain[:, None], (channels, part)), with_bias(w_in, b_in), w_out.T, shuffle_table(), tiles)

    returned = exchange(mixed.reshape(n_dev, ch_dev, BAND, part)).reshape(blocks)
    position = lax.axis_index(("rows", "cols")).astype(jnp.int32) * ch_dev
    taps = lax.dynamic_slice_in_dim(kernel, position, ch_dev, axis=2)
    taps = jnp.broadcast_to(taps[..., None], (3, 3, ch_dev, 128))
    plane = pltpu.VMEM((img // 128, img + 8, 128), F32)

    return pl.pallas_call(
        spread_kernel,
        out_shape=jax.ShapeDtypeStruct((ch_dev, img, img), BF16),
        in_specs=[VMEM] * 3,
        out_specs=HBM,
        scratch_shapes=[
            plane, plane, plane, pltpu.VMEM((ch_dev, img, img), BF16),
            pltpu.SemaphoreType.DMA((ch_dev * bands // 4,)),
        ],
        compiler_params=params(24),
        name="spread",
    )(taps, stepped, returned)


def solution(mesh):
    return jax.shard_map(
        local,
        mesh=mesh,
        in_specs=(
            P(("rows", "cols"), None, None),
            P(("rows", "cols"), None, None),
            P(("rows", "cols"), None, None),
            P(("rows", "cols")),
            P(),
            P(),
            P(),
            P(),
            P(),
        ),
        out_specs=P(("rows", "cols"), None, None),
        check_vma=False,
    )
```

```python
import functools
import math

import jax
import jax.numpy as jnp
import ml_dtypes
import numpy as np
from jax import lax
from jax.experimental import pallas as pl
from jax.experimental.pallas import tpu as pltpu
from jax.sharding import PartitionSpec as P

BAND = 16
GROUP = 64
MIB = 1024 * 1024
BF16, F32 = jnp.bfloat16, jnp.float32


def tables(img, psf):
    length = img + psf // 2
    half = length // 2
    phase = (2 * np.arange(half)[:, None] + 1) * np.arange(length)[None, :] % (2 * length)
    angle = (phase * (math.pi / length)).reshape(half // GROUP, 1, GROUP, length)
    table = np.concatenate([np.cos(angle), np.sin(angle)], axis=1).reshape(length, length)
    table = table.astype(ml_dtypes.bfloat16)
    return jnp.asarray(table), jnp.asarray(np.ascontiguousarray(table.T))


def shuffle_table():
    index = np.arange(BAND * BAND)
    source = (index % BAND) * BAND + index // BAND
    table = np.zeros((BAND * BAND, BAND * BAND), np.float32)
    table[index, source] = 1.0
    return jnp.asarray(table.astype(ml_dtypes.bfloat16))


def dot(a, b):
    return jnp.dot(a, b, preferred_element_type=F32)


def interleave(first, second):
    done = 0
    for i, step in enumerate(first):
        step()
        while done * len(first) < (i + 1) * len(second):
            second[done]()
            done += 1


def conv_kernel(
    rate_h, model_h, dirty_h, psf_h, table_h, turned_h, out_h,
    rate, model, dirty, psf, table, turned, cols_x, cols_q, spec_x, spec_q, prod, rows_y, out, sems, out_sems,
):
    img = model.shape[1]
    taps = psf.shape[1]
    shift = taps // 2
    length = table.shape[1]
    tiles = [slice(n, n + 256) for n in range(0, 2 * length, 256)]
    loads = {}

    def load(name, source, target, start, count, pieces):
        for i in range(pieces):
            rows = pl.ds(start + i * count // pieces, count // pieces)
            copy = pltpu.make_async_copy(source.at[rows], target.at[rows], sems.at[sum(map(len, loads.values()))])
            copy.start()
            loads.setdefault(name, []).append(copy)

    def arrived(name):
        for copy in loads[name]:
            copy.wait()

    load("psf", psf_h.at[0], psf.at[0], 0, taps, 1)
    load("turned_0", turned_h, turned, 0, taps, 4)
    load("psf", psf_h.at[1], psf.at[1], 0, taps, 1)
    load("model_0", model_h.at[0], model.at[0], 0, img, 2)
    load("turned_1", turned_h, turned, taps, img - taps, 2)
    load("model_1", model_h.at[1], model.at[1], 0, img, 2)
    load("table", table_h, table, 0, length, 4)
    load("rest", turned_h, turned, img, length - img, 1)
    load("dirty", dirty_h, dirty, 0, 2, 2)
    loads["rate"] = [pltpu.make_async_copy(rate_h, rate, sems.at[sum(map(len, loads.values()))])]
    loads["rate"][0].start()

    def columns(source, depth, target, waits):
        for ch in range(2):
            for wait in waits[ch]:
                arrived(wait)
            for m in range(0, depth, 128):
                rows = slice(m, m + 128)
                for n in range(0, length, 256):
                    lanes = slice(n, min(n + 256, length))
                    to = slice(ch * length + lanes.start, ch * length + lanes.stop)
                    target[rows, to] = dot(source[ch, rows, :], turned[:depth, lanes]).astype(BF16)

    columns(psf, taps, cols_q, (("psf", "turned_0"), ()))
    columns(model, img, cols_x, (("model_0", "turned_1"), ("model_1",)))

    def spectra(lanes):
        def one(target, source, depth, m):
            target[m : m + 160, lanes] = dot(table[m : m + 160, :depth], source[:, lanes])

        return [
            functools.partial(one, target, source, depth, m)
            for m in range(0, length, 160)
            for target, source, depth in ((spec_q, cols_q, taps), (spec_x, cols_x, img))
        ]

    lane = lax.broadcasted_iota(jnp.int32, (16, 2 * GROUP), 1)
    sign = jnp.where(lane < GROUP, -1.0, 1.0)

    def products(lanes):
        def one(row, at):
            c, s, columns = slice(row, row + 16), slice(row + GROUP, row + GROUP + 16), slice(at, at + 2 * GROUP)

            def parts(value):
                turn = pltpu.roll(value, GROUP, 1)
                return jnp.where(lane < GROUP, value, turn), jnp.where(lane < GROUP, turn, value)

            (c_re, c_im), (s_re, s_im) = parts(spec_x[c, columns]), parts(spec_x[s, columns])
            q_c, q_s = spec_q[c, columns], spec_q[s, columns]
            t_c, t_s = pltpu.roll(q_c, GROUP, 1) * sign, pltpu.roll(q_s, GROUP, 1) * sign
            prod[c, columns] = ((c_re * q_c + c_im * t_c) - (s_re * q_s + s_im * t_s)).astype(BF16)
            prod[s, columns] = ((s_re * q_c + s_im * t_c) + (c_re * q_s + c_im * t_s)).astype(BF16)

        return [
            functools.partial(one, base + row, at)
            for base in range(0, length, 2 * GROUP)
            for row in range(0, GROUP, 16)
            for at in range(lanes.start, lanes.stop, 2 * GROUP)
        ]

    def inverse(lanes):
        def one(m):
            back = turned[shift + m : shift + m + 128, :]
            rows_y[m : m + 128, lanes] = dot(back, prod[:, lanes]).astype(BF16)

        return [functools.partial(one, m) for m in range(0, img, 128)]

    arrived("table")
    arrived("rest")
    for step in spectra(tiles[0]):
        step()
    for t in range(len(tiles)):
        matrix = (inverse(tiles[t - 1]) if t else []) + (spectra(tiles[t + 1]) if t + 1 < len(tiles) else [])
        interleave(products(tiles[t]), matrix)
    for step in inverse(tiles[-1]):
        step()

    arrived("dirty")
    arrived("rate")
    bands, parts, _, band, part = out.shape
    step = 128
    sends = []
    for i in range(img // step):
        rows = slice(i * step, (i + 1) * step)
        where = slice(i * step // band, (i + 1) * step // band)
        for ch in range(2):
            inner = rows_y[rows, ch * length : (ch + 1) * length]
            blurred = jnp.concatenate(
                [dot(inner, table[:, shift + n : shift + n + 256]) for n in range(0, img, 256)], axis=1
            )
            scale = rate[ch] * (4.0 / (length * length))
            stepped = rate[ch] * dirty[ch, rows, :].astype(F32) - scale * blurred
            stepped = (model[ch, rows, :].astype(F32) + stepped).astype(BF16)
            for p in range(parts):
                piece = stepped[:, p * part : (p + 1) * part]
                out[where, p, ch] = piece.reshape(step // band, band, part)
        sends.append(pltpu.make_async_copy(out.at[where], out_h.at[where], out_sems.at[i]))
        sends[-1].start()
    for send in sends:
        send.wait()


def mix_kernel(gain, w_in_t, w_out_t, swap, tiles, out_h, normed, hidden, mixed, out, sems):
    channels, band, part = tiles.shape
    groups = channels // band

    normed[:, channels:, :] = jnp.ones((band, band, part), BF16)
    a = math.sqrt(2.0 / math.pi)
    sends = []

    def norm(lanes):
        size = lanes.stop - lanes.start
        power = jnp.zeros((band, size), F32)
        for c in range(channels):
            v = tiles[c, :, lanes].astype(F32)
            power = power + v * v
        inverse = lax.rsqrt(power * (1.0 / channels) + 1e-06)
        for g in range(groups):
            rows = [
                (tiles[c, :, lanes].astype(F32) * inverse * gain[c : c + 1, lanes]).astype(BF16)
                for c in range(g * band, (g + 1) * band)
            ]
            swapped = dot(swap[...], jnp.concatenate(rows, axis=0)).astype(BF16)
            normed[:, g * band : (g + 1) * band, lanes] = swapped.reshape(band, band, size)

    def first_layer(lanes):
        for r in range(band):
            for h in range(0, hidden.shape[1], 128):
                rows = slice(h, h + 128)
                inner = dot(w_in_t[rows, :], normed[r, :, lanes]).astype(BF16)
                bent = inner * (BF16(a) + BF16(a * 0.044715) * (inner * inner))
                hidden[r, rows, lanes] = inner + inner * jnp.tanh(bent)

    def second_layer(lanes):
        for r in range(band):
            mixed[r, :, lanes] = (0.5 * dot(w_out_t[...], hidden[r, :, lanes])).astype(BF16)

    def leave(lanes):
        size = lanes.stop - lanes.start
        for g in range(groups):
            block = mixed[:, g * band : (g + 1) * band, lanes].reshape(band * band, size)
            swapped = dot(swap[...], block).astype(BF16)
            where = pl.ds(g * band, band), slice(None), pl.ds(lanes.start, size)
            out[g * band : (g + 1) * band, :, lanes] = swapped.reshape(band, band, size)
            sends.append(pltpu.make_async_copy(out.at[where], out_h.at[where], sems.at[len(sends)]))
            sends[-1].start()

    blocks = [slice(n, min(n + 256, part)) for n in range(0, part, 256)]
    norm(blocks[0])
    for i, lanes in enumerate(blocks):
        first_layer(lanes)
        if i + 1 < len(blocks):
            norm(blocks[i + 1])
        second_layer(lanes)
        leave(lanes)
    for send in sends:
        send.wait()


def spread_kernel(taps, stepped, mixed, out, above, middle, below, result, sems):
    bands, parts, ch_dev, band, part = stepped.shape
    img = parts * part
    group = 4
    size = group * band

    def rows_of(source, start, ch):
        pieces = [source[start : start + group, p, ch].reshape(size, part) for p in range(parts)]
        return jnp.concatenate(pieces, axis=1).astype(F32)

    zero = jnp.zeros((img // 128, 8, 128), F32)
    above[:, 0:8, :] = zero
    below[:, img : img + 8, :] = zero
    lane = lax.broadcasted_iota(jnp.int32, (size, 128), 1)
    sends = []
    for ch in range(ch_dev):
        k = [[taps[i, j, ch : ch + 1, :] for j in range(3)] for i in range(3)]

        def across(start):
            x = rows_of(mixed, start, ch)
            low, high = pltpu.roll(x, 1, 1), pltpu.roll(x, img - 1, 1)
            at = start * band
            for n in range(img // 128):
                lanes = slice(n * 128, (n + 1) * 128)
                left, here, right = low[:, lanes], x[:, lanes], high[:, lanes]
                if n == 0:
                    left = jnp.where(lane == 0, 0.0, left)
                if n == img // 128 - 1:
                    right = jnp.where(lane == 127, 0.0, right)
                for target, row, off in ((above, 0, 8), (middle, 1, 0), (below, 2, 0)):
                    value = k[row][0] * left + k[row][1] * here + k[row][2] * right
                    target[n, at + off : at + off + size, :] = value

        def down(start):
            at = start * band
            base = rows_of(stepped, start, ch)
            for n in range(img // 128):
                total = above[n, at + 7 : at + 7 + size, :] + below[n, at + 1 : at + 1 + size, :]
                total = total + middle[n, at : at + size, :]
                total = base[:, n * 128 : (n + 1) * 128] + total
                result[ch, at : at + size, n * 128 : (n + 1) * 128] = total.astype(BF16)

        def leave(start):
            down(start)
            rows = pl.ds(start * band, size)
            at = sems.at[ch * (bands // group) + start // group]
            sends.append(pltpu.make_async_copy(result.at[ch, rows], out.at[ch, rows], at))
            sends[-1].start()

        for start in range(0, bands, group):
            across(start)
            if start:
                leave(start - group)
        leave(bands - group)
    for send in sends:
        send.wait()


VMEM = pl.BlockSpec(memory_space=pltpu.VMEM)
SMEM = pl.BlockSpec(memory_space=pltpu.SMEM)
HBM = pl.BlockSpec(memory_space=pltpu.HBM)


def params(mib):
    return pltpu.CompilerParams(vmem_limit_bytes=mib * MIB)


def exchange(blocks):
    return lax.all_to_all(blocks, ("rows", "cols"), split_axis=0, concat_axis=0, tiled=True)


def with_bias(w_in, b_in):
    columns = []
    for _ in range(3):
        columns.append(lax.reduce_precision(b_in, 8, 7))
        b_in = b_in - columns[-1]
    bias = jnp.stack(columns, axis=1).astype(BF16)
    return jnp.concatenate([w_in.T, jnp.pad(bias, ((0, 0), (0, BAND - 3)))], axis=1)


def local(model, dirty, psf, step_size, gain, w_in, b_in, w_out, kernel):
    ch_dev, img, _ = model.shape
    psf_len = psf.shape[1]
    assert ch_dev == 2
    n_dev = lax.axis_size("rows") * lax.axis_size("cols")
    channels = gain.shape[0]
    hidden = b_in.shape[0]
    part = img * img // (n_dev * BAND)
    parts = img // part
    bands = img // BAND
    table, turned = tables(img, psf_len)
    length = table.shape[0]
    blocks = (bands, parts, ch_dev, BAND, part)

    stepped = pl.pallas_call(
        conv_kernel,
        out_shape=jax.ShapeDtypeStruct(blocks, BF16),
        in_specs=[HBM] * 6,
        out_specs=HBM,
        scratch_shapes=[
            pltpu.SMEM(step_size.shape, F32),
            pltpu.VMEM(model.shape, BF16),
            pltpu.VMEM(model.shape, BF16),
            pltpu.VMEM(psf.shape, BF16),
            pltpu.VMEM(table.shape, BF16),
            pltpu.VMEM(turned.shape, BF16),
            pltpu.VMEM((img, 2 * length), BF16),
            pltpu.VMEM((psf_len, 2 * length), BF16),
            pltpu.VMEM((length, 2 * length), F32),
            pltpu.VMEM((length, 2 * length), F32),
            pltpu.VMEM((length, 2 * length), BF16),
            pltpu.VMEM((img, 2 * length), BF16),
            pltpu.VMEM(blocks, BF16),
            pltpu.SemaphoreType.DMA((20,)),
            pltpu.SemaphoreType.DMA((img // 128,)),
        ],
        compiler_params=params(58),
        name="conv",
    )(step_size, model, dirty, psf, table, turned)
    stepped, gain, w_in, b_in, w_out, kernel = lax.optimization_barrier(
        (stepped, gain, w_in, b_in, w_out, kernel)
    )

    tiles = exchange(stepped.reshape(n_dev, ch_dev, BAND, part)).reshape(channels, BAND, part)

    mixed = pl.pallas_call(
        mix_kernel,
        out_shape=jax.ShapeDtypeStruct((channels, BAND, part), BF16),
        in_specs=[VMEM] * 5,
        out_specs=HBM,
        scratch_shapes=[
            pltpu.VMEM((BAND, channels + BAND, part), BF16),
            pltpu.VMEM((BAND, hidden, part), BF16),
            pltpu.VMEM((BAND, channels, part), BF16),
            pltpu.VMEM((channels, BAND, part), BF16),
            pltpu.SemaphoreType.DMA((channels // BAND * max(1, part // 256),)),
        ],
        compiler_params=params(24),
        name="mix",
    )(jnp.broadcast_to(gain[:, None], (channels, part)), with_bias(w_in, b_in), w_out.T, shuffle_table(), tiles)

    returned = exchange(mixed.reshape(n_dev, ch_dev, BAND, part)).reshape(blocks)
    position = lax.axis_index(("rows", "cols")).astype(jnp.int32) * ch_dev
    taps = lax.dynamic_slice_in_dim(kernel, position, ch_dev, axis=2)
    taps = jnp.broadcast_to(taps[..., None], (3, 3, ch_dev, 128))
    plane = pltpu.VMEM((img // 128, img + 8, 128), F32)

    return pl.pallas_call(
        spread_kernel,
        out_shape=jax.ShapeDtypeStruct((ch_dev, img, img), BF16),
        in_specs=[VMEM] * 3,
        out_specs=HBM,
        scratch_shapes=[
            plane, plane, plane, pltpu.VMEM((ch_dev, img, img), BF16),
            pltpu.SemaphoreType.DMA((ch_dev * bands // 4,)),
        ],
        compiler_params=params(24),
        name="spread",
    )(taps, stepped, returned)


def solution(mesh):
    return jax.shard_map(
        local,
        mesh=mesh,
        in_specs=(
            P(("rows", "cols"), None, None),
            P(("rows", "cols"), None, None),
            P(("rows", "cols"), None, None),
            P(("rows", "cols")),
            P(),
            P(),
            P(),
            P(),
            P(),
        ),
        out_specs=P(("rows", "cols"), None, None),
        check_vma=False,
    )
```

```python
import functools
import math

import jax
import jax.numpy as jnp
import ml_dtypes
import numpy as np
from jax import lax
from jax.experimental import pallas as pl
from jax.experimental.pallas import tpu as pltpu
from jax.sharding import PartitionSpec as P

BAND = 16
GROUP = 64
MIB = 1024 * 1024
BF16, F32 = jnp.bfloat16, jnp.float32


def tables(img, psf):
    length = img + psf // 2
    half = length // 2
    phase = (2 * np.arange(half)[:, None] + 1) * np.arange(length)[None, :] % (2 * length)
    angle = (phase * (math.pi / length)).reshape(half // GROUP, 1, GROUP, length)
    table = np.concatenate([np.cos(angle), np.sin(angle)], axis=1).reshape(length, length)
    table = table.astype(ml_dtypes.bfloat16)
    return jnp.asarray(table), jnp.asarray(np.ascontiguousarray(table.T))


def dot(a, b):
    return jnp.dot(a, b, preferred_element_type=F32)


def interleave(first, second):
    done = 0
    for i, step in enumerate(first):
        step()
        while done * len(first) < (i + 1) * len(second):
            second[done]()
            done += 1


def conv_kernel(
    rate_h, model_h, dirty_h, psf_h, table_h, turned_h, out_h,
    rate, model, dirty, psf, table, turned, cols_x, cols_q, spec_x, spec_q, prod, rows_y, out, sems, out_sems,
):
    img = model.shape[1]
    taps = psf.shape[1]
    shift = taps // 2
    length = table.shape[1]
    tiles = [slice(n, n + 256) for n in range(0, 2 * length, 256)]
    tall = length // 2
    loads = {}

    def load(name, source, target, start, count, pieces):
        for i in range(pieces):
            rows = pl.ds(start + i * count // pieces, count // pieces)
            copy = pltpu.make_async_copy(source.at[rows], target.at[rows], sems.at[sum(map(len, loads.values()))])
            copy.start()
            loads.setdefault(name, []).append(copy)

    def arrived(name):
        for copy in loads[name]:
            copy.wait()

    load("psf", psf_h.at[0], psf.at[0], 0, taps, 1)
    load("turned_0", turned_h, turned, 0, taps, 4)
    load("psf", psf_h.at[1], psf.at[1], 0, taps, 1)
    load("model_0", model_h.at[0], model.at[0], 0, img, 2)
    load("turned_1", turned_h, turned, taps, img - taps, 2)
    load("model_1", model_h.at[1], model.at[1], 0, img, 2)
    load("table", table_h, table, 0, length, 4)
    load("rest", turned_h, turned, img, length - img, 1)
    load("dirty", dirty_h, dirty, 0, 2, 2)
    loads["rate"] = [pltpu.make_async_copy(rate_h, rate, sems.at[sum(map(len, loads.values()))])]
    loads["rate"][0].start()

    def columns(source, depth, target, waits):
        for ch in range(2):
            for wait in waits[ch]:
                arrived(wait)
            for m in range(0, depth, 256):
                rows = slice(m, m + 256)
                for n in range(0, length, 256):
                    lanes = slice(n, min(n + 256, length))
                    to = slice(ch * length + lanes.start, ch * length + lanes.stop)
                    target[rows, to] = dot(source[ch, rows, :], turned[:depth, lanes]).astype(BF16)

    columns(psf, taps, cols_q, (("psf", "turned_0"), ()))
    columns(model, img, cols_x, (("model_0", "turned_1"), ("model_1",)))

    def spectra(lanes):
        def one(target, source, depth, m):
            target[m : m + tall, lanes] = dot(table[m : m + tall, :depth], source[:, lanes])

        return [
            functools.partial(one, target, source, depth, m)
            for m in range(0, length, tall)
            for target, source, depth in ((spec_q, cols_q, taps), (spec_x, cols_x, img))
        ]

    lane = lax.broadcasted_iota(jnp.int32, (16, 2 * GROUP), 1)
    sign = jnp.where(lane < GROUP, -1.0, 1.0)

    def products(lanes):
        def one(row, at):
            c, s, columns = slice(row, row + 16), slice(row + GROUP, row + GROUP + 16), slice(at, at + 2 * GROUP)

            def parts(value):
                turn = pltpu.roll(value, GROUP, 1)
                return jnp.where(lane < GROUP, value, turn), jnp.where(lane < GROUP, turn, value)

            (c_re, c_im), (s_re, s_im) = parts(spec_x[c, columns]), parts(spec_x[s, columns])
            q_c, q_s = spec_q[c, columns], spec_q[s, columns]
            t_c, t_s = pltpu.roll(q_c, GROUP, 1) * sign, pltpu.roll(q_s, GROUP, 1) * sign
            prod[c, columns] = ((c_re * q_c + c_im * t_c) - (s_re * q_s + s_im * t_s)).astype(BF16)
            prod[s, columns] = ((s_re * q_c + s_im * t_c) + (c_re * q_s + c_im * t_s)).astype(BF16)

        return [
            functools.partial(one, base + row, at)
            for base in range(0, length, 2 * GROUP)
            for row in range(0, GROUP, 16)
            for at in range(lanes.start, lanes.stop, 2 * GROUP)
        ]

    def inverse(lanes):
        def one(m):
            back = turned[shift + m : shift + m + 256, :]
            rows_y[m : m + 256, lanes] = dot(back, prod[:, lanes]).astype(BF16)

        return [functools.partial(one, m) for m in range(0, img, 256)]

    arrived("table")
    arrived("rest")
    for step in spectra(tiles[0]):
        step()
    for t in range(len(tiles)):
        matrix = (inverse(tiles[t - 1]) if t else []) + (spectra(tiles[t + 1]) if t + 1 < len(tiles) else [])
        interleave(products(tiles[t]), matrix)
    for step in inverse(tiles[-1]):
        step()

    arrived("dirty")
    arrived("rate")
    bands, parts, _, band, part = out.shape
    step = 256
    sends = []
    for i in range(img // step):
        rows = slice(i * step, (i + 1) * step)
        where = slice(i * step // band, (i + 1) * step // band)
        for ch in range(2):
            scale = rate[ch] * (4.0 / (length * length))
            inner = rows_y[rows, ch * length : (ch + 1) * length]
            for n in range(0, img, 256):
                lanes = slice(n, n + 256)
                blurred = dot(inner, table[:, shift + n : shift + n + 256])
                stepped = rate[ch] * dirty[ch, rows, lanes].astype(F32) - scale * blurred
                stepped = (model[ch, rows, lanes].astype(F32) + stepped).astype(BF16)
                size = min(part, 256)
                for k in range(0, 256, size):
                    piece = stepped[:, k : k + size].reshape(step // band, band, size)
                    at = (n + k) % part
                    out[where, (n + k) // part, ch, :, at : at + size] = piece
            place = where, slice(None), ch
            sends.append(pltpu.make_async_copy(out.at[place], out_h.at[place], out_sems.at[len(sends)]))
            sends[-1].start()
    for send in sends:
        send.wait()


def mix_kernel(gain, weights, tiles, out_h, w_in_t, swap, normed, hidden, mixed, out, sems):
    channels, band, part = tiles.shape
    groups = channels // band

    depth = channels + band
    w_in_t[...] = weights[: w_in_t.shape[1], :].astype(F32).T.astype(BF16)
    w_out_t = weights[w_in_t.shape[1] :, :]
    place = [lax.broadcasted_iota(jnp.int32, swap.shape, axis) for axis in range(2)]
    swap[...] = jnp.where(place[0] % band * band + place[0] // band == place[1], 1.0, 0.0).astype(BF16)
    normed[:, channels:, :] = jnp.ones((band, band, part), BF16)
    power = jnp.zeros((band, part), F32)
    for c in range(channels):
        v = tiles[c].astype(F32)
        power = power + v * v
    inverse = lax.rsqrt(power * (1.0 / channels) + 1e-06)
    for g in range(groups):
        rows = [
            (tiles[c].astype(F32) * inverse * gain[c : c + 1, :]).astype(BF16)
            for c in range(g * band, (g + 1) * band)
        ]
        swapped = dot(swap[...], jnp.concatenate(rows, axis=0)).astype(BF16)
        normed[:, g * band : (g + 1) * band, :] = swapped.reshape(band, band, part)

    a = math.sqrt(2.0 / math.pi)
    blocks = [slice(n, min(n + 256, part)) for n in range(0, part, 256)]
    for r in range(band):
        for lanes in blocks:
            for h in range(0, hidden.shape[1], 128):
                rows = slice(h, h + 128)
                inner = dot(w_in_t[rows, :depth], normed[r, :, lanes]).astype(BF16)
                bent = inner * (BF16(a) + BF16(a * 0.044715) * (inner * inner))
                hidden[r, rows, lanes] = inner + inner * jnp.tanh(bent)
    for r in range(band):
        for lanes in blocks:
            mixed[r, :, lanes] = (0.5 * dot(w_out_t, hidden[r, :, lanes])).astype(BF16)

    sends = []
    for g in range(groups):
        block = mixed[:, g * band : (g + 1) * band, :].reshape(band * band, part)
        swapped = dot(swap[...], block).astype(BF16)
        where = pl.ds(g * band, band)
        out[where] = swapped.reshape(band, band, part)
        sends.append(pltpu.make_async_copy(out.at[where], out_h.at[where], sems.at[g]))
        sends[-1].start()
    for send in sends:
        send.wait()


def spread_kernel(taps, stepped, mixed, out, above, middle, below, result, sems):
    bands, parts, ch_dev, band, part = stepped.shape
    img = parts * part
    group = 4
    size = group * band

    def rows_of(source, start, ch):
        pieces = [source[start : start + group, p, ch].reshape(size, part) for p in range(parts)]
        return jnp.concatenate(pieces, axis=1).astype(F32)

    zero = jnp.zeros((img // 128, 8, 128), F32)
    above[:, 0:8, :] = zero
    below[:, img : img + 8, :] = zero
    lane = lax.broadcasted_iota(jnp.int32, (size, 128), 1)
    sends = []
    for ch in range(ch_dev):
        k = [[taps[i, j, ch : ch + 1, :] for j in range(3)] for i in range(3)]

        def across(start):
            x = rows_of(mixed, start, ch)
            low, high = pltpu.roll(x, 1, 1), pltpu.roll(x, img - 1, 1)
            at = start * band
            for n in range(img // 128):
                lanes = slice(n * 128, (n + 1) * 128)
                left, here, right = low[:, lanes], x[:, lanes], high[:, lanes]
                if n == 0:
                    left = jnp.where(lane == 0, 0.0, left)
                if n == img // 128 - 1:
                    right = jnp.where(lane == 127, 0.0, right)
                for target, row, off in ((above, 0, 8), (middle, 1, 0), (below, 2, 0)):
                    value = k[row][0] * left + k[row][1] * here + k[row][2] * right
                    target[n, at + off : at + off + size, :] = value

        def down(start):
            at = start * band
            base = rows_of(stepped, start, ch)
            for n in range(img // 128):
                total = above[n, at + 7 : at + 7 + size, :] + below[n, at + 1 : at + 1 + size, :]
                total = total + middle[n, at : at + size, :]
                total = base[:, n * 128 : (n + 1) * 128] + total
                result[ch, at : at + size, n * 128 : (n + 1) * 128] = total.astype(BF16)

        def leave(start):
            down(start)
            rows = pl.ds(start * band, size)
            at = sems.at[ch * (bands // group) + start // group]
            sends.append(pltpu.make_async_copy(result.at[ch, rows], out.at[ch, rows], at))
            sends[-1].start()

        for start in range(0, bands, group):
            across(start)
            if start:
                leave(start - group)
        leave(bands - group)
    for send in sends:
        send.wait()


VMEM = pl.BlockSpec(memory_space=pltpu.VMEM)
SMEM = pl.BlockSpec(memory_space=pltpu.SMEM)
HBM = pl.BlockSpec(memory_space=pltpu.HBM)


def params(mib):
    return pltpu.CompilerParams(vmem_limit_bytes=mib * MIB)


def exchange(blocks):
    return lax.all_to_all(blocks, ("rows", "cols"), split_axis=0, concat_axis=0, tiled=True)


def layers(w_in, b_in, w_out, wide):
    rows = []
    for _ in range(3):
        rows.append(lax.reduce_precision(b_in, 8, 7))
        b_in = b_in - rows[-1]
    zeros = jnp.zeros((wide - w_in.shape[0] - 3, w_in.shape[1]), BF16)
    return jnp.concatenate([w_in, jnp.stack(rows).astype(BF16), zeros, w_out.T], axis=0)


def local(model, dirty, psf, step_size, gain, w_in, b_in, w_out, kernel):
    ch_dev, img, _ = model.shape
    psf_len = psf.shape[1]
    assert ch_dev == 2
    n_dev = lax.axis_size("rows") * lax.axis_size("cols")
    channels = gain.shape[0]
    hidden = b_in.shape[0]
    part = img * img // (n_dev * BAND)
    parts = img // part
    bands = img // BAND
    table, turned = tables(img, psf_len)
    length = table.shape[0]
    wide = -(-(channels + BAND) // 128) * 128
    blocks = (bands, parts, ch_dev, BAND, part)

    stepped = pl.pallas_call(
        conv_kernel,
        out_shape=jax.ShapeDtypeStruct(blocks, BF16),
        in_specs=[HBM] * 6,
        out_specs=HBM,
        scratch_shapes=[
            pltpu.SMEM(step_size.shape, F32),
            pltpu.VMEM(model.shape, BF16),
            pltpu.VMEM(model.shape, BF16),
            pltpu.VMEM(psf.shape, BF16),
            pltpu.VMEM(table.shape, BF16),
            pltpu.VMEM(turned.shape, BF16),
            pltpu.VMEM((img, 2 * length), BF16),
            pltpu.VMEM((psf_len, 2 * length), BF16),
            pltpu.VMEM((length, 2 * length), F32),
            pltpu.VMEM((length, 2 * length), F32),
            pltpu.VMEM((length, 2 * length), BF16),
            pltpu.VMEM((img, 2 * length), BF16),
            pltpu.VMEM(blocks, BF16),
            pltpu.SemaphoreType.DMA((20,)),
            pltpu.SemaphoreType.DMA((img // 128,)),
        ],
        compiler_params=params(58),
        name="conv",
    )(step_size, model, dirty, psf, table, turned)
    stepped, gain, w_in, b_in, w_out, kernel = lax.optimization_barrier(
        (stepped, gain, w_in, b_in, w_out, kernel)
    )

    tiles = exchange(stepped.reshape(n_dev, ch_dev, BAND, part)).reshape(channels, BAND, part)

    mixed = pl.pallas_call(
        mix_kernel,
        out_shape=jax.ShapeDtypeStruct((channels, BAND, part), BF16),
        in_specs=[VMEM] * 3,
        out_specs=HBM,
        scratch_shapes=[
            pltpu.VMEM((hidden, wide), BF16),
            pltpu.VMEM((BAND * BAND, BAND * BAND), BF16),
            pltpu.VMEM((BAND, channels + BAND, part), BF16),
            pltpu.VMEM((BAND, hidden, part), BF16),
            pltpu.VMEM((BAND, channels, part), BF16),
            pltpu.VMEM((channels, BAND, part), BF16),
            pltpu.SemaphoreType.DMA((channels // BAND,)),
        ],
        compiler_params=params(24),
        name="mix",
    )(jnp.broadcast_to(gain[:, None], (channels, part)), layers(w_in, b_in, w_out, wide), tiles)

    returned = exchange(mixed.reshape(n_dev, ch_dev, BAND, part)).reshape(blocks)
    position = lax.axis_index(("rows", "cols")).astype(jnp.int32) * ch_dev
    taps = lax.dynamic_slice_in_dim(kernel, position, ch_dev, axis=2)
    taps = jnp.broadcast_to(taps[..., None], (3, 3, ch_dev, 128))
    plane = pltpu.VMEM((img // 128, img + 8, 128), F32)

    return pl.pallas_call(
        spread_kernel,
        out_shape=jax.ShapeDtypeStruct((ch_dev, img, img), BF16),
        in_specs=[VMEM] * 3,
        out_specs=HBM,
        scratch_shapes=[
            plane, plane, plane, pltpu.VMEM((ch_dev, img, img), BF16),
            pltpu.SemaphoreType.DMA((ch_dev * bands // 4,)),
        ],
        compiler_params=params(24),
        name="spread",
    )(taps, stepped, returned)


def solution(mesh):
    return jax.shard_map(
        local,
        mesh=mesh,
        in_specs=(
            P(("rows", "cols"), None, None),
            P(("rows", "cols"), None, None),
            P(("rows", "cols"), None, None),
            P(("rows", "cols")),
            P(),
            P(),
            P(),
            P(),
            P(),
        ),
        out_specs=P(("rows", "cols"), None, None),
        check_vma=False,
    )
```

```python
import functools
import math

import jax
import jax.numpy as jnp
import ml_dtypes
import numpy as np
from jax import lax
from jax.experimental import pallas as pl
from jax.experimental.pallas import tpu as pltpu
from jax.sharding import Mesh
from jax.sharding import PartitionSpec as P

BAND = 16
GROUP = 64
MIB = 1024 * 1024
BF16, F32 = jnp.bfloat16, jnp.float32


def tables(img, psf):
    length = img + psf // 2
    half = length // 2
    phase = (2 * np.arange(half)[:, None] + 1) * np.arange(length)[None, :] % (2 * length)
    angle = (phase * (math.pi / length)).reshape(half // GROUP, 1, GROUP, length)
    table = np.concatenate([np.cos(angle), np.sin(angle)], axis=1).reshape(length, length)
    table = table.astype(ml_dtypes.bfloat16)
    return jnp.asarray(table), jnp.asarray(np.ascontiguousarray(table.T))


def dot(a, b):
    return jnp.dot(a, b, preferred_element_type=F32)


def interleave(first, second):
    done = 0
    for i, step in enumerate(first):
        step()
        while done * len(first) < (i + 1) * len(second):
            second[done]()
            done += 1


def conv_kernel(
    rate_h, model_h, dirty_h, psf_h, table_h, turned_h, out_h,
    rate, model, dirty, psf, table, turned, cols_x, cols_q, spec_x, spec_q, prod, rows_y, out, sems, out_sems,
):
    img = model.shape[1]
    taps = psf.shape[1]
    shift = taps // 2
    length = table.shape[1]
    tiles = [slice(n, n + 256) for n in range(0, 2 * length, 256)]
    tall = length // 2
    loads = {}

    def load(name, source, target, start, count, pieces):
        for i in range(pieces):
            rows = pl.ds(start + i * count // pieces, count // pieces)
            copy = pltpu.make_async_copy(source.at[rows], target.at[rows], sems.at[sum(map(len, loads.values()))])
            copy.start()
            loads.setdefault(name, []).append(copy)

    def arrived(name):
        for copy in loads[name]:
            copy.wait()

    load("psf", psf_h.at[0], psf.at[0], 0, taps, 1)
    load("turned_0", turned_h, turned, 0, taps, 4)
    load("psf", psf_h.at[1], psf.at[1], 0, taps, 1)
    load("model_0", model_h.at[0], model.at[0], 0, img, 2)
    load("turned_1", turned_h, turned, taps, img - taps, 2)
    load("model_1", model_h.at[1], model.at[1], 0, img, 2)
    load("table", table_h, table, 0, length, 4)
    load("rest", turned_h, turned, img, length - img, 1)
    load("dirty", dirty_h, dirty, 0, 2, 2)
    loads["rate"] = [pltpu.make_async_copy(rate_h, rate, sems.at[sum(map(len, loads.values()))])]
    loads["rate"][0].start()

    def columns(source, depth, target, waits):
        for ch in range(2):
            for wait in waits[ch]:
                arrived(wait)
            for m in range(0, depth, 256):
                rows = slice(m, m + 256)
                for n in range(0, length, 256):
                    lanes = slice(n, min(n + 256, length))
                    to = slice(ch * length + lanes.start, ch * length + lanes.stop)
                    target[rows, to] = dot(source[ch, rows, :], turned[:depth, lanes]).astype(BF16)

    columns(psf, taps, cols_q, (("psf", "turned_0"), ()))
    columns(model, img, cols_x, (("model_0", "turned_1"), ("model_1",)))

    def spectra(lanes):
        def one(target, source, depth, m):
            target[m : m + tall, lanes] = dot(table[m : m + tall, :depth], source[:, lanes])

        return [
            functools.partial(one, target, source, depth, m)
            for m in range(0, length, tall)
            for target, source, depth in ((spec_q, cols_q, taps), (spec_x, cols_x, img))
        ]

    lane = lax.broadcasted_iota(jnp.int32, (16, 2 * GROUP), 1)
    sign = jnp.where(lane < GROUP, -1.0, 1.0)

    def products(lanes):
        def one(row, at):
            c, s, columns = slice(row, row + 16), slice(row + GROUP, row + GROUP + 16), slice(at, at + 2 * GROUP)

            def parts(value):
                turn = pltpu.roll(value, GROUP, 1)
                return jnp.where(lane < GROUP, value, turn), jnp.where(lane < GROUP, turn, value)

            (c_re, c_im), (s_re, s_im) = parts(spec_x[c, columns]), parts(spec_x[s, columns])
            q_c, q_s = spec_q[c, columns], spec_q[s, columns]
            t_c, t_s = pltpu.roll(q_c, GROUP, 1) * sign, pltpu.roll(q_s, GROUP, 1) * sign
            prod[c, columns] = ((c_re * q_c + c_im * t_c) - (s_re * q_s + s_im * t_s)).astype(BF16)
            prod[s, columns] = ((s_re * q_c + s_im * t_c) + (c_re * q_s + c_im * t_s)).astype(BF16)

        return [
            functools.partial(one, base + row, at)
            for base in range(0, length, 2 * GROUP)
            for row in range(0, GROUP, 16)
            for at in range(lanes.start, lanes.stop, 2 * GROUP)
        ]

    def inverse(lanes):
        def one(m):
            back = turned[shift + m : shift + m + 256, :]
            rows_y[m : m + 256, lanes] = dot(back, prod[:, lanes]).astype(BF16)

        return [functools.partial(one, m) for m in range(0, img, 256)]

    arrived("table")
    arrived("rest")
    for step in spectra(tiles[0]):
        step()
    for t in range(len(tiles)):
        matrix = (inverse(tiles[t - 1]) if t else []) + (spectra(tiles[t + 1]) if t + 1 < len(tiles) else [])
        interleave(products(tiles[t]), matrix)
    for step in inverse(tiles[-1]):
        step()

    arrived("dirty")
    arrived("rate")
    bands, parts, _, band, part = out.shape
    step = 256
    sends = []
    for i in range(img // step):
        rows = slice(i * step, (i + 1) * step)
        where = slice(i * step // band, (i + 1) * step // band)
        for ch in range(2):
            scale = rate[ch] * (4.0 / (length * length))
            inner = rows_y[rows, ch * length : (ch + 1) * length]
            for n in range(0, img, 256):
                lanes = slice(n, n + 256)
                blurred = dot(inner, table[:, shift + n : shift + n + 256])
                stepped = rate[ch] * dirty[ch, rows, lanes].astype(F32) - scale * blurred
                stepped = (model[ch, rows, lanes].astype(F32) + stepped).astype(BF16)
                size = min(part, 256)
                for k in range(0, 256, size):
                    piece = stepped[:, k : k + size].reshape(step // band, band, size)
                    at = (n + k) % part
                    out[where, (n + k) // part, ch, :, at : at + size] = piece
            place = where, slice(None), ch
            sends.append(pltpu.make_async_copy(out.at[place], out_h.at[place], out_sems.at[len(sends)]))
            sends[-1].start()
    for send in sends:
        send.wait()


def mix_kernel(gain, weights, tiles, out_h, w_in_t, swap, normed, hidden, mixed, out, sems):
    channels, band, part = tiles.shape
    groups = channels // band

    depth = channels + band
    w_in_t[...] = weights[: w_in_t.shape[1], :].astype(F32).T.astype(BF16)
    w_out_t = weights[w_in_t.shape[1] :, :]
    place = [lax.broadcasted_iota(jnp.int32, swap.shape, axis) for axis in range(2)]
    swap[...] = jnp.where(place[0] % band * band + place[0] // band == place[1], 1.0, 0.0).astype(BF16)
    normed[:, channels:, :] = jnp.ones((band, band, part), BF16)
    power = jnp.zeros((band, part), F32)
    for c in range(channels):
        v = tiles[c].astype(F32)
        power = power + v * v
    inverse = lax.rsqrt(power * (1.0 / channels) + 1e-06)
    for g in range(groups):
        rows = [
            (tiles[c].astype(F32) * inverse * gain[c : c + 1, :]).astype(BF16)
            for c in range(g * band, (g + 1) * band)
        ]
        swapped = dot(swap[...], jnp.concatenate(rows, axis=0)).astype(BF16)
        normed[:, g * band : (g + 1) * band, :] = swapped.reshape(band, band, part)

    a = math.sqrt(2.0 / math.pi)
    blocks = [slice(n, min(n + 256, part)) for n in range(0, part, 256)]
    for r in range(band):
        for lanes in blocks:
            for h in range(0, hidden.shape[1], 128):
                rows = slice(h, h + 128)
                inner = dot(w_in_t[rows, :depth], normed[r, :, lanes]).astype(BF16)
                bent = inner * (BF16(a) + BF16(a * 0.044715) * (inner * inner))
                hidden[r, rows, lanes] = inner + inner * jnp.tanh(bent)
    for r in range(band):
        for lanes in blocks:
            mixed[r, :, lanes] = (0.5 * dot(w_out_t, hidden[r, :, lanes])).astype(BF16)

    sends = []
    for g in range(groups):
        block = mixed[:, g * band : (g + 1) * band, :].reshape(band * band, part)
        swapped = dot(swap[...], block).astype(BF16)
        where = pl.ds(g * band, band)
        out[where] = swapped.reshape(band, band, part)
        sends.append(pltpu.make_async_copy(out.at[where], out_h.at[where], sems.at[g]))
        sends[-1].start()
    for send in sends:
        send.wait()


def spread_kernel(taps, stepped, mixed, out, above, middle, below, result, sems):
    bands, parts, ch_dev, band, part = stepped.shape
    img = parts * part
    group = 4
    size = group * band

    def rows_of(source, start, ch):
        pieces = [source[start : start + group, p, ch].reshape(size, part) for p in range(parts)]
        return jnp.concatenate(pieces, axis=1).astype(F32)

    zero = jnp.zeros((img // 128, 8, 128), F32)
    above[:, 0:8, :] = zero
    below[:, img : img + 8, :] = zero
    lane = lax.broadcasted_iota(jnp.int32, (size, 128), 1)
    sends = []
    for ch in range(ch_dev):
        k = [[taps[i, j, ch : ch + 1, :] for j in range(3)] for i in range(3)]

        def across(start):
            x = rows_of(mixed, start, ch)
            low, high = pltpu.roll(x, 1, 1), pltpu.roll(x, img - 1, 1)
            at = start * band
            for n in range(img // 128):
                lanes = slice(n * 128, (n + 1) * 128)
                left, here, right = low[:, lanes], x[:, lanes], high[:, lanes]
                if n == 0:
                    left = jnp.where(lane == 0, 0.0, left)
                if n == img // 128 - 1:
                    right = jnp.where(lane == 127, 0.0, right)
                for target, row, off in ((above, 0, 8), (middle, 1, 0), (below, 2, 0)):
                    value = k[row][0] * left + k[row][1] * here + k[row][2] * right
                    target[n, at + off : at + off + size, :] = value

        def down(start):
            at = start * band
            base = rows_of(stepped, start, ch)
            for n in range(img // 128):
                total = above[n, at + 7 : at + 7 + size, :] + below[n, at + 1 : at + 1 + size, :]
                total = total + middle[n, at : at + size, :]
                total = base[:, n * 128 : (n + 1) * 128] + total
                result[ch, at : at + size, n * 128 : (n + 1) * 128] = total.astype(BF16)

        def leave(start):
            down(start)
            rows = pl.ds(start * band, size)
            at = sems.at[ch * (bands // group) + start // group]
            sends.append(pltpu.make_async_copy(result.at[ch, rows], out.at[ch, rows], at))
            sends[-1].start()

        for start in range(0, bands, group):
            across(start)
            if start:
                leave(start - group)
        leave(bands - group)
    for send in sends:
        send.wait()


VMEM = pl.BlockSpec(memory_space=pltpu.VMEM)
SMEM = pl.BlockSpec(memory_space=pltpu.SMEM)
HBM = pl.BlockSpec(memory_space=pltpu.HBM)


def params(mib):
    return pltpu.CompilerParams(vmem_limit_bytes=mib * MIB)


def exchange(blocks, order):
    return lax.all_to_all(
        blocks, "all", split_axis=0, concat_axis=0, axis_index_groups=[order], tiled=True
    )


def layers(w_in, b_in, w_out_t, wide):
    rows = []
    for _ in range(3):
        rows.append(lax.reduce_precision(b_in, 8, 7))
        b_in = b_in - rows[-1]
    zeros = jnp.zeros((wide - w_in.shape[0] - 3, w_in.shape[1]), BF16)
    return jnp.concatenate([w_in, jnp.stack(rows).astype(BF16), zeros, w_out_t], axis=0)


def local(n_rows, n_cols, model, dirty, psf, step_size, gain, w_in, b_in, w_out, kernel):
    ch_dev, img, _ = model.shape
    psf_len = psf.shape[1]
    assert ch_dev == 2
    n_dev = n_rows * n_cols
    order = [r * n_cols + (c + n_cols // 2) % n_cols for r in range(n_rows) for c in range(n_cols)]
    channels = gain.shape[0]
    hidden = b_in.shape[0]
    part = img * img // (n_dev * BAND)
    parts = img // part
    bands = img // BAND
    table, turned = tables(img, psf_len)
    length = table.shape[0]
    wide = -(-(channels + BAND) // 128) * 128
    blocks = (bands, parts, ch_dev, BAND, part)

    stepped = pl.pallas_call(
        conv_kernel,
        out_shape=jax.ShapeDtypeStruct(blocks, BF16),
        in_specs=[HBM] * 6,
        out_specs=HBM,
        scratch_shapes=[
            pltpu.SMEM(step_size.shape, F32),
            pltpu.VMEM(model.shape, BF16),
            pltpu.VMEM(model.shape, BF16),
            pltpu.VMEM(psf.shape, BF16),
            pltpu.VMEM(table.shape, BF16),
            pltpu.VMEM(turned.shape, BF16),
            pltpu.VMEM((img, 2 * length), BF16),
            pltpu.VMEM((psf_len, 2 * length), BF16),
            pltpu.VMEM((length, 2 * length), F32),
            pltpu.VMEM((length, 2 * length), F32),
            pltpu.VMEM((length, 2 * length), BF16),
            pltpu.VMEM((img, 2 * length), BF16),
            pltpu.VMEM(blocks, BF16),
            pltpu.SemaphoreType.DMA((20,)),
            pltpu.SemaphoreType.DMA((img // 128,)),
        ],
        compiler_params=params(58),
        name="conv",
    )(step_size, model, dirty, psf, table, turned)
    stepped, gain, w_in, b_in, w_out, kernel = lax.optimization_barrier(
        (stepped, gain, w_in, b_in, w_out, kernel)
    )

    def ordered(values):
        return values.reshape(n_rows, 2, channels // (2 * n_rows), -1)[:, ::-1].reshape(values.shape)

    tiles = exchange(stepped.reshape(n_dev, ch_dev, BAND, part), order).reshape(channels, BAND, part)

    mixed = pl.pallas_call(
        mix_kernel,
        out_shape=jax.ShapeDtypeStruct((channels, BAND, part), BF16),
        in_specs=[VMEM] * 3,
        out_specs=HBM,
        scratch_shapes=[
            pltpu.VMEM((hidden, wide), BF16),
            pltpu.VMEM((BAND * BAND, BAND * BAND), BF16),
            pltpu.VMEM((BAND, channels + BAND, part), BF16),
            pltpu.VMEM((BAND, hidden, part), BF16),
            pltpu.VMEM((BAND, channels, part), BF16),
            pltpu.VMEM((channels, BAND, part), BF16),
            pltpu.SemaphoreType.DMA((channels // BAND,)),
        ],
        compiler_params=params(24),
        name="mix",
    )(
        jnp.broadcast_to(ordered(gain)[:, None], (channels, part)),
        layers(ordered(w_in), b_in, ordered(w_out.T), wide),
        tiles,
    )

    returned = exchange(mixed.reshape(n_dev, ch_dev, BAND, part), order).reshape(blocks)
    position = lax.axis_index("all").astype(jnp.int32) * ch_dev
    taps = lax.dynamic_slice_in_dim(kernel, position, ch_dev, axis=2)
    taps = jnp.broadcast_to(taps[..., None], (3, 3, ch_dev, 128))
    plane = pltpu.VMEM((img // 128, img + 8, 128), F32)

    return pl.pallas_call(
        spread_kernel,
        out_shape=jax.ShapeDtypeStruct((ch_dev, img, img), BF16),
        in_specs=[VMEM] * 3,
        out_specs=HBM,
        scratch_shapes=[
            plane, plane, plane, pltpu.VMEM((ch_dev, img, img), BF16),
            pltpu.SemaphoreType.DMA((ch_dev * bands // 4,)),
        ],
        compiler_params=params(24),
        name="spread",
    )(taps, stepped, returned)


def solution(mesh):
    line = Mesh(mesh.devices.reshape(-1), ("all",))
    planes = P("all", None, None)
    return jax.shard_map(
        functools.partial(local, *mesh.devices.shape),
        mesh=line,
        in_specs=(planes, planes, planes, P("all"), P(), P(), P(), P(), P()),
        out_specs=planes,
        check_vma=False,
    )
```

```python
import functools
import math

import jax
import jax.numpy as jnp
import ml_dtypes
import numpy as np
from jax import lax
from jax.experimental import pallas as pl
from jax.experimental.pallas import tpu as pltpu
from jax.sharding import Mesh
from jax.sharding import PartitionSpec as P

BAND = 16
GROUP = 64
MIB = 1024 * 1024
BF16, F32 = jnp.bfloat16, jnp.float32


def tables(img, psf):
    length = img + psf // 2
    half = length // 2
    phase = (2 * np.arange(half)[:, None] + 1) * np.arange(length)[None, :] % (2 * length)
    angle = (phase * (math.pi / length)).reshape(half // GROUP, 1, GROUP, length)
    table = np.concatenate([np.cos(angle), np.sin(angle)], axis=1).reshape(length, length)
    table = table.astype(ml_dtypes.bfloat16)
    return jnp.asarray(table), jnp.asarray(np.ascontiguousarray(table.T))


def dot(a, b):
    return jnp.dot(a, b, preferred_element_type=F32)


def interleave(first, second):
    done = 0
    for i, step in enumerate(first):
        step()
        while done * len(first) < (i + 1) * len(second):
            second[done]()
            done += 1


def conv_kernel(
    rate_h, model_h, dirty_h, psf_h, table_h, turned_h, out_h,
    rate, model, dirty, psf, table, turned, cols_x, cols_q, spec_x, spec_q, prod, rows_y, out, sems, out_sems,
):
    img = model.shape[1]
    taps = psf.shape[1]
    shift = taps // 2
    length = table.shape[1]
    tiles = [slice(n, n + 256) for n in range(0, 2 * length, 256)]
    tall = length // 2
    loads = {}

    def load(name, source, target, start, count, pieces):
        for i in range(pieces):
            rows = pl.ds(start + i * count // pieces, count // pieces)
            copy = pltpu.make_async_copy(source.at[rows], target.at[rows], sems.at[sum(map(len, loads.values()))])
            copy.start()
            loads.setdefault(name, []).append(copy)

    def arrived(name):
        for copy in loads[name]:
            copy.wait()

    load("psf", psf_h.at[0], psf.at[0], 0, taps, 1)
    load("turned_0", turned_h, turned, 0, taps, 4)
    load("psf", psf_h.at[1], psf.at[1], 0, taps, 1)
    load("model_0", model_h.at[0], model.at[0], 0, img, 2)
    load("turned_1", turned_h, turned, taps, img - taps, 2)
    load("model_1", model_h.at[1], model.at[1], 0, img, 2)
    load("table", table_h, table, 0, length, 4)
    load("rest", turned_h, turned, img, length - img, 1)
    load("dirty", dirty_h, dirty, 0, 2, 2)
    loads["rate"] = [pltpu.make_async_copy(rate_h, rate, sems.at[sum(map(len, loads.values()))])]
    loads["rate"][0].start()

    def columns(source, depth, target, waits):
        for ch in range(2):
            for wait in waits[ch]:
                arrived(wait)
            for m in range(0, depth, 256):
                rows = slice(m, m + 256)
                for n in range(0, length, 256):
                    lanes = slice(n, min(n + 256, length))
                    to = slice(ch * length + lanes.start, ch * length + lanes.stop)
                    target[rows, to] = dot(source[ch, rows, :], turned[:depth, lanes]).astype(BF16)

    columns(psf, taps, cols_q, (("psf", "turned_0"), ()))
    columns(model, img, cols_x, (("model_0", "turned_1"), ("model_1",)))

    def spectra(lanes):
        def one(target, source, depth, m):
            target[m : m + tall, lanes] = dot(table[m : m + tall, :depth], source[:, lanes])

        return [
            functools.partial(one, target, source, depth, m)
            for m in range(0, length, tall)
            for target, source, depth in ((spec_q, cols_q, taps), (spec_x, cols_x, img))
        ]

    lane = lax.broadcasted_iota(jnp.int32, (16, 2 * GROUP), 1)
    sign = jnp.where(lane < GROUP, -1.0, 1.0)

    def products(lanes):
        def one(row, at):
            c, s, columns = slice(row, row + 16), slice(row + GROUP, row + GROUP + 16), slice(at, at + 2 * GROUP)

            def parts(value):
                turn = pltpu.roll(value, GROUP, 1)
                return jnp.where(lane < GROUP, value, turn), jnp.where(lane < GROUP, turn, value)

            (c_re, c_im), (s_re, s_im) = parts(spec_x[c, columns]), parts(spec_x[s, columns])
            q_c, q_s = spec_q[c, columns], spec_q[s, columns]
            t_c, t_s = pltpu.roll(q_c, GROUP, 1) * sign, pltpu.roll(q_s, GROUP, 1) * sign
            prod[c, columns] = ((c_re * q_c + c_im * t_c) - (s_re * q_s + s_im * t_s)).astype(BF16)
            prod[s, columns] = ((s_re * q_c + s_im * t_c) + (c_re * q_s + c_im * t_s)).astype(BF16)

        return [
            functools.partial(one, base + row, at)
            for base in range(0, length, 2 * GROUP)
            for row in range(0, GROUP, 16)
            for at in range(lanes.start, lanes.stop, 2 * GROUP)
        ]

    def inverse(lanes):
        def one(m):
            back = turned[shift + m : shift + m + 256, :]
            rows_y[m : m + 256, lanes] = dot(back, prod[:, lanes]).astype(BF16)

        return [functools.partial(one, m) for m in range(0, img, 256)]

    arrived("table")
    arrived("rest")
    for step in spectra(tiles[0]):
        step()
    for t in range(len(tiles)):
        matrix = (inverse(tiles[t - 1]) if t else []) + (spectra(tiles[t + 1]) if t + 1 < len(tiles) else [])
        interleave(products(tiles[t]), matrix)
    for step in inverse(tiles[-1]):
        step()

    arrived("dirty")
    arrived("rate")
    bands, parts, _, band, part = out.shape
    step = 256
    sends = []
    for i in range(img // step):
        rows = slice(i * step, (i + 1) * step)
        where = slice(i * step // band, (i + 1) * step // band)
        for ch in range(2):
            scale = rate[ch] * (4.0 / (length * length))
            inner = rows_y[rows, ch * length : (ch + 1) * length]
            for n in range(0, img, 256):
                lanes = slice(n, n + 256)
                blurred = dot(inner, table[:, shift + n : shift + n + 256])
                stepped = rate[ch] * dirty[ch, rows, lanes].astype(F32) - scale * blurred
                stepped = (model[ch, rows, lanes].astype(F32) + stepped).astype(BF16)
                size = min(part, 256)
                for k in range(0, 256, size):
                    piece = stepped[:, k : k + size].reshape(step // band, band, size)
                    at = (n + k) % part
                    out[where, (n + k) // part, ch, :, at : at + size] = piece
            place = where, slice(None), ch
            sends.append(pltpu.make_async_copy(out.at[place], out_h.at[place], out_sems.at[len(sends)]))
            sends[-1].start()
    for send in sends:
        send.wait()


def mix_kernel(gain, weights, tiles, out_h, w_in_t, swap, normed, hidden, mixed, out, sems):
    channels, band, part = tiles.shape
    groups = channels // band

    depth = channels + band
    w_in_t[...] = weights[: w_in_t.shape[1], :].astype(F32).T.astype(BF16)
    w_out_t = weights[w_in_t.shape[1] :, :]
    place = [lax.broadcasted_iota(jnp.int32, swap.shape, axis) for axis in range(2)]
    swap[...] = jnp.where(place[0] % band * band + place[0] // band == place[1], 1.0, 0.0).astype(BF16)
    normed[:, channels:, :] = jnp.ones((band, band, part), BF16)
    power = jnp.zeros((band, part), F32)
    for c in range(channels):
        v = tiles[c].astype(F32)
        power = power + v * v
    inverse = lax.rsqrt(power * (1.0 / channels) + 1e-06)
    for g in range(groups):
        rows = [
            (tiles[c].astype(F32) * inverse * gain[c : c + 1, :]).astype(BF16)
            for c in range(g * band, (g + 1) * band)
        ]
        swapped = dot(swap[...], jnp.concatenate(rows, axis=0)).astype(BF16)
        normed[:, g * band : (g + 1) * band, :] = swapped.reshape(band, band, part)

    a = math.sqrt(2.0 / math.pi)
    blocks = [slice(n, min(n + 256, part)) for n in range(0, part, 256)]
    for r in range(band):
        for lanes in blocks:
            for h in range(0, hidden.shape[1], 128):
                rows = slice(h, h + 128)
                inner = dot(w_in_t[rows, :depth], normed[r, :, lanes]).astype(BF16)
                bent = inner * (BF16(a) + BF16(a * 0.044715) * (inner * inner))
                hidden[r, rows, lanes] = inner + inner * jnp.tanh(bent)
    for r in range(band):
        for lanes in blocks:
            mixed[r, :, lanes] = (0.5 * dot(w_out_t, hidden[r, :, lanes])).astype(BF16)

    sends = []
    for g in range(groups):
        block = mixed[:, g * band : (g + 1) * band, :].reshape(band * band, part)
        swapped = dot(swap[...], block).astype(BF16)
        where = pl.ds(g * band, band)
        out[where] = swapped.reshape(band, band, part)
        sends.append(pltpu.make_async_copy(out.at[where], out_h.at[where], sems.at[g]))
        sends[-1].start()
    for send in sends:
        send.wait()


def spread_kernel(taps, stepped, mixed, out, above, middle, below, result, sems):
    bands, parts, ch_dev, band, part = stepped.shape
    img = parts * part
    group = 4
    size = group * band

    def rows_of(source, start, ch):
        pieces = [source[start : start + group, p, ch].reshape(size, part) for p in range(parts)]
        return jnp.concatenate(pieces, axis=1).astype(F32)

    zero = jnp.zeros((img // 128, 8, 128), F32)
    above[:, 0:8, :] = zero
    below[:, img : img + 8, :] = zero
    lane = lax.broadcasted_iota(jnp.int32, (size, 128), 1)
    sends = []
    for ch in range(ch_dev):
        k = [[taps[i, j, ch : ch + 1, :] for j in range(3)] for i in range(3)]

        def across(start):
            x = rows_of(mixed, start, ch)
            low, high = pltpu.roll(x, 1, 1), pltpu.roll(x, img - 1, 1)
            at = start * band
            for n in range(img // 128):
                lanes = slice(n * 128, (n + 1) * 128)
                left, here, right = low[:, lanes], x[:, lanes], high[:, lanes]
                if n == 0:
                    left = jnp.where(lane == 0, 0.0, left)
                if n == img // 128 - 1:
                    right = jnp.where(lane == 127, 0.0, right)
                for target, row, off in ((above, 0, 8), (middle, 1, 0), (below, 2, 0)):
                    value = k[row][0] * left + k[row][1] * here + k[row][2] * right
                    target[n, at + off : at + off + size, :] = value

        def down(start):
            at = start * band
            base = rows_of(stepped, start, ch)
            for n in range(img // 128):
                total = above[n, at + 7 : at + 7 + size, :] + below[n, at + 1 : at + 1 + size, :]
                total = total + middle[n, at : at + size, :]
                total = base[:, n * 128 : (n + 1) * 128] + total
                result[ch, at : at + size, n * 128 : (n + 1) * 128] = total.astype(BF16)

        def leave(start):
            down(start)
            rows = pl.ds(start * band, size)
            at = sems.at[ch * (bands // group) + start // group]
            sends.append(pltpu.make_async_copy(result.at[ch, rows], out.at[ch, rows], at))
            sends[-1].start()

        for start in range(0, bands, group):
            across(start)
            if start:
                leave(start - group)
        leave(bands - group)
    for send in sends:
        send.wait()


VMEM = pl.BlockSpec(memory_space=pltpu.VMEM)
SMEM = pl.BlockSpec(memory_space=pltpu.SMEM)
HBM = pl.BlockSpec(memory_space=pltpu.HBM)


def params(mib):
    return pltpu.CompilerParams(vmem_limit_bytes=mib * MIB)


def exchange(blocks, order):
    return lax.all_to_all(
        blocks, "all", split_axis=0, concat_axis=0, axis_index_groups=[order], tiled=True
    )


def layers(w_in, b_in, w_out_t, wide):
    rows = []
    for _ in range(3):
        rows.append(lax.reduce_precision(b_in, 8, 7))
        b_in = b_in - rows[-1]
    zeros = jnp.zeros((wide - w_in.shape[0] - 3, w_in.shape[1]), BF16)
    return jnp.concatenate([w_in, jnp.stack(rows).astype(BF16), zeros, w_out_t], axis=0)


def local(n_rows, n_cols, model, dirty, psf, step_size, gain, w_in, b_in, w_out, kernel):
    ch_dev, img, _ = model.shape
    psf_len = psf.shape[1]
    assert ch_dev == 2
    n_dev = n_rows * n_cols
    side = n_cols // 2
    order = [r * n_cols + half * side + k for r in range(n_rows) for k in range(side) for half in (1, 0)]
    channels = gain.shape[0]
    hidden = b_in.shape[0]
    part = img * img // (n_dev * BAND)
    parts = img // part
    bands = img // BAND
    table, turned = tables(img, psf_len)
    length = table.shape[0]
    wide = -(-(channels + BAND) // 128) * 128
    blocks = (bands, parts, ch_dev, BAND, part)

    stepped = pl.pallas_call(
        conv_kernel,
        out_shape=jax.ShapeDtypeStruct(blocks, BF16),
        in_specs=[HBM] * 6,
        out_specs=HBM,
        scratch_shapes=[
            pltpu.SMEM(step_size.shape, F32),
            pltpu.VMEM(model.shape, BF16),
            pltpu.VMEM(model.shape, BF16),
            pltpu.VMEM(psf.shape, BF16),
            pltpu.VMEM(table.shape, BF16),
            pltpu.VMEM(turned.shape, BF16),
            pltpu.VMEM((img, 2 * length), BF16),
            pltpu.VMEM((psf_len, 2 * length), BF16),
            pltpu.VMEM((length, 2 * length), F32),
            pltpu.VMEM((length, 2 * length), F32),
            pltpu.VMEM((length, 2 * length), BF16),
            pltpu.VMEM((img, 2 * length), BF16),
            pltpu.VMEM(blocks, BF16),
            pltpu.SemaphoreType.DMA((20,)),
            pltpu.SemaphoreType.DMA((img // 128,)),
        ],
        compiler_params=params(58),
        name="conv",
    )(step_size, model, dirty, psf, table, turned)
    stepped, gain, w_in, b_in, w_out, kernel = lax.optimization_barrier(
        (stepped, gain, w_in, b_in, w_out, kernel)
    )

    def ordered(values):
        grid = values.reshape(n_rows, 2, side, ch_dev, -1)[:, ::-1]
        return grid.transpose(0, 2, 1, 3, 4).reshape(values.shape)

    tiles = exchange(stepped.reshape(n_dev, ch_dev, BAND, part), order).reshape(channels, BAND, part)

    mixed = pl.pallas_call(
        mix_kernel,
        out_shape=jax.ShapeDtypeStruct((channels, BAND, part), BF16),
        in_specs=[VMEM] * 3,
        out_specs=HBM,
        scratch_shapes=[
            pltpu.VMEM((hidden, wide), BF16),
            pltpu.VMEM((BAND * BAND, BAND * BAND), BF16),
            pltpu.VMEM((BAND, channels + BAND, part), BF16),
            pltpu.VMEM((BAND, hidden, part), BF16),
            pltpu.VMEM((BAND, channels, part), BF16),
            pltpu.VMEM((channels, BAND, part), BF16),
            pltpu.SemaphoreType.DMA((channels // BAND,)),
        ],
        compiler_params=params(24),
        name="mix",
    )(
        jnp.broadcast_to(ordered(gain)[:, None], (channels, part)),
        layers(ordered(w_in), b_in, ordered(w_out.T), wide),
        tiles,
    )

    returned = exchange(mixed.reshape(n_dev, ch_dev, BAND, part), order).reshape(blocks)
    position = lax.axis_index("all").astype(jnp.int32) * ch_dev
    taps = lax.dynamic_slice_in_dim(kernel, position, ch_dev, axis=2)
    taps = jnp.broadcast_to(taps[..., None], (3, 3, ch_dev, 128))
    plane = pltpu.VMEM((img // 128, img + 8, 128), F32)

    return pl.pallas_call(
        spread_kernel,
        out_shape=jax.ShapeDtypeStruct((ch_dev, img, img), BF16),
        in_specs=[VMEM] * 3,
        out_specs=HBM,
        scratch_shapes=[
            plane, plane, plane, pltpu.VMEM((ch_dev, img, img), BF16),
            pltpu.SemaphoreType.DMA((ch_dev * bands // 4,)),
        ],
        compiler_params=params(24),
        name="spread",
    )(taps, stepped, returned)


def solution(mesh):
    line = Mesh(mesh.devices.reshape(-1), ("all",))
    planes = P("all", None, None)
    return jax.shard_map(
        functools.partial(local, *mesh.devices.shape),
        mesh=line,
        in_specs=(planes, planes, planes, P("all"), P(), P(), P(), P(), P()),
        out_specs=planes,
        check_vma=False,
    )
```

```python
import functools
import math

import jax
import jax.numpy as jnp
import ml_dtypes
import numpy as np
from jax import lax
from jax.experimental import pallas as pl
from jax.experimental.pallas import tpu as pltpu
from jax.sharding import Mesh
from jax.sharding import PartitionSpec as P

BAND = 16
GROUP = 64
MIB = 1024 * 1024
BF16, F32 = jnp.bfloat16, jnp.float32


def tables(img, psf):
    length = img + psf // 2
    half = length // 2
    phase = (2 * np.arange(half)[:, None] + 1) * np.arange(length)[None, :] % (2 * length)
    angle = (phase * (math.pi / length)).reshape(half // GROUP, 1, GROUP, length)
    table = np.concatenate([np.cos(angle), np.sin(angle)], axis=1).reshape(length, length)
    table = table.astype(ml_dtypes.bfloat16)
    return jnp.asarray(table), jnp.asarray(np.ascontiguousarray(table.T))


def dot(a, b):
    return jnp.dot(a, b, preferred_element_type=F32)


def interleave(first, second):
    done = 0
    for i, step in enumerate(first):
        step()
        while done * len(first) < (i + 1) * len(second):
            second[done]()
            done += 1


def conv_kernel(
    rate_h, model_h, dirty_h, psf_h, table_h, turned_h, out_h,
    rate, model, dirty, psf, table, turned, cols_x, cols_q, spec_x, spec_q, prod, rows_y, out, sems, out_sems,
):
    img = model.shape[1]
    taps = psf.shape[1]
    shift = taps // 2
    length = table.shape[1]
    tiles = [slice(n, n + 256) for n in range(0, 2 * length, 256)]
    tall = length // 2
    loads = {}

    def load(name, source, target, start, count, pieces):
        for i in range(pieces):
            rows = pl.ds(start + i * count // pieces, count // pieces)
            copy = pltpu.make_async_copy(source.at[rows], target.at[rows], sems.at[sum(map(len, loads.values()))])
            copy.start()
            loads.setdefault(name, []).append(copy)

    def arrived(name):
        for copy in loads[name]:
            copy.wait()

    load("psf", psf_h.at[0], psf.at[0], 0, taps, 1)
    load("turned_0", turned_h, turned, 0, taps, 4)
    load("psf", psf_h.at[1], psf.at[1], 0, taps, 1)
    load("model_0", model_h.at[0], model.at[0], 0, img, 2)
    load("turned_1", turned_h, turned, taps, img - taps, 2)
    load("model_1", model_h.at[1], model.at[1], 0, img, 2)
    load("table", table_h, table, 0, length, 4)
    load("rest", turned_h, turned, img, length - img, 1)
    load("dirty", dirty_h, dirty, 0, 2, 2)
    loads["rate"] = [pltpu.make_async_copy(rate_h, rate, sems.at[sum(map(len, loads.values()))])]
    loads["rate"][0].start()

    def columns(source, depth, target, waits):
        for ch in range(2):
            for wait in waits[ch]:
                arrived(wait)
            for m in range(0, depth, 256):
                rows = slice(m, m + 256)
                for n in range(0, length, 256):
                    lanes = slice(n, min(n + 256, length))
                    to = slice(ch * length + lanes.start, ch * length + lanes.stop)
                    target[rows, to] = dot(source[ch, rows, :], turned[:depth, lanes]).astype(BF16)

    columns(psf, taps, cols_q, (("psf", "turned_0"), ()))
    columns(model, img, cols_x, (("model_0", "turned_1"), ("model_1",)))

    def spectra(lanes):
        def one(target, source, depth, m):
            target[m : m + tall, lanes] = dot(table[m : m + tall, :depth], source[:, lanes])

        return [
            functools.partial(one, target, source, depth, m)
            for m in range(0, length, tall)
            for target, source, depth in ((spec_q, cols_q, taps), (spec_x, cols_x, img))
        ]

    lane = lax.broadcasted_iota(jnp.int32, (16, 2 * GROUP), 1)
    sign = jnp.where(lane < GROUP, -1.0, 1.0)

    def products(lanes):
        def one(row, at):
            c, s, columns = slice(row, row + 16), slice(row + GROUP, row + GROUP + 16), slice(at, at + 2 * GROUP)

            def parts(value):
                turn = pltpu.roll(value, GROUP, 1)
                return jnp.where(lane < GROUP, value, turn), jnp.where(lane < GROUP, turn, value)

            (c_re, c_im), (s_re, s_im) = parts(spec_x[c, columns]), parts(spec_x[s, columns])
            q_c, q_s = spec_q[c, columns], spec_q[s, columns]
            t_c, t_s = pltpu.roll(q_c, GROUP, 1) * sign, pltpu.roll(q_s, GROUP, 1) * sign
            prod[c, columns] = ((c_re * q_c + c_im * t_c) - (s_re * q_s + s_im * t_s)).astype(BF16)
            prod[s, columns] = ((s_re * q_c + s_im * t_c) + (c_re * q_s + c_im * t_s)).astype(BF16)

        return [
            functools.partial(one, base + row, at)
            for base in range(0, length, 2 * GROUP)
            for row in range(0, GROUP, 16)
            for at in range(lanes.start, lanes.stop, 2 * GROUP)
        ]

    def inverse(lanes):
        def one(m):
            back = turned[shift + m : shift + m + 256, :]
            rows_y[m : m + 256, lanes] = dot(back, prod[:, lanes]).astype(BF16)

        return [functools.partial(one, m) for m in range(0, img, 256)]

    arrived("table")
    arrived("rest")
    for step in spectra(tiles[0]):
        step()
    for t in range(len(tiles)):
        matrix = (inverse(tiles[t - 1]) if t else []) + (spectra(tiles[t + 1]) if t + 1 < len(tiles) else [])
        interleave(products(tiles[t]), matrix)
    for step in inverse(tiles[-1]):
        step()

    arrived("dirty")
    arrived("rate")
    bands, parts, _, band, part = out.shape
    step = 256
    sends = []
    for i in range(img // step):
        rows = slice(i * step, (i + 1) * step)
        where = slice(i * step // band, (i + 1) * step // band)
        for ch in range(2):
            scale = rate[ch] * (4.0 / (length * length))
            inner = rows_y[rows, ch * length : (ch + 1) * length]
            for n in range(0, img, 256):
                lanes = slice(n, n + 256)
                blurred = dot(inner, table[:, shift + n : shift + n + 256])
                stepped = rate[ch] * dirty[ch, rows, lanes].astype(F32) - scale * blurred
                stepped = (model[ch, rows, lanes].astype(F32) + stepped).astype(BF16)
                size = min(part, 256)
                for k in range(0, 256, size):
                    piece = stepped[:, k : k + size].reshape(step // band, band, size)
                    at = (n + k) % part
                    out[where, (n + k) // part, ch, :, at : at + size] = piece
            place = where, slice(None), ch
            sends.append(pltpu.make_async_copy(out.at[place], out_h.at[place], out_sems.at[len(sends)]))
            sends[-1].start()
    for send in sends:
        send.wait()


def mix_kernel(gain, weights, tiles, out_h, w_in_t, swap, normed, hidden, mixed, out, sems):
    channels, band, part = tiles.shape
    groups = channels // band

    depth = channels + band
    w_in_t[...] = weights[: w_in_t.shape[1], :].astype(F32).T.astype(BF16)
    w_out_t = weights[w_in_t.shape[1] :, :]
    place = [lax.broadcasted_iota(jnp.int32, swap.shape, axis) for axis in range(2)]
    swap[...] = jnp.where(place[0] % band * band + place[0] // band == place[1], 1.0, 0.0).astype(BF16)
    normed[:, channels:, :] = jnp.ones((band, band, part), BF16)
    power = jnp.zeros((band, part), F32)
    for c in range(channels):
        v = tiles[c].astype(F32)
        power = power + v * v
    inverse = lax.rsqrt(power * (1.0 / channels) + 1e-06)
    for g in range(groups):
        rows = [
            (tiles[c].astype(F32) * inverse * gain[c : c + 1, :]).astype(BF16)
            for c in range(g * band, (g + 1) * band)
        ]
        swapped = dot(swap[...], jnp.concatenate(rows, axis=0)).astype(BF16)
        normed[:, g * band : (g + 1) * band, :] = swapped.reshape(band, band, part)

    a = math.sqrt(2.0 / math.pi)
    blocks = [slice(n, min(n + 256, part)) for n in range(0, part, 256)]
    for r in range(band):
        for lanes in blocks:
            for h in range(0, hidden.shape[1], 128):
                rows = slice(h, h + 128)
                inner = dot(w_in_t[rows, :depth], normed[r, :, lanes]).astype(BF16)
                bent = inner * (BF16(a) + BF16(a * 0.044715) * (inner * inner))
                hidden[r, rows, lanes] = inner + inner * jnp.tanh(bent)
    for r in range(band):
        for lanes in blocks:
            mixed[r, :, lanes] = (0.5 * dot(w_out_t, hidden[r, :, lanes])).astype(BF16)

    sends = []
    for g in range(groups):
        block = mixed[:, g * band : (g + 1) * band, :].reshape(band * band, part)
        swapped = dot(swap[...], block).astype(BF16)
        where = pl.ds(g * band, band)
        out[where] = swapped.reshape(band, band, part)
        sends.append(pltpu.make_async_copy(out.at[where], out_h.at[where], sems.at[g]))
        sends[-1].start()
    for send in sends:
        send.wait()


def spread_kernel(taps, stepped, mixed, out, above, middle, below, result, sems):
    bands, parts, ch_dev, band, part = stepped.shape
    img = parts * part
    group = 4
    size = group * band

    def rows_of(source, start, ch):
        pieces = [source[start : start + group, p, ch].reshape(size, part) for p in range(parts)]
        return jnp.concatenate(pieces, axis=1).astype(F32)

    zero = jnp.zeros((img // 128, 8, 128), F32)
    above[:, 0:8, :] = zero
    below[:, img : img + 8, :] = zero
    lane = lax.broadcasted_iota(jnp.int32, (size, 128), 1)
    sends = []
    for ch in range(ch_dev):
        k = [[taps[i, j, ch : ch + 1, :] for j in range(3)] for i in range(3)]

        def across(start):
            x = rows_of(mixed, start, ch)
            low, high = pltpu.roll(x, 1, 1), pltpu.roll(x, img - 1, 1)
            at = start * band
            for n in range(img // 128):
                lanes = slice(n * 128, (n + 1) * 128)
                left, here, right = low[:, lanes], x[:, lanes], high[:, lanes]
                if n == 0:
                    left = jnp.where(lane == 0, 0.0, left)
                if n == img // 128 - 1:
                    right = jnp.where(lane == 127, 0.0, right)
                for target, row, off in ((above, 0, 8), (middle, 1, 0), (below, 2, 0)):
                    value = k[row][0] * left + k[row][1] * here + k[row][2] * right
                    target[n, at + off : at + off + size, :] = value

        def down(start):
            at = start * band
            base = rows_of(stepped, start, ch)
            for n in range(img // 128):
                total = above[n, at + 7 : at + 7 + size, :] + below[n, at + 1 : at + 1 + size, :]
                total = total + middle[n, at : at + size, :]
                total = base[:, n * 128 : (n + 1) * 128] + total
                result[ch, at : at + size, n * 128 : (n + 1) * 128] = total.astype(BF16)

        def leave(start):
            down(start)
            rows = pl.ds(start * band, size)
            at = sems.at[ch * (bands // group) + start // group]
            sends.append(pltpu.make_async_copy(result.at[ch, rows], out.at[ch, rows], at))
            sends[-1].start()

        for start in range(0, bands, group):
            across(start)
            if start:
                leave(start - group)
        leave(bands - group)
    for send in sends:
        send.wait()


VMEM = pl.BlockSpec(memory_space=pltpu.VMEM)
SMEM = pl.BlockSpec(memory_space=pltpu.SMEM)
HBM = pl.BlockSpec(memory_space=pltpu.HBM)


def params(mib):
    return pltpu.CompilerParams(vmem_limit_bytes=mib * MIB)


def partner_order(n_rows, n_cols):
    y, x = n_rows // 2 * n_cols, n_rows // 4 * n_cols
    half, near, core = n_cols // 2, n_cols // 4, 1
    steps = [y | x | half | near, core, y | half, y, x]
    steps += [bit for bit in (1 << k for k in range(1, 16)) if bit < n_rows * n_cols and bit not in (y, x, half, near)]
    order = [half]
    for step in steps:
        order += [device ^ step for device in order]
    return order


def exchange(blocks, order):
    return lax.all_to_all(
        blocks, "all", split_axis=0, concat_axis=0, axis_index_groups=[order], tiled=True
    )


def layers(w_in, b_in, w_out_t, wide):
    rows = []
    for _ in range(3):
        rows.append(lax.reduce_precision(b_in, 8, 7))
        b_in = b_in - rows[-1]
    zeros = jnp.zeros((wide - w_in.shape[0] - 3, w_in.shape[1]), BF16)
    return jnp.concatenate([w_in, jnp.stack(rows).astype(BF16), zeros, w_out_t], axis=0)


def local(n_rows, n_cols, model, dirty, psf, step_size, gain, w_in, b_in, w_out, kernel):
    ch_dev, img, _ = model.shape
    psf_len = psf.shape[1]
    assert ch_dev == 2
    n_dev = n_rows * n_cols
    order = partner_order(n_rows, n_cols)
    channels = gain.shape[0]
    hidden = b_in.shape[0]
    part = img * img // (n_dev * BAND)
    parts = img // part
    bands = img // BAND
    table, turned = tables(img, psf_len)
    length = table.shape[0]
    wide = -(-(channels + BAND) // 128) * 128
    blocks = (bands, parts, ch_dev, BAND, part)

    stepped = pl.pallas_call(
        conv_kernel,
        out_shape=jax.ShapeDtypeStruct(blocks, BF16),
        in_specs=[HBM] * 6,
        out_specs=HBM,
        scratch_shapes=[
            pltpu.SMEM(step_size.shape, F32),
            pltpu.VMEM(model.shape, BF16),
            pltpu.VMEM(model.shape, BF16),
            pltpu.VMEM(psf.shape, BF16),
            pltpu.VMEM(table.shape, BF16),
            pltpu.VMEM(turned.shape, BF16),
            pltpu.VMEM((img, 2 * length), BF16),
            pltpu.VMEM((psf_len, 2 * length), BF16),
            pltpu.VMEM((length, 2 * length), F32),
            pltpu.VMEM((length, 2 * length), F32),
            pltpu.VMEM((length, 2 * length), BF16),
            pltpu.VMEM((img, 2 * length), BF16),
            pltpu.VMEM(blocks, BF16),
            pltpu.SemaphoreType.DMA((20,)),
            pltpu.SemaphoreType.DMA((img // 128,)),
        ],
        compiler_params=params(58),
        name="conv",
    )(step_size, model, dirty, psf, table, turned)
    stepped, gain, w_in, b_in, w_out, kernel = lax.optimization_barrier(
        (stepped, gain, w_in, b_in, w_out, kernel)
    )

    def ordered(values):
        return jnp.concatenate([values[d * ch_dev : (d + 1) * ch_dev] for d in order], axis=0)

    tiles = exchange(stepped.reshape(n_dev, ch_dev, BAND, part), order).reshape(channels, BAND, part)

    mixed = pl.pallas_call(
        mix_kernel,
        out_shape=jax.ShapeDtypeStruct((channels, BAND, part), BF16),
        in_specs=[VMEM] * 3,
        out_specs=HBM,
        scratch_shapes=[
            pltpu.VMEM((hidden, wide), BF16),
            pltpu.VMEM((BAND * BAND, BAND * BAND), BF16),
            pltpu.VMEM((BAND, channels + BAND, part), BF16),
            pltpu.VMEM((BAND, hidden, part), BF16),
            pltpu.VMEM((BAND, channels, part), BF16),
            pltpu.VMEM((channels, BAND, part), BF16),
            pltpu.SemaphoreType.DMA((channels // BAND,)),
        ],
        compiler_params=params(24),
        name="mix",
    )(
        jnp.broadcast_to(ordered(gain)[:, None], (channels, part)),
        layers(ordered(w_in), b_in, ordered(w_out.T), wide),
        tiles,
    )

    returned = exchange(mixed.reshape(n_dev, ch_dev, BAND, part), order).reshape(blocks)
    position = lax.axis_index("all").astype(jnp.int32) * ch_dev
    taps = lax.dynamic_slice_in_dim(kernel, position, ch_dev, axis=2)
    taps = jnp.broadcast_to(taps[..., None], (3, 3, ch_dev, 128))
    plane = pltpu.VMEM((img // 128, img + 8, 128), F32)

    return pl.pallas_call(
        spread_kernel,
        out_shape=jax.ShapeDtypeStruct((ch_dev, img, img), BF16),
        in_specs=[VMEM] * 3,
        out_specs=HBM,
        scratch_shapes=[
            plane, plane, plane, pltpu.VMEM((ch_dev, img, img), BF16),
            pltpu.SemaphoreType.DMA((ch_dev * bands // 4,)),
        ],
        compiler_params=params(24),
        name="spread",
    )(taps, stepped, returned)


def solution(mesh):
    line = Mesh(mesh.devices.reshape(-1), ("all",))
    planes = P("all", None, None)
    return jax.shard_map(
        functools.partial(local, *mesh.devices.shape),
        mesh=line,
        in_specs=(planes, planes, planes, P("all"), P(), P(), P(), P(), P()),
        out_specs=planes,
        check_vma=False,
    )
```

```python
import functools
import math

import jax
import jax.numpy as jnp
import ml_dtypes
import numpy as np
from jax import lax
from jax.experimental import pallas as pl
from jax.experimental.pallas import tpu as pltpu
from jax.sharding import Mesh
from jax.sharding import PartitionSpec as P

BAND = 16
GROUP = 64
MIB = 1024 * 1024
BF16, F32 = jnp.bfloat16, jnp.float32


def tables(img, psf):
    length = img + psf // 2
    half = length // 2
    phase = (2 * np.arange(half)[:, None] + 1) * np.arange(length)[None, :] % (2 * length)
    angle = (phase * (math.pi / length)).reshape(half // GROUP, 1, GROUP, length)
    table = np.concatenate([np.cos(angle), np.sin(angle)], axis=1).reshape(length, length)
    table = table.astype(ml_dtypes.bfloat16)
    return jnp.asarray(table), jnp.asarray(np.ascontiguousarray(table.T))


def dot(a, b):
    return jnp.dot(a, b, preferred_element_type=F32)


def interleave(first, second):
    done = 0
    for i, step in enumerate(first):
        step()
        while done * len(first) < (i + 1) * len(second):
            second[done]()
            done += 1


def conv_kernel(
    rate_h, model_h, dirty_h, psf_h, table_h, turned_h, out_h,
    rate, model, dirty, psf, table, turned, cols_x, cols_q, spec_x, spec_q, prod, rows_y, out, sems, out_sems,
):
    img = model.shape[1]
    taps = psf.shape[1]
    shift = taps // 2
    length = table.shape[1]
    tiles = [slice(n, n + 256) for n in range(0, 2 * length, 256)]
    tall = length // 2
    loads = {}

    def load(name, source, target, start, count, pieces):
        for i in range(pieces):
            rows = pl.ds(start + i * count // pieces, count // pieces)
            copy = pltpu.make_async_copy(source.at[rows], target.at[rows], sems.at[sum(map(len, loads.values()))])
            copy.start()
            loads.setdefault(name, []).append(copy)

    def arrived(name):
        for copy in loads[name]:
            copy.wait()

    load("psf", psf_h.at[0], psf.at[0], 0, taps, 1)
    load("turned_0", turned_h, turned, 0, taps, 4)
    load("psf", psf_h.at[1], psf.at[1], 0, taps, 1)
    load("model_0", model_h.at[0], model.at[0], 0, img, 2)
    load("turned_1", turned_h, turned, taps, img - taps, 2)
    load("model_1", model_h.at[1], model.at[1], 0, img, 2)
    load("table", table_h, table, 0, length, 4)
    load("rest", turned_h, turned, img, length - img, 1)
    load("dirty", dirty_h, dirty, 0, 2, 2)
    loads["rate"] = [pltpu.make_async_copy(rate_h, rate, sems.at[sum(map(len, loads.values()))])]
    loads["rate"][0].start()

    def columns(source, depth, target, waits):
        for ch in range(2):
            for wait in waits[ch]:
                arrived(wait)
            for m in range(0, depth, 256):
                rows = slice(m, m + 256)
                for n in range(0, length, 256):
                    lanes = slice(n, min(n + 256, length))
                    to = slice(ch * length + lanes.start, ch * length + lanes.stop)
                    target[rows, to] = dot(source[ch, rows, :], turned[:depth, lanes]).astype(BF16)

    columns(psf, taps, cols_q, (("psf", "turned_0"), ()))
    columns(model, img, cols_x, (("model_0", "turned_1"), ("model_1",)))

    def spectra(lanes):
        def one(target, source, depth, m):
            target[m : m + tall, lanes] = dot(table[m : m + tall, :depth], source[:, lanes])

        return [
            functools.partial(one, target, source, depth, m)
            for m in range(0, length, tall)
            for target, source, depth in ((spec_q, cols_q, taps), (spec_x, cols_x, img))
        ]

    lane = lax.broadcasted_iota(jnp.int32, (16, 2 * GROUP), 1)
    sign = jnp.where(lane < GROUP, -1.0, 1.0)

    def products(lanes):
        def one(row, at):
            c, s, columns = slice(row, row + 16), slice(row + GROUP, row + GROUP + 16), slice(at, at + 2 * GROUP)

            def parts(value):
                turn = pltpu.roll(value, GROUP, 1)
                return jnp.where(lane < GROUP, value, turn), jnp.where(lane < GROUP, turn, value)

            (c_re, c_im), (s_re, s_im) = parts(spec_x[c, columns]), parts(spec_x[s, columns])
            q_c, q_s = spec_q[c, columns], spec_q[s, columns]
            t_c, t_s = pltpu.roll(q_c, GROUP, 1) * sign, pltpu.roll(q_s, GROUP, 1) * sign
            prod[c, columns] = ((c_re * q_c + c_im * t_c) - (s_re * q_s + s_im * t_s)).astype(BF16)
            prod[s, columns] = ((s_re * q_c + s_im * t_c) + (c_re * q_s + c_im * t_s)).astype(BF16)

        return [
            functools.partial(one, base + row, at)
            for base in range(0, length, 2 * GROUP)
            for row in range(0, GROUP, 16)
            for at in range(lanes.start, lanes.stop, 2 * GROUP)
        ]

    def inverse(lanes):
        def one(m):
            back = turned[shift + m : shift + m + 256, :]
            rows_y[m : m + 256, lanes] = dot(back, prod[:, lanes]).astype(BF16)

        return [functools.partial(one, m) for m in range(0, img, 256)]

    arrived("table")
    arrived("rest")
    for step in spectra(tiles[0]):
        step()
    for t in range(len(tiles)):
        matrix = (inverse(tiles[t - 1]) if t else []) + (spectra(tiles[t + 1]) if t + 1 < len(tiles) else [])
        interleave(products(tiles[t]), matrix)
    for step in inverse(tiles[-1]):
        step()

    arrived("dirty")
    arrived("rate")
    bands, parts, _, band, part = out.shape
    step = 256
    sends = []
    for i in range(img // step):
        rows = slice(i * step, (i + 1) * step)
        where = slice(i * step // band, (i + 1) * step // band)
        for ch in range(2):
            scale = rate[ch] * (4.0 / (length * length))
            inner = rows_y[rows, ch * length : (ch + 1) * length]
            for n in range(0, img, 256):
                lanes = slice(n, n + 256)
                blurred = dot(inner, table[:, shift + n : shift + n + 256])
                stepped = rate[ch] * dirty[ch, rows, lanes].astype(F32) - scale * blurred
                stepped = (model[ch, rows, lanes].astype(F32) + stepped).astype(BF16)
                size = min(part, 256)
                for k in range(0, 256, size):
                    piece = stepped[:, k : k + size].reshape(step // band, band, size)
                    at = (n + k) % part
                    out[where, (n + k) // part, ch, :, at : at + size] = piece
            place = where, slice(None), ch
            sends.append(pltpu.make_async_copy(out.at[place], out_h.at[place], out_sems.at[len(sends)]))
            sends[-1].start()
    for send in sends:
        send.wait()


def mix_kernel(place_of, gain, weights, tiles, out_h, w_in_t, swap, normed, hidden, mixed, out, sems):
    channels, band, part = tiles.shape
    groups = channels // band

    depth = channels + band
    w_in_t[...] = weights[: w_in_t.shape[1], :].astype(F32).T.astype(BF16)
    w_out_t = weights[w_in_t.shape[1] :, :]
    index = [lax.broadcasted_iota(jnp.int32, swap.shape, axis) for axis in range(2)]
    swap[...] = jnp.where(index[0] % band * band + index[0] // band == index[1], 1.0, 0.0).astype(BF16)
    normed[:, channels:, :] = jnp.ones((band, band, part), BF16)
    power = jnp.zeros((band, part), F32)
    for c in range(channels):
        v = tiles[c].astype(F32)
        power = power + v * v
    inverse = lax.rsqrt(power * (1.0 / channels) + 1e-06)
    for g in range(groups):
        rows = [
            (tiles[c].astype(F32) * inverse * gain[c : c + 1, :]).astype(BF16)
            for c in range(g * band, (g + 1) * band)
        ]
        swapped = dot(swap[...], jnp.concatenate(rows, axis=0)).astype(BF16)
        normed[:, g * band : (g + 1) * band, :] = swapped.reshape(band, band, part)

    a = math.sqrt(2.0 / math.pi)
    blocks = [slice(n, min(n + 256, part)) for n in range(0, part, 256)]
    for r in range(band):
        for lanes in blocks:
            for h in range(0, hidden.shape[1], 128):
                rows = slice(h, h + 128)
                inner = dot(w_in_t[rows, :depth], normed[r, :, lanes]).astype(BF16)
                bent = inner * (BF16(a) + BF16(a * 0.044715) * (inner * inner))
                hidden[r, rows, lanes] = inner + inner * jnp.tanh(bent)
    for r in range(band):
        for lanes in blocks:
            mixed[r, :, lanes] = (0.5 * dot(w_out_t, hidden[r, :, lanes])).astype(BF16)

    sends = []
    for g in range(groups):
        block = mixed[:, g * band : (g + 1) * band, :].reshape(band * band, part)
        swapped = dot(swap[...], block).astype(BF16)
        swapped = swapped.reshape(band, band, part)
        for k in range(0, band, 2):
            at = 2 * place_of[(g * band + k) // 2]
            out[at : at + 2] = swapped[k : k + 2]
            where = pl.ds(at, 2)
            sends.append(pltpu.make_async_copy(out.at[where], out_h.at[where], sems.at[len(sends)]))
            sends[-1].start()
    for send in sends:
        send.wait()


def spread_kernel(place_of, taps, stepped, mixed, out, above, middle, below, result, sems):
    bands, parts, ch_dev, band, part = stepped.shape
    img = parts * part
    group = 4
    size = group * band

    def rows_of(block):
        return jnp.concatenate([jnp.concatenate([block(p, b) for b in range(group)]) for p in range(parts)], axis=1).astype(F32)

    zero = jnp.zeros((img // 128, 8, 128), F32)
    above[:, 0:8, :] = zero
    below[:, img : img + 8, :] = zero
    lane = lax.broadcasted_iota(jnp.int32, (size, 128), 1)
    sends = []
    for ch in range(ch_dev):
        k = [[taps[i, j, ch : ch + 1, :] for j in range(3)] for i in range(3)]

        def across(start):
            x = rows_of(lambda p, b: mixed[place_of[(start + b) * parts + p], ch])
            low, high = pltpu.roll(x, 1, 1), pltpu.roll(x, img - 1, 1)
            at = start * band
            for n in range(img // 128):
                lanes = slice(n * 128, (n + 1) * 128)
                left, here, right = low[:, lanes], x[:, lanes], high[:, lanes]
                if n == 0:
                    left = jnp.where(lane == 0, 0.0, left)
                if n == img // 128 - 1:
                    right = jnp.where(lane == 127, 0.0, right)
                for target, row, off in ((above, 0, 8), (middle, 1, 0), (below, 2, 0)):
                    value = k[row][0] * left + k[row][1] * here + k[row][2] * right
                    target[n, at + off : at + off + size, :] = value

        def down(start):
            at = start * band
            base = rows_of(lambda p, b: stepped[start + b, p, ch])
            for n in range(img // 128):
                total = above[n, at + 7 : at + 7 + size, :] + below[n, at + 1 : at + 1 + size, :]
                total = total + middle[n, at : at + size, :]
                total = base[:, n * 128 : (n + 1) * 128] + total
                result[ch, at : at + size, n * 128 : (n + 1) * 128] = total.astype(BF16)

        def leave(start):
            down(start)
            rows = pl.ds(start * band, size)
            at = sems.at[ch * (bands // group) + start // group]
            sends.append(pltpu.make_async_copy(result.at[ch, rows], out.at[ch, rows], at))
            sends[-1].start()

        for start in range(0, bands, group):
            across(start)
            if start:
                leave(start - group)
        leave(bands - group)
    for send in sends:
        send.wait()


VMEM = pl.BlockSpec(memory_space=pltpu.VMEM)
SMEM = pl.BlockSpec(memory_space=pltpu.SMEM)
HBM = pl.BlockSpec(memory_space=pltpu.HBM)


def params(mib):
    return pltpu.CompilerParams(vmem_limit_bytes=mib * MIB)


def partner_order(n_rows, n_cols, back):
    y, x = n_rows // 2 * n_cols, n_rows // 4 * n_cols
    half, near, core = n_cols // 2, n_cols // 4, 1
    steps = [half | near, core, near, x, y] if back else [half, near, core, x, y]
    steps += [bit for bit in (1 << k for k in range(1, 16)) if bit < n_rows * n_cols and bit not in (y, x, half, near)]
    order = [half]
    for step in steps:
        order += [device ^ step for device in order]
    return order


def exchange(blocks, order):
    return lax.all_to_all(
        blocks, "all", split_axis=0, concat_axis=0, axis_index_groups=[order], tiled=True
    )


def layers(w_in, b_in, w_out_t, wide):
    rows = []
    for _ in range(3):
        rows.append(lax.reduce_precision(b_in, 8, 7))
        b_in = b_in - rows[-1]
    zeros = jnp.zeros((wide - w_in.shape[0] - 3, w_in.shape[1]), BF16)
    return jnp.concatenate([w_in, jnp.stack(rows).astype(BF16), zeros, w_out_t], axis=0)


def local(n_rows, n_cols, model, dirty, psf, step_size, gain, w_in, b_in, w_out, kernel):
    ch_dev, img, _ = model.shape
    psf_len = psf.shape[1]
    assert ch_dev == 2
    n_dev = n_rows * n_cols
    forth, back = (partner_order(n_rows, n_cols, way) for way in (False, True))
    channels = gain.shape[0]
    hidden = b_in.shape[0]
    part = img * img // (n_dev * BAND)
    parts = img // part
    bands = img // BAND
    table, turned = tables(img, psf_len)
    length = table.shape[0]
    wide = -(-(channels + BAND) // 128) * 128
    blocks = (bands, parts, ch_dev, BAND, part)

    stepped = pl.pallas_call(
        conv_kernel,
        out_shape=jax.ShapeDtypeStruct(blocks, BF16),
        in_specs=[HBM] * 6,
        out_specs=HBM,
        scratch_shapes=[
            pltpu.SMEM(step_size.shape, F32),
            pltpu.VMEM(model.shape, BF16),
            pltpu.VMEM(model.shape, BF16),
            pltpu.VMEM(psf.shape, BF16),
            pltpu.VMEM(table.shape, BF16),
            pltpu.VMEM(turned.shape, BF16),
            pltpu.VMEM((img, 2 * length), BF16),
            pltpu.VMEM((psf_len, 2 * length), BF16),
            pltpu.VMEM((length, 2 * length), F32),
            pltpu.VMEM((length, 2 * length), F32),
            pltpu.VMEM((length, 2 * length), BF16),
            pltpu.VMEM((img, 2 * length), BF16),
            pltpu.VMEM(blocks, BF16),
            pltpu.SemaphoreType.DMA((20,)),
            pltpu.SemaphoreType.DMA((img // 128,)),
        ],
        compiler_params=params(58),
        name="conv",
    )(step_size, model, dirty, psf, table, turned)
    stepped, gain, w_in, b_in, w_out, kernel = lax.optimization_barrier(
        (stepped, gain, w_in, b_in, w_out, kernel)
    )

    def ordered(values):
        return jnp.concatenate([values[d * ch_dev : (d + 1) * ch_dev] for d in forth], axis=0)

    tiles = exchange(stepped.reshape(n_dev, ch_dev, BAND, part), forth).reshape(channels, BAND, part)

    mixed = pl.pallas_call(
        functools.partial(mix_kernel, [back.index(device) for device in forth]),
        out_shape=jax.ShapeDtypeStruct((channels, BAND, part), BF16),
        in_specs=[VMEM] * 3,
        out_specs=HBM,
        scratch_shapes=[
            pltpu.VMEM((hidden, wide), BF16),
            pltpu.VMEM((BAND * BAND, BAND * BAND), BF16),
            pltpu.VMEM((BAND, channels + BAND, part), BF16),
            pltpu.VMEM((BAND, hidden, part), BF16),
            pltpu.VMEM((BAND, channels, part), BF16),
            pltpu.VMEM((channels, BAND, part), BF16),
            pltpu.SemaphoreType.DMA((n_dev,)),
        ],
        compiler_params=params(24),
        name="mix",
    )(
        jnp.broadcast_to(ordered(gain)[:, None], (channels, part)),
        layers(ordered(w_in), b_in, ordered(w_out.T), wide),
        tiles,
    )

    returned = exchange(mixed.reshape(n_dev, ch_dev, BAND, part), back)
    position = lax.axis_index("all").astype(jnp.int32) * ch_dev
    taps = lax.dynamic_slice_in_dim(kernel, position, ch_dev, axis=2)
    taps = jnp.broadcast_to(taps[..., None], (3, 3, ch_dev, 128))
    plane = pltpu.VMEM((img // 128, img + 8, 128), F32)

    return pl.pallas_call(
        functools.partial(spread_kernel, [back.index(device) for device in forth]),
        out_shape=jax.ShapeDtypeStruct((ch_dev, img, img), BF16),
        in_specs=[VMEM] * 3,
        out_specs=HBM,
        scratch_shapes=[
            plane, plane, plane, pltpu.VMEM((ch_dev, img, img), BF16),
            pltpu.SemaphoreType.DMA((ch_dev * bands // 4,)),
        ],
        compiler_params=params(24),
        name="spread",
    )(taps, stepped, returned)


def solution(mesh):
    line = Mesh(mesh.devices.reshape(-1), ("all",))
    planes = P("all", None, None)
    return jax.shard_map(
        functools.partial(local, *mesh.devices.shape),
        mesh=line,
        in_specs=(planes, planes, planes, P("all"), P(), P(), P(), P(), P()),
        out_specs=planes,
        check_vma=False,
    )
```

```python
import functools
import math

import jax
import jax.numpy as jnp
import ml_dtypes
import numpy as np
from jax import lax
from jax.experimental import pallas as pl
from jax.experimental.pallas import tpu as pltpu
from jax.sharding import Mesh
from jax.sharding import PartitionSpec as P

BAND = 16
GROUP = 64
MIB = 1024 * 1024
BF16, F32 = jnp.bfloat16, jnp.float32


def tables(img, psf):
    length = img + psf // 2
    half = length // 2
    phase = (2 * np.arange(half)[:, None] + 1) * np.arange(length)[None, :] % (2 * length)
    angle = (phase * (math.pi / length)).reshape(half // GROUP, 1, GROUP, length)
    table = np.concatenate([np.cos(angle), np.sin(angle)], axis=1).reshape(length, length)
    table = table.astype(ml_dtypes.bfloat16)
    return jnp.asarray(table), jnp.asarray(np.ascontiguousarray(table.T))


def dot(a, b):
    return jnp.dot(a, b, preferred_element_type=F32)


def interleave(first, second):
    done = 0
    for i, step in enumerate(first):
        step()
        while done * len(first) < (i + 1) * len(second):
            second[done]()
            done += 1


def conv_kernel(
    rate_h, model_h, dirty_h, psf_h, table_h, turned_h, out_h,
    rate, model, dirty, psf, table, turned, cols_x, cols_q, spec_x, spec_q, prod, rows_y, out, sems, out_sems,
):
    img = model.shape[1]
    taps = psf.shape[1]
    shift = taps // 2
    length = table.shape[1]
    tiles = [slice(n, n + 256) for n in range(0, 2 * length, 256)]
    tall = length // 2
    loads = {}

    def load(name, source, target, start, count, pieces):
        for i in range(pieces):
            rows = pl.ds(start + i * count // pieces, count // pieces)
            copy = pltpu.make_async_copy(source.at[rows], target.at[rows], sems.at[sum(map(len, loads.values()))])
            copy.start()
            loads.setdefault(name, []).append(copy)

    def arrived(name):
        for copy in loads[name]:
            copy.wait()

    load("psf", psf_h.at[0], psf.at[0], 0, taps, 1)
    load("turned_0", turned_h, turned, 0, taps, 4)
    load("psf", psf_h.at[1], psf.at[1], 0, taps, 1)
    load("model_0", model_h.at[0], model.at[0], 0, img, 2)
    load("turned_1", turned_h, turned, taps, img - taps, 2)
    load("model_1", model_h.at[1], model.at[1], 0, img, 2)
    load("table", table_h, table, 0, length, 4)
    load("rest", turned_h, turned, img, length - img, 1)
    load("dirty", dirty_h, dirty, 0, 2, 2)
    loads["rate"] = [pltpu.make_async_copy(rate_h, rate, sems.at[sum(map(len, loads.values()))])]
    loads["rate"][0].start()

    def columns(source, depth, target, waits):
        for ch in range(2):
            for wait in waits[ch]:
                arrived(wait)
            for m in range(0, depth, 256):
                rows = slice(m, m + 256)
                for n in range(0, length, 256):
                    lanes = slice(n, min(n + 256, length))
                    to = slice(ch * length + lanes.start, ch * length + lanes.stop)
                    target[rows, to] = dot(source[ch, rows, :], turned[:depth, lanes]).astype(BF16)

    columns(psf, taps, cols_q, (("psf", "turned_0"), ()))
    columns(model, img, cols_x, (("model_0", "turned_1"), ("model_1",)))

    def spectra(lanes):
        def one(target, source, depth, m):
            target[m : m + tall, lanes] = dot(table[m : m + tall, :depth], source[:, lanes])

        return [
            functools.partial(one, target, source, depth, m)
            for m in range(0, length, tall)
            for target, source, depth in ((spec_q, cols_q, taps), (spec_x, cols_x, img))
        ]

    lane = lax.broadcasted_iota(jnp.int32, (16, 2 * GROUP), 1)
    sign = jnp.where(lane < GROUP, -1.0, 1.0)

    def products(lanes):
        def one(row, at):
            c, s, columns = slice(row, row + 16), slice(row + GROUP, row + GROUP + 16), slice(at, at + 2 * GROUP)

            def parts(value):
                turn = pltpu.roll(value, GROUP, 1)
                return jnp.where(lane < GROUP, value, turn), jnp.where(lane < GROUP, turn, value)

            (c_re, c_im), (s_re, s_im) = parts(spec_x[c, columns]), parts(spec_x[s, columns])
            q_c, q_s = spec_q[c, columns], spec_q[s, columns]
            t_c, t_s = pltpu.roll(q_c, GROUP, 1) * sign, pltpu.roll(q_s, GROUP, 1) * sign
            prod[c, columns] = ((c_re * q_c + c_im * t_c) - (s_re * q_s + s_im * t_s)).astype(BF16)
            prod[s, columns] = ((s_re * q_c + s_im * t_c) + (c_re * q_s + c_im * t_s)).astype(BF16)

        return [
            functools.partial(one, base + row, at)
            for base in range(0, length, 2 * GROUP)
            for row in range(0, GROUP, 16)
            for at in range(lanes.start, lanes.stop, 2 * GROUP)
        ]

    def inverse(lanes):
        def one(m):
            back = turned[shift + m : shift + m + 256, :]
            rows_y[m : m + 256, lanes] = dot(back, prod[:, lanes]).astype(BF16)

        return [functools.partial(one, m) for m in range(0, img, 256)]

    arrived("table")
    arrived("rest")
    for step in spectra(tiles[0]):
        step()
    for t in range(len(tiles)):
        matrix = (inverse(tiles[t - 1]) if t else []) + (spectra(tiles[t + 1]) if t + 1 < len(tiles) else [])
        interleave(products(tiles[t]), matrix)
    for step in inverse(tiles[-1]):
        step()

    arrived("dirty")
    arrived("rate")
    bands, parts, _, band, part = out.shape
    step = 256
    sends = []
    for i in range(img // step):
        rows = slice(i * step, (i + 1) * step)
        where = slice(i * step // band, (i + 1) * step // band)
        for ch in range(2):
            scale = rate[ch] * (4.0 / (length * length))
            inner = rows_y[rows, ch * length : (ch + 1) * length]
            for n in range(0, img, 256):
                lanes = slice(n, n + 256)
                blurred = dot(inner, table[:, shift + n : shift + n + 256])
                stepped = rate[ch] * dirty[ch, rows, lanes].astype(F32) - scale * blurred
                stepped = (model[ch, rows, lanes].astype(F32) + stepped).astype(BF16)
                size = min(part, 256)
                for k in range(0, 256, size):
                    piece = stepped[:, k : k + size].reshape(step // band, band, size)
                    at = (n + k) % part
                    out[where, (n + k) // part, ch, :, at : at + size] = piece
            place = where, slice(None), ch
            sends.append(pltpu.make_async_copy(out.at[place], out_h.at[place], out_sems.at[len(sends)]))
            sends[-1].start()
    for send in sends:
        send.wait()


def mix_kernel(gain, weights, tiles, out_h, w_in_t, swap, normed, hidden, mixed, out, sems):
    channels, band, part = tiles.shape
    groups = channels // band

    depth = channels + band
    w_in_t[...] = weights[: w_in_t.shape[1], :].astype(F32).T.astype(BF16)
    w_out_t = weights[w_in_t.shape[1] :, :]
    place = [lax.broadcasted_iota(jnp.int32, swap.shape, axis) for axis in range(2)]
    swap[...] = jnp.where(place[0] % band * band + place[0] // band == place[1], 1.0, 0.0).astype(BF16)
    normed[:, channels:, :] = jnp.ones((band, band, part), BF16)
    power = jnp.zeros((band, part), F32)
    for c in range(channels):
        v = tiles[c].astype(F32)
        power = power + v * v
    inverse = lax.rsqrt(power * (1.0 / channels) + 1e-06)
    for g in range(groups):
        rows = [
            (tiles[c].astype(F32) * inverse * gain[c : c + 1, :]).astype(BF16)
            for c in range(g * band, (g + 1) * band)
        ]
        swapped = dot(swap[...], jnp.concatenate(rows, axis=0)).astype(BF16)
        normed[:, g * band : (g + 1) * band, :] = swapped.reshape(band, band, part)

    a = math.sqrt(2.0 / math.pi)
    blocks = [slice(n, min(n + 256, part)) for n in range(0, part, 256)]
    for r in range(band):
        for lanes in blocks:
            for h in range(0, hidden.shape[1], 128):
                rows = slice(h, h + 128)
                inner = dot(w_in_t[rows, :depth], normed[r, :, lanes]).astype(BF16)
                bent = inner * (BF16(a) + BF16(a * 0.044715) * (inner * inner))
                hidden[r, rows, lanes] = inner + inner * jnp.tanh(bent)
    for r in range(band):
        for lanes in blocks:
            mixed[r, :, lanes] = (0.5 * dot(w_out_t, hidden[r, :, lanes])).astype(BF16)

    sends = []
    for g in range(groups):
        block = mixed[:, g * band : (g + 1) * band, :].reshape(band * band, part)
        swapped = dot(swap[...], block).astype(BF16)
        where = pl.ds(g * band, band)
        out[where] = swapped.reshape(band, band, part)
        sends.append(pltpu.make_async_copy(out.at[where], out_h.at[where], sems.at[g]))
        sends[-1].start()
    for send in sends:
        send.wait()


def spread_kernel(taps, stepped, mixed, out, above, middle, below, result, sems):
    bands, parts, ch_dev, band, part = stepped.shape
    img = parts * part
    group = 4
    size = group * band

    def rows_of(source, start, ch):
        pieces = [source[start : start + group, p, ch].reshape(size, part) for p in range(parts)]
        return jnp.concatenate(pieces, axis=1).astype(F32)

    zero = jnp.zeros((img // 128, 8, 128), F32)
    above[:, 0:8, :] = zero
    below[:, img : img + 8, :] = zero
    lane = lax.broadcasted_iota(jnp.int32, (size, 128), 1)
    sends = []
    for ch in range(ch_dev):
        k = [[taps[i, j, ch : ch + 1, :] for j in range(3)] for i in range(3)]

        def across(start):
            x = rows_of(mixed, start, ch)
            low, high = pltpu.roll(x, 1, 1), pltpu.roll(x, img - 1, 1)
            at = start * band
            for n in range(img // 128):
                lanes = slice(n * 128, (n + 1) * 128)
                left, here, right = low[:, lanes], x[:, lanes], high[:, lanes]
                if n == 0:
                    left = jnp.where(lane == 0, 0.0, left)
                if n == img // 128 - 1:
                    right = jnp.where(lane == 127, 0.0, right)
                for target, row, off in ((above, 0, 8), (middle, 1, 0), (below, 2, 0)):
                    value = k[row][0] * left + k[row][1] * here + k[row][2] * right
                    target[n, at + off : at + off + size, :] = value

        def down(start):
            at = start * band
            base = rows_of(stepped, start, ch)
            for n in range(img // 128):
                total = above[n, at + 7 : at + 7 + size, :] + below[n, at + 1 : at + 1 + size, :]
                total = total + middle[n, at : at + size, :]
                total = base[:, n * 128 : (n + 1) * 128] + total
                result[ch, at : at + size, n * 128 : (n + 1) * 128] = total.astype(BF16)

        def leave(start):
            down(start)
            rows = pl.ds(start * band, size)
            at = sems.at[ch * (bands // group) + start // group]
            sends.append(pltpu.make_async_copy(result.at[ch, rows], out.at[ch, rows], at))
            sends[-1].start()

        for start in range(0, bands, group):
            across(start)
            if start:
                leave(start - group)
        leave(bands - group)
    for send in sends:
        send.wait()


VMEM = pl.BlockSpec(memory_space=pltpu.VMEM)
SMEM = pl.BlockSpec(memory_space=pltpu.SMEM)
HBM = pl.BlockSpec(memory_space=pltpu.HBM)


def params(mib):
    return pltpu.CompilerParams(vmem_limit_bytes=mib * MIB)


def partner_order(n_rows, n_cols):
    half, near, core = n_cols // 2, n_cols // 4, 1
    steps = [half, core]
    steps += [bit for bit in (1 << k for k in range(1, 16)) if bit < n_rows * n_cols and bit != half]
    order = [near]
    for step in steps:
        order += [device ^ step for device in order]
    return order


def exchange(blocks, order):
    return lax.all_to_all(
        blocks, "all", split_axis=0, concat_axis=0, axis_index_groups=[order], tiled=True
    )


def layers(w_in, b_in, w_out_t, wide):
    rows = []
    for _ in range(3):
        rows.append(lax.reduce_precision(b_in, 8, 7))
        b_in = b_in - rows[-1]
    zeros = jnp.zeros((wide - w_in.shape[0] - 3, w_in.shape[1]), BF16)
    return jnp.concatenate([w_in, jnp.stack(rows).astype(BF16), zeros, w_out_t], axis=0)


def local(n_rows, n_cols, model, dirty, psf, step_size, gain, w_in, b_in, w_out, kernel):
    ch_dev, img, _ = model.shape
    psf_len = psf.shape[1]
    assert ch_dev == 2
    n_dev = n_rows * n_cols
    order = partner_order(n_rows, n_cols)
    channels = gain.shape[0]
    hidden = b_in.shape[0]
    part = img * img // (n_dev * BAND)
    parts = img // part
    bands = img // BAND
    table, turned = tables(img, psf_len)
    length = table.shape[0]
    wide = -(-(channels + BAND) // 128) * 128
    blocks = (bands, parts, ch_dev, BAND, part)

    stepped = pl.pallas_call(
        conv_kernel,
        out_shape=jax.ShapeDtypeStruct(blocks, BF16),
        in_specs=[HBM] * 6,
        out_specs=HBM,
        scratch_shapes=[
            pltpu.SMEM(step_size.shape, F32),
            pltpu.VMEM(model.shape, BF16),
            pltpu.VMEM(model.shape, BF16),
            pltpu.VMEM(psf.shape, BF16),
            pltpu.VMEM(table.shape, BF16),
            pltpu.VMEM(turned.shape, BF16),
            pltpu.VMEM((img, 2 * length), BF16),
            pltpu.VMEM((psf_len, 2 * length), BF16),
            pltpu.VMEM((length, 2 * length), F32),
            pltpu.VMEM((length, 2 * length), F32),
            pltpu.VMEM((length, 2 * length), BF16),
            pltpu.VMEM((img, 2 * length), BF16),
            pltpu.VMEM(blocks, BF16),
            pltpu.SemaphoreType.DMA((20,)),
            pltpu.SemaphoreType.DMA((img // 128,)),
        ],
        compiler_params=params(58),
        name="conv",
    )(step_size, model, dirty, psf, table, turned)
    stepped, gain, w_in, b_in, w_out, kernel = lax.optimization_barrier(
        (stepped, gain, w_in, b_in, w_out, kernel)
    )

    def ordered(values):
        return jnp.concatenate([values[d * ch_dev : (d + 1) * ch_dev] for d in order], axis=0)

    tiles = exchange(stepped.reshape(n_dev, ch_dev, BAND, part), order).reshape(channels, BAND, part)

    mixed = pl.pallas_call(
        mix_kernel,
        out_shape=jax.ShapeDtypeStruct((channels, BAND, part), BF16),
        in_specs=[VMEM] * 3,
        out_specs=HBM,
        scratch_shapes=[
            pltpu.VMEM((hidden, wide), BF16),
            pltpu.VMEM((BAND * BAND, BAND * BAND), BF16),
            pltpu.VMEM((BAND, channels + BAND, part), BF16),
            pltpu.VMEM((BAND, hidden, part), BF16),
            pltpu.VMEM((BAND, channels, part), BF16),
            pltpu.VMEM((channels, BAND, part), BF16),
            pltpu.SemaphoreType.DMA((channels // BAND,)),
        ],
        compiler_params=params(24),
        name="mix",
    )(
        jnp.broadcast_to(ordered(gain)[:, None], (channels, part)),
        layers(ordered(w_in), b_in, ordered(w_out.T), wide),
        tiles,
    )

    returned = exchange(mixed.reshape(n_dev, ch_dev, BAND, part), order).reshape(blocks)
    position = lax.axis_index("all").astype(jnp.int32) * ch_dev
    taps = lax.dynamic_slice_in_dim(kernel, position, ch_dev, axis=2)
    taps = jnp.broadcast_to(taps[..., None], (3, 3, ch_dev, 128))
    plane = pltpu.VMEM((img // 128, img + 8, 128), F32)

    return pl.pallas_call(
        spread_kernel,
        out_shape=jax.ShapeDtypeStruct((ch_dev, img, img), BF16),
        in_specs=[VMEM] * 3,
        out_specs=HBM,
        scratch_shapes=[
            plane, plane, plane, pltpu.VMEM((ch_dev, img, img), BF16),
            pltpu.SemaphoreType.DMA((ch_dev * bands // 4,)),
        ],
        compiler_params=params(24),
        name="spread",
    )(taps, stepped, returned)


def solution(mesh):
    line = Mesh(mesh.devices.reshape(-1), ("all",))
    planes = P("all", None, None)
    return jax.shard_map(
        functools.partial(local, *mesh.devices.shape),
        mesh=line,
        in_specs=(planes, planes, planes, P("all"), P(), P(), P(), P(), P()),
        out_specs=planes,
        check_vma=False,
    )
```

```python
import functools
import math

import jax
import jax.numpy as jnp
import ml_dtypes
import numpy as np
from jax import lax
from jax.experimental import pallas as pl
from jax.experimental.pallas import tpu as pltpu
from jax.sharding import Mesh
from jax.sharding import PartitionSpec as P

BAND = 16
GROUP = 64
MIB = 1024 * 1024
BF16, F32 = jnp.bfloat16, jnp.float32


def tables(img, psf):
    length = img + psf // 2
    half = length // 2
    phase = (2 * np.arange(half)[:, None] + 1) * np.arange(length)[None, :] % (2 * length)
    angle = (phase * (math.pi / length)).reshape(half // GROUP, 1, GROUP, length)
    table = np.concatenate([np.cos(angle), np.sin(angle)], axis=1).reshape(length, length)
    table = table.astype(ml_dtypes.bfloat16)
    return jnp.asarray(table), jnp.asarray(np.ascontiguousarray(table.T))


def dot(a, b):
    return jnp.dot(a, b, preferred_element_type=F32)


def interleave(first, second):
    done = 0
    for i, step in enumerate(first):
        step()
        while done * len(first) < (i + 1) * len(second):
            second[done]()
            done += 1


def conv_kernel(
    rate_h, model_h, dirty_h, psf_h, table_h, turned_h, out_h,
    rate, model, dirty, psf, table, turned, cols_x, cols_q, spec_x, spec_q, prod, rows_y, out, sems, out_sems,
):
    img = model.shape[1]
    taps = psf.shape[1]
    shift = taps // 2
    length = table.shape[1]
    tiles = [slice(n, n + 256) for n in range(0, 2 * length, 256)]
    tall = length // 2
    loads = {}

    def load(name, source, target, start, count, pieces):
        for i in range(pieces):
            rows = pl.ds(start + i * count // pieces, count // pieces)
            copy = pltpu.make_async_copy(source.at[rows], target.at[rows], sems.at[sum(map(len, loads.values()))])
            copy.start()
            loads.setdefault(name, []).append(copy)

    def arrived(name):
        for copy in loads[name]:
            copy.wait()

    load("psf", psf_h.at[0], psf.at[0], 0, taps, 1)
    load("turned_0", turned_h, turned, 0, taps, 4)
    load("psf", psf_h.at[1], psf.at[1], 0, taps, 1)
    load("model_0", model_h.at[0], model.at[0], 0, img, 2)
    load("turned_1", turned_h, turned, taps, img - taps, 2)
    load("model_1", model_h.at[1], model.at[1], 0, img, 2)
    load("table", table_h, table, 0, length, 4)
    loads["rate"] = [pltpu.make_async_copy(rate_h, rate, sems.at[sum(map(len, loads.values()))])]
    loads["rate"][0].start()

    def columns(source, depth, target, waits):
        for ch in range(2):
            for wait in waits[ch]:
                arrived(wait)
            for m in range(0, depth, 256):
                rows = slice(m, m + 256)
                for n in range(0, length, 256):
                    lanes = slice(n, min(n + 256, length))
                    to = slice(ch * length + lanes.start, ch * length + lanes.stop)
                    target[rows, to] = dot(source[ch, rows, :], turned[:depth, lanes]).astype(BF16)

    columns(psf, taps, cols_q, (("psf", "turned_0"), ()))
    load("rest", turned_h, turned, img, length - img, 1)
    load("dirty", dirty_h, dirty, 0, 2, 2)
    columns(model, img, cols_x, (("model_0", "turned_1"), ("model_1",)))

    def spectra(lanes):
        def one(target, source, depth, m):
            target[m : m + tall, lanes] = dot(table[m : m + tall, :depth], source[:, lanes])

        return [
            functools.partial(one, target, source, depth, m)
            for m in range(0, length, tall)
            for target, source, depth in ((spec_q, cols_q, taps), (spec_x, cols_x, img))
        ]

    lane = lax.broadcasted_iota(jnp.int32, (16, 2 * GROUP), 1)
    sign = jnp.where(lane < GROUP, -1.0, 1.0)

    def products(lanes):
        def one(row, at):
            c, s, columns = slice(row, row + 16), slice(row + GROUP, row + GROUP + 16), slice(at, at + 2 * GROUP)

            def parts(value):
                turn = pltpu.roll(value, GROUP, 1)
                return jnp.where(lane < GROUP, value, turn), jnp.where(lane < GROUP, turn, value)

            (c_re, c_im), (s_re, s_im) = parts(spec_x[c, columns]), parts(spec_x[s, columns])
            q_c, q_s = spec_q[c, columns], spec_q[s, columns]
            t_c, t_s = pltpu.roll(q_c, GROUP, 1) * sign, pltpu.roll(q_s, GROUP, 1) * sign
            prod[c, columns] = ((c_re * q_c + c_im * t_c) - (s_re * q_s + s_im * t_s)).astype(BF16)
            prod[s, columns] = ((s_re * q_c + s_im * t_c) + (c_re * q_s + c_im * t_s)).astype(BF16)

        return [
            functools.partial(one, base + row, at)
            for base in range(0, length, 2 * GROUP)
            for row in range(0, GROUP, 16)
            for at in range(lanes.start, lanes.stop, 2 * GROUP)
        ]

    def inverse(lanes):
        def one(m):
            back = turned[shift + m : shift + m + 256, :]
            rows_y[m : m + 256, lanes] = dot(back, prod[:, lanes]).astype(BF16)

        return [functools.partial(one, m) for m in range(0, img, 256)]

    arrived("table")
    arrived("rest")
    for step in spectra(tiles[0]):
        step()
    for t in range(len(tiles)):
        matrix = (inverse(tiles[t - 1]) if t else []) + (spectra(tiles[t + 1]) if t + 1 < len(tiles) else [])
        interleave(products(tiles[t]), matrix)
    for step in inverse(tiles[-1]):
        step()

    arrived("dirty")
    arrived("rate")
    bands, parts, _, band, part = out.shape
    step = 256
    sends = []
    for i in range(img // step):
        rows = slice(i * step, (i + 1) * step)
        where = slice(i * step // band, (i + 1) * step // band)
        for ch in range(2):
            scale = rate[ch] * (4.0 / (length * length))
            inner = rows_y[rows, ch * length : (ch + 1) * length]
            for n in range(0, img, 256):
                lanes = slice(n, n + 256)
                blurred = dot(inner, table[:, shift + n : shift + n + 256])
                stepped = rate[ch] * dirty[ch, rows, lanes].astype(F32) - scale * blurred
                stepped = (model[ch, rows, lanes].astype(F32) + stepped).astype(BF16)
                size = min(part, 256)
                for k in range(0, 256, size):
                    piece = stepped[:, k : k + size].reshape(step // band, band, size)
                    at = (n + k) % part
                    out[where, (n + k) // part, ch, :, at : at + size] = piece
            place = where, slice(None), ch
            sends.append(pltpu.make_async_copy(out.at[place], out_h.at[place], out_sems.at[len(sends)]))
            sends[-1].start()
    for send in sends:
        send.wait()


def mix_kernel(gain, weights, tiles, out_h, w_in_t, swap, normed, hidden, mixed, out, sems):
    channels, band, part = tiles.shape
    groups = channels // band

    depth = channels + band
    w_in_t[...] = weights[: w_in_t.shape[1], :].astype(F32).T.astype(BF16)
    w_out_t = weights[w_in_t.shape[1] :, :]
    place = [lax.broadcasted_iota(jnp.int32, swap.shape, axis) for axis in range(2)]
    swap[...] = jnp.where(place[0] % band * band + place[0] // band == place[1], 1.0, 0.0).astype(BF16)
    normed[:, channels:, :] = jnp.ones((band, band, part), BF16)
    power = jnp.zeros((band, part), F32)
    for c in range(channels):
        v = tiles[c].astype(F32)
        power = power + v * v
    inverse = lax.rsqrt(power * (1.0 / channels) + 1e-06)
    for g in range(groups):
        rows = [
            (tiles[c].astype(F32) * inverse * gain[c : c + 1, :]).astype(BF16)
            for c in range(g * band, (g + 1) * band)
        ]
        swapped = dot(swap[...], jnp.concatenate(rows, axis=0)).astype(BF16)
        normed[:, g * band : (g + 1) * band, :] = swapped.reshape(band, band, part)

    a = math.sqrt(2.0 / math.pi)
    blocks = [slice(n, min(n + 256, part)) for n in range(0, part, 256)]
    for r in range(band):
        for lanes in blocks:
            for h in range(0, hidden.shape[1], 128):
                rows = slice(h, h + 128)
                inner = dot(w_in_t[rows, :depth], normed[r, :, lanes]).astype(BF16)
                bent = inner * (BF16(a) + BF16(a * 0.044715) * (inner * inner))
                hidden[r, rows, lanes] = inner + inner * jnp.tanh(bent)
    for r in range(band):
        for lanes in blocks:
            mixed[r, :, lanes] = (0.5 * dot(w_out_t, hidden[r, :, lanes])).astype(BF16)

    sends = []
    for g in range(groups):
        block = mixed[:, g * band : (g + 1) * band, :].reshape(band * band, part)
        swapped = dot(swap[...], block).astype(BF16)
        where = pl.ds(g * band, band)
        out[where] = swapped.reshape(band, band, part)
        sends.append(pltpu.make_async_copy(out.at[where], out_h.at[where], sems.at[g]))
        sends[-1].start()
    for send in sends:
        send.wait()


def spread_kernel(taps, stepped, mixed, out, above, middle, below, result, sems):
    bands, parts, ch_dev, band, part = stepped.shape
    img = parts * part
    group = 4
    size = group * band

    def rows_of(source, start, ch):
        pieces = [source[start : start + group, p, ch].reshape(size, part) for p in range(parts)]
        return jnp.concatenate(pieces, axis=1).astype(F32)

    zero = jnp.zeros((img // 128, 8, 128), F32)
    above[:, 0:8, :] = zero
    below[:, img : img + 8, :] = zero
    lane = lax.broadcasted_iota(jnp.int32, (size, 128), 1)
    sends = []
    for ch in range(ch_dev):
        k = [[taps[i, j, ch : ch + 1, :] for j in range(3)] for i in range(3)]

        def across(start):
            x = rows_of(mixed, start, ch)
            low, high = pltpu.roll(x, 1, 1), pltpu.roll(x, img - 1, 1)
            at = start * band
            for n in range(img // 128):
                lanes = slice(n * 128, (n + 1) * 128)
                left, here, right = low[:, lanes], x[:, lanes], high[:, lanes]
                if n == 0:
                    left = jnp.where(lane == 0, 0.0, left)
                if n == img // 128 - 1:
                    right = jnp.where(lane == 127, 0.0, right)
                for target, row, off in ((above, 0, 8), (middle, 1, 0), (below, 2, 0)):
                    value = k[row][0] * left + k[row][1] * here + k[row][2] * right
                    target[n, at + off : at + off + size, :] = value

        def down(start):
            at = start * band
            base = rows_of(stepped, start, ch)
            for n in range(img // 128):
                total = above[n, at + 7 : at + 7 + size, :] + below[n, at + 1 : at + 1 + size, :]
                total = total + middle[n, at : at + size, :]
                total = base[:, n * 128 : (n + 1) * 128] + total
                result[ch, at : at + size, n * 128 : (n + 1) * 128] = total.astype(BF16)

        def leave(start):
            down(start)
            rows = pl.ds(start * band, size)
            at = sems.at[ch * (bands // group) + start // group]
            sends.append(pltpu.make_async_copy(result.at[ch, rows], out.at[ch, rows], at))
            sends[-1].start()

        for start in range(0, bands, group):
            across(start)
            if start:
                leave(start - group)
        leave(bands - group)
    for send in sends:
        send.wait()


VMEM = pl.BlockSpec(memory_space=pltpu.VMEM)
SMEM = pl.BlockSpec(memory_space=pltpu.SMEM)
HBM = pl.BlockSpec(memory_space=pltpu.HBM)


def params(mib):
    return pltpu.CompilerParams(vmem_limit_bytes=mib * MIB)


def partner_order(n_rows, n_cols):
    half, near, core = n_cols // 2, n_cols // 4, 1
    steps = [half | near, core]
    steps += [bit for bit in (1 << k for k in range(1, 16)) if bit < n_rows * n_cols and bit != half]
    order = [half | near]
    for step in steps:
        order += [device ^ step for device in order]
    return order


def exchange(blocks, order):
    return lax.all_to_all(
        blocks, "all", split_axis=0, concat_axis=0, axis_index_groups=[order], tiled=True
    )


def layers(w_in, b_in, w_out_t, wide):
    rows = []
    for _ in range(3):
        rows.append(lax.reduce_precision(b_in, 8, 7))
        b_in = b_in - rows[-1]
    zeros = jnp.zeros((wide - w_in.shape[0] - 3, w_in.shape[1]), BF16)
    return jnp.concatenate([w_in, jnp.stack(rows).astype(BF16), zeros, w_out_t], axis=0)


def local(n_rows, n_cols, model, dirty, psf, step_size, gain, w_in, b_in, w_out, kernel):
    ch_dev, img, _ = model.shape
    psf_len = psf.shape[1]
    assert ch_dev == 2
    n_dev = n_rows * n_cols
    order = partner_order(n_rows, n_cols)
    channels = gain.shape[0]
    hidden = b_in.shape[0]
    part = img * img // (n_dev * BAND)
    parts = img // part
    bands = img // BAND
    table, turned = tables(img, psf_len)
    length = table.shape[0]
    wide = -(-(channels + BAND) // 128) * 128
    blocks = (bands, parts, ch_dev, BAND, part)

    stepped = pl.pallas_call(
        conv_kernel,
        out_shape=jax.ShapeDtypeStruct(blocks, BF16),
        in_specs=[HBM] * 6,
        out_specs=HBM,
        scratch_shapes=[
            pltpu.SMEM(step_size.shape, F32),
            pltpu.VMEM(model.shape, BF16),
            pltpu.VMEM(model.shape, BF16),
            pltpu.VMEM(psf.shape, BF16),
            pltpu.VMEM(table.shape, BF16),
            pltpu.VMEM(turned.shape, BF16),
            pltpu.VMEM((img, 2 * length), BF16),
            pltpu.VMEM((psf_len, 2 * length), BF16),
            pltpu.VMEM((length, 2 * length), F32),
            pltpu.VMEM((length, 2 * length), F32),
            pltpu.VMEM((length, 2 * length), BF16),
            pltpu.VMEM((img, 2 * length), BF16),
            pltpu.VMEM(blocks, BF16),
            pltpu.SemaphoreType.DMA((20,)),
            pltpu.SemaphoreType.DMA((img // 128,)),
        ],
        compiler_params=params(58),
        name="conv",
    )(step_size, model, dirty, psf, table, turned)
    stepped, gain, w_in, b_in, w_out, kernel = lax.optimization_barrier(
        (stepped, gain, w_in, b_in, w_out, kernel)
    )

    def ordered(values):
        return jnp.concatenate([values[d * ch_dev : (d + 1) * ch_dev] for d in order], axis=0)

    tiles = exchange(stepped.reshape(n_dev, ch_dev, BAND, part), order).reshape(channels, BAND, part)

    mixed = pl.pallas_call(
        mix_kernel,
        out_shape=jax.ShapeDtypeStruct((channels, BAND, part), BF16),
        in_specs=[VMEM] * 3,
        out_specs=HBM,
        scratch_shapes=[
            pltpu.VMEM((hidden, wide), BF16),
            pltpu.VMEM((BAND * BAND, BAND * BAND), BF16),
            pltpu.VMEM((BAND, channels + BAND, part), BF16),
            pltpu.VMEM((BAND, hidden, part), BF16),
            pltpu.VMEM((BAND, channels, part), BF16),
            pltpu.VMEM((channels, BAND, part), BF16),
            pltpu.SemaphoreType.DMA((channels // BAND,)),
        ],
        compiler_params=params(24),
        name="mix",
    )(
        jnp.broadcast_to(ordered(gain)[:, None], (channels, part)),
        layers(ordered(w_in), b_in, ordered(w_out.T), wide),
        tiles,
    )

    returned = exchange(mixed.reshape(n_dev, ch_dev, BAND, part), order).reshape(blocks)
    position = lax.axis_index("all").astype(jnp.int32) * ch_dev
    taps = lax.dynamic_slice_in_dim(kernel, position, ch_dev, axis=2)
    taps = jnp.broadcast_to(taps[..., None], (3, 3, ch_dev, 128))
    plane = pltpu.VMEM((img // 128, img + 8, 128), F32)

    return pl.pallas_call(
        spread_kernel,
        out_shape=jax.ShapeDtypeStruct((ch_dev, img, img), BF16),
        in_specs=[VMEM] * 3,
        out_specs=HBM,
        scratch_shapes=[
            plane, plane, plane, pltpu.VMEM((ch_dev, img, img), BF16),
            pltpu.SemaphoreType.DMA((ch_dev * bands // 4,)),
        ],
        compiler_params=params(24),
        name="spread",
    )(taps, stepped, returned)


def solution(mesh):
    line = Mesh(mesh.devices.reshape(-1), ("all",))
    planes = P("all", None, None)
    return jax.shard_map(
        functools.partial(local, *mesh.devices.shape),
        mesh=line,
        in_specs=(planes, planes, planes, P("all"), P(), P(), P(), P(), P()),
        out_specs=planes,
        check_vma=False,
    )
```

```python
import functools
import math

import jax
import jax.numpy as jnp
import ml_dtypes
import numpy as np
from jax import lax
from jax.experimental import pallas as pl
from jax.experimental.pallas import tpu as pltpu
from jax.sharding import Mesh
from jax.sharding import PartitionSpec as P

BAND = 16
GROUP = 64
MIB = 1024 * 1024
BF16, F32 = jnp.bfloat16, jnp.float32


def tables(img, psf):
    length = img + psf // 2
    half = length // 2
    phase = (2 * np.arange(half)[:, None] + 1) * np.arange(length)[None, :] % (2 * length)
    angle = (phase * (math.pi / length)).reshape(half // GROUP, 1, GROUP, length)
    table = np.concatenate([np.cos(angle), np.sin(angle)], axis=1).reshape(length, length)
    table = table.astype(ml_dtypes.bfloat16)
    return jnp.asarray(table), jnp.asarray(np.ascontiguousarray(table.T))


def dot(a, b):
    return jnp.dot(a, b, preferred_element_type=F32)


def interleave(first, second):
    done = 0
    for i, step in enumerate(first):
        step()
        while done * len(first) < (i + 1) * len(second):
            second[done]()
            done += 1


def conv_kernel(
    rate_h, model_h, dirty_h, psf_h, table_h, turned_h, out_h,
    rate, model, dirty, psf, table, turned, cols_x, cols_q, spec_x, spec_q, prod, rows_y, out, sems, out_sems,
):
    img = model.shape[1]
    taps = psf.shape[1]
    shift = taps // 2
    length = table.shape[1]
    tiles = [slice(n, n + 256) for n in range(0, 2 * length, 256)]
    tall = length // 2
    loads = {}

    def load(name, source, target, start, count, pieces):
        for i in range(pieces):
            rows = pl.ds(start + i * count // pieces, count // pieces)
            copy = pltpu.make_async_copy(source.at[rows], target.at[rows], sems.at[sum(map(len, loads.values()))])
            copy.start()
            loads.setdefault(name, []).append(copy)

    def arrived(name):
        for copy in loads[name]:
            copy.wait()

    load("psf", psf_h.at[0], psf.at[0], 0, taps, 1)
    load("turned_0", turned_h, turned, 0, taps, 4)
    load("psf", psf_h.at[1], psf.at[1], 0, taps, 1)
    load("model_0", model_h.at[0], model.at[0], 0, img, 2)
    load("turned_1", turned_h, turned, taps, img - taps, 2)
    load("model_1", model_h.at[1], model.at[1], 0, img, 2)
    load("table", table_h, table, 0, length, 4)
    loads["rate"] = [pltpu.make_async_copy(rate_h, rate, sems.at[sum(map(len, loads.values()))])]
    loads["rate"][0].start()

    def columns(source, depth, target, waits):
        for ch in range(2):
            for wait in waits[ch]:
                arrived(wait)
            for m in range(0, depth, 256):
                rows = slice(m, m + 256)
                for n in range(0, length, 256):
                    lanes = slice(n, min(n + 256, length))
                    to = slice(ch * length + lanes.start, ch * length + lanes.stop)
                    target[rows, to] = dot(source[ch, rows, :], turned[:depth, lanes]).astype(BF16)

    columns(psf, taps, cols_q, (("psf", "turned_0"), ()))
    load("rest", turned_h, turned, img, length - img, 1)
    load("dirty", dirty_h, dirty, 0, 2, 2)
    columns(model, img, cols_x, (("model_0", "turned_1"), ("model_1",)))

    def spectra(lanes):
        def one(target, source, depth, m):
            target[m : m + tall, lanes] = dot(table[m : m + tall, :depth], source[:, lanes])

        return [
            functools.partial(one, target, source, depth, m)
            for m in range(0, length, tall)
            for target, source, depth in ((spec_q, cols_q, taps), (spec_x, cols_x, img))
        ]

    lane = lax.broadcasted_iota(jnp.int32, (16, 2 * GROUP), 1)
    sign = jnp.where(lane < GROUP, -1.0, 1.0)

    def products(lanes):
        def one(row, at):
            c, s, columns = slice(row, row + 16), slice(row + GROUP, row + GROUP + 16), slice(at, at + 2 * GROUP)

            def parts(value):
                turn = pltpu.roll(value, GROUP, 1)
                return jnp.where(lane < GROUP, value, turn), jnp.where(lane < GROUP, turn, value)

            (c_re, c_im), (s_re, s_im) = parts(spec_x[c, columns]), parts(spec_x[s, columns])
            q_c, q_s = spec_q[c, columns], spec_q[s, columns]
            t_c, t_s = pltpu.roll(q_c, GROUP, 1) * sign, pltpu.roll(q_s, GROUP, 1) * sign
            prod[c, columns] = ((c_re * q_c + c_im * t_c) - (s_re * q_s + s_im * t_s)).astype(BF16)
            prod[s, columns] = ((s_re * q_c + s_im * t_c) + (c_re * q_s + c_im * t_s)).astype(BF16)

        return [
            functools.partial(one, base + row, at)
            for base in range(0, length, 2 * GROUP)
            for row in range(0, GROUP, 16)
            for at in range(lanes.start, lanes.stop, 2 * GROUP)
        ]

    def inverse(lanes):
        def one(m):
            back = turned[shift + m : shift + m + 256, :]
            rows_y[m : m + 256, lanes] = dot(back, prod[:, lanes]).astype(BF16)

        return [functools.partial(one, m) for m in range(0, img, 256)]

    arrived("table")
    arrived("rest")
    for step in spectra(tiles[0]):
        step()
    for t in range(len(tiles)):
        matrix = (inverse(tiles[t - 1]) if t else []) + (spectra(tiles[t + 1]) if t + 1 < len(tiles) else [])
        interleave(products(tiles[t]), matrix)
    for step in inverse(tiles[-1]):
        step()

    arrived("dirty")
    arrived("rate")
    bands, parts, _, band, part = out.shape
    step = 256
    sends = []
    for i in range(img // step):
        rows = slice(i * step, (i + 1) * step)
        where = slice(i * step // band, (i + 1) * step // band)
        for ch in range(2):
            scale = rate[ch] * (4.0 / (length * length))
            inner = rows_y[rows, ch * length : (ch + 1) * length]
            for n in range(0, img, 256):
                lanes = slice(n, n + 256)
                blurred = dot(inner, table[:, shift + n : shift + n + 256])
                stepped = rate[ch] * dirty[ch, rows, lanes].astype(F32) - scale * blurred
                stepped = (model[ch, rows, lanes].astype(F32) + stepped).astype(BF16)
                size = min(part, 256)
                for k in range(0, 256, size):
                    piece = stepped[:, k : k + size].reshape(step // band, band, size)
                    at = (n + k) % part
                    out[where, (n + k) // part, ch, :, at : at + size] = piece
            place = where, slice(None), ch
            sends.append(pltpu.make_async_copy(out.at[place], out_h.at[place], out_sems.at[len(sends)]))
            sends[-1].start()
    for send in sends:
        send.wait()


def mix_kernel(gain, weights, tiles, out_h, w_in_t, swap, normed, hidden, mixed, out, sems):
    channels, band, part = tiles.shape
    groups = channels // band

    depth = channels + band
    w_in_t[...] = weights[: w_in_t.shape[1], :].astype(F32).T.astype(BF16)
    w_out_t = weights[w_in_t.shape[1] :, :]
    place = [lax.broadcasted_iota(jnp.int32, swap.shape, axis) for axis in range(2)]
    swap[...] = jnp.where(place[0] % band * band + place[0] // band == place[1], 1.0, 0.0).astype(BF16)
    normed[:, channels:, :] = jnp.ones((band, band, part), BF16)
    power = jnp.zeros((band, part), F32)
    for c in range(channels):
        v = tiles[c].astype(F32)
        power = power + v * v
    inverse = lax.rsqrt(power * (1.0 / channels) + 1e-06)
    for g in range(groups):
        rows = [
            (tiles[c].astype(F32) * inverse * gain[c : c + 1, :]).astype(BF16)
            for c in range(g * band, (g + 1) * band)
        ]
        swapped = dot(swap[...], jnp.concatenate(rows, axis=0)).astype(BF16)
        normed[:, g * band : (g + 1) * band, :] = swapped.reshape(band, band, part)

    a = math.sqrt(2.0 / math.pi)
    blocks = [slice(n, min(n + 256, part)) for n in range(0, part, 256)]
    for r in range(band):
        for lanes in blocks:
            for h in range(0, hidden.shape[1], 128):
                rows = slice(h, h + 128)
                inner = dot(w_in_t[rows, :depth], normed[r, :, lanes]).astype(BF16)
                bent = inner * (BF16(a) + BF16(a * 0.044715) * (inner * inner))
                hidden[r, rows, lanes] = inner + inner * jnp.tanh(bent)
    for r in range(band):
        for lanes in blocks:
            mixed[r, :, lanes] = (0.5 * dot(w_out_t, hidden[r, :, lanes])).astype(BF16)

    sends = []
    for g in range(groups):
        block = mixed[:, g * band : (g + 1) * band, :].reshape(band * band, part)
        swapped = dot(swap[...], block).astype(BF16)
        where = pl.ds(g * band, band)
        out[where] = swapped.reshape(band, band, part)
        sends.append(pltpu.make_async_copy(out.at[where], out_h.at[where], sems.at[g]))
        sends[-1].start()
    for send in sends:
        send.wait()


def spread_kernel(taps, stepped, mixed, out, above, middle, below, result, sems):
    bands, parts, ch_dev, band, part = stepped.shape
    img = parts * part
    group = 4
    size = group * band

    def rows_of(source, start, ch):
        pieces = [source[start : start + group, p, ch].reshape(size, part) for p in range(parts)]
        return jnp.concatenate(pieces, axis=1).astype(F32)

    zero = jnp.zeros((img // 128, 8, 128), F32)
    above[:, 0:8, :] = zero
    below[:, img : img + 8, :] = zero
    lane = lax.broadcasted_iota(jnp.int32, (size, 128), 1)
    sends = []
    for ch in range(ch_dev):
        k = [[taps[i, j, ch : ch + 1, :] for j in range(3)] for i in range(3)]

        def across(start):
            x = rows_of(mixed, start, ch)
            low, high = pltpu.roll(x, 1, 1), pltpu.roll(x, img - 1, 1)
            at = start * band
            for n in range(img // 128):
                lanes = slice(n * 128, (n + 1) * 128)
                left, here, right = low[:, lanes], x[:, lanes], high[:, lanes]
                if n == 0:
                    left = jnp.where(lane == 0, 0.0, left)
                if n == img // 128 - 1:
                    right = jnp.where(lane == 127, 0.0, right)
                for target, row, off in ((above, 0, 8), (middle, 1, 0), (below, 2, 0)):
                    value = k[row][0] * left + k[row][1] * here + k[row][2] * right
                    target[n, at + off : at + off + size, :] = value

        def down(start):
            at = start * band
            base = rows_of(stepped, start, ch)
            for n in range(img // 128):
                total = above[n, at + 7 : at + 7 + size, :] + below[n, at + 1 : at + 1 + size, :]
                total = total + middle[n, at : at + size, :]
                total = base[:, n * 128 : (n + 1) * 128] + total
                result[ch, at : at + size, n * 128 : (n + 1) * 128] = total.astype(BF16)

        def leave(start):
            down(start)
            rows = pl.ds(start * band, size)
            at = sems.at[ch * (bands // group) + start // group]
            sends.append(pltpu.make_async_copy(result.at[ch, rows], out.at[ch, rows], at))
            sends[-1].start()

        for start in range(0, bands, group):
            across(start)
            if start:
                leave(start - group)
        leave(bands - group)
    for send in sends:
        send.wait()


VMEM = pl.BlockSpec(memory_space=pltpu.VMEM)
SMEM = pl.BlockSpec(memory_space=pltpu.SMEM)
HBM = pl.BlockSpec(memory_space=pltpu.HBM)


def params(mib):
    return pltpu.CompilerParams(vmem_limit_bytes=mib * MIB)


def partner_order(n_rows, n_cols):
    side = n_cols // 2
    up = [half * side + k for k in range(side) for half in (0, 1)]
    order = []
    for i in range(n_rows):
        row = i ^ (i >> 1)
        order += [row * n_cols + c for c in (reversed(up) if i % 2 else up)]
    return order


def exchange(blocks, order):
    return lax.all_to_all(
        blocks, "all", split_axis=0, concat_axis=0, axis_index_groups=[order], tiled=True
    )


def layers(w_in, b_in, w_out_t, wide):
    rows = []
    for _ in range(3):
        rows.append(lax.reduce_precision(b_in, 8, 7))
        b_in = b_in - rows[-1]
    zeros = jnp.zeros((wide - w_in.shape[0] - 3, w_in.shape[1]), BF16)
    return jnp.concatenate([w_in, jnp.stack(rows).astype(BF16), zeros, w_out_t], axis=0)


def local(n_rows, n_cols, model, dirty, psf, step_size, gain, w_in, b_in, w_out, kernel):
    ch_dev, img, _ = model.shape
    psf_len = psf.shape[1]
    assert ch_dev == 2
    n_dev = n_rows * n_cols
    order = partner_order(n_rows, n_cols)
    channels = gain.shape[0]
    hidden = b_in.shape[0]
    part = img * img // (n_dev * BAND)
    parts = img // part
    bands = img // BAND
    table, turned = tables(img, psf_len)
    length = table.shape[0]
    wide = -(-(channels + BAND) // 128) * 128
    blocks = (bands, parts, ch_dev, BAND, part)

    stepped = pl.pallas_call(
        conv_kernel,
        out_shape=jax.ShapeDtypeStruct(blocks, BF16),
        in_specs=[HBM] * 6,
        out_specs=HBM,
        scratch_shapes=[
            pltpu.SMEM(step_size.shape, F32),
            pltpu.VMEM(model.shape, BF16),
            pltpu.VMEM(model.shape, BF16),
            pltpu.VMEM(psf.shape, BF16),
            pltpu.VMEM(table.shape, BF16),
            pltpu.VMEM(turned.shape, BF16),
            pltpu.VMEM((img, 2 * length), BF16),
            pltpu.VMEM((psf_len, 2 * length), BF16),
            pltpu.VMEM((length, 2 * length), F32),
            pltpu.VMEM((length, 2 * length), F32),
            pltpu.VMEM((length, 2 * length), BF16),
            pltpu.VMEM((img, 2 * length), BF16),
            pltpu.VMEM(blocks, BF16),
            pltpu.SemaphoreType.DMA((20,)),
            pltpu.SemaphoreType.DMA((img // 128,)),
        ],
        compiler_params=params(58),
        name="conv",
    )(step_size, model, dirty, psf, table, turned)
    stepped, gain, w_in, b_in, w_out, kernel = lax.optimization_barrier(
        (stepped, gain, w_in, b_in, w_out, kernel)
    )

    def ordered(values):
        return jnp.concatenate([values[d * ch_dev : (d + 1) * ch_dev] for d in order], axis=0)

    tiles = exchange(stepped.reshape(n_dev, ch_dev, BAND, part), order).reshape(channels, BAND, part)

    mixed = pl.pallas_call(
        mix_kernel,
        out_shape=jax.ShapeDtypeStruct((channels, BAND, part), BF16),
        in_specs=[VMEM] * 3,
        out_specs=HBM,
        scratch_shapes=[
            pltpu.VMEM((hidden, wide), BF16),
            pltpu.VMEM((BAND * BAND, BAND * BAND), BF16),
            pltpu.VMEM((BAND, channels + BAND, part), BF16),
            pltpu.VMEM((BAND, hidden, part), BF16),
            pltpu.VMEM((BAND, channels, part), BF16),
            pltpu.VMEM((channels, BAND, part), BF16),
            pltpu.SemaphoreType.DMA((channels // BAND,)),
        ],
        compiler_params=params(24),
        name="mix",
    )(
        jnp.broadcast_to(ordered(gain)[:, None], (channels, part)),
        layers(ordered(w_in), b_in, ordered(w_out.T), wide),
        tiles,
    )

    returned = exchange(mixed.reshape(n_dev, ch_dev, BAND, part), order).reshape(blocks)
    position = lax.axis_index("all").astype(jnp.int32) * ch_dev
    taps = lax.dynamic_slice_in_dim(kernel, position, ch_dev, axis=2)
    taps = jnp.broadcast_to(taps[..., None], (3, 3, ch_dev, 128))
    plane = pltpu.VMEM((img // 128, img + 8, 128), F32)

    return pl.pallas_call(
        spread_kernel,
        out_shape=jax.ShapeDtypeStruct((ch_dev, img, img), BF16),
        in_specs=[VMEM] * 3,
        out_specs=HBM,
        scratch_shapes=[
            plane, plane, plane, pltpu.VMEM((ch_dev, img, img), BF16),
            pltpu.SemaphoreType.DMA((ch_dev * bands // 4,)),
        ],
        compiler_params=params(24),
        name="spread",
    )(taps, stepped, returned)


def solution(mesh):
    line = Mesh(mesh.devices.reshape(-1), ("all",))
    planes = P("all", None, None)
    return jax.shard_map(
        functools.partial(local, *mesh.devices.shape),
        mesh=line,
        in_specs=(planes, planes, planes, P("all"), P(), P(), P(), P(), P()),
        out_specs=planes,
        check_vma=False,
    )
```

```python
import functools
import math

import jax
import jax.numpy as jnp
import ml_dtypes
import numpy as np
from jax import lax
from jax.experimental import pallas as pl
from jax.experimental.pallas import tpu as pltpu
from jax.sharding import Mesh
from jax.sharding import PartitionSpec as P

BAND = 16
GROUP = 64
MIB = 1024 * 1024
BF16, F32 = jnp.bfloat16, jnp.float32


def tables(img, psf):
    length = img + psf // 2
    half = length // 2
    phase = (2 * np.arange(half)[:, None] + 1) * np.arange(length)[None, :] % (2 * length)
    angle = (phase * (math.pi / length)).reshape(half // GROUP, 1, GROUP, length)
    table = np.concatenate([np.cos(angle), np.sin(angle)], axis=1).reshape(length, length)
    table = table.astype(ml_dtypes.bfloat16)
    return jnp.asarray(table), jnp.asarray(np.ascontiguousarray(table.T))


def dot(a, b):
    return jnp.dot(a, b, preferred_element_type=F32)


def interleave(first, second):
    done = 0
    for i, step in enumerate(first):
        step()
        while done * len(first) < (i + 1) * len(second):
            second[done]()
            done += 1


def conv_kernel(
    rate_h, model_h, dirty_h, psf_h, table_h, turned_h, out_h,
    rate, model, dirty, psf, table, turned, cols_x, cols_q, spec_x, spec_q, prod, rows_y, out, sems, out_sems,
):
    img = model.shape[1]
    taps = psf.shape[1]
    shift = taps // 2
    length = table.shape[1]
    tiles = [slice(n, n + 256) for n in range(0, 2 * length, 256)]
    tall = length // 2
    loads = {}

    def load(name, source, target, start, count, pieces):
        for i in range(pieces):
            rows = pl.ds(start + i * count // pieces, count // pieces)
            copy = pltpu.make_async_copy(source.at[rows], target.at[rows], sems.at[sum(map(len, loads.values()))])
            copy.start()
            loads.setdefault(name, []).append(copy)

    def arrived(name):
        for copy in loads[name]:
            copy.wait()

    load("psf", psf_h.at[0], psf.at[0], 0, taps, 1)
    load("turned_0", turned_h, turned, 0, taps, 4)
    load("psf", psf_h.at[1], psf.at[1], 0, taps, 1)
    load("model_0", model_h.at[0], model.at[0], 0, img, 2)
    load("turned_1", turned_h, turned, taps, img - taps, 2)
    load("model_1", model_h.at[1], model.at[1], 0, img, 2)
    load("table", table_h, table, 0, length, 4)
    loads["rate"] = [pltpu.make_async_copy(rate_h, rate, sems.at[sum(map(len, loads.values()))])]
    loads["rate"][0].start()

    def columns(source, depth, target, waits):
        for ch in range(2):
            for wait in waits[ch]:
                arrived(wait)
            for m in range(0, depth, 256):
                rows = slice(m, m + 256)
                for n in range(0, length, 256):
                    lanes = slice(n, min(n + 256, length))
                    to = slice(ch * length + lanes.start, ch * length + lanes.stop)
                    target[rows, to] = dot(source[ch, rows, :], turned[:depth, lanes]).astype(BF16)

    columns(psf, taps, cols_q, (("psf", "turned_0"), ()))
    load("rest", turned_h, turned, img, length - img, 1)
    load("dirty", dirty_h, dirty, 0, 2, 2)
    columns(model, img, cols_x, (("model_0", "turned_1"), ("model_1",)))

    def spectra(lanes):
        def one(target, source, depth, m):
            target[m : m + tall, lanes] = dot(table[m : m + tall, :depth], source[:, lanes])

        return [
            functools.partial(one, target, source, depth, m)
            for m in range(0, length, tall)
            for target, source, depth in ((spec_q, cols_q, taps), (spec_x, cols_x, img))
        ]

    lane = lax.broadcasted_iota(jnp.int32, (16, 2 * GROUP), 1)
    sign = jnp.where(lane < GROUP, -1.0, 1.0)

    def products(lanes):
        def one(row, at):
            c, s, columns = slice(row, row + 16), slice(row + GROUP, row + GROUP + 16), slice(at, at + 2 * GROUP)

            def parts(value):
                turn = pltpu.roll(value, GROUP, 1)
                return jnp.where(lane < GROUP, value, turn), jnp.where(lane < GROUP, turn, value)

            (c_re, c_im), (s_re, s_im) = parts(spec_x[c, columns]), parts(spec_x[s, columns])
            q_c, q_s = spec_q[c, columns], spec_q[s, columns]
            t_c, t_s = pltpu.roll(q_c, GROUP, 1) * sign, pltpu.roll(q_s, GROUP, 1) * sign
            prod[c, columns] = ((c_re * q_c + c_im * t_c) - (s_re * q_s + s_im * t_s)).astype(BF16)
            prod[s, columns] = ((s_re * q_c + s_im * t_c) + (c_re * q_s + c_im * t_s)).astype(BF16)

        return [
            functools.partial(one, base + row, at)
            for base in range(0, length, 2 * GROUP)
            for row in range(0, GROUP, 16)
            for at in range(lanes.start, lanes.stop, 2 * GROUP)
        ]

    def inverse(lanes):
        def one(m):
            back = turned[shift + m : shift + m + 256, :]
            rows_y[m : m + 256, lanes] = dot(back, prod[:, lanes]).astype(BF16)

        return [functools.partial(one, m) for m in range(0, img, 256)]

    arrived("table")
    arrived("rest")
    for step in spectra(tiles[0]):
        step()
    for t in range(len(tiles)):
        matrix = (inverse(tiles[t - 1]) if t else []) + (spectra(tiles[t + 1]) if t + 1 < len(tiles) else [])
        interleave(products(tiles[t]), matrix)
    for step in inverse(tiles[-1]):
        step()

    arrived("dirty")
    arrived("rate")
    bands, parts, _, band, part = out.shape
    step = 256
    sends = []
    for i in range(img // step):
        rows = slice(i * step, (i + 1) * step)
        where = slice(i * step // band, (i + 1) * step // band)
        for ch in range(2):
            scale = rate[ch] * (4.0 / (length * length))
            inner = rows_y[rows, ch * length : (ch + 1) * length]
            for n in range(0, img, 256):
                lanes = slice(n, n + 256)
                blurred = dot(inner, table[:, shift + n : shift + n + 256])
                stepped = rate[ch] * dirty[ch, rows, lanes].astype(F32) - scale * blurred
                stepped = (model[ch, rows, lanes].astype(F32) + stepped).astype(BF16)
                size = min(part, 256)
                for k in range(0, 256, size):
                    piece = stepped[:, k : k + size].reshape(step // band, band, size)
                    at = (n + k) % part
                    out[where, (n + k) // part, ch, :, at : at + size] = piece
            place = where, slice(None), ch
            sends.append(pltpu.make_async_copy(out.at[place], out_h.at[place], out_sems.at[len(sends)]))
            sends[-1].start()
    for send in sends:
        send.wait()


def mix_kernel(gain, weights, tiles, out_h, w_in_t, swap, normed, hidden, mixed, out, sems):
    channels, band, part = tiles.shape
    groups = channels // band

    depth = channels + band
    w_in_t[...] = weights[: w_in_t.shape[1], :].astype(F32).T.astype(BF16)
    w_out_t = weights[w_in_t.shape[1] :, :]
    place = [lax.broadcasted_iota(jnp.int32, swap.shape, axis) for axis in range(2)]
    swap[...] = jnp.where(place[0] % band * band + place[0] // band == place[1], 1.0, 0.0).astype(BF16)
    normed[:, channels:, :] = jnp.ones((band, band, part), BF16)
    power = jnp.zeros((band, part), F32)
    for c in range(channels):
        v = tiles[c].astype(F32)
        power = power + v * v
    inverse = lax.rsqrt(power * (1.0 / channels) + 1e-06)
    for g in range(groups):
        rows = [
            (tiles[c].astype(F32) * inverse * gain[c : c + 1, :]).astype(BF16)
            for c in range(g * band, (g + 1) * band)
        ]
        swapped = dot(swap[...], jnp.concatenate(rows, axis=0)).astype(BF16)
        normed[:, g * band : (g + 1) * band, :] = swapped.reshape(band, band, part)

    a = math.sqrt(2.0 / math.pi)
    blocks = [slice(n, min(n + 256, part)) for n in range(0, part, 256)]
    for r in range(band):
        for lanes in blocks:
            for h in range(0, hidden.shape[1], 128):
                rows = slice(h, h + 128)
                inner = dot(w_in_t[rows, :depth], normed[r, :, lanes]).astype(BF16)
                bent = inner * (BF16(a) + BF16(a * 0.044715) * (inner * inner))
                hidden[r, rows, lanes] = inner + inner * jnp.tanh(bent)
    for r in range(band):
        for lanes in blocks:
            mixed[r, :, lanes] = (0.5 * dot(w_out_t, hidden[r, :, lanes])).astype(BF16)

    sends = []
    for g in range(groups):
        block = mixed[:, g * band : (g + 1) * band, :].reshape(band * band, part)
        swapped = dot(swap[...], block).astype(BF16)
        where = pl.ds(g * band, band)
        out[where] = swapped.reshape(band, band, part)
        sends.append(pltpu.make_async_copy(out.at[where], out_h.at[where], sems.at[g]))
        sends[-1].start()
    for send in sends:
        send.wait()


def spread_kernel(taps, stepped, mixed, out, rows_0, rows_1, result, sems):
    bands, parts, ch_dev, band, part = stepped.shape
    img = parts * part
    group = 2
    size = group * band
    strips = [slice(n, n + 128) for n in range(0, img, 128)]
    lane = lax.broadcasted_iota(jnp.int32, (size, 128), 1)
    zero = jnp.zeros((len(strips), 8, 128), F32)
    sends = []

    def rows_of(source, start, ch):
        pieces = [source[start : start + group, p, ch].reshape(size, part) for p in range(parts)]
        return jnp.concatenate(pieces, axis=1).astype(F32)

    for ch, padded in ((0, rows_0), (1, rows_1)):
        k = [[taps[i, j, ch : ch + 1, :] for j in range(3)] for i in range(3)]
        padded[:, 0:8, :] = zero
        padded[:, img + 8 : img + 16, :] = zero

        def fill(start):
            x = rows_of(mixed, start, ch)
            for n, lanes in enumerate(strips):
                padded[n, start * band + 8 : start * band + 8 + size, :] = x[:, lanes]

        def finish(start):
            at = start * band
            sums = [[], [], []]
            for n in range(len(strips)):
                x = [padded[n, at + 7 + i : at + 7 + i + size, :] for i in range(3)]
                for j in range(3):
                    sums[j].append(k[0][j] * x[0] + k[1][j] * x[1] + k[2][j] * x[2])
            left = pltpu.roll(jnp.concatenate(sums[0], axis=1), 1, 1)
            right = pltpu.roll(jnp.concatenate(sums[2], axis=1), img - 1, 1)
            base = rows_of(stepped, start, ch)
            for n, lanes in enumerate(strips):
                low, high = left[:, lanes], right[:, lanes]
                if n == 0:
                    low = jnp.where(lane == 0, 0.0, low)
                if n == len(strips) - 1:
                    high = jnp.where(lane == 127, 0.0, high)
                total = base[:, lanes] + (sums[1][n] + (low + high))
                result[ch, at : at + size, lanes] = total.astype(BF16)
            if (at + size) % 64 == 0:
                rows = pl.ds(at + size - 64, 64)
                sends.append(pltpu.make_async_copy(result.at[ch, rows], out.at[ch, rows], sems.at[len(sends)]))
                sends[-1].start()

        fill(0)
        for start in range(0, bands, group):
            if start + group < bands:
                fill(start + group)
            finish(start)
    for send in sends:
        send.wait()


VMEM = pl.BlockSpec(memory_space=pltpu.VMEM)
SMEM = pl.BlockSpec(memory_space=pltpu.SMEM)
HBM = pl.BlockSpec(memory_space=pltpu.HBM)


def params(mib):
    return pltpu.CompilerParams(vmem_limit_bytes=mib * MIB)


def partner_order(n_rows, n_cols):
    side = n_cols // 2
    up = [half * side + k for k in range(side) for half in (0, 1)]
    order = []
    for i in range(n_rows):
        row = i ^ (i >> 1)
        order += [row * n_cols + c for c in (reversed(up) if i % 2 else up)]
    return order


def exchange(blocks, order):
    return lax.all_to_all(
        blocks, "all", split_axis=0, concat_axis=0, axis_index_groups=[order], tiled=True
    )


def layers(w_in, b_in, w_out_t, wide):
    rows = []
    for _ in range(3):
        rows.append(lax.reduce_precision(b_in, 8, 7))
        b_in = b_in - rows[-1]
    zeros = jnp.zeros((wide - w_in.shape[0] - 3, w_in.shape[1]), BF16)
    return jnp.concatenate([w_in, jnp.stack(rows).astype(BF16), zeros, w_out_t], axis=0)


def local(n_rows, n_cols, model, dirty, psf, step_size, gain, w_in, b_in, w_out, kernel):
    ch_dev, img, _ = model.shape
    psf_len = psf.shape[1]
    assert ch_dev == 2
    n_dev = n_rows * n_cols
    order = partner_order(n_rows, n_cols)
    channels = gain.shape[0]
    hidden = b_in.shape[0]
    part = img * img // (n_dev * BAND)
    parts = img // part
    bands = img // BAND
    table, turned = tables(img, psf_len)
    length = table.shape[0]
    wide = -(-(channels + BAND) // 128) * 128
    blocks = (bands, parts, ch_dev, BAND, part)

    stepped = pl.pallas_call(
        conv_kernel,
        out_shape=jax.ShapeDtypeStruct(blocks, BF16),
        in_specs=[HBM] * 6,
        out_specs=HBM,
        scratch_shapes=[
            pltpu.SMEM(step_size.shape, F32),
            pltpu.VMEM(model.shape, BF16),
            pltpu.VMEM(model.shape, BF16),
            pltpu.VMEM(psf.shape, BF16),
            pltpu.VMEM(table.shape, BF16),
            pltpu.VMEM(turned.shape, BF16),
            pltpu.VMEM((img, 2 * length), BF16),
            pltpu.VMEM((psf_len, 2 * length), BF16),
            pltpu.VMEM((length, 2 * length), F32),
            pltpu.VMEM((length, 2 * length), F32),
            pltpu.VMEM((length, 2 * length), BF16),
            pltpu.VMEM((img, 2 * length), BF16),
            pltpu.VMEM(blocks, BF16),
            pltpu.SemaphoreType.DMA((20,)),
            pltpu.SemaphoreType.DMA((img // 128,)),
        ],
        compiler_params=params(58),
        name="conv",
    )(step_size, model, dirty, psf, table, turned)
    stepped, gain, w_in, b_in, w_out, kernel = lax.optimization_barrier(
        (stepped, gain, w_in, b_in, w_out, kernel)
    )

    def ordered(values):
        return jnp.concatenate([values[d * ch_dev : (d + 1) * ch_dev] for d in order], axis=0)

    tiles = exchange(stepped.reshape(n_dev, ch_dev, BAND, part), order).reshape(channels, BAND, part)

    mixed = pl.pallas_call(
        mix_kernel,
        out_shape=jax.ShapeDtypeStruct((channels, BAND, part), BF16),
        in_specs=[VMEM] * 3,
        out_specs=HBM,
        scratch_shapes=[
            pltpu.VMEM((hidden, wide), BF16),
            pltpu.VMEM((BAND * BAND, BAND * BAND), BF16),
            pltpu.VMEM((BAND, channels + BAND, part), BF16),
            pltpu.VMEM((BAND, hidden, part), BF16),
            pltpu.VMEM((BAND, channels, part), BF16),
            pltpu.VMEM((channels, BAND, part), BF16),
            pltpu.SemaphoreType.DMA((channels // BAND,)),
        ],
        compiler_params=params(24),
        name="mix",
    )(
        jnp.broadcast_to(ordered(gain)[:, None], (channels, part)),
        layers(ordered(w_in), b_in, ordered(w_out.T), wide),
        tiles,
    )

    returned = exchange(mixed.reshape(n_dev, ch_dev, BAND, part), order).reshape(blocks)
    position = lax.axis_index("all").astype(jnp.int32) * ch_dev
    taps = lax.dynamic_slice_in_dim(kernel, position, ch_dev, axis=2)
    taps = jnp.broadcast_to(taps[..., None], (3, 3, ch_dev, 128))
    plane = pltpu.VMEM((img // 128, img + 16, 128), F32)

    return pl.pallas_call(
        spread_kernel,
        out_shape=jax.ShapeDtypeStruct((ch_dev, img, img), BF16),
        in_specs=[VMEM] * 3,
        out_specs=HBM,
        scratch_shapes=[
            plane, plane, pltpu.VMEM((ch_dev, img, img), BF16),
            pltpu.SemaphoreType.DMA((ch_dev * img // 64,)),
        ],
        compiler_params=params(24),
        name="spread",
    )(taps, stepped, returned)


def solution(mesh):
    line = Mesh(mesh.devices.reshape(-1), ("all",))
    planes = P("all", None, None)
    return jax.shard_map(
        functools.partial(local, *mesh.devices.shape),
        mesh=line,
        in_specs=(planes, planes, planes, P("all"), P(), P(), P(), P(), P()),
        out_specs=planes,
        check_vma=False,
    )
```

```python
import functools
import math

import jax
import jax.numpy as jnp
import ml_dtypes
import numpy as np
from jax import lax
from jax.experimental import pallas as pl
from jax.experimental.pallas import tpu as pltpu
from jax.sharding import Mesh
from jax.sharding import PartitionSpec as P

BAND = 16
GROUP = 64
MIB = 1024 * 1024
BF16, F32 = jnp.bfloat16, jnp.float32


def tables(img, psf):
    length = img + psf // 2
    half = length // 2
    phase = (2 * np.arange(half)[:, None] + 1) * np.arange(length)[None, :] % (2 * length)
    angle = (phase * (math.pi / length)).reshape(half // GROUP, 1, GROUP, length)
    table = np.concatenate([np.cos(angle), np.sin(angle)], axis=1).reshape(length, length)
    table = table.astype(ml_dtypes.bfloat16)
    return jnp.asarray(table), jnp.asarray(np.ascontiguousarray(table.T))


def dot(a, b):
    return jnp.dot(a, b, preferred_element_type=F32)


def interleave(first, second):
    done = 0
    for i, step in enumerate(first):
        step()
        while done * len(first) < (i + 1) * len(second):
            second[done]()
            done += 1


def conv_kernel(
    rate_h, model_h, dirty_h, psf_h, table_h, turned_h, out_h,
    rate, model, dirty, psf, table, turned, cols_x, cols_q, spec_x, spec_q, prod, rows_y, out, sems, out_sems,
):
    img = model.shape[1]
    taps = psf.shape[1]
    shift = taps // 2
    length = table.shape[1]
    tiles = [slice(n, n + 256) for n in range(0, 2 * length, 256)]
    tall = length // 2
    loads = {}

    def load(name, source, target, start, count, pieces):
        for i in range(pieces):
            rows = pl.ds(start + i * count // pieces, count // pieces)
            copy = pltpu.make_async_copy(source.at[rows], target.at[rows], sems.at[sum(map(len, loads.values()))])
            copy.start()
            loads.setdefault(name, []).append(copy)

    def arrived(name):
        for copy in loads[name]:
            copy.wait()

    load("psf", psf_h.at[0], psf.at[0], 0, taps, 1)
    load("turned_0", turned_h, turned, 0, taps, 4)
    load("psf", psf_h.at[1], psf.at[1], 0, taps, 1)
    load("model_0", model_h.at[0], model.at[0], 0, img, 2)
    load("turned_1", turned_h, turned, taps, img - taps, 2)
    load("model_1", model_h.at[1], model.at[1], 0, img, 2)
    load("table", table_h, table, 0, length, 4)
    loads["rate"] = [pltpu.make_async_copy(rate_h, rate, sems.at[sum(map(len, loads.values()))])]
    loads["rate"][0].start()

    def columns(source, depth, target, waits):
        for ch in range(2):
            for wait in waits[ch]:
                arrived(wait)
            for m in range(0, depth, 256):
                rows = slice(m, m + 256)
                for n in range(0, length, 256):
                    lanes = slice(n, min(n + 256, length))
                    to = slice(ch * length + lanes.start, ch * length + lanes.stop)
                    target[rows, to] = dot(source[ch, rows, :], turned[:depth, lanes]).astype(BF16)

    columns(psf, taps, cols_q, (("psf", "turned_0"), ()))
    load("rest", turned_h, turned, img, length - img, 1)
    load("dirty", dirty_h, dirty, 0, 2, 2)
    columns(model, img, cols_x, (("model_0", "turned_1"), ("model_1",)))

    def spectra(lanes):
        def one(target, source, depth, m):
            target[m : m + tall, lanes] = dot(table[m : m + tall, :depth], source[:, lanes])

        return [
            functools.partial(one, target, source, depth, m)
            for m in range(0, length, tall)
            for target, source, depth in ((spec_q, cols_q, taps), (spec_x, cols_x, img))
        ]

    lane = lax.broadcasted_iota(jnp.int32, (16, 2 * GROUP), 1)
    sign = jnp.where(lane < GROUP, -1.0, 1.0)

    def products(lanes):
        def one(row, at):
            c, s, columns = slice(row, row + 16), slice(row + GROUP, row + GROUP + 16), slice(at, at + 2 * GROUP)

            def parts(value):
                turn = pltpu.roll(value, GROUP, 1)
                return jnp.where(lane < GROUP, value, turn), jnp.where(lane < GROUP, turn, value)

            (c_re, c_im), (s_re, s_im) = parts(spec_x[c, columns]), parts(spec_x[s, columns])
            q_c, q_s = spec_q[c, columns], spec_q[s, columns]
            t_c, t_s = pltpu.roll(q_c, GROUP, 1) * sign, pltpu.roll(q_s, GROUP, 1) * sign
            prod[c, columns] = ((c_re * q_c + c_im * t_c) - (s_re * q_s + s_im * t_s)).astype(BF16)
            prod[s, columns] = ((s_re * q_c + s_im * t_c) + (c_re * q_s + c_im * t_s)).astype(BF16)

        return [
            functools.partial(one, base + row, at)
            for base in range(0, length, 2 * GROUP)
            for row in range(0, GROUP, 16)
            for at in range(lanes.start, lanes.stop, 2 * GROUP)
        ]

    def inverse(lanes):
        def one(m):
            back = turned[shift + m : shift + m + 256, :]
            rows_y[m : m + 256, lanes] = dot(back, prod[:, lanes]).astype(BF16)

        return [functools.partial(one, m) for m in range(0, img, 256)]

    arrived("table")
    arrived("rest")
    for step in spectra(tiles[0]):
        step()
    for t in range(len(tiles)):
        matrix = (inverse(tiles[t - 1]) if t else []) + (spectra(tiles[t + 1]) if t + 1 < len(tiles) else [])
        interleave(products(tiles[t]), matrix)
    for step in inverse(tiles[-1]):
        step()

    arrived("dirty")
    arrived("rate")
    bands, parts, _, band, part = out.shape
    step = 256
    sends = []
    for i in range(img // step):
        rows = slice(i * step, (i + 1) * step)
        where = slice(i * step // band, (i + 1) * step // band)
        for ch in range(2):
            scale = rate[ch] * (4.0 / (length * length))
            inner = rows_y[rows, ch * length : (ch + 1) * length]
            for n in range(0, img, 256):
                lanes = slice(n, n + 256)
                blurred = dot(inner, table[:, shift + n : shift + n + 256])
                stepped = rate[ch] * dirty[ch, rows, lanes].astype(F32) - scale * blurred
                stepped = (model[ch, rows, lanes].astype(F32) + stepped).astype(BF16)
                size = min(part, 256)
                for k in range(0, 256, size):
                    piece = stepped[:, k : k + size].reshape(step // band, band, size)
                    at = (n + k) % part
                    out[where, (n + k) // part, ch, :, at : at + size] = piece
            place = where, slice(None), ch
            sends.append(pltpu.make_async_copy(out.at[place], out_h.at[place], out_sems.at[len(sends)]))
            sends[-1].start()
    for send in sends:
        send.wait()


def mix_kernel(gain, weights, tiles, out_h, w_in_t, swap, normed, hidden, mixed, out, sems):
    channels, band, part = tiles.shape
    groups = channels // band

    depth = channels + band
    blocks = [slice(n, min(n + 256, part)) for n in range(0, part, 256)]
    w_in_t[...] = weights[: w_in_t.shape[1], :].astype(F32).T.astype(BF16)
    w_out_t = weights[w_in_t.shape[1] :, :]
    place = [lax.broadcasted_iota(jnp.int32, swap.shape, axis) for axis in range(2)]
    swap[...] = jnp.where(place[0] % band * band + place[0] // band == place[1], 1.0, 0.0).astype(BF16)
    normed[:, channels:, :] = jnp.ones((band, band, part), BF16)
    power = jnp.zeros((band, part), F32)
    for c in range(channels):
        v = tiles[c].astype(F32)
        power = power + v * v
    inverse = lax.rsqrt(power * (1.0 / channels) + 1e-06)
    for g in range(groups):
        rows = [
            (tiles[c].astype(F32) * inverse * gain[c : c + 1, :]).astype(BF16)
            for c in range(g * band, (g + 1) * band)
        ]
        block = jnp.concatenate(rows, axis=0)
        for lanes in blocks:
            for h in range(0, band, 8):
                swapped = dot(swap[h * band : (h + 8) * band, :], block[:, lanes]).astype(BF16)
                normed[h : h + 8, g * band : (g + 1) * band, lanes] = swapped.reshape(8, band, -1)

    a = math.sqrt(2.0 / math.pi)
    for r in range(band):
        for lanes in blocks:
            for h in range(0, hidden.shape[1], 128):
                rows = slice(h, h + 128)
                inner = dot(w_in_t[rows, :depth], normed[r, :, lanes]).astype(BF16)
                bent = inner * (BF16(a) + BF16(a * 0.044715) * (inner * inner))
                hidden[r, rows, lanes] = inner + inner * jnp.tanh(bent)
    for r in range(band):
        for lanes in blocks:
            mixed[r, :, lanes] = (0.5 * dot(w_out_t, hidden[r, :, lanes])).astype(BF16)

    sends = []
    for g in range(groups):
        block = mixed[:, g * band : (g + 1) * band, :].reshape(band * band, part)
        for lanes in blocks:
            for h in range(0, band, 8):
                swapped = dot(swap[h * band : (h + 8) * band, :], block[:, lanes]).astype(BF16)
                out[g * band + h : g * band + h + 8, :, lanes] = swapped.reshape(8, band, -1)
        where = pl.ds(g * band, band)
        sends.append(pltpu.make_async_copy(out.at[where], out_h.at[where], sems.at[g]))
        sends[-1].start()
    for send in sends:
        send.wait()


def spread_kernel(taps, stepped, mixed, out, rows_0, rows_1, result, sems):
    bands, parts, ch_dev, band, part = stepped.shape
    img = parts * part
    group = 2
    size = group * band
    strips = [slice(n, n + 128) for n in range(0, img, 128)]
    lane = lax.broadcasted_iota(jnp.int32, (size, 128), 1)
    zero = jnp.zeros((len(strips), 8, 128), F32)
    sends = []

    def rows_of(source, start, ch):
        pieces = [source[start : start + group, p, ch].reshape(size, part) for p in range(parts)]
        return jnp.concatenate(pieces, axis=1).astype(F32)

    for ch, padded in ((0, rows_0), (1, rows_1)):
        k = [[taps[i, j, ch : ch + 1, :] for j in range(3)] for i in range(3)]
        padded[:, 0:8, :] = zero
        padded[:, img + 8 : img + 16, :] = zero

        def fill(start):
            x = rows_of(mixed, start, ch)
            for n, lanes in enumerate(strips):
                padded[n, start * band + 8 : start * band + 8 + size, :] = x[:, lanes]

        def finish(start):
            at = start * band
            sums = [[], [], []]
            for n in range(len(strips)):
                x = [padded[n, at + 7 + i : at + 7 + i + size, :] for i in range(3)]
                for j in range(3):
                    sums[j].append(k[0][j] * x[0] + k[1][j] * x[1] + k[2][j] * x[2])
            left = pltpu.roll(jnp.concatenate(sums[0], axis=1), 1, 1)
            right = pltpu.roll(jnp.concatenate(sums[2], axis=1), img - 1, 1)
            base = rows_of(stepped, start, ch)
            for n, lanes in enumerate(strips):
                low, high = left[:, lanes], right[:, lanes]
                if n == 0:
                    low = jnp.where(lane == 0, 0.0, low)
                if n == len(strips) - 1:
                    high = jnp.where(lane == 127, 0.0, high)
                total = base[:, lanes] + (sums[1][n] + (low + high))
                result[ch, at : at + size, lanes] = total.astype(BF16)
            if (at + size) % 64 == 0:
                rows = pl.ds(at + size - 64, 64)
                sends.append(pltpu.make_async_copy(result.at[ch, rows], out.at[ch, rows], sems.at[len(sends)]))
                sends[-1].start()

        fill(0)
        for start in range(0, bands, group):
            if start + group < bands:
                fill(start + group)
            finish(start)
    for send in sends:
        send.wait()


VMEM = pl.BlockSpec(memory_space=pltpu.VMEM)
SMEM = pl.BlockSpec(memory_space=pltpu.SMEM)
HBM = pl.BlockSpec(memory_space=pltpu.HBM)


def params(mib):
    return pltpu.CompilerParams(vmem_limit_bytes=mib * MIB)


def partner_order(n_rows, n_cols):
    side = n_cols // 2
    up = [half * side + k + c for k in range(0, side, 2) for half, c in ((1, 0), (0, 0), (0, 1), (1, 1))]
    return [row * n_cols + c for row in range(n_rows) for c in up]


def exchange(blocks, order):
    return lax.all_to_all(
        blocks, "all", split_axis=0, concat_axis=0, axis_index_groups=[order], tiled=True
    )


def layers(w_in, b_in, w_out_t, wide):
    rows = []
    for _ in range(3):
        rows.append(lax.reduce_precision(b_in, 8, 7))
        b_in = b_in - rows[-1]
    zeros = jnp.zeros((wide - w_in.shape[0] - 3, w_in.shape[1]), BF16)
    return jnp.concatenate([w_in, jnp.stack(rows).astype(BF16), zeros, w_out_t], axis=0)


def local(n_rows, n_cols, model, dirty, psf, step_size, gain, w_in, b_in, w_out, kernel):
    ch_dev, img, _ = model.shape
    psf_len = psf.shape[1]
    assert ch_dev == 2
    n_dev = n_rows * n_cols
    order = partner_order(n_rows, n_cols)
    channels = gain.shape[0]
    hidden = b_in.shape[0]
    part = img * img // (n_dev * BAND)
    parts = img // part
    bands = img // BAND
    table, turned = tables(img, psf_len)
    length = table.shape[0]
    wide = -(-(channels + BAND) // 128) * 128
    blocks = (bands, parts, ch_dev, BAND, part)

    stepped = pl.pallas_call(
        conv_kernel,
        out_shape=jax.ShapeDtypeStruct(blocks, BF16),
        in_specs=[HBM] * 6,
        out_specs=HBM,
        scratch_shapes=[
            pltpu.SMEM(step_size.shape, F32),
            pltpu.VMEM(model.shape, BF16),
            pltpu.VMEM(model.shape, BF16),
            pltpu.VMEM(psf.shape, BF16),
            pltpu.VMEM(table.shape, BF16),
            pltpu.VMEM(turned.shape, BF16),
            pltpu.VMEM((img, 2 * length), BF16),
            pltpu.VMEM((psf_len, 2 * length), BF16),
            pltpu.VMEM((length, 2 * length), F32),
            pltpu.VMEM((length, 2 * length), F32),
            pltpu.VMEM((length, 2 * length), BF16),
            pltpu.VMEM((img, 2 * length), BF16),
            pltpu.VMEM(blocks, BF16),
            pltpu.SemaphoreType.DMA((20,)),
            pltpu.SemaphoreType.DMA((img // 128,)),
        ],
        compiler_params=params(58),
        name="conv",
    )(step_size, model, dirty, psf, table, turned)
    stepped, gain, w_in, b_in, w_out, kernel = lax.optimization_barrier(
        (stepped, gain, w_in, b_in, w_out, kernel)
    )

    def ordered(values):
        return jnp.concatenate([values[d * ch_dev : (d + 1) * ch_dev] for d in order], axis=0)

    tiles = exchange(stepped.reshape(n_dev, ch_dev, BAND, part), order).reshape(channels, BAND, part)

    mixed = pl.pallas_call(
        mix_kernel,
        out_shape=jax.ShapeDtypeStruct((channels, BAND, part), BF16),
        in_specs=[VMEM] * 3,
        out_specs=HBM,
        scratch_shapes=[
            pltpu.VMEM((hidden, wide), BF16),
            pltpu.VMEM((BAND * BAND, BAND * BAND), BF16),
            pltpu.VMEM((BAND, channels + BAND, part), BF16),
            pltpu.VMEM((BAND, hidden, part), BF16),
            pltpu.VMEM((BAND, channels, part), BF16),
            pltpu.VMEM((channels, BAND, part), BF16),
            pltpu.SemaphoreType.DMA((channels // BAND,)),
        ],
        compiler_params=params(24),
        name="mix",
    )(
        jnp.broadcast_to(ordered(gain)[:, None], (channels, part)),
        layers(ordered(w_in), b_in, ordered(w_out.T), wide),
        tiles,
    )

    returned = exchange(mixed.reshape(n_dev, ch_dev, BAND, part), order).reshape(blocks)
    position = lax.axis_index("all").astype(jnp.int32) * ch_dev
    taps = lax.dynamic_slice_in_dim(kernel, position, ch_dev, axis=2)
    taps = jnp.broadcast_to(taps[..., None], (3, 3, ch_dev, 128))
    plane = pltpu.VMEM((img // 128, img + 16, 128), F32)

    return pl.pallas_call(
        spread_kernel,
        out_shape=jax.ShapeDtypeStruct((ch_dev, img, img), BF16),
        in_specs=[VMEM] * 3,
        out_specs=HBM,
        scratch_shapes=[
            plane, plane, pltpu.VMEM((ch_dev, img, img), BF16),
            pltpu.SemaphoreType.DMA((ch_dev * img // 64,)),
        ],
        compiler_params=params(24),
        name="spread",
    )(taps, stepped, returned)


def solution(mesh):
    line = Mesh(mesh.devices.reshape(-1), ("all",))
    planes = P("all", None, None)
    return jax.shard_map(
        functools.partial(local, *mesh.devices.shape),
        mesh=line,
        in_specs=(planes, planes, planes, P("all"), P(), P(), P(), P(), P()),
        out_specs=planes,
        check_vma=False,
    )
```

```python
import functools
import math

import jax
import jax.numpy as jnp
import ml_dtypes
import numpy as np
from jax import lax
from jax.experimental import pallas as pl
from jax.experimental.pallas import tpu as pltpu
from jax.sharding import Mesh
from jax.sharding import PartitionSpec as P

BAND = 16
GROUP = 64
MIB = 1024 * 1024
BF16, F32 = jnp.bfloat16, jnp.float32


def tables(img, psf):
    length = img + psf // 2
    half = length // 2
    phase = (2 * np.arange(half)[:, None] + 1) * np.arange(length)[None, :] % (2 * length)
    angle = (phase * (math.pi / length)).reshape(half // GROUP, 1, GROUP, length)
    table = np.concatenate([np.cos(angle), np.sin(angle)], axis=1).reshape(length, length)
    table = table.astype(ml_dtypes.bfloat16)
    return jnp.asarray(table), jnp.asarray(np.ascontiguousarray(table.T))


def dot(a, b):
    return jnp.dot(a, b, preferred_element_type=F32)


def interleave(first, second):
    done = 0
    for i, step in enumerate(first):
        step()
        while done * len(first) < (i + 1) * len(second):
            second[done]()
            done += 1


def conv_kernel(
    rate_h, model_h, dirty_h, psf_h, table_h, turned_h, out_h,
    rate, model, dirty, psf, table, turned, cols_x, cols_q, spec_x, spec_q, prod, rows_y, out, sems, out_sems,
):
    img = model.shape[1]
    taps = psf.shape[1]
    shift = taps // 2
    length = table.shape[1]
    tiles = [slice(n, n + 256) for n in range(0, 2 * length, 256)]
    tall = length // 2
    loads = {}

    def load(name, source, target, start, count, pieces):
        for i in range(pieces):
            rows = pl.ds(start + i * count // pieces, count // pieces)
            copy = pltpu.make_async_copy(source.at[rows], target.at[rows], sems.at[sum(map(len, loads.values()))])
            copy.start()
            loads.setdefault(name, []).append(copy)

    def arrived(name):
        for copy in loads[name]:
            copy.wait()

    load("psf", psf_h.at[0], psf.at[0], 0, taps, 1)
    load("turned_0", turned_h, turned, 0, taps, 4)
    load("psf", psf_h.at[1], psf.at[1], 0, taps, 1)
    load("model_0", model_h.at[0], model.at[0], 0, img, 2)
    load("turned_1", turned_h, turned, taps, img - taps, 2)
    load("model_1", model_h.at[1], model.at[1], 0, img, 2)
    load("table", table_h, table, 0, length, 4)
    loads["rate"] = [pltpu.make_async_copy(rate_h, rate, sems.at[sum(map(len, loads.values()))])]
    loads["rate"][0].start()

    def columns(source, depth, target, waits):
        for ch in range(2):
            for wait in waits[ch]:
                arrived(wait)
            for m in range(0, depth, 256):
                rows = slice(m, m + 256)
                for n in range(0, length, 256):
                    lanes = slice(n, min(n + 256, length))
                    to = slice(ch * length + lanes.start, ch * length + lanes.stop)
                    target[rows, to] = dot(source[ch, rows, :], turned[:depth, lanes]).astype(BF16)

    columns(psf, taps, cols_q, (("psf", "turned_0"), ()))
    load("rest", turned_h, turned, img, length - img, 1)
    load("dirty", dirty_h, dirty, 0, 2, 2)
    columns(model, img, cols_x, (("model_0", "turned_1"), ("model_1",)))

    def spectra(lanes):
        def one(target, source, depth, m):
            target[m : m + tall, lanes] = dot(table[m : m + tall, :depth], source[:, lanes])

        return [
            functools.partial(one, target, source, depth, m)
            for m in range(0, length, tall)
            for target, source, depth in ((spec_q, cols_q, taps), (spec_x, cols_x, img))
        ]

    lane = lax.broadcasted_iota(jnp.int32, (16, 2 * GROUP), 1)
    sign = jnp.where(lane < GROUP, -1.0, 1.0)

    def products(lanes):
        def one(row, at):
            c, s, columns = slice(row, row + 16), slice(row + GROUP, row + GROUP + 16), slice(at, at + 2 * GROUP)

            def parts(value):
                turn = pltpu.roll(value, GROUP, 1)
                return jnp.where(lane < GROUP, value, turn), jnp.where(lane < GROUP, turn, value)

            (c_re, c_im), (s_re, s_im) = parts(spec_x[c, columns]), parts(spec_x[s, columns])
            q_c, q_s = spec_q[c, columns], spec_q[s, columns]
            t_c, t_s = pltpu.roll(q_c, GROUP, 1) * sign, pltpu.roll(q_s, GROUP, 1) * sign
            prod[c, columns] = ((c_re * q_c + c_im * t_c) - (s_re * q_s + s_im * t_s)).astype(BF16)
            prod[s, columns] = ((s_re * q_c + s_im * t_c) + (c_re * q_s + c_im * t_s)).astype(BF16)

        return [
            functools.partial(one, base + row, at)
            for base in range(0, length, 2 * GROUP)
            for row in range(0, GROUP, 16)
            for at in range(lanes.start, lanes.stop, 2 * GROUP)
        ]

    def inverse(lanes):
        def one(m):
            back = turned[shift + m : shift + m + 256, :]
            rows_y[m : m + 256, lanes] = dot(back, prod[:, lanes]).astype(BF16)

        return [functools.partial(one, m) for m in range(0, img, 256)]

    arrived("table")
    arrived("rest")
    for step in spectra(tiles[0]):
        step()
    for t in range(len(tiles)):
        matrix = (inverse(tiles[t - 1]) if t else []) + (spectra(tiles[t + 1]) if t + 1 < len(tiles) else [])
        interleave(products(tiles[t]), matrix)
    for step in inverse(tiles[-1]):
        step()

    arrived("dirty")
    arrived("rate")
    bands, parts, _, band, part = out.shape
    step = 256
    sends = []
    for i in range(img // step):
        rows = slice(i * step, (i + 1) * step)
        where = slice(i * step // band, (i + 1) * step // band)
        for ch in range(2):
            scale = rate[ch] * (4.0 / (length * length))
            inner = rows_y[rows, ch * length : (ch + 1) * length]
            for n in range(0, img, 256):
                lanes = slice(n, n + 256)
                blurred = dot(inner, table[:, shift + n : shift + n + 256])
                stepped = rate[ch] * dirty[ch, rows, lanes].astype(F32) - scale * blurred
                stepped = (model[ch, rows, lanes].astype(F32) + stepped).astype(BF16)
                size = min(part, 256)
                for k in range(0, 256, size):
                    piece = stepped[:, k : k + size].reshape(step // band, band, size)
                    at = (n + k) % part
                    out[where, (n + k) // part, ch, :, at : at + size] = piece
            place = where, slice(None), ch
            sends.append(pltpu.make_async_copy(out.at[place], out_h.at[place], out_sems.at[len(sends)]))
            sends[-1].start()
    for send in sends:
        send.wait()


def mix_kernel(gain, weights, tiles, out_h, w_in_t, swap, normed, hidden, mixed, out, sems):
    channels, band, part = tiles.shape
    groups = channels // band

    depth = channels + band
    blocks = [slice(n, min(n + 256, part)) for n in range(0, part, 256)]
    w_in_t[...] = weights[: w_in_t.shape[1], :].astype(F32).T.astype(BF16)
    w_out_t = weights[w_in_t.shape[1] :, :]
    place = [lax.broadcasted_iota(jnp.int32, swap.shape, axis) for axis in range(2)]
    swap[...] = jnp.where(place[0] % band * band + place[0] // band == place[1], 1.0, 0.0).astype(BF16)
    normed[:, channels:, :] = jnp.ones((band, band, part), BF16)
    power = jnp.zeros((band, part), F32)
    for c in range(channels):
        v = tiles[c].astype(F32)
        power = power + v * v
    inverse = lax.rsqrt(power * (1.0 / channels) + 1e-06)
    for g in range(groups):
        rows = [
            (tiles[c].astype(F32) * inverse * gain[c : c + 1, :]).astype(BF16)
            for c in range(g * band, (g + 1) * band)
        ]
        block = jnp.concatenate(rows, axis=0)
        for lanes in blocks:
            for h in range(0, band, 8):
                swapped = dot(swap[h * band : (h + 8) * band, :], block[:, lanes]).astype(BF16)
                normed[h : h + 8, g * band : (g + 1) * band, lanes] = swapped.reshape(8, band, -1)

    a = math.sqrt(2.0 / math.pi)
    for r in range(band):
        for lanes in blocks:
            for h in range(0, hidden.shape[1], 128):
                rows = slice(h, h + 128)
                inner = dot(w_in_t[rows, :depth], normed[r, :, lanes]).astype(BF16)
                bent = inner * (BF16(a) + BF16(a * 0.044715) * (inner * inner))
                hidden[r, rows, lanes] = inner + inner * jnp.tanh(bent)
    for r in range(band):
        for lanes in blocks:
            mixed[r, :, lanes] = (0.5 * dot(w_out_t, hidden[r, :, lanes])).astype(BF16)

    sends = []
    for g in range(groups):
        block = mixed[:, g * band : (g + 1) * band, :].reshape(band * band, part)
        for lanes in blocks:
            for h in range(0, band, 8):
                swapped = dot(swap[h * band : (h + 8) * band, :], block[:, lanes]).astype(BF16)
                out[g * band + h : g * band + h + 8, :, lanes] = swapped.reshape(8, band, -1)
        where = pl.ds(g * band, band)
        sends.append(pltpu.make_async_copy(out.at[where], out_h.at[where], sems.at[g]))
        sends[-1].start()
    for send in sends:
        send.wait()


def spread_kernel(taps, stepped, mixed, out, rows_0, rows_1, result, sems):
    bands, parts, ch_dev, band, part = stepped.shape
    img = parts * part
    group = 2
    size = group * band
    strips = [slice(n, n + 128) for n in range(0, img, 128)]
    lane = lax.broadcasted_iota(jnp.int32, (size, 128), 1)
    zero = jnp.zeros((len(strips), 8, 128), F32)
    sends = []

    def rows_of(source, start, ch):
        pieces = [source[start : start + group, p, ch].reshape(size, part) for p in range(parts)]
        return jnp.concatenate(pieces, axis=1).astype(F32)

    for ch, padded in ((0, rows_0), (1, rows_1)):
        k = [[taps[i, j, ch : ch + 1, :] for j in range(3)] for i in range(3)]
        padded[:, 0:8, :] = zero
        padded[:, img + 8 : img + 16, :] = zero

        def fill(start):
            x = rows_of(mixed, start, ch)
            for n, lanes in enumerate(strips):
                padded[n, start * band + 8 : start * band + 8 + size, :] = x[:, lanes]

        def finish(start):
            at = start * band
            sums = [[], [], []]
            for n in range(len(strips)):
                x = [padded[n, at + 7 + i : at + 7 + i + size, :] for i in range(3)]
                for j in range(3):
                    sums[j].append(k[0][j] * x[0] + k[1][j] * x[1] + k[2][j] * x[2])
            left = pltpu.roll(jnp.concatenate(sums[0], axis=1), 1, 1)
            right = pltpu.roll(jnp.concatenate(sums[2], axis=1), img - 1, 1)
            base = rows_of(stepped, start, ch)
            for n, lanes in enumerate(strips):
                low, high = left[:, lanes], right[:, lanes]
                if n == 0:
                    low = jnp.where(lane == 0, 0.0, low)
                if n == len(strips) - 1:
                    high = jnp.where(lane == 127, 0.0, high)
                total = base[:, lanes] + (sums[1][n] + (low + high))
                result[ch, at : at + size, lanes] = total.astype(BF16)
            if (at + size) % 64 == 0:
                rows = pl.ds(at + size - 64, 64)
                sends.append(pltpu.make_async_copy(result.at[ch, rows], out.at[ch, rows], sems.at[len(sends)]))
                sends[-1].start()

        fill(0)
        for start in range(0, bands, group):
            if start + group < bands:
                fill(start + group)
            finish(start)
    for send in sends:
        send.wait()


VMEM = pl.BlockSpec(memory_space=pltpu.VMEM)
SMEM = pl.BlockSpec(memory_space=pltpu.SMEM)
HBM = pl.BlockSpec(memory_space=pltpu.HBM)


def params(mib):
    return pltpu.CompilerParams(vmem_limit_bytes=mib * MIB)


def partner_order(n_rows, n_cols):
    side = n_cols // 2
    up = [half * side + k for k in range(0, side, 2) for half in (0, 1)]
    order = []
    for core in range(2):
        for i in range(n_rows):
            row = i ^ (i >> 1)
            order += [row * n_cols + c + core for c in (reversed(up) if i % 2 else up)]
    return order


def exchange(blocks, order):
    return lax.all_to_all(
        blocks, "all", split_axis=0, concat_axis=0, axis_index_groups=[order], tiled=True
    )


def layers(w_in, b_in, w_out_t, wide):
    rows = []
    for _ in range(3):
        rows.append(lax.reduce_precision(b_in, 8, 7))
        b_in = b_in - rows[-1]
    zeros = jnp.zeros((wide - w_in.shape[0] - 3, w_in.shape[1]), BF16)
    return jnp.concatenate([w_in, jnp.stack(rows).astype(BF16), zeros, w_out_t], axis=0)


def local(n_rows, n_cols, model, dirty, psf, step_size, gain, w_in, b_in, w_out, kernel):
    ch_dev, img, _ = model.shape
    psf_len = psf.shape[1]
    assert ch_dev == 2
    n_dev = n_rows * n_cols
    order = partner_order(n_rows, n_cols)
    channels = gain.shape[0]
    hidden = b_in.shape[0]
    part = img * img // (n_dev * BAND)
    parts = img // part
    bands = img // BAND
    table, turned = tables(img, psf_len)
    length = table.shape[0]
    wide = -(-(channels + BAND) // 128) * 128
    blocks = (bands, parts, ch_dev, BAND, part)

    stepped = pl.pallas_call(
        conv_kernel,
        out_shape=jax.ShapeDtypeStruct(blocks, BF16),
        in_specs=[HBM] * 6,
        out_specs=HBM,
        scratch_shapes=[
            pltpu.SMEM(step_size.shape, F32),
            pltpu.VMEM(model.shape, BF16),
            pltpu.VMEM(model.shape, BF16),
            pltpu.VMEM(psf.shape, BF16),
            pltpu.VMEM(table.shape, BF16),
            pltpu.VMEM(turned.shape, BF16),
            pltpu.VMEM((img, 2 * length), BF16),
            pltpu.VMEM((psf_len, 2 * length), BF16),
            pltpu.VMEM((length, 2 * length), F32),
            pltpu.VMEM((length, 2 * length), F32),
            pltpu.VMEM((length, 2 * length), BF16),
            pltpu.VMEM((img, 2 * length), BF16),
            pltpu.VMEM(blocks, BF16),
            pltpu.SemaphoreType.DMA((20,)),
            pltpu.SemaphoreType.DMA((img // 128,)),
        ],
        compiler_params=params(58),
        name="conv",
    )(step_size, model, dirty, psf, table, turned)
    stepped, gain, w_in, b_in, w_out, kernel = lax.optimization_barrier(
        (stepped, gain, w_in, b_in, w_out, kernel)
    )

    def ordered(values):
        return jnp.concatenate([values[d * ch_dev : (d + 1) * ch_dev] for d in order], axis=0)

    tiles = exchange(stepped.reshape(n_dev, ch_dev, BAND, part), order).reshape(channels, BAND, part)

    mixed = pl.pallas_call(
        mix_kernel,
        out_shape=jax.ShapeDtypeStruct((channels, BAND, part), BF16),
        in_specs=[VMEM] * 3,
        out_specs=HBM,
        scratch_shapes=[
            pltpu.VMEM((hidden, wide), BF16),
            pltpu.VMEM((BAND * BAND, BAND * BAND), BF16),
            pltpu.VMEM((BAND, channels + BAND, part), BF16),
            pltpu.VMEM((BAND, hidden, part), BF16),
            pltpu.VMEM((BAND, channels, part), BF16),
            pltpu.VMEM((channels, BAND, part), BF16),
            pltpu.SemaphoreType.DMA((channels // BAND,)),
        ],
        compiler_params=params(24),
        name="mix",
    )(
        jnp.broadcast_to(ordered(gain)[:, None], (channels, part)),
        layers(ordered(w_in), b_in, ordered(w_out.T), wide),
        tiles,
    )

    returned = exchange(mixed.reshape(n_dev, ch_dev, BAND, part), order).reshape(blocks)
    position = lax.axis_index("all").astype(jnp.int32) * ch_dev
    taps = lax.dynamic_slice_in_dim(kernel, position, ch_dev, axis=2)
    taps = jnp.broadcast_to(taps[..., None], (3, 3, ch_dev, 128))
    plane = pltpu.VMEM((img // 128, img + 16, 128), F32)

    return pl.pallas_call(
        spread_kernel,
        out_shape=jax.ShapeDtypeStruct((ch_dev, img, img), BF16),
        in_specs=[VMEM] * 3,
        out_specs=HBM,
        scratch_shapes=[
            plane, plane, pltpu.VMEM((ch_dev, img, img), BF16),
            pltpu.SemaphoreType.DMA((ch_dev * img // 64,)),
        ],
        compiler_params=params(24),
        name="spread",
    )(taps, stepped, returned)


def solution(mesh):
    line = Mesh(mesh.devices.reshape(-1), ("all",))
    planes = P("all", None, None)
    return jax.shard_map(
        functools.partial(local, *mesh.devices.shape),
        mesh=line,
        in_specs=(planes, planes, planes, P("all"), P(), P(), P(), P(), P()),
        out_specs=planes,
        check_vma=False,
    )
```

```python
import functools
import math

import jax
import jax.numpy as jnp
import ml_dtypes
import numpy as np
from jax import lax
from jax.experimental import pallas as pl
from jax.experimental.pallas import tpu as pltpu
from jax.sharding import Mesh
from jax.sharding import PartitionSpec as P

BAND = 16
GROUP = 64
MIB = 1024 * 1024
BF16, F32 = jnp.bfloat16, jnp.float32


def tables(img, psf):
    length = img + psf // 2
    half = length // 2
    phase = (2 * np.arange(half)[:, None] + 1) * np.arange(length)[None, :] % (2 * length)
    angle = (phase * (math.pi / length)).reshape(half // GROUP, 1, GROUP, length)
    table = np.concatenate([np.cos(angle), np.sin(angle)], axis=1).reshape(length, length)
    table = table.astype(ml_dtypes.bfloat16)
    return jnp.asarray(table), jnp.asarray(np.ascontiguousarray(table.T))


def dot(a, b):
    return jnp.dot(a, b, preferred_element_type=F32)


def interleave(first, second):
    done = 0
    for i, step in enumerate(first):
        step()
        while done * len(first) < (i + 1) * len(second):
            second[done]()
            done += 1


def conv_kernel(
    rate_h, model_h, dirty_h, psf_h, table_h, turned_h, out_h,
    rate, model, dirty, psf, table, turned, cols_x, cols_q, spec_x, spec_q, prod, rows_y, out, sems, out_sems,
):
    img = model.shape[1]
    taps = psf.shape[1]
    shift = taps // 2
    length = table.shape[1]
    tiles = [slice(n, n + 256) for n in range(0, 2 * length, 256)]
    tall = length // 2
    loads = {}

    def load(name, source, target, start, count, pieces):
        for i in range(pieces):
            rows = pl.ds(start + i * count // pieces, count // pieces)
            copy = pltpu.make_async_copy(source.at[rows], target.at[rows], sems.at[sum(map(len, loads.values()))])
            copy.start()
            loads.setdefault(name, []).append(copy)

    def arrived(name):
        for copy in loads[name]:
            copy.wait()

    load("psf", psf_h.at[0], psf.at[0], 0, taps, 1)
    load("turned_0", turned_h, turned, 0, taps, 4)
    load("psf", psf_h.at[1], psf.at[1], 0, taps, 1)
    load("model_0", model_h.at[0], model.at[0], 0, img, 2)
    load("turned_1", turned_h, turned, taps, img - taps, 2)
    load("model_1", model_h.at[1], model.at[1], 0, img, 2)
    load("table", table_h, table, 0, length, 4)
    loads["rate"] = [pltpu.make_async_copy(rate_h, rate, sems.at[sum(map(len, loads.values()))])]
    loads["rate"][0].start()

    def columns(source, depth, target, waits):
        for ch in range(2):
            for wait in waits[ch]:
                arrived(wait)
            for m in range(0, depth, 256):
                rows = slice(m, m + 256)
                for n in range(0, length, 256):
                    lanes = slice(n, min(n + 256, length))
                    to = slice(ch * length + lanes.start, ch * length + lanes.stop)
                    target[rows, to] = dot(source[ch, rows, :], turned[:depth, lanes]).astype(BF16)

    columns(psf, taps, cols_q, (("psf", "turned_0"), ()))
    load("rest", turned_h, turned, img, length - img, 1)
    load("dirty", dirty_h, dirty, 0, 2, 2)
    columns(model, img, cols_x, (("model_0", "turned_1"), ("model_1",)))

    def spectra(lanes):
        def one(target, source, depth, m):
            target[m : m + tall, lanes] = dot(table[m : m + tall, :depth], source[:, lanes])

        return [
            functools.partial(one, target, source, depth, m)
            for m in range(0, length, tall)
            for target, source, depth in ((spec_q, cols_q, taps), (spec_x, cols_x, img))
        ]

    lane = lax.broadcasted_iota(jnp.int32, (16, 2 * GROUP), 1)
    sign = jnp.where(lane < GROUP, -1.0, 1.0)

    def products(lanes):
        def one(row, at):
            c, s, columns = slice(row, row + 16), slice(row + GROUP, row + GROUP + 16), slice(at, at + 2 * GROUP)

            def parts(value):
                turn = pltpu.roll(value, GROUP, 1)
                return jnp.where(lane < GROUP, value, turn), jnp.where(lane < GROUP, turn, value)

            (c_re, c_im), (s_re, s_im) = parts(spec_x[c, columns]), parts(spec_x[s, columns])
            q_c, q_s = spec_q[c, columns], spec_q[s, columns]
            t_c, t_s = pltpu.roll(q_c, GROUP, 1) * sign, pltpu.roll(q_s, GROUP, 1) * sign
            prod[c, columns] = ((c_re * q_c + c_im * t_c) - (s_re * q_s + s_im * t_s)).astype(BF16)
            prod[s, columns] = ((s_re * q_c + s_im * t_c) + (c_re * q_s + c_im * t_s)).astype(BF16)

        return [
            functools.partial(one, base + row, at)
            for base in range(0, length, 2 * GROUP)
            for row in range(0, GROUP, 16)
            for at in range(lanes.start, lanes.stop, 2 * GROUP)
        ]

    def inverse(lanes):
        def one(m):
            back = turned[shift + m : shift + m + 256, :]
            rows_y[m : m + 256, lanes] = dot(back, prod[:, lanes]).astype(BF16)

        return [functools.partial(one, m) for m in range(0, img, 256)]

    arrived("table")
    arrived("rest")
    for step in spectra(tiles[0]):
        step()
    for t in range(len(tiles)):
        matrix = (inverse(tiles[t - 1]) if t else []) + (spectra(tiles[t + 1]) if t + 1 < len(tiles) else [])
        interleave(products(tiles[t]), matrix)
    for step in inverse(tiles[-1]):
        step()

    arrived("dirty")
    arrived("rate")
    bands, parts, _, band, part = out.shape
    step = 256
    sends = []
    for i in range(img // step):
        rows = slice(i * step, (i + 1) * step)
        where = slice(i * step // band, (i + 1) * step // band)
        for ch in range(2):
            scale = rate[ch] * (4.0 / (length * length))
            inner = rows_y[rows, ch * length : (ch + 1) * length]
            for n in range(0, img, 256):
                lanes = slice(n, n + 256)
                blurred = dot(inner, table[:, shift + n : shift + n + 256])
                stepped = rate[ch] * dirty[ch, rows, lanes].astype(F32) - scale * blurred
                stepped = (model[ch, rows, lanes].astype(F32) + stepped).astype(BF16)
                size = min(part, 256)
                for k in range(0, 256, size):
                    piece = stepped[:, k : k + size].reshape(step // band, band, size)
                    at = (n + k) % part
                    out[where, (n + k) // part, ch, :, at : at + size] = piece
            place = where, slice(None), ch
            sends.append(pltpu.make_async_copy(out.at[place], out_h.at[place], out_sems.at[len(sends)]))
            sends[-1].start()
    for send in sends:
        send.wait()


def mix_kernel(gain, weights, tiles, out_h, w_in_t, swap, normed, hidden, mixed, out, sems):
    channels, band, part = tiles.shape
    groups = channels // band

    depth = channels + band
    blocks = [slice(n, min(n + 256, part)) for n in range(0, part, 256)]
    w_in_t[...] = weights[: w_in_t.shape[1], :].astype(F32).T.astype(BF16)
    w_out_t = weights[w_in_t.shape[1] :, :]
    place = [lax.broadcasted_iota(jnp.int32, swap.shape, axis) for axis in range(2)]
    swap[...] = jnp.where(place[0] % band * band + place[0] // band == place[1], 1.0, 0.0).astype(BF16)
    normed[:, channels:, :] = jnp.ones((band, band, part), BF16)
    power = jnp.zeros((band, part), F32)
    for c in range(channels):
        v = tiles[c].astype(F32)
        power = power + v * v
    inverse = lax.rsqrt(power * (1.0 / channels) + 1e-06)
    for g in range(groups):
        rows = [
            (tiles[c].astype(F32) * inverse * gain[c : c + 1, :]).astype(BF16)
            for c in range(g * band, (g + 1) * band)
        ]
        block = jnp.concatenate(rows, axis=0)
        for lanes in blocks:
            for h in range(0, band, 8):
                swapped = dot(swap[h * band : (h + 8) * band, :], block[:, lanes]).astype(BF16)
                normed[h : h + 8, g * band : (g + 1) * band, lanes] = swapped.reshape(8, band, -1)

    a = math.sqrt(2.0 / math.pi)
    for r in range(band):
        for lanes in blocks:
            for h in range(0, hidden.shape[1], 128):
                rows = slice(h, h + 128)
                inner = dot(w_in_t[rows, :depth], normed[r, :, lanes]).astype(BF16)
                bent = inner * (BF16(a) + BF16(a * 0.044715) * (inner * inner))
                hidden[r, rows, lanes] = inner + inner * jnp.tanh(bent)
    for r in range(band):
        for lanes in blocks:
            mixed[r, :, lanes] = (0.5 * dot(w_out_t, hidden[r, :, lanes])).astype(BF16)

    sends = []
    for g in range(groups):
        block = mixed[:, g * band : (g + 1) * band, :].reshape(band * band, part)
        for lanes in blocks:
            for h in range(0, band, 8):
                swapped = dot(swap[h * band : (h + 8) * band, :], block[:, lanes]).astype(BF16)
                out[g * band + h : g * band + h + 8, :, lanes] = swapped.reshape(8, band, -1)
        where = pl.ds(g * band, band)
        sends.append(pltpu.make_async_copy(out.at[where], out_h.at[where], sems.at[g]))
        sends[-1].start()
    for send in sends:
        send.wait()


def spread_kernel(taps, stepped, mixed, out, rows_0, rows_1, result, sems):
    bands, parts, ch_dev, band, part = stepped.shape
    img = parts * part
    group = 2
    size = group * band
    strips = [slice(n, n + 128) for n in range(0, img, 128)]
    lane = lax.broadcasted_iota(jnp.int32, (size, 128), 1)
    zero = jnp.zeros((len(strips), 8, 128), F32)
    sends = []

    def rows_of(source, start, ch):
        pieces = [source[start : start + group, p, ch].reshape(size, part) for p in range(parts)]
        return jnp.concatenate(pieces, axis=1).astype(F32)

    for ch, padded in ((0, rows_0), (1, rows_1)):
        k = [[taps[i, j, ch : ch + 1, :] for j in range(3)] for i in range(3)]
        padded[:, 0:8, :] = zero
        padded[:, img + 8 : img + 16, :] = zero

        def fill(start):
            x = rows_of(mixed, start, ch)
            for n, lanes in enumerate(strips):
                padded[n, start * band + 8 : start * band + 8 + size, :] = x[:, lanes]

        def finish(start):
            at = start * band
            sums = [[], [], []]
            for n in range(len(strips)):
                x = [padded[n, at + 7 + i : at + 7 + i + size, :] for i in range(3)]
                for j in range(3):
                    sums[j].append(k[0][j] * x[0] + k[1][j] * x[1] + k[2][j] * x[2])
            left = pltpu.roll(jnp.concatenate(sums[0], axis=1), 1, 1)
            right = pltpu.roll(jnp.concatenate(sums[2], axis=1), img - 1, 1)
            base = rows_of(stepped, start, ch)
            for n, lanes in enumerate(strips):
                low, high = left[:, lanes], right[:, lanes]
                if n == 0:
                    low = jnp.where(lane == 0, 0.0, low)
                if n == len(strips) - 1:
                    high = jnp.where(lane == 127, 0.0, high)
                total = base[:, lanes] + (sums[1][n] + (low + high))
                result[ch, at : at + size, lanes] = total.astype(BF16)
            if (at + size) % 64 == 0:
                rows = pl.ds(at + size - 64, 64)
                sends.append(pltpu.make_async_copy(result.at[ch, rows], out.at[ch, rows], sems.at[len(sends)]))
                sends[-1].start()

        fill(0)
        for start in range(0, bands, group):
            if start + group < bands:
                fill(start + group)
            finish(start)
    for send in sends:
        send.wait()


VMEM = pl.BlockSpec(memory_space=pltpu.VMEM)
SMEM = pl.BlockSpec(memory_space=pltpu.SMEM)
HBM = pl.BlockSpec(memory_space=pltpu.HBM)


def params(mib):
    return pltpu.CompilerParams(vmem_limit_bytes=mib * MIB)


def partner_order(n_rows, n_cols):
    side = n_cols // 2
    down = [half * side + k for k in reversed(range(0, side, 2)) for half in (1, 0)]
    return [(i ^ (i >> 1)) * n_cols + c + core for core in range(2) for i in range(n_rows) for c in down]


def exchange(blocks, order):
    return lax.all_to_all(
        blocks, "all", split_axis=0, concat_axis=0, axis_index_groups=[order], tiled=True
    )


def layers(w_in, b_in, w_out_t, wide):
    rows = []
    for _ in range(3):
        rows.append(lax.reduce_precision(b_in, 8, 7))
        b_in = b_in - rows[-1]
    zeros = jnp.zeros((wide - w_in.shape[0] - 3, w_in.shape[1]), BF16)
    return jnp.concatenate([w_in, jnp.stack(rows).astype(BF16), zeros, w_out_t], axis=0)


def local(n_rows, n_cols, model, dirty, psf, step_size, gain, w_in, b_in, w_out, kernel):
    ch_dev, img, _ = model.shape
    psf_len = psf.shape[1]
    assert ch_dev == 2
    n_dev = n_rows * n_cols
    order = partner_order(n_rows, n_cols)
    channels = gain.shape[0]
    hidden = b_in.shape[0]
    part = img * img // (n_dev * BAND)
    parts = img // part
    bands = img // BAND
    table, turned = tables(img, psf_len)
    length = table.shape[0]
    wide = -(-(channels + BAND) // 128) * 128
    blocks = (bands, parts, ch_dev, BAND, part)

    stepped = pl.pallas_call(
        conv_kernel,
        out_shape=jax.ShapeDtypeStruct(blocks, BF16),
        in_specs=[HBM] * 6,
        out_specs=HBM,
        scratch_shapes=[
            pltpu.SMEM(step_size.shape, F32),
            pltpu.VMEM(model.shape, BF16),
            pltpu.VMEM(model.shape, BF16),
            pltpu.VMEM(psf.shape, BF16),
            pltpu.VMEM(table.shape, BF16),
            pltpu.VMEM(turned.shape, BF16),
            pltpu.VMEM((img, 2 * length), BF16),
            pltpu.VMEM((psf_len, 2 * length), BF16),
            pltpu.VMEM((length, 2 * length), F32),
            pltpu.VMEM((length, 2 * length), F32),
            pltpu.VMEM((length, 2 * length), BF16),
            pltpu.VMEM((img, 2 * length), BF16),
            pltpu.VMEM(blocks, BF16),
            pltpu.SemaphoreType.DMA((20,)),
            pltpu.SemaphoreType.DMA((img // 128,)),
        ],
        compiler_params=params(58),
        name="conv",
    )(step_size, model, dirty, psf, table, turned)
    stepped, gain, w_in, b_in, w_out, kernel = lax.optimization_barrier(
        (stepped, gain, w_in, b_in, w_out, kernel)
    )

    def ordered(values):
        return jnp.concatenate([values[d * ch_dev : (d + 1) * ch_dev] for d in order], axis=0)

    tiles = exchange(stepped.reshape(n_dev, ch_dev, BAND, part), order).reshape(channels, BAND, part)

    mixed = pl.pallas_call(
        mix_kernel,
        out_shape=jax.ShapeDtypeStruct((channels, BAND, part), BF16),
        in_specs=[VMEM] * 3,
        out_specs=HBM,
        scratch_shapes=[
            pltpu.VMEM((hidden, wide), BF16),
            pltpu.VMEM((BAND * BAND, BAND * BAND), BF16),
            pltpu.VMEM((BAND, channels + BAND, part), BF16),
            pltpu.VMEM((BAND, hidden, part), BF16),
            pltpu.VMEM((BAND, channels, part), BF16),
            pltpu.VMEM((channels, BAND, part), BF16),
            pltpu.SemaphoreType.DMA((channels // BAND,)),
        ],
        compiler_params=params(24),
        name="mix",
    )(
        jnp.broadcast_to(ordered(gain)[:, None], (channels, part)),
        layers(ordered(w_in), b_in, ordered(w_out.T), wide),
        tiles,
    )

    returned = exchange(mixed.reshape(n_dev, ch_dev, BAND, part), order).reshape(blocks)
    position = lax.axis_index("all").astype(jnp.int32) * ch_dev
    taps = lax.dynamic_slice_in_dim(kernel, position, ch_dev, axis=2)
    taps = jnp.broadcast_to(taps[..., None], (3, 3, ch_dev, 128))
    plane = pltpu.VMEM((img // 128, img + 16, 128), F32)

    return pl.pallas_call(
        spread_kernel,
        out_shape=jax.ShapeDtypeStruct((ch_dev, img, img), BF16),
        in_specs=[VMEM] * 3,
        out_specs=HBM,
        scratch_shapes=[
            plane, plane, pltpu.VMEM((ch_dev, img, img), BF16),
            pltpu.SemaphoreType.DMA((ch_dev * img // 64,)),
        ],
        compiler_params=params(24),
        name="spread",
    )(taps, stepped, returned)


def solution(mesh):
    line = Mesh(mesh.devices.reshape(-1), ("all",))
    planes = P("all", None, None)
    return jax.shard_map(
        functools.partial(local, *mesh.devices.shape),
        mesh=line,
        in_specs=(planes, planes, planes, P("all"), P(), P(), P(), P(), P()),
        out_specs=planes,
        check_vma=False,
    )
```

```python
import functools
import math

import jax
import jax.numpy as jnp
import ml_dtypes
import numpy as np
from jax import lax
from jax.experimental import pallas as pl
from jax.experimental.pallas import tpu as pltpu
from jax.sharding import Mesh
from jax.sharding import PartitionSpec as P

BAND = 16
GROUP = 64
MIB = 1024 * 1024
BF16, F32 = jnp.bfloat16, jnp.float32


def tables(img, psf):
    length = img + psf // 2
    half = length // 2
    phase = (2 * np.arange(half)[:, None] + 1) * np.arange(length)[None, :] % (2 * length)
    angle = (phase * (math.pi / length)).reshape(half // GROUP, 1, GROUP, length)
    table = np.concatenate([np.cos(angle), np.sin(angle)], axis=1).reshape(length, length)
    table = table.astype(ml_dtypes.bfloat16)
    return jnp.asarray(table), jnp.asarray(np.ascontiguousarray(table.T))


def dot(a, b):
    return jnp.dot(a, b, preferred_element_type=F32)


def interleave(first, second):
    done = 0
    for i, step in enumerate(first):
        step()
        while done * len(first) < (i + 1) * len(second):
            second[done]()
            done += 1


def conv_kernel(
    rate_h, model_h, dirty_h, psf_h, table_h, turned_h, out_h,
    rate, model, dirty, psf, table, turned, cols_x, cols_q, spec_x, spec_q, prod, rows_y, out, sems, out_sems,
):
    img = model.shape[1]
    taps = psf.shape[1]
    shift = taps // 2
    length = table.shape[1]
    tiles = [slice(n, n + 256) for n in range(0, 2 * length, 256)]
    tall = length // 2
    loads = {}

    def load(name, source, target, start, count, pieces):
        for i in range(pieces):
            rows = pl.ds(start + i * count // pieces, count // pieces)
            copy = pltpu.make_async_copy(source.at[rows], target.at[rows], sems.at[sum(map(len, loads.values()))])
            copy.start()
            loads.setdefault(name, []).append(copy)

    def arrived(name):
        for copy in loads[name]:
            copy.wait()

    load("psf", psf_h.at[0], psf.at[0], 0, taps, 1)
    load("turned_0", turned_h, turned, 0, taps, 4)
    load("psf", psf_h.at[1], psf.at[1], 0, taps, 1)
    load("model_0", model_h.at[0], model.at[0], 0, img, 2)
    load("turned_1", turned_h, turned, taps, img - taps, 2)
    load("model_1", model_h.at[1], model.at[1], 0, img, 2)
    load("table", table_h, table, 0, length, 4)
    loads["rate"] = [pltpu.make_async_copy(rate_h, rate, sems.at[sum(map(len, loads.values()))])]
    loads["rate"][0].start()

    def columns(source, depth, target, waits):
        for ch in range(2):
            for wait in waits[ch]:
                arrived(wait)
            for m in range(0, depth, 256):
                rows = slice(m, m + 256)
                for n in range(0, length, 256):
                    lanes = slice(n, min(n + 256, length))
                    to = slice(ch * length + lanes.start, ch * length + lanes.stop)
                    target[rows, to] = dot(source[ch, rows, :], turned[:depth, lanes]).astype(BF16)

    columns(psf, taps, cols_q, (("psf", "turned_0"), ()))
    load("rest", turned_h, turned, img, length - img, 1)
    load("dirty", dirty_h, dirty, 0, 2, 2)
    columns(model, img, cols_x, (("model_0", "turned_1"), ("model_1",)))

    def spectra(lanes):
        def one(target, source, depth, m):
            target[m : m + tall, lanes] = dot(table[m : m + tall, :depth], source[:, lanes])

        return [
            functools.partial(one, target, source, depth, m)
            for m in range(0, length, tall)
            for target, source, depth in ((spec_q, cols_q, taps), (spec_x, cols_x, img))
        ]

    lane = lax.broadcasted_iota(jnp.int32, (16, 2 * GROUP), 1)
    sign = jnp.where(lane < GROUP, -1.0, 1.0)

    def products(lanes):
        def one(row, at):
            c, s, columns = slice(row, row + 16), slice(row + GROUP, row + GROUP + 16), slice(at, at + 2 * GROUP)

            def parts(value):
                turn = pltpu.roll(value, GROUP, 1)
                return jnp.where(lane < GROUP, value, turn), jnp.where(lane < GROUP, turn, value)

            (c_re, c_im), (s_re, s_im) = parts(spec_x[c, columns]), parts(spec_x[s, columns])
            q_c, q_s = spec_q[c, columns], spec_q[s, columns]
            t_c, t_s = pltpu.roll(q_c, GROUP, 1) * sign, pltpu.roll(q_s, GROUP, 1) * sign
            prod[c, columns] = ((c_re * q_c + c_im * t_c) - (s_re * q_s + s_im * t_s)).astype(BF16)
            prod[s, columns] = ((s_re * q_c + s_im * t_c) + (c_re * q_s + c_im * t_s)).astype(BF16)

        return [
            functools.partial(one, base + row, at)
            for base in range(0, length, 2 * GROUP)
            for row in range(0, GROUP, 16)
            for at in range(lanes.start, lanes.stop, 2 * GROUP)
        ]

    def inverse(lanes):
        def one(m):
            back = turned[shift + m : shift + m + 256, :]
            rows_y[m : m + 256, lanes] = dot(back, prod[:, lanes]).astype(BF16)

        return [functools.partial(one, m) for m in range(0, img, 256)]

    arrived("table")
    arrived("rest")
    for step in spectra(tiles[0]):
        step()
    for t in range(len(tiles)):
        matrix = (inverse(tiles[t - 1]) if t else []) + (spectra(tiles[t + 1]) if t + 1 < len(tiles) else [])
        interleave(products(tiles[t]), matrix)
    for step in inverse(tiles[-1]):
        step()

    arrived("dirty")
    arrived("rate")
    bands, parts, _, band, part = out.shape
    step = 256
    sends = []
    for i in range(img // step):
        rows = slice(i * step, (i + 1) * step)
        where = slice(i * step // band, (i + 1) * step // band)
        for ch in range(2):
            scale = rate[ch] * (4.0 / (length * length))
            inner = rows_y[rows, ch * length : (ch + 1) * length]
            for n in range(0, img, 256):
                lanes = slice(n, n + 256)
                blurred = dot(inner, table[:, shift + n : shift + n + 256])
                stepped = rate[ch] * dirty[ch, rows, lanes].astype(F32) - scale * blurred
                stepped = (model[ch, rows, lanes].astype(F32) + stepped).astype(BF16)
                size = min(part, 256)
                for k in range(0, 256, size):
                    piece = stepped[:, k : k + size].reshape(step // band, band, size)
                    at = (n + k) % part
                    out[where, (n + k) // part, ch, :, at : at + size] = piece
            place = where, slice(None), ch
            sends.append(pltpu.make_async_copy(out.at[place], out_h.at[place], out_sems.at[len(sends)]))
            sends[-1].start()
    for send in sends:
        send.wait()


def mix_kernel(gain, weights, tiles, out_h, w_in_t, swap, normed, hidden, mixed, out, sems):
    channels, band, part = tiles.shape
    groups = channels // band

    depth = channels + band
    blocks = [slice(n, min(n + 256, part)) for n in range(0, part, 256)]
    w_in_t[...] = weights[: w_in_t.shape[1], :].astype(F32).T.astype(BF16)
    w_out_t = weights[w_in_t.shape[1] :, :]
    place = [lax.broadcasted_iota(jnp.int32, swap.shape, axis) for axis in range(2)]
    swap[...] = jnp.where(place[0] % band * band + place[0] // band == place[1], 1.0, 0.0).astype(BF16)
    normed[:, channels:, :] = jnp.ones((band, band, part), BF16)
    power = jnp.zeros((band, part), F32)
    for c in range(channels):
        v = tiles[c].astype(F32)
        power = power + v * v
    inverse = lax.rsqrt(power * (1.0 / channels) + 1e-06)
    for g in range(groups):
        rows = [
            (tiles[c].astype(F32) * inverse * gain[c : c + 1, :]).astype(BF16)
            for c in range(g * band, (g + 1) * band)
        ]
        block = jnp.concatenate(rows, axis=0)
        for lanes in blocks:
            for h in range(0, band, 8):
                swapped = dot(swap[h * band : (h + 8) * band, :], block[:, lanes]).astype(BF16)
                normed[h : h + 8, g * band : (g + 1) * band, lanes] = swapped.reshape(8, band, -1)

    a = math.sqrt(2.0 / math.pi)
    for r in range(band):
        for lanes in blocks:
            for h in range(0, hidden.shape[1], 128):
                rows = slice(h, h + 128)
                inner = dot(w_in_t[rows, :depth], normed[r, :, lanes]).astype(BF16)
                bent = inner * (BF16(a) + BF16(a * 0.044715) * (inner * inner))
                hidden[r, rows, lanes] = inner + inner * jnp.tanh(bent)
    for r in range(band):
        for lanes in blocks:
            mixed[r, :, lanes] = (0.5 * dot(w_out_t, hidden[r, :, lanes])).astype(BF16)

    sends = []
    for g in range(groups):
        block = mixed[:, g * band : (g + 1) * band, :].reshape(band * band, part)
        for lanes in blocks:
            for h in range(0, band, 8):
                swapped = dot(swap[h * band : (h + 8) * band, :], block[:, lanes]).astype(BF16)
                out[g * band + h : g * band + h + 8, :, lanes] = swapped.reshape(8, band, -1)
        where = pl.ds(g * band, band)
        sends.append(pltpu.make_async_copy(out.at[where], out_h.at[where], sems.at[g]))
        sends[-1].start()
    for send in sends:
        send.wait()


def spread_kernel(place_of, taps, stepped, mixed, out, rows_0, rows_1, result, sems):
    bands, parts, ch_dev, band, part = stepped.shape
    img = parts * part
    group = 2
    size = group * band
    strips = [slice(n, n + 128) for n in range(0, img, 128)]
    lane = lax.broadcasted_iota(jnp.int32, (size, 128), 1)
    zero = jnp.zeros((len(strips), 8, 128), F32)
    sends = []

    def rows_of(block):
        columns = [jnp.concatenate([block(b, p) for b in range(group)], axis=0) for p in range(parts)]
        return jnp.concatenate(columns, axis=1).astype(F32)

    for ch, padded in ((0, rows_0), (1, rows_1)):
        k = [[taps[i, j, ch : ch + 1, :] for j in range(3)] for i in range(3)]
        padded[:, 0:8, :] = zero
        padded[:, img + 8 : img + 16, :] = zero

        def fill(start):
            x = rows_of(lambda b, p: mixed[place_of[(start + b) * parts + p], ch])
            for n, lanes in enumerate(strips):
                padded[n, start * band + 8 : start * band + 8 + size, :] = x[:, lanes]

        def finish(start):
            at = start * band
            sums = [[], [], []]
            for n in range(len(strips)):
                x = [padded[n, at + 7 + i : at + 7 + i + size, :] for i in range(3)]
                for j in range(3):
                    sums[j].append(k[0][j] * x[0] + k[1][j] * x[1] + k[2][j] * x[2])
            left = pltpu.roll(jnp.concatenate(sums[0], axis=1), 1, 1)
            right = pltpu.roll(jnp.concatenate(sums[2], axis=1), img - 1, 1)
            base = rows_of(lambda b, p: stepped[start + b, p, ch])
            for n, lanes in enumerate(strips):
                low, high = left[:, lanes], right[:, lanes]
                if n == 0:
                    low = jnp.where(lane == 0, 0.0, low)
                if n == len(strips) - 1:
                    high = jnp.where(lane == 127, 0.0, high)
                total = base[:, lanes] + (sums[1][n] + (low + high))
                result[ch, at : at + size, lanes] = total.astype(BF16)
            if (at + size) % 64 == 0:
                rows = pl.ds(at + size - 64, 64)
                sends.append(pltpu.make_async_copy(result.at[ch, rows], out.at[ch, rows], sems.at[len(sends)]))
                sends[-1].start()

        fill(0)
        for start in range(0, bands, group):
            if start + group < bands:
                fill(start + group)
            finish(start)
    for send in sends:
        send.wait()


VMEM = pl.BlockSpec(memory_space=pltpu.VMEM)
SMEM = pl.BlockSpec(memory_space=pltpu.SMEM)
HBM = pl.BlockSpec(memory_space=pltpu.HBM)


def params(mib):
    return pltpu.CompilerParams(vmem_limit_bytes=mib * MIB)


def forth_order(n_rows, n_cols):
    side = n_cols // 2
    up = [half * side + k + c for k in range(0, side, 2) for half, c in ((1, 0), (0, 0), (0, 1), (1, 1))]
    return [row * n_cols + c for row in range(n_rows) for c in up]


def back_order(n_rows, n_cols):
    side = n_cols // 2
    up = [half * side + k for k in range(side) for half in (0, 1)]
    order = []
    for i in range(n_rows):
        order += [(i ^ (i >> 1)) * n_cols + c for c in (reversed(up) if i % 2 else up)]
    return order


def exchange(blocks, order):
    return lax.all_to_all(
        blocks, "all", split_axis=0, concat_axis=0, axis_index_groups=[order], tiled=True
    )


def layers(w_in, b_in, w_out_t, wide):
    rows = []
    for _ in range(3):
        rows.append(lax.reduce_precision(b_in, 8, 7))
        b_in = b_in - rows[-1]
    zeros = jnp.zeros((wide - w_in.shape[0] - 3, w_in.shape[1]), BF16)
    return jnp.concatenate([w_in, jnp.stack(rows).astype(BF16), zeros, w_out_t], axis=0)


def local(n_rows, n_cols, model, dirty, psf, step_size, gain, w_in, b_in, w_out, kernel):
    ch_dev, img, _ = model.shape
    psf_len = psf.shape[1]
    assert ch_dev == 2
    n_dev = n_rows * n_cols
    forth, back = forth_order(n_rows, n_cols), back_order(n_rows, n_cols)
    channels = gain.shape[0]
    hidden = b_in.shape[0]
    part = img * img // (n_dev * BAND)
    parts = img // part
    bands = img // BAND
    table, turned = tables(img, psf_len)
    length = table.shape[0]
    wide = -(-(channels + BAND) // 128) * 128
    blocks = (bands, parts, ch_dev, BAND, part)

    stepped = pl.pallas_call(
        conv_kernel,
        out_shape=jax.ShapeDtypeStruct(blocks, BF16),
        in_specs=[HBM] * 6,
        out_specs=HBM,
        scratch_shapes=[
            pltpu.SMEM(step_size.shape, F32),
            pltpu.VMEM(model.shape, BF16),
            pltpu.VMEM(model.shape, BF16),
            pltpu.VMEM(psf.shape, BF16),
            pltpu.VMEM(table.shape, BF16),
            pltpu.VMEM(turned.shape, BF16),
            pltpu.VMEM((img, 2 * length), BF16),
            pltpu.VMEM((psf_len, 2 * length), BF16),
            pltpu.VMEM((length, 2 * length), F32),
            pltpu.VMEM((length, 2 * length), F32),
            pltpu.VMEM((length, 2 * length), BF16),
            pltpu.VMEM((img, 2 * length), BF16),
            pltpu.VMEM(blocks, BF16),
            pltpu.SemaphoreType.DMA((20,)),
            pltpu.SemaphoreType.DMA((img // 128,)),
        ],
        compiler_params=params(58),
        name="conv",
    )(step_size, model, dirty, psf, table, turned)
    stepped, gain, w_in, b_in, w_out, kernel = lax.optimization_barrier(
        (stepped, gain, w_in, b_in, w_out, kernel)
    )

    def ordered(values, order):
        return jnp.concatenate([values[d * ch_dev : (d + 1) * ch_dev] for d in order], axis=0)

    tiles = exchange(stepped.reshape(n_dev, ch_dev, BAND, part), forth).reshape(channels, BAND, part)

    mixed = pl.pallas_call(
        mix_kernel,
        out_shape=jax.ShapeDtypeStruct((channels, BAND, part), BF16),
        in_specs=[VMEM] * 3,
        out_specs=HBM,
        scratch_shapes=[
            pltpu.VMEM((hidden, wide), BF16),
            pltpu.VMEM((BAND * BAND, BAND * BAND), BF16),
            pltpu.VMEM((BAND, channels + BAND, part), BF16),
            pltpu.VMEM((BAND, hidden, part), BF16),
            pltpu.VMEM((BAND, channels, part), BF16),
            pltpu.VMEM((channels, BAND, part), BF16),
            pltpu.SemaphoreType.DMA((channels // BAND,)),
        ],
        compiler_params=params(24),
        name="mix",
    )(
        jnp.broadcast_to(ordered(gain, forth)[:, None], (channels, part)),
        layers(ordered(w_in, forth), b_in, ordered(w_out.T, back), wide),
        tiles,
    )

    returned = exchange(mixed.reshape(n_dev, ch_dev, BAND, part), back)
    position = lax.axis_index("all").astype(jnp.int32) * ch_dev
    taps = lax.dynamic_slice_in_dim(kernel, position, ch_dev, axis=2)
    taps = jnp.broadcast_to(taps[..., None], (3, 3, ch_dev, 128))
    plane = pltpu.VMEM((img // 128, img + 16, 128), F32)

    return pl.pallas_call(
        functools.partial(spread_kernel, [back.index(device) for device in forth]),
        out_shape=jax.ShapeDtypeStruct((ch_dev, img, img), BF16),
        in_specs=[VMEM] * 3,
        out_specs=HBM,
        scratch_shapes=[
            plane, plane, pltpu.VMEM((ch_dev, img, img), BF16),
            pltpu.SemaphoreType.DMA((ch_dev * img // 64,)),
        ],
        compiler_params=params(24),
        name="spread",
    )(taps, stepped, returned)


def solution(mesh):
    line = Mesh(mesh.devices.reshape(-1), ("all",))
    planes = P("all", None, None)
    return jax.shard_map(
        functools.partial(local, *mesh.devices.shape),
        mesh=line,
        in_specs=(planes, planes, planes, P("all"), P(), P(), P(), P(), P()),
        out_specs=planes,
        check_vma=False,
    )
```

```python
import functools
import math

import jax
import jax.numpy as jnp
import ml_dtypes
import numpy as np
from jax import lax
from jax.experimental import pallas as pl
from jax.experimental.pallas import tpu as pltpu
from jax.sharding import Mesh
from jax.sharding import PartitionSpec as P

BAND = 16
GROUP = 64
MIB = 1024 * 1024
BF16, F32 = jnp.bfloat16, jnp.float32


def tables(img, psf):
    length = img + psf // 2
    half = length // 2
    phase = (2 * np.arange(half)[:, None] + 1) * np.arange(length)[None, :] % (2 * length)
    angle = (phase * (math.pi / length)).reshape(half // GROUP, 1, GROUP, length)
    table = np.concatenate([np.cos(angle), np.sin(angle)], axis=1).reshape(length, length)
    table = table.astype(ml_dtypes.bfloat16)
    return jnp.asarray(table), jnp.asarray(np.ascontiguousarray(table.T))


def dot(a, b):
    return jnp.dot(a, b, preferred_element_type=F32)


def interleave(first, second):
    done = 0
    for i, step in enumerate(first):
        step()
        while done * len(first) < (i + 1) * len(second):
            second[done]()
            done += 1


def conv_kernel(
    rate_h, model_h, dirty_h, psf_h, table_h, turned_h, out_h,
    rate, model, dirty, psf, table, turned, cols_x, cols_q, spec_x, spec_q, prod, rows_y, out, sems, out_sems,
):
    img = model.shape[1]
    taps = psf.shape[1]
    shift = taps // 2
    length = table.shape[1]
    tiles = [slice(n, n + 256) for n in range(0, 2 * length, 256)]
    tall = length // 2
    loads = {}

    def load(name, source, target, start, count, pieces):
        for i in range(pieces):
            rows = pl.ds(start + i * count // pieces, count // pieces)
            copy = pltpu.make_async_copy(source.at[rows], target.at[rows], sems.at[sum(map(len, loads.values()))])
            copy.start()
            loads.setdefault(name, []).append(copy)

    def arrived(name):
        for copy in loads[name]:
            copy.wait()

    load("psf", psf_h.at[0], psf.at[0], 0, taps, 1)
    load("turned_0", turned_h, turned, 0, taps, 4)
    load("psf", psf_h.at[1], psf.at[1], 0, taps, 1)
    load("model_0", model_h.at[0], model.at[0], 0, img, 2)
    load("turned_1", turned_h, turned, taps, img - taps, 2)
    load("model_1", model_h.at[1], model.at[1], 0, img, 2)
    load("table", table_h, table, 0, length, 4)
    loads["rate"] = [pltpu.make_async_copy(rate_h, rate, sems.at[sum(map(len, loads.values()))])]
    loads["rate"][0].start()

    def columns(source, depth, target, waits):
        for ch in range(2):
            for wait in waits[ch]:
                arrived(wait)
            for m in range(0, depth, 256):
                rows = slice(m, m + 256)
                for n in range(0, length, 256):
                    lanes = slice(n, min(n + 256, length))
                    to = slice(ch * length + lanes.start, ch * length + lanes.stop)
                    target[rows, to] = dot(source[ch, rows, :], turned[:depth, lanes]).astype(BF16)

    columns(psf, taps, cols_q, (("psf", "turned_0"), ()))
    load("rest", turned_h, turned, img, length - img, 1)
    load("dirty", dirty_h, dirty, 0, 2, 2)
    columns(model, img, cols_x, (("model_0", "turned_1"), ("model_1",)))

    def spectra(lanes):
        def one(target, source, depth, m):
            target[m : m + tall, lanes] = dot(table[m : m + tall, :depth], source[:, lanes])

        return [
            functools.partial(one, target, source, depth, m)
            for m in range(0, length, tall)
            for target, source, depth in ((spec_q, cols_q, taps), (spec_x, cols_x, img))
        ]

    lane = lax.broadcasted_iota(jnp.int32, (16, 2 * GROUP), 1)
    sign = jnp.where(lane < GROUP, -1.0, 1.0)

    def products(lanes):
        def one(row, at):
            c, s, columns = slice(row, row + 16), slice(row + GROUP, row + GROUP + 16), slice(at, at + 2 * GROUP)

            def parts(value):
                turn = pltpu.roll(value, GROUP, 1)
                return jnp.where(lane < GROUP, value, turn), jnp.where(lane < GROUP, turn, value)

            (c_re, c_im), (s_re, s_im) = parts(spec_x[c, columns]), parts(spec_x[s, columns])
            q_c, q_s = spec_q[c, columns], spec_q[s, columns]
            t_c, t_s = pltpu.roll(q_c, GROUP, 1) * sign, pltpu.roll(q_s, GROUP, 1) * sign
            prod[c, columns] = ((c_re * q_c + c_im * t_c) - (s_re * q_s + s_im * t_s)).astype(BF16)
            prod[s, columns] = ((s_re * q_c + s_im * t_c) + (c_re * q_s + c_im * t_s)).astype(BF16)

        return [
            functools.partial(one, base + row, at)
            for base in range(0, length, 2 * GROUP)
            for row in range(0, GROUP, 16)
            for at in range(lanes.start, lanes.stop, 2 * GROUP)
        ]

    def inverse(lanes):
        def one(m):
            back = turned[shift + m : shift + m + 256, :]
            rows_y[m : m + 256, lanes] = dot(back, prod[:, lanes]).astype(BF16)

        return [functools.partial(one, m) for m in range(0, img, 256)]

    arrived("table")
    arrived("rest")
    for step in spectra(tiles[0]):
        step()
    for t in range(len(tiles)):
        matrix = (inverse(tiles[t - 1]) if t else []) + (spectra(tiles[t + 1]) if t + 1 < len(tiles) else [])
        interleave(products(tiles[t]), matrix)
    for step in inverse(tiles[-1]):
        step()

    arrived("dirty")
    arrived("rate")
    bands, parts, _, band, part = out.shape
    step = 256
    sends = []
    for i in range(img // step):
        rows = slice(i * step, (i + 1) * step)
        where = slice(i * step // band, (i + 1) * step // band)
        for ch in range(2):
            scale = rate[ch] * (4.0 / (length * length))
            inner = rows_y[rows, ch * length : (ch + 1) * length]
            for n in range(0, img, 256):
                lanes = slice(n, n + 256)
                blurred = dot(inner, table[:, shift + n : shift + n + 256])
                stepped = rate[ch] * dirty[ch, rows, lanes].astype(F32) - scale * blurred
                stepped = (model[ch, rows, lanes].astype(F32) + stepped).astype(BF16)
                size = min(part, 256)
                for k in range(0, 256, size):
                    piece = stepped[:, k : k + size].reshape(step // band, band, size)
                    at = (n + k) % part
                    out[where, (n + k) // part, ch, :, at : at + size] = piece
            place = where, slice(None), ch
            sends.append(pltpu.make_async_copy(out.at[place], out_h.at[place], out_sems.at[len(sends)]))
            sends[-1].start()
    for send in sends:
        send.wait()


def mix_kernel(gain, weights, tiles, out_h, w_in_t, swap, normed, hidden, mixed, out, sems):
    channels, band, part = tiles.shape
    groups = channels // band

    depth = channels + band
    blocks = [slice(n, min(n + 256, part)) for n in range(0, part, 256)]
    w_in_t[...] = weights[: w_in_t.shape[1], :].astype(F32).T.astype(BF16)
    w_out_t = weights[w_in_t.shape[1] :, :]
    place = [lax.broadcasted_iota(jnp.int32, swap.shape, axis) for axis in range(2)]
    swap[...] = jnp.where(place[0] % band * band + place[0] // band == place[1], 1.0, 0.0).astype(BF16)
    normed[:, channels:, :] = jnp.ones((band, band, part), BF16)
    power = jnp.zeros((band, part), F32)
    for c in range(channels):
        v = tiles[c].astype(F32)
        power = power + v * v
    inverse = lax.rsqrt(power * (1.0 / channels) + 1e-06)
    for g in range(groups):
        rows = [
            (tiles[c].astype(F32) * inverse * gain[c : c + 1, :]).astype(BF16)
            for c in range(g * band, (g + 1) * band)
        ]
        block = jnp.concatenate(rows, axis=0)
        for lanes in blocks:
            for h in range(0, band, 8):
                swapped = dot(swap[h * band : (h + 8) * band, :], block[:, lanes]).astype(BF16)
                normed[h : h + 8, g * band : (g + 1) * band, lanes] = swapped.reshape(8, band, -1)

    a = math.sqrt(2.0 / math.pi)
    for r in range(band):
        for lanes in blocks:
            for h in range(0, hidden.shape[1], 128):
                rows = slice(h, h + 128)
                inner = dot(w_in_t[rows, :depth], normed[r, :, lanes])
                bent = inner * (a + (a * 0.044715) * (inner * inner))
                hidden[r, rows, lanes] = (inner + inner * jnp.tanh(bent)).astype(BF16)
    for r in range(band):
        for lanes in blocks:
            mixed[r, :, lanes] = (0.5 * dot(w_out_t, hidden[r, :, lanes])).astype(BF16)

    sends = []
    for g in range(groups):
        block = mixed[:, g * band : (g + 1) * band, :].reshape(band * band, part)
        for lanes in blocks:
            for h in range(0, band, 8):
                swapped = dot(swap[h * band : (h + 8) * band, :], block[:, lanes]).astype(BF16)
                out[g * band + h : g * band + h + 8, :, lanes] = swapped.reshape(8, band, -1)
        where = pl.ds(g * band, band)
        sends.append(pltpu.make_async_copy(out.at[where], out_h.at[where], sems.at[g]))
        sends[-1].start()
    for send in sends:
        send.wait()


def spread_kernel(place_of, taps, stepped, mixed, out, rows_0, rows_1, result, sems):
    bands, parts, ch_dev, band, part = stepped.shape
    img = parts * part
    group = 2
    size = group * band
    strips = [slice(n, n + 128) for n in range(0, img, 128)]
    lane = lax.broadcasted_iota(jnp.int32, (size, 128), 1)
    zero = jnp.zeros((len(strips), 8, 128), F32)
    sends = []

    def rows_of(block):
        columns = [jnp.concatenate([block(b, p) for b in range(group)], axis=0) for p in range(parts)]
        return jnp.concatenate(columns, axis=1).astype(F32)

    for ch, padded in ((0, rows_0), (1, rows_1)):
        k = [[taps[i, j, ch : ch + 1, :] for j in range(3)] for i in range(3)]
        padded[:, 0:8, :] = zero
        padded[:, img + 8 : img + 16, :] = zero

        def fill(start):
            x = rows_of(lambda b, p: mixed[place_of[(start + b) * parts + p], ch])
            for n, lanes in enumerate(strips):
                padded[n, start * band + 8 : start * band + 8 + size, :] = x[:, lanes]

        def finish(start):
            at = start * band
            sums = [[], [], []]
            for n in range(len(strips)):
                x = [padded[n, at + 7 + i : at + 7 + i + size, :] for i in range(3)]
                for j in range(3):
                    sums[j].append(k[0][j] * x[0] + k[1][j] * x[1] + k[2][j] * x[2])
            left = pltpu.roll(jnp.concatenate(sums[0], axis=1), 1, 1)
            right = pltpu.roll(jnp.concatenate(sums[2], axis=1), img - 1, 1)
            base = rows_of(lambda b, p: stepped[start + b, p, ch])
            for n, lanes in enumerate(strips):
                low, high = left[:, lanes], right[:, lanes]
                if n == 0:
                    low = jnp.where(lane == 0, 0.0, low)
                if n == len(strips) - 1:
                    high = jnp.where(lane == 127, 0.0, high)
                total = base[:, lanes] + (sums[1][n] + (low + high))
                result[ch, at : at + size, lanes] = total.astype(BF16)
            if (at + size) % 64 == 0:
                rows = pl.ds(at + size - 64, 64)
                sends.append(pltpu.make_async_copy(result.at[ch, rows], out.at[ch, rows], sems.at[len(sends)]))
                sends[-1].start()

        fill(0)
        for start in range(0, bands, group):
            if start + group < bands:
                fill(start + group)
            finish(start)
    for send in sends:
        send.wait()


VMEM = pl.BlockSpec(memory_space=pltpu.VMEM)
SMEM = pl.BlockSpec(memory_space=pltpu.SMEM)
HBM = pl.BlockSpec(memory_space=pltpu.HBM)


def params(mib):
    return pltpu.CompilerParams(vmem_limit_bytes=mib * MIB)


def forth_order(n_rows, n_cols):
    side = n_cols // 2
    up = [half * side + k + c for k in range(0, side, 2) for half, c in ((1, 0), (0, 0), (0, 1), (1, 1))]
    return [row * n_cols + c for row in range(n_rows) for c in up]


def back_order(n_rows, n_cols):
    side = n_cols // 2
    up = [half * side + k for k in range(side) for half in (0, 1)]
    order = []
    for i in range(n_rows):
        order += [(i ^ (i >> 1)) * n_cols + c for c in (reversed(up) if i % 2 else up)]
    return order


def exchange(blocks, order):
    return lax.all_to_all(
        blocks, "all", split_axis=0, concat_axis=0, axis_index_groups=[order], tiled=True
    )


def layers(w_in, b_in, w_out_t, wide):
    rows = []
    for _ in range(3):
        rows.append(lax.reduce_precision(b_in, 8, 7))
        b_in = b_in - rows[-1]
    zeros = jnp.zeros((wide - w_in.shape[0] - 3, w_in.shape[1]), BF16)
    return jnp.concatenate([w_in, jnp.stack(rows).astype(BF16), zeros, w_out_t], axis=0)


def local(n_rows, n_cols, model, dirty, psf, step_size, gain, w_in, b_in, w_out, kernel):
    ch_dev, img, _ = model.shape
    psf_len = psf.shape[1]
    assert ch_dev == 2
    n_dev = n_rows * n_cols
    forth, back = forth_order(n_rows, n_cols), back_order(n_rows, n_cols)
    channels = gain.shape[0]
    hidden = b_in.shape[0]
    part = img * img // (n_dev * BAND)
    parts = img // part
    bands = img // BAND
    table, turned = tables(img, psf_len)
    length = table.shape[0]
    wide = -(-(channels + BAND) // 128) * 128
    blocks = (bands, parts, ch_dev, BAND, part)

    stepped = pl.pallas_call(
        conv_kernel,
        out_shape=jax.ShapeDtypeStruct(blocks, BF16),
        in_specs=[HBM] * 6,
        out_specs=HBM,
        scratch_shapes=[
            pltpu.SMEM(step_size.shape, F32),
            pltpu.VMEM(model.shape, BF16),
            pltpu.VMEM(model.shape, BF16),
            pltpu.VMEM(psf.shape, BF16),
            pltpu.VMEM(table.shape, BF16),
            pltpu.VMEM(turned.shape, BF16),
            pltpu.VMEM((img, 2 * length), BF16),
            pltpu.VMEM((psf_len, 2 * length), BF16),
            pltpu.VMEM((length, 2 * length), F32),
            pltpu.VMEM((length, 2 * length), F32),
            pltpu.VMEM((length, 2 * length), BF16),
            pltpu.VMEM((img, 2 * length), BF16),
            pltpu.VMEM(blocks, BF16),
            pltpu.SemaphoreType.DMA((20,)),
            pltpu.SemaphoreType.DMA((img // 128,)),
        ],
        compiler_params=params(58),
        name="conv",
    )(step_size, model, dirty, psf, table, turned)
    stepped, gain, w_in, b_in, w_out, kernel = lax.optimization_barrier(
        (stepped, gain, w_in, b_in, w_out, kernel)
    )

    def ordered(values, order):
        return jnp.concatenate([values[d * ch_dev : (d + 1) * ch_dev] for d in order], axis=0)

    tiles = exchange(stepped.reshape(n_dev, ch_dev, BAND, part), forth).reshape(channels, BAND, part)

    mixed = pl.pallas_call(
        mix_kernel,
        out_shape=jax.ShapeDtypeStruct((channels, BAND, part), BF16),
        in_specs=[VMEM] * 3,
        out_specs=HBM,
        scratch_shapes=[
            pltpu.VMEM((hidden, wide), BF16),
            pltpu.VMEM((BAND * BAND, BAND * BAND), BF16),
            pltpu.VMEM((BAND, channels + BAND, part), BF16),
            pltpu.VMEM((BAND, hidden, part), BF16),
            pltpu.VMEM((BAND, channels, part), BF16),
            pltpu.VMEM((channels, BAND, part), BF16),
            pltpu.SemaphoreType.DMA((channels // BAND,)),
        ],
        compiler_params=params(24),
        name="mix",
    )(
        jnp.broadcast_to(ordered(gain, forth)[:, None], (channels, part)),
        layers(ordered(w_in, forth), b_in, ordered(w_out.T, back), wide),
        tiles,
    )

    returned = exchange(mixed.reshape(n_dev, ch_dev, BAND, part), back)
    position = lax.axis_index("all").astype(jnp.int32) * ch_dev
    taps = lax.dynamic_slice_in_dim(kernel, position, ch_dev, axis=2)
    taps = jnp.broadcast_to(taps[..., None], (3, 3, ch_dev, 128))
    plane = pltpu.VMEM((img // 128, img + 16, 128), F32)

    return pl.pallas_call(
        functools.partial(spread_kernel, [back.index(device) for device in forth]),
        out_shape=jax.ShapeDtypeStruct((ch_dev, img, img), BF16),
        in_specs=[VMEM] * 3,
        out_specs=HBM,
        scratch_shapes=[
            plane, plane, pltpu.VMEM((ch_dev, img, img), BF16),
            pltpu.SemaphoreType.DMA((ch_dev * img // 64,)),
        ],
        compiler_params=params(24),
        name="spread",
    )(taps, stepped, returned)


def solution(mesh):
    line = Mesh(mesh.devices.reshape(-1), ("all",))
    planes = P("all", None, None)
    return jax.shard_map(
        functools.partial(local, *mesh.devices.shape),
        mesh=line,
        in_specs=(planes, planes, planes, P("all"), P(), P(), P(), P(), P()),
        out_specs=planes,
        check_vma=False,
    )
```

```python
import functools
import math

import jax
import jax.numpy as jnp
import ml_dtypes
import numpy as np
from jax import lax
from jax.experimental import pallas as pl
from jax.experimental.pallas import tpu as pltpu
from jax.sharding import Mesh
from jax.sharding import PartitionSpec as P

BAND = 16
GROUP = 64
MIB = 1024 * 1024
BF16, F32 = jnp.bfloat16, jnp.float32


def tables(img, psf):
    length = img + psf // 2
    half = length // 2
    phase = (2 * np.arange(half)[:, None] + 1) * np.arange(length)[None, :] % (2 * length)
    angle = (phase * (math.pi / length)).reshape(half // GROUP, 1, GROUP, length)
    table = np.concatenate([np.cos(angle), np.sin(angle)], axis=1).reshape(length, length)
    table = table.astype(ml_dtypes.bfloat16)
    return jnp.asarray(table), jnp.asarray(np.ascontiguousarray(table.T))


def dot(a, b):
    return jnp.dot(a, b, preferred_element_type=F32)


def interleave(first, second):
    done = 0
    for i, step in enumerate(first):
        step()
        while done * len(first) < (i + 1) * len(second):
            second[done]()
            done += 1


def conv_kernel(
    rate_h, model_h, dirty_h, psf_h, table_h, turned_h, out_h,
    rate, model, dirty, psf, table, turned, cols_x, cols_q, spec_x, spec_q, prod, rows_y, out, sems, out_sems,
):
    img = model.shape[1]
    taps = psf.shape[1]
    shift = taps // 2
    length = table.shape[1]
    tiles = [slice(n, n + 256) for n in range(0, 2 * length, 256)]
    tall = length // 2
    loads = {}

    def load(name, source, target, start, count, pieces):
        for i in range(pieces):
            rows = pl.ds(start + i * count // pieces, count // pieces)
            copy = pltpu.make_async_copy(source.at[rows], target.at[rows], sems.at[sum(map(len, loads.values()))])
            copy.start()
            loads.setdefault(name, []).append(copy)

    def arrived(name):
        for copy in loads[name]:
            copy.wait()

    load("psf", psf_h.at[0], psf.at[0], 0, taps, 1)
    load("turned_0", turned_h, turned, 0, taps, 4)
    load("psf", psf_h.at[1], psf.at[1], 0, taps, 1)
    load("model_0", model_h.at[0], model.at[0], 0, img, 2)
    load("turned_1", turned_h, turned, taps, img - taps, 2)
    load("model_1", model_h.at[1], model.at[1], 0, img, 2)
    load("table", table_h, table, 0, length, 4)
    loads["rate"] = [pltpu.make_async_copy(rate_h, rate, sems.at[sum(map(len, loads.values()))])]
    loads["rate"][0].start()

    def columns(source, depth, target, waits):
        for ch in range(2):
            for wait in waits[ch]:
                arrived(wait)
            for m in range(0, depth, 256):
                rows = slice(m, m + 256)
                for n in range(0, length, 256):
                    lanes = slice(n, min(n + 256, length))
                    to = slice(ch * length + lanes.start, ch * length + lanes.stop)
                    target[rows, to] = dot(source[ch, rows, :], turned[:depth, lanes]).astype(BF16)

    columns(psf, taps, cols_q, (("psf", "turned_0"), ()))
    load("rest", turned_h, turned, img, length - img, 1)
    load("dirty", dirty_h, dirty, 0, 2, 2)
    columns(model, img, cols_x, (("model_0", "turned_1"), ("model_1",)))

    def spectra(lanes):
        def one(target, source, depth, m):
            target[m : m + tall, lanes] = dot(table[m : m + tall, :depth], source[:, lanes])

        return [
            functools.partial(one, target, source, depth, m)
            for m in range(0, length, tall)
            for target, source, depth in ((spec_q, cols_q, taps), (spec_x, cols_x, img))
        ]

    lane = lax.broadcasted_iota(jnp.int32, (16, 2 * GROUP), 1)
    sign = jnp.where(lane < GROUP, -1.0, 1.0)

    def products(lanes):
        def one(row, at):
            c, s, columns = slice(row, row + 16), slice(row + GROUP, row + GROUP + 16), slice(at, at + 2 * GROUP)

            def parts(value):
                turn = pltpu.roll(value, GROUP, 1)
                return jnp.where(lane < GROUP, value, turn), jnp.where(lane < GROUP, turn, value)

            (c_re, c_im), (s_re, s_im) = parts(spec_x[c, columns]), parts(spec_x[s, columns])
            q_c, q_s = spec_q[c, columns], spec_q[s, columns]
            t_c, t_s = pltpu.roll(q_c, GROUP, 1) * sign, pltpu.roll(q_s, GROUP, 1) * sign
            prod[c, columns] = ((c_re * q_c + c_im * t_c) - (s_re * q_s + s_im * t_s)).astype(BF16)
            prod[s, columns] = ((s_re * q_c + s_im * t_c) + (c_re * q_s + c_im * t_s)).astype(BF16)

        return [
            functools.partial(one, base + row, at)
            for base in range(0, length, 2 * GROUP)
            for row in range(0, GROUP, 16)
            for at in range(lanes.start, lanes.stop, 2 * GROUP)
        ]

    def inverse(lanes):
        def one(m):
            back = turned[shift + m : shift + m + 256, :]
            rows_y[m : m + 256, lanes] = dot(back, prod[:, lanes]).astype(BF16)

        return [functools.partial(one, m) for m in range(0, img, 256)]

    arrived("table")
    arrived("rest")
    for step in spectra(tiles[0]):
        step()
    for t in range(len(tiles)):
        matrix = (inverse(tiles[t - 1]) if t else []) + (spectra(tiles[t + 1]) if t + 1 < len(tiles) else [])
        interleave(products(tiles[t]), matrix)
    for step in inverse(tiles[-1]):
        step()

    arrived("dirty")
    arrived("rate")
    bands, parts, _, band, part = out.shape
    step = 256
    sends = []
    for i in range(img // step):
        rows = slice(i * step, (i + 1) * step)
        where = slice(i * step // band, (i + 1) * step // band)
        for ch in range(2):
            scale = rate[ch] * (4.0 / (length * length))
            inner = rows_y[rows, ch * length : (ch + 1) * length]
            for n in range(0, img, 256):
                lanes = slice(n, n + 256)
                blurred = dot(inner, table[:, shift + n : shift + n + 256])
                stepped = rate[ch] * dirty[ch, rows, lanes].astype(F32) - scale * blurred
                stepped = (model[ch, rows, lanes].astype(F32) + stepped).astype(BF16)
                size = min(part, 256)
                for k in range(0, 256, size):
                    piece = stepped[:, k : k + size].reshape(step // band, band, size)
                    at = (n + k) % part
                    out[where, (n + k) // part, ch, :, at : at + size] = piece
            place = where, slice(None), ch
            sends.append(pltpu.make_async_copy(out.at[place], out_h.at[place], out_sems.at[len(sends)]))
            sends[-1].start()
    for send in sends:
        send.wait()


def mix_kernel(gain, weights, tiles, out_h, w_in_t, swap, normed, hidden, mixed, out, sems):
    channels, band, part = tiles.shape
    groups = channels // band

    depth = channels + band
    blocks = [slice(n, min(n + 256, part)) for n in range(0, part, 256)]
    w_in_t[...] = weights[: w_in_t.shape[1], :].astype(F32).T.astype(BF16)
    w_out_t = weights[w_in_t.shape[1] :, :]
    place = [lax.broadcasted_iota(jnp.int32, swap.shape, axis) for axis in range(2)]
    swap[...] = jnp.where(place[0] % band * band + place[0] // band == place[1], 1.0, 0.0).astype(BF16)
    normed[:, channels:, :] = jnp.ones((band, band, part), BF16)
    power = jnp.zeros((band, part), F32)
    for c in range(channels):
        v = tiles[c].astype(F32)
        power = power + v * v
    inverse = lax.rsqrt(power * (1.0 / channels) + 1e-06)
    for g in range(groups):
        rows = [
            (tiles[c].astype(F32) * inverse * gain[c : c + 1, :]).astype(BF16)
            for c in range(g * band, (g + 1) * band)
        ]
        block = jnp.concatenate(rows, axis=0)
        for lanes in blocks:
            for h in range(0, band, 8):
                swapped = dot(swap[h * band : (h + 8) * band, :], block[:, lanes]).astype(BF16)
                normed[h : h + 8, g * band : (g + 1) * band, lanes] = swapped.reshape(8, band, -1)

    a = math.sqrt(2.0 / math.pi)
    lag = 2
    for r in range(band + lag):
        for lanes in blocks:
            for h in range(0, hidden.shape[1], 128) if r < band else ():
                rows = slice(h, h + 128)
                inner = dot(w_in_t[rows, :depth], normed[r, :, lanes])
                bent = inner * (a + (a * 0.044715) * (inner * inner))
                hidden[r, rows, lanes] = (inner + inner * jnp.tanh(bent)).astype(BF16)
            if r >= lag:
                mixed[r - lag, :, lanes] = (0.5 * dot(w_out_t, hidden[r - lag, :, lanes])).astype(BF16)

    sends = []
    for g in range(groups):
        block = mixed[:, g * band : (g + 1) * band, :].reshape(band * band, part)
        for lanes in blocks:
            for h in range(0, band, 8):
                swapped = dot(swap[h * band : (h + 8) * band, :], block[:, lanes]).astype(BF16)
                out[g * band + h : g * band + h + 8, :, lanes] = swapped.reshape(8, band, -1)
        where = pl.ds(g * band, band)
        sends.append(pltpu.make_async_copy(out.at[where], out_h.at[where], sems.at[g]))
        sends[-1].start()
    for send in sends:
        send.wait()


def spread_kernel(place_of, taps, stepped, mixed, out, rows_0, rows_1, result, sems):
    bands, parts, ch_dev, band, part = stepped.shape
    img = parts * part
    group = 2
    size = group * band
    strips = [slice(n, n + 128) for n in range(0, img, 128)]
    lane = lax.broadcasted_iota(jnp.int32, (size, 128), 1)
    zero = jnp.zeros((len(strips), 8, 128), F32)
    sends = []

    def rows_of(block):
        columns = [jnp.concatenate([block(b, p) for b in range(group)], axis=0) for p in range(parts)]
        return jnp.concatenate(columns, axis=1).astype(F32)

    for ch, padded in ((0, rows_0), (1, rows_1)):
        k = [[taps[i, j, ch : ch + 1, :] for j in range(3)] for i in range(3)]
        padded[:, 0:8, :] = zero
        padded[:, img + 8 : img + 16, :] = zero

        def fill(start):
            x = rows_of(lambda b, p: mixed[place_of[(start + b) * parts + p], ch])
            for n, lanes in enumerate(strips):
                padded[n, start * band + 8 : start * band + 8 + size, :] = x[:, lanes]

        def finish(start):
            at = start * band
            sums = [[], [], []]
            for n in range(len(strips)):
                x = [padded[n, at + 7 + i : at + 7 + i + size, :] for i in range(3)]
                for j in range(3):
                    sums[j].append(k[0][j] * x[0] + k[1][j] * x[1] + k[2][j] * x[2])
            left = pltpu.roll(jnp.concatenate(sums[0], axis=1), 1, 1)
            right = pltpu.roll(jnp.concatenate(sums[2], axis=1), img - 1, 1)
            base = rows_of(lambda b, p: stepped[start + b, p, ch])
            for n, lanes in enumerate(strips):
                low, high = left[:, lanes], right[:, lanes]
                if n == 0:
                    low = jnp.where(lane == 0, 0.0, low)
                if n == len(strips) - 1:
                    high = jnp.where(lane == 127, 0.0, high)
                total = base[:, lanes] + (sums[1][n] + (low + high))
                result[ch, at : at + size, lanes] = total.astype(BF16)
            if (at + size) % 64 == 0:
                rows = pl.ds(at + size - 64, 64)
                sends.append(pltpu.make_async_copy(result.at[ch, rows], out.at[ch, rows], sems.at[len(sends)]))
                sends[-1].start()

        fill(0)
        for start in range(0, bands, group):
            if start + group < bands:
                fill(start + group)
            finish(start)
    for send in sends:
        send.wait()


VMEM = pl.BlockSpec(memory_space=pltpu.VMEM)
SMEM = pl.BlockSpec(memory_space=pltpu.SMEM)
HBM = pl.BlockSpec(memory_space=pltpu.HBM)


def params(mib):
    return pltpu.CompilerParams(vmem_limit_bytes=mib * MIB)


def forth_order(n_rows, n_cols):
    side = n_cols // 2
    up = [half * side + k + c for k in range(0, side, 2) for half, c in ((1, 0), (0, 0), (0, 1), (1, 1))]
    return [row * n_cols + c for row in range(n_rows) for c in up]


def back_order(n_rows, n_cols):
    side = n_cols // 2
    up = [half * side + k for k in range(side) for half in (0, 1)]
    order = []
    for i in range(n_rows):
        order += [(i ^ (i >> 1)) * n_cols + c for c in (reversed(up) if i % 2 else up)]
    return order


def exchange(blocks, order):
    return lax.all_to_all(
        blocks, "all", split_axis=0, concat_axis=0, axis_index_groups=[order], tiled=True
    )


def layers(w_in, b_in, w_out_t, wide):
    rows = []
    for _ in range(3):
        rows.append(lax.reduce_precision(b_in, 8, 7))
        b_in = b_in - rows[-1]
    zeros = jnp.zeros((wide - w_in.shape[0] - 3, w_in.shape[1]), BF16)
    return jnp.concatenate([w_in, jnp.stack(rows).astype(BF16), zeros, w_out_t], axis=0)


def local(n_rows, n_cols, model, dirty, psf, step_size, gain, w_in, b_in, w_out, kernel):
    ch_dev, img, _ = model.shape
    psf_len = psf.shape[1]
    assert ch_dev == 2
    n_dev = n_rows * n_cols
    forth, back = forth_order(n_rows, n_cols), back_order(n_rows, n_cols)
    channels = gain.shape[0]
    hidden = b_in.shape[0]
    part = img * img // (n_dev * BAND)
    parts = img // part
    bands = img // BAND
    table, turned = tables(img, psf_len)
    length = table.shape[0]
    wide = -(-(channels + BAND) // 128) * 128
    blocks = (bands, parts, ch_dev, BAND, part)

    stepped = pl.pallas_call(
        conv_kernel,
        out_shape=jax.ShapeDtypeStruct(blocks, BF16),
        in_specs=[HBM] * 6,
        out_specs=HBM,
        scratch_shapes=[
            pltpu.SMEM(step_size.shape, F32),
            pltpu.VMEM(model.shape, BF16),
            pltpu.VMEM(model.shape, BF16),
            pltpu.VMEM(psf.shape, BF16),
            pltpu.VMEM(table.shape, BF16),
            pltpu.VMEM(turned.shape, BF16),
            pltpu.VMEM((img, 2 * length), BF16),
            pltpu.VMEM((psf_len, 2 * length), BF16),
            pltpu.VMEM((length, 2 * length), F32),
            pltpu.VMEM((length, 2 * length), F32),
            pltpu.VMEM((length, 2 * length), BF16),
            pltpu.VMEM((img, 2 * length), BF16),
            pltpu.VMEM(blocks, BF16),
            pltpu.SemaphoreType.DMA((20,)),
            pltpu.SemaphoreType.DMA((img // 128,)),
        ],
        compiler_params=params(58),
        name="conv",
    )(step_size, model, dirty, psf, table, turned)
    stepped, gain, w_in, b_in, w_out, kernel = lax.optimization_barrier(
        (stepped, gain, w_in, b_in, w_out, kernel)
    )

    def ordered(values, order):
        return jnp.concatenate([values[d * ch_dev : (d + 1) * ch_dev] for d in order], axis=0)

    tiles = exchange(stepped.reshape(n_dev, ch_dev, BAND, part), forth).reshape(channels, BAND, part)

    mixed = pl.pallas_call(
        mix_kernel,
        out_shape=jax.ShapeDtypeStruct((channels, BAND, part), BF16),
        in_specs=[VMEM] * 3,
        out_specs=HBM,
        scratch_shapes=[
            pltpu.VMEM((hidden, wide), BF16),
            pltpu.VMEM((BAND * BAND, BAND * BAND), BF16),
            pltpu.VMEM((BAND, channels + BAND, part), BF16),
            pltpu.VMEM((BAND, hidden, part), BF16),
            pltpu.VMEM((BAND, channels, part), BF16),
            pltpu.VMEM((channels, BAND, part), BF16),
            pltpu.SemaphoreType.DMA((channels // BAND,)),
        ],
        compiler_params=params(24),
        name="mix",
    )(
        jnp.broadcast_to(ordered(gain, forth)[:, None], (channels, part)),
        layers(ordered(w_in, forth), b_in, ordered(w_out.T, back), wide),
        tiles,
    )

    returned = exchange(mixed.reshape(n_dev, ch_dev, BAND, part), back)
    position = lax.axis_index("all").astype(jnp.int32) * ch_dev
    taps = lax.dynamic_slice_in_dim(kernel, position, ch_dev, axis=2)
    taps = jnp.broadcast_to(taps[..., None], (3, 3, ch_dev, 128))
    plane = pltpu.VMEM((img // 128, img + 16, 128), F32)

    return pl.pallas_call(
        functools.partial(spread_kernel, [back.index(device) for device in forth]),
        out_shape=jax.ShapeDtypeStruct((ch_dev, img, img), BF16),
        in_specs=[VMEM] * 3,
        out_specs=HBM,
        scratch_shapes=[
            plane, plane, pltpu.VMEM((ch_dev, img, img), BF16),
            pltpu.SemaphoreType.DMA((ch_dev * img // 64,)),
        ],
        compiler_params=params(24),
        name="spread",
    )(taps, stepped, returned)


def solution(mesh):
    line = Mesh(mesh.devices.reshape(-1), ("all",))
    planes = P("all", None, None)
    return jax.shard_map(
        functools.partial(local, *mesh.devices.shape),
        mesh=line,
        in_specs=(planes, planes, planes, P("all"), P(), P(), P(), P(), P()),
        out_specs=planes,
        check_vma=False,
    )
```

```python
import functools
import math

import jax
import jax.numpy as jnp
import ml_dtypes
import numpy as np
from jax import lax
from jax.experimental import pallas as pl
from jax.experimental.pallas import tpu as pltpu
from jax.sharding import Mesh
from jax.sharding import PartitionSpec as P

BAND = 16
GROUP = 64
MIB = 1024 * 1024
BF16, F32 = jnp.bfloat16, jnp.float32


def tables(img, psf):
    length = img + psf // 2
    half = length // 2
    phase = (2 * np.arange(half)[:, None] + 1) * np.arange(length)[None, :] % (2 * length)
    angle = (phase * (math.pi / length)).reshape(half // GROUP, 1, GROUP, length)
    table = np.concatenate([np.cos(angle), np.sin(angle)], axis=1).reshape(length, length)
    table = table.astype(ml_dtypes.bfloat16)
    return jnp.asarray(table), jnp.asarray(np.ascontiguousarray(table.T))


def dot(a, b):
    return jnp.dot(a, b, preferred_element_type=F32)


def interleave(first, second):
    done = 0
    for i, step in enumerate(first):
        step()
        while done * len(first) < (i + 1) * len(second):
            second[done]()
            done += 1


def conv_kernel(
    rate_h, model_h, dirty_h, psf_h, table_h, turned_h, out_h,
    rate, model, dirty, psf, table, turned, cols_x, cols_q, spec_x, spec_q, prod, rows_y, out, sems, out_sems,
):
    img = model.shape[1]
    taps = psf.shape[1]
    shift = taps // 2
    length = table.shape[1]
    tiles = [slice(n, n + 256) for n in range(0, 2 * length, 256)]
    tall = length // 2
    loads = {}

    def load(name, source, target, start, count, pieces):
        for i in range(pieces):
            rows = pl.ds(start + i * count // pieces, count // pieces)
            copy = pltpu.make_async_copy(source.at[rows], target.at[rows], sems.at[sum(map(len, loads.values()))])
            copy.start()
            loads.setdefault(name, []).append(copy)

    def arrived(name):
        for copy in loads[name]:
            copy.wait()

    load("psf", psf_h.at[0], psf.at[0], 0, taps, 1)
    load("turned_0", turned_h, turned, 0, taps, 4)
    load("psf", psf_h.at[1], psf.at[1], 0, taps, 1)
    load("model_0", model_h.at[0], model.at[0], 0, img, 2)
    load("turned_1", turned_h, turned, taps, img - taps, 2)
    load("model_1", model_h.at[1], model.at[1], 0, img, 2)
    load("table", table_h, table, 0, length, 4)
    loads["rate"] = [pltpu.make_async_copy(rate_h, rate, sems.at[sum(map(len, loads.values()))])]
    loads["rate"][0].start()

    def columns(source, depth, target, waits):
        for ch in range(2):
            for wait in waits[ch]:
                arrived(wait)
            for m in range(0, depth, 256):
                rows = slice(m, m + 256)
                for n in range(0, length, 256):
                    lanes = slice(n, min(n + 256, length))
                    to = slice(ch * length + lanes.start, ch * length + lanes.stop)
                    target[rows, to] = dot(source[ch, rows, :], turned[:depth, lanes]).astype(BF16)

    columns(psf, taps, cols_q, (("psf", "turned_0"), ()))
    load("rest", turned_h, turned, img, length - img, 1)
    load("dirty", dirty_h, dirty, 0, 2, 2)
    columns(model, img, cols_x, (("model_0", "turned_1"), ("model_1",)))

    def spectra(lanes):
        def one(target, source, depth, m):
            target[m : m + tall, lanes] = dot(table[m : m + tall, :depth], source[:, lanes])

        return [
            functools.partial(one, target, source, depth, m)
            for m in range(0, length, tall)
            for target, source, depth in ((spec_q, cols_q, taps), (spec_x, cols_x, img))
        ]

    lane = lax.broadcasted_iota(jnp.int32, (16, 2 * GROUP), 1)
    sign = jnp.where(lane < GROUP, -1.0, 1.0)

    def products(lanes):
        def one(row, at):
            c, s, columns = slice(row, row + 16), slice(row + GROUP, row + GROUP + 16), slice(at, at + 2 * GROUP)

            def parts(value):
                turn = pltpu.roll(value, GROUP, 1)
                return jnp.where(lane < GROUP, value, turn), jnp.where(lane < GROUP, turn, value)

            (c_re, c_im), (s_re, s_im) = parts(spec_x[c, columns]), parts(spec_x[s, columns])
            q_c, q_s = spec_q[c, columns], spec_q[s, columns]
            t_c, t_s = pltpu.roll(q_c, GROUP, 1) * sign, pltpu.roll(q_s, GROUP, 1) * sign
            prod[c, columns] = ((c_re * q_c + c_im * t_c) - (s_re * q_s + s_im * t_s)).astype(BF16)
            prod[s, columns] = ((s_re * q_c + s_im * t_c) + (c_re * q_s + c_im * t_s)).astype(BF16)

        return [
            functools.partial(one, base + row, at)
            for base in range(0, length, 2 * GROUP)
            for row in range(0, GROUP, 16)
            for at in range(lanes.start, lanes.stop, 2 * GROUP)
        ]

    def inverse(lanes):
        def one(m):
            back = turned[shift + m : shift + m + 256, :]
            rows_y[m : m + 256, lanes] = dot(back, prod[:, lanes]).astype(BF16)

        return [functools.partial(one, m) for m in range(0, img, 256)]

    arrived("table")
    arrived("rest")
    for step in spectra(tiles[0]):
        step()
    for t in range(len(tiles)):
        matrix = (inverse(tiles[t - 1]) if t else []) + (spectra(tiles[t + 1]) if t + 1 < len(tiles) else [])
        interleave(products(tiles[t]), matrix)
    for step in inverse(tiles[-1]):
        step()

    arrived("dirty")
    arrived("rate")
    bands, parts, _, band, part = out.shape
    step = 256
    sends = []
    for i in range(img // step):
        rows = slice(i * step, (i + 1) * step)
        where = slice(i * step // band, (i + 1) * step // band)
        for ch in range(2):
            scale = rate[ch] * (4.0 / (length * length))
            inner = rows_y[rows, ch * length : (ch + 1) * length]
            for n in range(0, img, 256):
                lanes = slice(n, n + 256)
                blurred = dot(inner, table[:, shift + n : shift + n + 256])
                stepped = rate[ch] * dirty[ch, rows, lanes].astype(F32) - scale * blurred
                stepped = (model[ch, rows, lanes].astype(F32) + stepped).astype(BF16)
                size = min(part, 256)
                for k in range(0, 256, size):
                    piece = stepped[:, k : k + size].reshape(step // band, band, size)
                    at = (n + k) % part
                    out[where, (n + k) // part, ch, :, at : at + size] = piece
            place = where, slice(None), ch
            sends.append(pltpu.make_async_copy(out.at[place], out_h.at[place], out_sems.at[len(sends)]))
            sends[-1].start()
    for send in sends:
        send.wait()


def mix_kernel(gain, weights, tiles, out_h, w_in_t, swap, normed, hidden, mixed, out, sems):
    channels, band, part = tiles.shape
    groups = channels // band

    depth = channels + band
    blocks = [slice(n, min(n + 256, part)) for n in range(0, part, 256)]
    w_in_t[...] = weights[: w_in_t.shape[1], :].astype(F32).T.astype(BF16)
    w_out_t = weights[w_in_t.shape[1] :, :]
    place = [lax.broadcasted_iota(jnp.int32, swap.shape, axis) for axis in range(2)]
    swap[...] = jnp.where(place[0] % band * band + place[0] // band == place[1], 1.0, 0.0).astype(BF16)
    normed[:, channels:, :] = jnp.ones((band, band, part), BF16)
    power = jnp.zeros((band, part), F32)
    for c in range(channels):
        v = tiles[c].astype(F32)
        power = power + v * v
    inverse = lax.rsqrt(power * (1.0 / channels) + 1e-06)
    for g in range(groups):
        rows = [
            (tiles[c].astype(F32) * inverse * gain[c : c + 1, :]).astype(BF16)
            for c in range(g * band, (g + 1) * band)
        ]
        block = jnp.concatenate(rows, axis=0)
        for lanes in blocks:
            for h in range(0, band, 8):
                swapped = dot(swap[h * band : (h + 8) * band, :], block[:, lanes]).astype(BF16)
                normed[h : h + 8, g * band : (g + 1) * band, lanes] = swapped.reshape(8, band, -1)

    a = math.sqrt(2.0 / math.pi)
    lag = 2
    for r in range(band + lag):
        for lanes in blocks:
            for h in range(0, hidden.shape[1], 128) if r < band else ():
                rows = slice(h, h + 128)
                inner = dot(w_in_t[rows, :depth], normed[r, :, lanes])
                bent = inner * (a + (a * 0.044715) * (inner * inner))
                hidden[r, rows, lanes] = (inner + inner * jnp.tanh(bent)).astype(BF16)
            if r >= lag:
                mixed[r - lag, :, lanes] = (0.5 * dot(w_out_t, hidden[r - lag, :, lanes])).astype(BF16)

    sends = []
    for g in range(groups):
        block = mixed[:, g * band : (g + 1) * band, :].reshape(band * band, part)
        for lanes in blocks:
            for h in range(0, band, 8):
                swapped = dot(swap[h * band : (h + 8) * band, :], block[:, lanes]).astype(BF16)
                out[g * band + h : g * band + h + 8, :, lanes] = swapped.reshape(8, band, -1)
        where = pl.ds(g * band, band)
        sends.append(pltpu.make_async_copy(out.at[where], out_h.at[where], sems.at[g]))
        sends[-1].start()
    for send in sends:
        send.wait()


def spread_kernel(place_of, taps, stepped, mixed, out, rows_0, rows_1, result, sems):
    bands, parts, ch_dev, band, part = stepped.shape
    img = parts * part
    group = 2
    size = group * band
    strips = [slice(n, n + 128) for n in range(0, img, 128)]
    lane = lax.broadcasted_iota(jnp.int32, (size, 128), 1)
    zero = jnp.zeros((len(strips), 8, 128), F32)
    sends = []

    def rows_of(block):
        columns = [jnp.concatenate([block(b, p) for b in range(group)], axis=0) for p in range(parts)]
        return jnp.concatenate(columns, axis=1).astype(F32)

    for ch, padded in ((0, rows_0), (1, rows_1)):
        k = [[taps[i, j, ch : ch + 1, :] for j in range(3)] for i in range(3)]
        padded[:, 0:8, :] = zero
        padded[:, img + 8 : img + 16, :] = zero

        def fill(start):
            x = rows_of(lambda b, p: mixed[place_of[(start + b) * parts + p], ch])
            for n, lanes in enumerate(strips):
                padded[n, start * band + 8 : start * band + 8 + size, :] = x[:, lanes]

        def finish(start):
            at = start * band
            sums = [[], [], []]
            for n in range(len(strips)):
                x = [padded[n, at + 7 + i : at + 7 + i + size, :] for i in range(3)]
                for j in range(3):
                    sums[j].append(k[0][j] * x[0] + k[1][j] * x[1] + k[2][j] * x[2])
            left = pltpu.roll(jnp.concatenate(sums[0], axis=1), 1, 1)
            right = pltpu.roll(jnp.concatenate(sums[2], axis=1), img - 1, 1)
            base = rows_of(lambda b, p: stepped[start + b, p, ch])
            for n, lanes in enumerate(strips):
                low, high = left[:, lanes], right[:, lanes]
                if n == 0:
                    low = jnp.where(lane == 0, 0.0, low)
                if n == len(strips) - 1:
                    high = jnp.where(lane == 127, 0.0, high)
                total = base[:, lanes] + (sums[1][n] + (low + high))
                result[ch, at : at + size, lanes] = total.astype(BF16)
            if (at + size) % 64 == 0:
                rows = pl.ds(at + size - 64, 64)
                sends.append(pltpu.make_async_copy(result.at[ch, rows], out.at[ch, rows], sems.at[len(sends)]))
                sends[-1].start()

        fill(0)
        for start in range(0, bands, group):
            if start + group < bands:
                fill(start + group)
            finish(start)
    for send in sends:
        send.wait()


VMEM = pl.BlockSpec(memory_space=pltpu.VMEM)
SMEM = pl.BlockSpec(memory_space=pltpu.SMEM)
HBM = pl.BlockSpec(memory_space=pltpu.HBM)


def params(mib):
    return pltpu.CompilerParams(vmem_limit_bytes=mib * MIB)


def forth_order(n_rows, n_cols):
    side = n_cols // 2
    up = [half * side + k + c for k in range(0, side, 2) for half, c in ((1, 0), (0, 0), (0, 1), (1, 1))]
    return [row * n_cols + c for row in range(n_rows) for c in up]


def back_order(n_rows, n_cols):
    side = n_cols // 2
    order = []
    for row in range(n_rows):
        shift = 0 if row % 2 else side // 2
        places = [(k + shift) % side for k in range(side)]
        order += [row * n_cols + half * side + k for k in places for half in (1, 0)]
    return order


def exchange(blocks, order):
    return lax.all_to_all(
        blocks, "all", split_axis=0, concat_axis=0, axis_index_groups=[order], tiled=True
    )


def layers(w_in, b_in, w_out_t, wide):
    rows = []
    for _ in range(3):
        rows.append(lax.reduce_precision(b_in, 8, 7))
        b_in = b_in - rows[-1]
    zeros = jnp.zeros((wide - w_in.shape[0] - 3, w_in.shape[1]), BF16)
    return jnp.concatenate([w_in, jnp.stack(rows).astype(BF16), zeros, w_out_t], axis=0)


def local(n_rows, n_cols, model, dirty, psf, step_size, gain, w_in, b_in, w_out, kernel):
    ch_dev, img, _ = model.shape
    psf_len = psf.shape[1]
    assert ch_dev == 2
    n_dev = n_rows * n_cols
    forth, back = forth_order(n_rows, n_cols), back_order(n_rows, n_cols)
    channels = gain.shape[0]
    hidden = b_in.shape[0]
    part = img * img // (n_dev * BAND)
    parts = img // part
    bands = img // BAND
    table, turned = tables(img, psf_len)
    length = table.shape[0]
    wide = -(-(channels + BAND) // 128) * 128
    blocks = (bands, parts, ch_dev, BAND, part)

    stepped = pl.pallas_call(
        conv_kernel,
        out_shape=jax.ShapeDtypeStruct(blocks, BF16),
        in_specs=[HBM] * 6,
        out_specs=HBM,
        scratch_shapes=[
            pltpu.SMEM(step_size.shape, F32),
            pltpu.VMEM(model.shape, BF16),
            pltpu.VMEM(model.shape, BF16),
            pltpu.VMEM(psf.shape, BF16),
            pltpu.VMEM(table.shape, BF16),
            pltpu.VMEM(turned.shape, BF16),
            pltpu.VMEM((img, 2 * length), BF16),
            pltpu.VMEM((psf_len, 2 * length), BF16),
            pltpu.VMEM((length, 2 * length), F32),
            pltpu.VMEM((length, 2 * length), F32),
            pltpu.VMEM((length, 2 * length), BF16),
            pltpu.VMEM((img, 2 * length), BF16),
            pltpu.VMEM(blocks, BF16),
            pltpu.SemaphoreType.DMA((20,)),
            pltpu.SemaphoreType.DMA((img // 128,)),
        ],
        compiler_params=params(58),
        name="conv",
    )(step_size, model, dirty, psf, table, turned)
    stepped, gain, w_in, b_in, w_out, kernel = lax.optimization_barrier(
        (stepped, gain, w_in, b_in, w_out, kernel)
    )

    def ordered(values, order):
        return jnp.concatenate([values[d * ch_dev : (d + 1) * ch_dev] for d in order], axis=0)

    tiles = exchange(stepped.reshape(n_dev, ch_dev, BAND, part), forth).reshape(channels, BAND, part)

    mixed = pl.pallas_call(
        mix_kernel,
        out_shape=jax.ShapeDtypeStruct((channels, BAND, part), BF16),
        in_specs=[VMEM] * 3,
        out_specs=HBM,
        scratch_shapes=[
            pltpu.VMEM((hidden, wide), BF16),
            pltpu.VMEM((BAND * BAND, BAND * BAND), BF16),
            pltpu.VMEM((BAND, channels + BAND, part), BF16),
            pltpu.VMEM((BAND, hidden, part), BF16),
            pltpu.VMEM((BAND, channels, part), BF16),
            pltpu.VMEM((channels, BAND, part), BF16),
            pltpu.SemaphoreType.DMA((channels // BAND,)),
        ],
        compiler_params=params(24),
        name="mix",
    )(
        jnp.broadcast_to(ordered(gain, forth)[:, None], (channels, part)),
        layers(ordered(w_in, forth), b_in, ordered(w_out.T, back), wide),
        tiles,
    )

    returned = exchange(mixed.reshape(n_dev, ch_dev, BAND, part), back)
    position = lax.axis_index("all").astype(jnp.int32) * ch_dev
    taps = lax.dynamic_slice_in_dim(kernel, position, ch_dev, axis=2)
    taps = jnp.broadcast_to(taps[..., None], (3, 3, ch_dev, 128))
    plane = pltpu.VMEM((img // 128, img + 16, 128), F32)

    return pl.pallas_call(
        functools.partial(spread_kernel, [back.index(device) for device in forth]),
        out_shape=jax.ShapeDtypeStruct((ch_dev, img, img), BF16),
        in_specs=[VMEM] * 3,
        out_specs=HBM,
        scratch_shapes=[
            plane, plane, pltpu.VMEM((ch_dev, img, img), BF16),
            pltpu.SemaphoreType.DMA((ch_dev * img // 64,)),
        ],
        compiler_params=params(24),
        name="spread",
    )(taps, stepped, returned)


def solution(mesh):
    line = Mesh(mesh.devices.reshape(-1), ("all",))
    planes = P("all", None, None)
    return jax.shard_map(
        functools.partial(local, *mesh.devices.shape),
        mesh=line,
        in_specs=(planes, planes, planes, P("all"), P(), P(), P(), P(), P()),
        out_specs=planes,
        check_vma=False,
    )
```

```python
import functools
import math

import jax
import jax.numpy as jnp
import ml_dtypes
import numpy as np
from jax import lax
from jax.experimental import pallas as pl
from jax.experimental.pallas import tpu as pltpu
from jax.sharding import Mesh
from jax.sharding import PartitionSpec as P

BAND = 16
GROUP = 64
MIB = 1024 * 1024
BF16, F32 = jnp.bfloat16, jnp.float32


def tables(img, psf):
    length = img + psf // 2
    half = length // 2
    phase = (2 * np.arange(half)[:, None] + 1) * np.arange(length)[None, :] % (2 * length)
    angle = (phase * (math.pi / length)).reshape(half // GROUP, 1, GROUP, length)
    table = np.concatenate([np.cos(angle), np.sin(angle)], axis=1).reshape(length, length)
    table = table.astype(ml_dtypes.bfloat16)
    return jnp.asarray(table), jnp.asarray(np.ascontiguousarray(table.T))


def dot(a, b):
    return jnp.dot(a, b, preferred_element_type=F32)


def interleave(first, second):
    done = 0
    for i, step in enumerate(first):
        step()
        while done * len(first) < (i + 1) * len(second):
            second[done]()
            done += 1


def conv_kernel(
    rate_h, model_h, dirty_h, psf_h, table_h, turned_h, out_h,
    rate, model, dirty, psf, table, turned, cols_x, cols_q, spec_x, spec_q, prod, rows_y, out, sems, out_sems,
):
    img = model.shape[1]
    taps = psf.shape[1]
    shift = taps // 2
    length = table.shape[1]
    tiles = [slice(n, n + 256) for n in range(0, 2 * length, 256)]
    tall = length // 2
    loads = {}

    def load(name, source, target, start, count, pieces):
        for i in range(pieces):
            rows = pl.ds(start + i * count // pieces, count // pieces)
            copy = pltpu.make_async_copy(source.at[rows], target.at[rows], sems.at[sum(map(len, loads.values()))])
            copy.start()
            loads.setdefault(name, []).append(copy)

    def arrived(name):
        for copy in loads[name]:
            copy.wait()

    load("psf", psf_h.at[0], psf.at[0], 0, taps, 1)
    load("turned_0", turned_h, turned, 0, taps, 4)
    load("psf", psf_h.at[1], psf.at[1], 0, taps, 1)
    load("model_0", model_h.at[0], model.at[0], 0, img, 2)
    load("turned_1", turned_h, turned, taps, img - taps, 2)
    load("model_1", model_h.at[1], model.at[1], 0, img, 2)
    load("table", table_h, table, 0, length, 4)
    loads["rate"] = [pltpu.make_async_copy(rate_h, rate, sems.at[sum(map(len, loads.values()))])]
    loads["rate"][0].start()

    def columns(source, depth, target, waits):
        for ch in range(2):
            for wait in waits[ch]:
                arrived(wait)
            for m in range(0, depth, 256):
                rows = slice(m, m + 256)
                for n in range(0, length, 256):
                    lanes = slice(n, min(n + 256, length))
                    to = slice(ch * length + lanes.start, ch * length + lanes.stop)
                    target[rows, to] = dot(source[ch, rows, :], turned[:depth, lanes]).astype(BF16)

    columns(psf, taps, cols_q, (("psf", "turned_0"), ()))
    load("rest", turned_h, turned, img, length - img, 1)
    load("dirty", dirty_h, dirty, 0, 2, 2)
    columns(model, img, cols_x, (("model_0", "turned_1"), ("model_1",)))

    def spectra(lanes):
        def one(target, source, depth, m):
            target[m : m + tall, lanes] = dot(table[m : m + tall, :depth], source[:, lanes])

        return [
            functools.partial(one, target, source, depth, m)
            for m in range(0, length, tall)
            for target, source, depth in ((spec_q, cols_q, taps), (spec_x, cols_x, img))
        ]

    lane = lax.broadcasted_iota(jnp.int32, (16, 2 * GROUP), 1)
    sign = jnp.where(lane < GROUP, -1.0, 1.0)

    def products(lanes):
        def one(row, at):
            c, s, columns = slice(row, row + 16), slice(row + GROUP, row + GROUP + 16), slice(at, at + 2 * GROUP)

            def parts(value):
                turn = pltpu.roll(value, GROUP, 1)
                return jnp.where(lane < GROUP, value, turn), jnp.where(lane < GROUP, turn, value)

            (c_re, c_im), (s_re, s_im) = parts(spec_x[c, columns]), parts(spec_x[s, columns])
            q_c, q_s = spec_q[c, columns], spec_q[s, columns]
            t_c, t_s = pltpu.roll(q_c, GROUP, 1) * sign, pltpu.roll(q_s, GROUP, 1) * sign
            prod[c, columns] = ((c_re * q_c + c_im * t_c) - (s_re * q_s + s_im * t_s)).astype(BF16)
            prod[s, columns] = ((s_re * q_c + s_im * t_c) + (c_re * q_s + c_im * t_s)).astype(BF16)

        return [
            functools.partial(one, base + row, at)
            for base in range(0, length, 2 * GROUP)
            for row in range(0, GROUP, 16)
            for at in range(lanes.start, lanes.stop, 2 * GROUP)
        ]

    def inverse(lanes):
        def one(m):
            back = turned[shift + m : shift + m + 256, :]
            rows_y[m : m + 256, lanes] = dot(back, prod[:, lanes]).astype(BF16)

        return [functools.partial(one, m) for m in range(0, img, 256)]

    arrived("table")
    arrived("rest")
    for step in spectra(tiles[0]):
        step()
    for t in range(len(tiles)):
        matrix = (inverse(tiles[t - 1]) if t else []) + (spectra(tiles[t + 1]) if t + 1 < len(tiles) else [])
        interleave(products(tiles[t]), matrix)
    for step in inverse(tiles[-1]):
        step()

    arrived("dirty")
    arrived("rate")
    bands, parts, _, band, part = out.shape
    step = 256
    sends = []
    for i in range(img // step):
        rows = slice(i * step, (i + 1) * step)
        where = slice(i * step // band, (i + 1) * step // band)
        for ch in range(2):
            scale = rate[ch] * (4.0 / (length * length))
            inner = rows_y[rows, ch * length : (ch + 1) * length]
            for n in range(0, img, 256):
                lanes = slice(n, n + 256)
                blurred = dot(inner, table[:, shift + n : shift + n + 256])
                stepped = rate[ch] * dirty[ch, rows, lanes].astype(F32) - scale * blurred
                stepped = (model[ch, rows, lanes].astype(F32) + stepped).astype(BF16)
                size = min(part, 256)
                for k in range(0, 256, size):
                    piece = stepped[:, k : k + size].reshape(step // band, band, size)
                    at = (n + k) % part
                    out[where, (n + k) // part, ch, :, at : at + size] = piece
            place = where, slice(None), ch
            sends.append(pltpu.make_async_copy(out.at[place], out_h.at[place], out_sems.at[len(sends)]))
            sends[-1].start()
    for send in sends:
        send.wait()


def mix_kernel(gain, weights, tiles, out_h, w_in_t, swap, normed, hidden, mixed, out, sems):
    channels, band, part = tiles.shape
    groups = channels // band

    depth = channels + band
    blocks = [slice(n, min(n + 256, part)) for n in range(0, part, 256)]
    w_in_t[...] = weights[: w_in_t.shape[1], :].astype(F32).T.astype(BF16)
    w_out_t = weights[w_in_t.shape[1] :, :]
    place = [lax.broadcasted_iota(jnp.int32, swap.shape, axis) for axis in range(2)]
    swap[...] = jnp.where(place[0] % band * band + place[0] // band == place[1], 1.0, 0.0).astype(BF16)
    normed[:, channels:, :] = jnp.ones((band, band, part), BF16)
    power = jnp.zeros((band, part), F32)
    for c in range(channels):
        v = tiles[c].astype(F32)
        power = power + v * v
    inverse = lax.rsqrt(power * (1.0 / channels) + 1e-06)
    for g in range(groups):
        rows = [
            (tiles[c].astype(F32) * inverse * gain[c : c + 1, :]).astype(BF16)
            for c in range(g * band, (g + 1) * band)
        ]
        block = jnp.concatenate(rows, axis=0)
        for lanes in blocks:
            for h in range(0, band, 8):
                swapped = dot(swap[h * band : (h + 8) * band, :], block[:, lanes]).astype(BF16)
                normed[h : h + 8, g * band : (g + 1) * band, lanes] = swapped.reshape(8, band, -1)

    a = math.sqrt(2.0 / math.pi)
    lag = 2
    for r in range(band + lag):
        for lanes in blocks:
            for h in range(0, hidden.shape[1], 256) if r < band else ():
                rows = slice(h, h + 256)
                inner = dot(w_in_t[rows, :depth], normed[r, :, lanes])
                bent = inner * (a + (a * 0.044715) * (inner * inner))
                hidden[r, rows, lanes] = (inner + inner * jnp.tanh(bent)).astype(BF16)
            if r >= lag:
                mixed[r - lag, :, lanes] = (0.5 * dot(w_out_t, hidden[r - lag, :, lanes])).astype(BF16)

    sends = []
    for g in range(groups):
        block = mixed[:, g * band : (g + 1) * band, :].reshape(band * band, part)
        for lanes in blocks:
            for h in range(0, band, 8):
                swapped = dot(swap[h * band : (h + 8) * band, :], block[:, lanes]).astype(BF16)
                out[g * band + h : g * band + h + 8, :, lanes] = swapped.reshape(8, band, -1)
        where = pl.ds(g * band, band)
        sends.append(pltpu.make_async_copy(out.at[where], out_h.at[where], sems.at[g]))
        sends[-1].start()
    for send in sends:
        send.wait()


def spread_kernel(place_of, taps, stepped, mixed, out, rows_0, rows_1, result, sems):
    bands, parts, ch_dev, band, part = stepped.shape
    img = parts * part
    group = 2
    size = group * band
    strips = [slice(n, n + 128) for n in range(0, img, 128)]
    lane = lax.broadcasted_iota(jnp.int32, (size, 128), 1)
    zero = jnp.zeros((len(strips), 8, 128), F32)
    sends = []

    def rows_of(block):
        columns = [jnp.concatenate([block(b, p) for b in range(group)], axis=0) for p in range(parts)]
        return jnp.concatenate(columns, axis=1).astype(F32)

    for ch, padded in ((0, rows_0), (1, rows_1)):
        k = [[taps[i, j, ch : ch + 1, :] for j in range(3)] for i in range(3)]
        padded[:, 0:8, :] = zero
        padded[:, img + 8 : img + 16, :] = zero

        def fill(start):
            x = rows_of(lambda b, p: mixed[place_of[(start + b) * parts + p], ch])
            for n, lanes in enumerate(strips):
                padded[n, start * band + 8 : start * band + 8 + size, :] = x[:, lanes]

        def finish(start):
            at = start * band
            sums = [[], [], []]
            for n in range(len(strips)):
                x = [padded[n, at + 7 + i : at + 7 + i + size, :] for i in range(3)]
                for j in range(3):
                    sums[j].append(k[0][j] * x[0] + k[1][j] * x[1] + k[2][j] * x[2])
            left = pltpu.roll(jnp.concatenate(sums[0], axis=1), 1, 1)
            right = pltpu.roll(jnp.concatenate(sums[2], axis=1), img - 1, 1)
            base = rows_of(lambda b, p: stepped[start + b, p, ch])
            for n, lanes in enumerate(strips):
                low, high = left[:, lanes], right[:, lanes]
                if n == 0:
                    low = jnp.where(lane == 0, 0.0, low)
                if n == len(strips) - 1:
                    high = jnp.where(lane == 127, 0.0, high)
                total = base[:, lanes] + (sums[1][n] + (low + high))
                result[ch, at : at + size, lanes] = total.astype(BF16)
            if (at + size) % 64 == 0:
                rows = pl.ds(at + size - 64, 64)
                sends.append(pltpu.make_async_copy(result.at[ch, rows], out.at[ch, rows], sems.at[len(sends)]))
                sends[-1].start()

        fill(0)
        for start in range(0, bands, group):
            if start + group < bands:
                fill(start + group)
            finish(start)
    for send in sends:
        send.wait()


VMEM = pl.BlockSpec(memory_space=pltpu.VMEM)
SMEM = pl.BlockSpec(memory_space=pltpu.SMEM)
HBM = pl.BlockSpec(memory_space=pltpu.HBM)


def params(mib):
    return pltpu.CompilerParams(vmem_limit_bytes=mib * MIB)


def forth_order(n_rows, n_cols):
    side = n_cols // 2
    up = [half * side + k + c for k in range(0, side, 2) for half, c in ((1, 0), (0, 0), (0, 1), (1, 1))]
    return [row * n_cols + c for row in range(n_rows) for c in up]


def back_order(n_rows, n_cols):
    side = n_cols // 2
    up = [half * side + k for k in range(side) for half in (0, 1)]
    order = []
    for i in range(n_rows):
        order += [(i ^ (i >> 1)) * n_cols + c for c in (reversed(up) if i % 2 else up)]
    return order


def exchange(blocks, order):
    return lax.all_to_all(
        blocks, "all", split_axis=0, concat_axis=0, axis_index_groups=[order], tiled=True
    )


def layers(w_in, b_in, w_out_t, wide):
    rows = []
    for _ in range(3):
        rows.append(lax.reduce_precision(b_in, 8, 7))
        b_in = b_in - rows[-1]
    zeros = jnp.zeros((wide - w_in.shape[0] - 3, w_in.shape[1]), BF16)
    return jnp.concatenate([w_in, jnp.stack(rows).astype(BF16), zeros, w_out_t], axis=0)


def local(n_rows, n_cols, model, dirty, psf, step_size, gain, w_in, b_in, w_out, kernel):
    ch_dev, img, _ = model.shape
    psf_len = psf.shape[1]
    assert ch_dev == 2
    n_dev = n_rows * n_cols
    forth, back = forth_order(n_rows, n_cols), back_order(n_rows, n_cols)
    channels = gain.shape[0]
    hidden = b_in.shape[0]
    part = img * img // (n_dev * BAND)
    parts = img // part
    bands = img // BAND
    table, turned = tables(img, psf_len)
    length = table.shape[0]
    wide = -(-(channels + BAND) // 128) * 128
    blocks = (bands, parts, ch_dev, BAND, part)

    stepped = pl.pallas_call(
        conv_kernel,
        out_shape=jax.ShapeDtypeStruct(blocks, BF16),
        in_specs=[HBM] * 6,
        out_specs=HBM,
        scratch_shapes=[
            pltpu.SMEM(step_size.shape, F32),
            pltpu.VMEM(model.shape, BF16),
            pltpu.VMEM(model.shape, BF16),
            pltpu.VMEM(psf.shape, BF16),
            pltpu.VMEM(table.shape, BF16),
            pltpu.VMEM(turned.shape, BF16),
            pltpu.VMEM((img, 2 * length), BF16),
            pltpu.VMEM((psf_len, 2 * length), BF16),
            pltpu.VMEM((length, 2 * length), F32),
            pltpu.VMEM((length, 2 * length), F32),
            pltpu.VMEM((length, 2 * length), BF16),
            pltpu.VMEM((img, 2 * length), BF16),
            pltpu.VMEM(blocks, BF16),
            pltpu.SemaphoreType.DMA((20,)),
            pltpu.SemaphoreType.DMA((img // 128,)),
        ],
        compiler_params=params(58),
        name="conv",
    )(step_size, model, dirty, psf, table, turned)
    stepped, gain, w_in, b_in, w_out, kernel = lax.optimization_barrier(
        (stepped, gain, w_in, b_in, w_out, kernel)
    )

    def ordered(values, order):
        return jnp.concatenate([values[d * ch_dev : (d + 1) * ch_dev] for d in order], axis=0)

    tiles = exchange(stepped.reshape(n_dev, ch_dev, BAND, part), forth).reshape(channels, BAND, part)

    mixed = pl.pallas_call(
        mix_kernel,
        out_shape=jax.ShapeDtypeStruct((channels, BAND, part), BF16),
        in_specs=[VMEM] * 3,
        out_specs=HBM,
        scratch_shapes=[
            pltpu.VMEM((hidden, wide), BF16),
            pltpu.VMEM((BAND * BAND, BAND * BAND), BF16),
            pltpu.VMEM((BAND, channels + BAND, part), BF16),
            pltpu.VMEM((BAND, hidden, part), BF16),
            pltpu.VMEM((BAND, channels, part), BF16),
            pltpu.VMEM((channels, BAND, part), BF16),
            pltpu.SemaphoreType.DMA((channels // BAND,)),
        ],
        compiler_params=params(24),
        name="mix",
    )(
        jnp.broadcast_to(ordered(gain, forth)[:, None], (channels, part)),
        layers(ordered(w_in, forth), b_in, ordered(w_out.T, back), wide),
        tiles,
    )

    returned = exchange(mixed.reshape(n_dev, ch_dev, BAND, part), back)
    position = lax.axis_index("all").astype(jnp.int32) * ch_dev
    taps = lax.dynamic_slice_in_dim(kernel, position, ch_dev, axis=2)
    taps = jnp.broadcast_to(taps[..., None], (3, 3, ch_dev, 128))
    plane = pltpu.VMEM((img // 128, img + 16, 128), F32)

    return pl.pallas_call(
        functools.partial(spread_kernel, [back.index(device) for device in forth]),
        out_shape=jax.ShapeDtypeStruct((ch_dev, img, img), BF16),
        in_specs=[VMEM] * 3,
        out_specs=HBM,
        scratch_shapes=[
            plane, plane, pltpu.VMEM((ch_dev, img, img), BF16),
            pltpu.SemaphoreType.DMA((ch_dev * img // 64,)),
        ],
        compiler_params=params(24),
        name="spread",
    )(taps, stepped, returned)


def solution(mesh):
    line = Mesh(mesh.devices.reshape(-1), ("all",))
    planes = P("all", None, None)
    return jax.shard_map(
        functools.partial(local, *mesh.devices.shape),
        mesh=line,
        in_specs=(planes, planes, planes, P("all"), P(), P(), P(), P(), P()),
        out_specs=planes,
        check_vma=False,
    )
```
